32 devices in a mesh: section: 8 (over z, y), tensor: 4 (over x, core).
Axes of the slice: x: 2, y: 2, z: 4, core: 2. Of those that a mesh axis runs over, the one named last changes fastest.
Arguments:
- layer_input: bfloat16 [8, 512, 6144], P('section', None, 'tensor'), may hold values from -200 to 200
- grad_input: bfloat16 [8, 512, 6144], P('section', None, 'tensor'), may hold values from -8 to 8
- stashed: bfloat16 [8, 2, 512, 6144], P('section', None, None, 'tensor'), may hold values from -200 to 200
- eviction: int32 [8], P('section'), may hold values from 0 to 1, as said below
- query_gain: float32 [8, 6144], P('section', 'tensor'), may hold values from 0.5 to 2
- key_gain: float32 [8, 6144], P('section', 'tensor'), may hold values from 0.5 to 2
Outputs:
- layer_output: bfloat16 [8, 512, 6144], P('section', None, 'tensor')
- grad_output: bfloat16 [8, 512, 6144], P('section', None, 'tensor')
The draws below stay inside these ranges and needn't reach their ends.
Inputs may be any that keep to these rules, and one draw needn't show every extreme that they name: `eviction`: section 0 always evicts.
All inputs are finite; a program needn't handle non-finite values.
Results may differ from the reference program's by a relative error of at most 0.0078.
Values may be sent and summed in bfloat16 or wider, within the bound.
No kernel may reach another device: no remote copies, remote signals or barrier semaphores. Data moves between devices by JAX's collectives and lax.ppermute only.
A program may use at most 128 MiB of HBM per device.

```python
import math
import jax
import jax.numpy as jnp
from jax import lax

HEADS = 48
HDIM = 128
SEQ = 512
DW = 6144
SECTIONS = 8


def shared_direction(key):
    return jnp.clip(jax.random.normal(jax.random.fold_in(key, 77), (SECTIONS, DW), jnp.float32), -4.0, 4.0)


def column_scale(key):
    rising = jnp.exp(math.log(3.0) * jnp.arange(DW, dtype=jnp.float32) / DW)
    spread = jnp.exp(jax.random.uniform(jax.random.fold_in(key, 78), (DW,), jnp.float32, math.log(0.3), math.log(3.0)))
    return rising * spread / 1.7


def activation_block(key, label, count):
    own_key = jax.random.fold_in(key, label)
    shape = (SECTIONS, count, SEQ, DW)
    noise = jnp.clip(jax.random.normal(jax.random.fold_in(own_key, 1), shape, jnp.float32), -5.0, 5.0)
    weight_common = 0.8
    common = shared_direction(key)[:, None, None, :]
    row_scale = jnp.exp(jax.random.uniform(jax.random.fold_in(own_key, 2), (SECTIONS, count, SEQ, 1), jnp.float32, math.log(0.3), math.log(3.0)))
    values = (noise + weight_common * common) * row_scale * column_scale(key)
    return jnp.clip(values, -200.0, 200.0)


def draw_layer_input(key, part):
    return activation_block(key, 21, 1)[:, 0].astype(jnp.bfloat16)


def draw_stashed(key, part):
    return activation_block(key, 31, 2).astype(jnp.bfloat16)


def draw_grad_input(key, part):
    own_key = jax.random.fold_in(key, 41)
    shape = (SECTIONS, SEQ, DW)
    noise = jnp.clip(jax.random.normal(own_key, shape, jnp.float32), -5.0, 5.0)
    weight_common = 0.8
    values = noise + weight_common * shared_direction(key)[:, None, :]
    return jnp.clip(values, -8.0, 8.0).astype(jnp.bfloat16)


def draw_eviction(key, part):
    plan = jax.random.randint(jax.random.fold_in(key, 51), (SECTIONS,), 0, 2).astype(jnp.int32)
    first = (jnp.arange(SECTIONS) == 0).astype(jnp.int32)
    return jnp.maximum(plan, first).astype(jnp.int32)


def level_of(rng, dims, split, low, largest):
    level = 1.0
    for dim, shards_of in split:
        steps = jax.random.uniform(jax.random.fold_in(jax.random.fold_in(rng, 6), dim), (shards_of,), jnp.float32, low / len(split), largest / len(split))
        level = level * jnp.repeat(jnp.exp(steps), dims[dim] // shards_of).reshape((-1,) + (1,) * (len(dims) - 1 - dim))
    return level


def setup_inputs(seed: int = 0) -> dict:
    streams_of = jax.random.split(jax.random.key(seed), 7)
    layer_input = draw_layer_input(jax.random.fold_in(streams_of[6], 71), 0)
    grad_input = draw_grad_input(jax.random.fold_in(streams_of[6], 71), 0)
    stashed = draw_stashed(jax.random.fold_in(streams_of[6], 71), 0)
    eviction = draw_eviction(jax.random.fold_in(streams_of[6], 71), 0)
    query_gain = jnp.clip(jnp.exp(math.log(2.0) - 1.3862944 * jax.random.uniform(streams_of[4], (SECTIONS, DW), jnp.float32) ** level_of(streams_of[4], (SECTIONS, DW), ((0, 8), (1, 4)), -0.2, 0.2)), 0.5, 2.0)
    key_gain = jnp.clip(jnp.exp(math.log(2.0) - 1.3862944 * jax.random.uniform(streams_of[5], (SECTIONS, DW), jnp.float32) ** level_of(streams_of[5], (SECTIONS, DW), ((0, 8), (1, 4)), -0.2, 0.2)), 0.5, 2.0)
    return {"layer_input": layer_input, "grad_input": grad_input, "stashed": stashed, "eviction": eviction, "query_gain": query_gain, "key_gain": key_gain}


EPSILON = 1e-05

def normalize(activations, gain_query, gain_key):
    widened = activations.astype(jnp.float32)
    factor = lax.rsqrt(lax.optimization_barrier(jnp.mean(widened * widened, axis=-1)) + EPSILON)
    normed = widened * factor[:, None]
    queries = (normed * gain_query).astype(jnp.bfloat16)
    keys_all = (normed * gain_key).astype(jnp.bfloat16)
    values = normed.astype(jnp.bfloat16)
    return (widened, factor, queries, keys_all, values)

def split_heads(matrix):
    return matrix.astype(jnp.float32).reshape(SEQ, HEADS, HDIM)

def attention_weights(query_heads, key_heads):
    scores = jnp.einsum('qhd,khd->hqk', query_heads, key_heads) * (1.0 / math.sqrt(HDIM))
    causal = jnp.arange(SEQ)[:, None] >= jnp.arange(SEQ)[None, :]
    scores = jnp.where(causal[None], scores, -1e+30)
    shifted = scores - lax.optimization_barrier(jnp.max(scores, axis=-1, keepdims=True))
    exponent = jnp.exp(shifted)
    return exponent / lax.optimization_barrier(jnp.sum(exponent, axis=-1, keepdims=True))

def forward_layer(activations, gain_query, gain_key):
    widened, factor, queries, keys_all, values = normalize(activations, gain_query, gain_key)
    weights = attention_weights(split_heads(queries), split_heads(keys_all))
    rounded = weights.astype(jnp.bfloat16).astype(jnp.float32)
    mixed_heads = jnp.einsum('hqk,khd->qhd', rounded, split_heads(values)).reshape(SEQ, DW)
    return (widened + mixed_heads).astype(jnp.bfloat16)

def backward_layer(activations, upstream, gain_query, gain_key):
    widened, factor, queries, keys_all, values = normalize(activations, gain_query, gain_key)
    weights = attention_weights(split_heads(queries), split_heads(keys_all))
    rounded = weights.astype(jnp.bfloat16).astype(jnp.float32)
    grad_heads = split_heads(upstream)
    d_values = jnp.einsum('hqk,qhd->khd', rounded, grad_heads)
    d_weights = jnp.einsum('qhd,khd->hqk', grad_heads, split_heads(values))
    row_delta = lax.optimization_barrier(jnp.sum(weights * d_weights, axis=-1, keepdims=True))
    d_scores = (weights * (d_weights - row_delta) * (1.0 / math.sqrt(HDIM))).astype(jnp.bfloat16).astype(jnp.float32)
    d_queries = jnp.einsum('hqk,khd->qhd', d_scores, split_heads(keys_all))
    d_keys = jnp.einsum('hqk,qhd->khd', d_scores, split_heads(queries))
    d_normed = d_queries.reshape(SEQ, DW) * gain_query + d_keys.reshape(SEQ, DW) * gain_key + d_values.reshape(SEQ, DW)
    inner_sum = lax.optimization_barrier(jnp.sum(d_normed * widened, axis=-1))
    result = upstream.astype(jnp.float32) + factor[:, None] * d_normed - widened * (factor ** 3)[:, None] * inner_sum[:, None] / DW
    return result.astype(jnp.bfloat16)

def reference(layer_input, grad_input, stashed, eviction, query_gain, key_gain):
    half_sections = SECTIONS // 2

    def per_section(index):
        output = forward_layer(layer_input[index], query_gain[index], key_gain[index])
        partner = ((index + half_sections) % SECTIONS).astype(jnp.int32)
        chosen = jnp.where(eviction[index] == 1, stashed[partner, 1], stashed[index, 0])
        result = backward_layer(chosen, grad_input[index], query_gain[index], key_gain[index])
        return (output, result)
    outputs, results = lax.map(per_section, jnp.arange(SECTIONS, dtype=jnp.int32))
    grad_output = jnp.concatenate([results[1:], results[:1]], axis=0)
    return (outputs, grad_output)
```

```python
import functools
import math

import jax
import jax.numpy as jnp
from jax import lax
from jax.experimental import pallas as pl
from jax.experimental.pallas import tpu as pltpu
from jax.sharding import PartitionSpec as P

HDIM = 128
EPSILON = 1e-05
SCALE = 1.0 / math.sqrt(HDIM)
LOG2E = math.log2(math.e)
VMEM = 48 * 1024 * 1024

F32 = jnp.float32
BF16 = jnp.bfloat16


def dot(a, b, contract):
    return lax.dot_general(a, b, ((contract[0], contract[1]), ((), ())), preferred_element_type=F32)


def nt(a, b):
    return dot(a, b, ((1,), (1,)))


def nn(a, b):
    return dot(a, b, ((1,), (0,)))


def block_of(tokens):
    return 256 if tokens % 256 == 0 else tokens


def masked(block, kept):
    return jnp.where(kept, block, -1e30)


def kept_keys(size):
    keys = lax.broadcasted_iota(jnp.int32, (size, size), 0)
    return keys <= lax.broadcasted_iota(jnp.int32, (size, size), 1)


def scores_of(keys, queries, j, size, kept):
    mine = queries[j * size : (j + 1) * size]
    diagonal = masked(nt(keys[j * size : (j + 1) * size], mine), kept)
    if j == 0:
        return [diagonal]
    return [nt(keys[: j * size], mine), diagonal]


def exponents(parts):
    top = functools.reduce(jnp.maximum, [jnp.max(p, axis=0, keepdims=True) for p in parts])
    exps = [jnp.exp2((p - top) * (SCALE * LOG2E)) for p in parts]
    total = sum(jnp.sum(e, axis=0, keepdims=True) for e in exps)
    return exps, total


def stacked(parts):
    return parts[0] if len(parts) == 1 else jnp.concatenate(parts, axis=0)


def normed_head(x, factor, gain_q, gain_k):
    wide = x.astype(F32)
    normed = wide * factor
    return wide, (normed * gain_q).astype(BF16), (normed * gain_k).astype(BF16), normed.astype(BF16)


def column_of(row):
    return jnp.broadcast_to(row, (HDIM, row.shape[1])).T[:, 0:1]


def forward_kernel(heads, x_ref, f_ref, gq_ref, gk_ref, o_ref):
    tokens = x_ref.shape[0]
    size = block_of(tokens)
    kept = kept_keys(size)
    factor = column_of(f_ref[...])
    for h in range(heads):
        lanes = slice(h * HDIM, (h + 1) * HDIM)
        wide, q, k, v = normed_head(x_ref[:, lanes], factor, gq_ref[:, lanes], gk_ref[:, lanes])
        vt = v.T
        for j in range(tokens // size):
            exps, total = exponents(scores_of(k, q, j, size, kept))
            mixed = nn(vt[:, : (j + 1) * size], stacked(exps).astype(BF16)) * (1.0 / total)
            rows = slice(j * size, (j + 1) * size)
            o_ref[rows, lanes] = (wide[rows] + mixed.T).astype(BF16)


def forward(x, factor, gain_q, gain_k, heads):
    tokens, width = x.shape
    lanes = heads * HDIM
    block = pl.BlockSpec((tokens, lanes), lambda i: (0, i))
    gain = pl.BlockSpec((1, lanes), lambda i: (0, i))
    n = width // HDIM
    return pl.pallas_call(
        functools.partial(forward_kernel, heads),
        out_shape=jax.ShapeDtypeStruct(x.shape, BF16),
        grid=(width // lanes,),
        in_specs=[block, pl.BlockSpec((1, tokens), lambda i: (0, 0)), gain, gain],
        out_specs=block,
        compiler_params=pltpu.CompilerParams(vmem_limit_bytes=VMEM),
        cost_estimate=pl.CostEstimate(
            flops=4 * n * tokens * tokens * HDIM, bytes_accessed=4 * tokens * width,
            transcendentals=n * tokens * tokens,
        ),
        name="forward",
    )(x, factor, gain_q, gain_k)


def backward_head(x, g, factor, gain_q, gain_k):
    tokens = x.shape[0]
    size = block_of(tokens)
    kept = kept_keys(size)
    wide, q, k, v = normed_head(x, factor, gain_q, gain_k)
    kt = k.T
    blocks = tokens // size
    d_q = []
    d_k = [None] * blocks
    d_v = [None] * blocks
    for j in range(blocks):
        rows = slice(j * size, (j + 1) * size)
        exps, total = exponents(scores_of(k, q, j, size, kept))
        inverse = 1.0 / total
        weights = [e * inverse for e in exps]
        grads = [nt(v[: j * size], g[rows])] if j else []
        grads.append(nt(v[rows], g[rows]))
        delta = sum(jnp.sum(w * d, axis=0, keepdims=True) for w, d in zip(weights, grads))
        scores = stacked([(w * ((d - delta) * SCALE)).astype(BF16) for w, d in zip(weights, grads)])
        rounded = stacked([w.astype(BF16) for w in weights])
        d_q.append(nn(kt[:, : (j + 1) * size], scores).T)
        part_k = nn(scores, q[rows])
        part_v = nn(rounded, g[rows])
        for i in range(j + 1):
            mine = slice(i * size, (i + 1) * size)
            d_k[i] = part_k[mine] if d_k[i] is None else d_k[i] + part_k[mine]
            d_v[i] = part_v[mine] if d_v[i] is None else d_v[i] + part_v[mine]
    d_normed = stacked(d_q) * gain_q + stacked(d_k) * gain_k + stacked(d_v)
    return wide, d_normed


def backward_kernel(heads, x_ref, g_ref, f_ref, gq_ref, gk_ref, a_ref, inner_ref):
    factor = column_of(f_ref[...])
    part = None
    for h in range(heads):
        lanes = slice(h * HDIM, (h + 1) * HDIM)
        g = g_ref[:, lanes]
        wide, d_normed = backward_head(x_ref[:, lanes], g, factor, gq_ref[:, lanes], gk_ref[:, lanes])
        a_ref[:, lanes] = g.astype(F32) + factor * d_normed
        product = d_normed * wide
        part = product if part is None else part + product
    inner = jnp.sum(part.T, axis=0, keepdims=True)

    @pl.when(pl.program_id(0) == 0)
    def _():
        inner_ref[...] = inner

    @pl.when(pl.program_id(0) > 0)
    def _():
        inner_ref[...] += inner


def backward(x, g, factor, gain_q, gain_k, heads):
    tokens, width = x.shape
    lanes = heads * HDIM
    block = pl.BlockSpec((tokens, lanes), lambda i: (0, i))
    gain = pl.BlockSpec((1, lanes), lambda i: (0, i))
    row = pl.BlockSpec((1, tokens), lambda i: (0, 0))
    n = width // HDIM
    return pl.pallas_call(
        functools.partial(backward_kernel, heads),
        out_shape=(jax.ShapeDtypeStruct(x.shape, F32), jax.ShapeDtypeStruct((1, tokens), F32)),
        grid=(width // lanes,),
        in_specs=[block, block, row, gain, gain],
        out_specs=(block, row),
        compiler_params=pltpu.CompilerParams(vmem_limit_bytes=VMEM),
        cost_estimate=pl.CostEstimate(
            flops=10 * n * tokens * tokens * HDIM, bytes_accessed=8 * tokens * width,
            transcendentals=n * tokens * tokens,
        ),
        name="backward",
    )(x, g, factor, gain_q, gain_k)


def passed_along(x, axis, by):
    size = lax.axis_size(axis)
    return lax.ppermute(x, axis, [(i, (i + by) % size) for i in range(size)])


def squares(x):
    wide = x.astype(F32)
    return jnp.sum(wide * wide, axis=-1)[None]


def local(width_all, layer_input, grad_input, stashed, eviction, query_gain, key_gain):
    half_sections = lax.axis_size("section") // 2
    current = layer_input[0]
    upstream = grad_input[0]
    heads_here = current.shape[1] // HDIM
    chunks = next(c for c in (4, 3, 2, 1) if heads_here % c == 0)
    heads = heads_here // chunks
    step = heads * HDIM
    evicted = eviction[0] == 1
    parts = [slice(c * step, (c + 1) * step) for c in range(chunks)]
    fetched = [passed_along(stashed[0, 1][:, p], "section", -half_sections) for p in parts]
    totals = lax.psum(
        jnp.concatenate([squares(current), squares(stashed[0, 0]), squares(stashed[0, 1])], axis=0), "tensor"
    )
    fetched_total = passed_along(totals[2:3], "section", -half_sections)
    chosen_total = jnp.where(evicted, fetched_total, totals[1:2])
    forward_factor = lax.rsqrt(totals[0:1] / width_all + EPSILON)
    factor = lax.rsqrt(chosen_total / width_all + EPSILON)
    output = forward(current, forward_factor, query_gain, key_gain, heads)
    terms = []
    inner = 0.0
    for p, f in zip(parts, fetched):
        x = jnp.where(evicted, f, stashed[0, 0][:, p])
        a, part = backward(x, upstream[:, p], factor, query_gain[:, p], key_gain[:, p], heads)
        terms.append((x, a))
        inner = inner + part
    inner = lax.psum(inner, "tensor")
    row = (factor**3 * inner / width_all).T
    passed = [passed_along((a - x.astype(F32) * row).astype(BF16), "section", -1) for x, a in terms]
    return (output[None], jnp.concatenate(passed, axis=1)[None])


def solution(mesh):
    placed = (
        P("section", None, "tensor"),
        P("section", None, "tensor"),
        P("section", None, None, "tensor"),
        P("section"),
        P("section", "tensor"),
        P("section", "tensor"),
    )

    def whole(layer_input, *others):
        return jax.shard_map(
            functools.partial(local, layer_input.shape[-1]),
            mesh=mesh,
            in_specs=placed,
            out_specs=(P("section", None, "tensor"), P("section", None, "tensor")),
            check_vma=False,
        )(layer_input, *others)

    return whole
```

```python
import functools
import math

import jax
import jax.numpy as jnp
from jax import lax
from jax.experimental import pallas as pl
from jax.experimental.pallas import tpu as pltpu
from jax.sharding import PartitionSpec as P

HDIM = 128
EPSILON = 1e-05
SCALE = 1.0 / math.sqrt(HDIM)
LOG2E = math.log2(math.e)
VMEM = 48 * 1024 * 1024

F32 = jnp.float32
BF16 = jnp.bfloat16


def dot(a, b, contract):
    return lax.dot_general(a, b, ((contract[0], contract[1]), ((), ())), preferred_element_type=F32)


def nt(a, b):
    return dot(a, b, ((1,), (1,)))


def nn(a, b):
    return dot(a, b, ((1,), (0,)))


def block_of(tokens):
    return 256 if tokens % 256 == 0 else tokens


def masked(block, kept):
    return jnp.where(kept, block, -1e30)


def kept_keys(size):
    keys = lax.broadcasted_iota(jnp.int32, (size, size), 0)
    return keys <= lax.broadcasted_iota(jnp.int32, (size, size), 1)


def scores_of(keys, queries, j, size, kept):
    mine = queries[j * size : (j + 1) * size]
    diagonal = masked(nt(keys[j * size : (j + 1) * size], mine), kept)
    if j == 0:
        return [diagonal]
    return [nt(keys[: j * size], mine), diagonal]


def exponents(parts):
    top = functools.reduce(jnp.maximum, [jnp.max(p, axis=0, keepdims=True) for p in parts])
    exps = [jnp.exp2((p - top) * (SCALE * LOG2E)) for p in parts]
    total = sum(jnp.sum(e, axis=0, keepdims=True) for e in exps)
    return exps, total


def stacked(parts):
    return parts[0] if len(parts) == 1 else jnp.concatenate(parts, axis=0)


def normed_head(x, factor, gain_q, gain_k):
    wide = x.astype(F32)
    normed = wide * factor
    return wide, (normed * gain_q).astype(BF16), (normed * gain_k).astype(BF16), normed.astype(BF16)


def column_of(row):
    return jnp.broadcast_to(row, (HDIM, row.shape[1])).T[:, 0:1]


def forward_kernel(heads, x_ref, f_ref, gq_ref, gk_ref, o_ref):
    tokens = x_ref.shape[0]
    size = block_of(tokens)
    kept = kept_keys(size)
    factor = column_of(f_ref[...])
    for h in range(heads):
        lanes = slice(h * HDIM, (h + 1) * HDIM)
        wide, q, k, v = normed_head(x_ref[:, lanes], factor, gq_ref[:, lanes], gk_ref[:, lanes])
        vt = v.T
        for j in range(tokens // size):
            exps, total = exponents(scores_of(k, q, j, size, kept))
            mixed = nn(vt[:, : (j + 1) * size], stacked(exps).astype(BF16)) * (1.0 / total)
            rows = slice(j * size, (j + 1) * size)
            o_ref[rows, lanes] = (wide[rows] + mixed.T).astype(BF16)


def forward(x, factor, gain_q, gain_k, heads):
    tokens, width = x.shape
    lanes = heads * HDIM
    block = pl.BlockSpec((tokens, lanes), lambda i: (0, i))
    gain = pl.BlockSpec((1, lanes), lambda i: (0, i))
    n = width // HDIM
    return pl.pallas_call(
        functools.partial(forward_kernel, heads),
        out_shape=jax.ShapeDtypeStruct(x.shape, BF16),
        grid=(width // lanes,),
        in_specs=[block, pl.BlockSpec((1, tokens), lambda i: (0, 0)), gain, gain],
        out_specs=block,
        compiler_params=pltpu.CompilerParams(vmem_limit_bytes=VMEM),
        cost_estimate=pl.CostEstimate(
            flops=4 * n * tokens * tokens * HDIM, bytes_accessed=4 * tokens * width,
            transcendentals=n * tokens * tokens,
        ),
        name="forward",
    )(x, factor, gain_q, gain_k)


def backward_head(x, g, factor, gain_q, gain_k):
    tokens = x.shape[0]
    size = block_of(tokens)
    kept = kept_keys(size)
    wide, q, k, v = normed_head(x, factor, gain_q, gain_k)
    kt = k.T
    blocks = tokens // size
    d_q = []
    d_k = [None] * blocks
    d_v = [None] * blocks
    for j in range(blocks):
        rows = slice(j * size, (j + 1) * size)
        exps, total = exponents(scores_of(k, q, j, size, kept))
        inverse = 1.0 / total
        weights = [e * inverse for e in exps]
        grads = [nt(v[: j * size], g[rows])] if j else []
        grads.append(nt(v[rows], g[rows]))
        delta = sum(jnp.sum(w * d, axis=0, keepdims=True) for w, d in zip(weights, grads))
        scores = stacked([(w * ((d - delta) * SCALE)).astype(BF16) for w, d in zip(weights, grads)])
        rounded = stacked([w.astype(BF16) for w in weights])
        d_q.append(nn(kt[:, : (j + 1) * size], scores).T)
        part_k = nn(scores, q[rows])
        part_v = nn(rounded, g[rows])
        for i in range(j + 1):
            mine = slice(i * size, (i + 1) * size)
            d_k[i] = part_k[mine] if d_k[i] is None else d_k[i] + part_k[mine]
            d_v[i] = part_v[mine] if d_v[i] is None else d_v[i] + part_v[mine]
    d_normed = stacked(d_q) * gain_q + stacked(d_k) * gain_k + stacked(d_v)
    return wide, d_normed


def backward_kernel(heads, pick_ref, x_ref, g1_ref, g2_ref, f_ref, gq_ref, gk_ref, *rest):
    a_ref, inner_ref = rest[-2:]
    first = pl.program_id(0) == 0

    @pl.when(jnp.logical_and(first, pick_ref[0] == 0))
    def _():
        inner_ref[...] = jnp.zeros_like(inner_ref)

    @pl.when(pick_ref[0] == 1)
    def _():
        factor = column_of(f_ref[...])
        other = pick_ref[1] == 1
        part = None
        for h in range(heads):
            lanes = slice(h * HDIM, (h + 1) * HDIM)
            g = jnp.where(other, g2_ref[:, lanes], g1_ref[:, lanes])
            wide, d_normed = backward_head(x_ref[:, lanes], g, factor, gq_ref[:, lanes], gk_ref[:, lanes])
            a_ref[:, lanes] = g.astype(F32) + factor * d_normed
            product = d_normed * wide
            part = product if part is None else part + product
        inner = jnp.sum(part.T, axis=0, keepdims=True)

        @pl.when(first)
        def _():
            inner_ref[...] = inner

        @pl.when(jnp.logical_not(first))
        def _():
            inner_ref[...] += inner


def backward(pick, x, g1, g2, factor, gain_q, gain_k, heads, steps, starts, sofar=None, after=()):
    tokens = x.shape[0]
    width = gain_q.shape[1]
    lanes = heads * HDIM
    x0, g10, g20, c0 = starts
    at = lambda first: pl.BlockSpec((tokens, lanes), lambda i, pick: (0, first + i))
    gain = pl.BlockSpec((1, lanes), lambda i, pick: (0, c0 + i))
    row = pl.BlockSpec((1, tokens), lambda i, pick: (0, 0))
    n = heads * steps
    extra = (() if sofar is None else (sofar,)) + tuple(after)
    return pl.pallas_call(
        functools.partial(backward_kernel, heads),
        out_shape=(jax.ShapeDtypeStruct((tokens, width), F32), jax.ShapeDtypeStruct((1, tokens), F32)),
        grid_spec=pltpu.PrefetchScalarGridSpec(
            num_scalar_prefetch=1,
            grid=(steps,),
            in_specs=[at(x0), at(g10), at(g20), row, gain, gain] + [pl.BlockSpec(memory_space=pl.ANY)] * len(extra),
            out_specs=(at(c0), row),
        ),
        input_output_aliases={} if sofar is None else {7: 0},
        compiler_params=pltpu.CompilerParams(vmem_limit_bytes=VMEM),
        cost_estimate=pl.CostEstimate(
            flops=10 * n * tokens * tokens * HDIM, bytes_accessed=10 * tokens * n * HDIM,
            transcendentals=n * tokens * tokens,
        ),
        name="backward",
    )(pick, x, g1, g2, factor, gain_q, gain_k, *extra)


def choose_kernel(mode_ref, own_ref, near_ref, far_ref, held_ref, next_ref, *rest):
    sent_ref = rest[-2]
    for m, ref in enumerate((own_ref, near_ref, far_ref, held_ref)):

        @pl.when(mode_ref[0] == m)
        def _():
            sent_ref[...] = ref[...]

    rest[-1][...] = next_ref[...]


def choose(mode, stash, near, far, c, step, coming, after=()):
    tokens = near.shape[0]
    block = (tokens, step)
    whole = lambda at: pl.BlockSpec(block, lambda i, mode: (0, at))
    of_stash = lambda which, at: pl.BlockSpec((None, None, tokens, step), lambda i, mode: (0, which, 0, at))
    return pl.pallas_call(
        choose_kernel,
        out_shape=[jax.ShapeDtypeStruct(block, BF16)] * 2,
        grid_spec=pltpu.PrefetchScalarGridSpec(
            num_scalar_prefetch=1,
            grid=(1,),
            in_specs=[of_stash(0, c), whole(0), whole(c), of_stash(1, c), of_stash(1, coming)]
            + [pl.BlockSpec(memory_space=pl.ANY)] * len(after),
            out_specs=[whole(0)] * 2,
        ),
        compiler_params=pltpu.CompilerParams(vmem_limit_bytes=VMEM),
        cost_estimate=pl.CostEstimate(flops=0, bytes_accessed=14 * tokens * step, transcendentals=0),
        name="choose",
    )(mode, stash, near, far, stash, stash, *after)


def finish_kernel(chunks, pieces, pick_ref, a_ref, row_ref, *rest):
    o_ref = rest[-1]
    xs, slots = rest[:chunks], rest[chunks : chunks + pieces]
    row = column_of(row_ref[...])
    lanes = xs[0].shape[1]
    each = chunks // pieces
    for c in range(chunks):

        @pl.when(jnp.logical_and(pl.program_id(0) == c, pick_ref[0] == 0))
        def _():
            o_ref[...] = (a_ref[...] - xs[c][...].astype(F32) * row).astype(BF16)

        @pl.when(jnp.logical_and(pl.program_id(0) == c, pick_ref[0] == 1))
        def _():
            at = (c % each) * lanes
            o_ref[...] = slots[c // each][:, at : at + lanes]


def finish(pick, a, row, xs, slots):
    tokens, width = a.shape
    chunks = len(xs)
    lanes = width // chunks
    block = pl.BlockSpec((tokens, lanes), lambda i, pick: (0, i))
    still = lambda x: pl.BlockSpec(x.shape, lambda i, pick: (0, 0))
    return pl.pallas_call(
        functools.partial(finish_kernel, chunks, len(slots)),
        out_shape=jax.ShapeDtypeStruct(a.shape, BF16),
        grid_spec=pltpu.PrefetchScalarGridSpec(
            num_scalar_prefetch=1,
            grid=(chunks,),
            in_specs=[block, still(row)] + [still(x) for x in xs] + [still(x) for x in slots],
            out_specs=block,
        ),
        compiler_params=pltpu.CompilerParams(vmem_limit_bytes=VMEM),
        cost_estimate=pl.CostEstimate(flops=2 * a.size, bytes_accessed=10 * a.size, transcendentals=0),
        name="finish",
    )(pick, a, row, *xs, *slots)


def squares(x):
    wide = x.astype(F32)
    return jnp.sum(wide * wide, axis=-1)[None]


def send(x, pairs):
    return lax.ppermute(x, "section", pairs)


def local(width_all, layer_input, grad_input, stashed, eviction, query_gain, key_gain):
    n = lax.axis_size("section")
    half = n // 2
    special = (0, half)
    me = lax.axis_index("section")
    is_special = jnp.logical_or(me == 0, me == half)
    evicted = eviction[0] == 1
    word = lambda *flags: jnp.stack([f.astype(jnp.int32) for f in flags])

    prior = [(s, (s - 1) % n) for s in range(n)]
    inside = [(s, s - 1) for s in range(n) if s not in special]
    within = inside + [(0, half - 1), (half, n - 1)]
    across = [(half, half - 1), (0, n - 1)]
    partner = [(s, (s + half) % n) for s in range(n)]
    near_pairs = [p for p in partner if p[0] % 2 == 1]
    far_pairs = [p for p in partner if p[0] % 2 == 0 and p[0] not in special]

    current = layer_input[0]
    upstream = grad_input[0]
    tokens, width = current.shape
    heads_here = width // HDIM
    chunks = next(c for c in (4, 3, 2, 1) if heads_here % c == 0)
    pieces = 2 if chunks % 2 == 0 else 1
    heads = heads_here // chunks
    step = heads * HDIM
    held = stashed[0, 1]
    part = lambda x, c: x[:, c * step : (c + 1) * step]

    near = {c: send(part(held, c), near_pairs) for c in range(min(2, chunks))}
    far = send(held, far_pairs)
    arrived = send(upstream, inside)

    totals = lax.psum(
        jnp.concatenate([squares(current), squares(stashed[0, 0]), squares(held)], axis=0), "tensor"
    )
    factor_of = lambda total: lax.rsqrt(total / width_all + EPSILON)

    kept_here = jnp.logical_and(me == half, jnp.logical_not(evicted))
    own_factor = factor_of(totals[1:2])
    own_a, own_inner = backward(
        word(kept_here, kept_here), stashed[0, 0], upstream, upstream, own_factor, query_gain, key_gain,
        heads, chunks, (0, 0, 0, 0),
    )
    own_inner = lax.psum(own_inner, "tensor")
    own_row = (own_factor**3 * own_inner / width_all).T
    slot = jnp.where(kept_here, (own_a - stashed[0, 0].astype(F32) * own_row).astype(BF16), upstream)
    wide = width // pieces
    slots = [send(slot[:, p * wide : (p + 1) * wide], across) for p in range(pieces)]

    fetched_total = send(totals[2:3], partner)
    chosen_total = jnp.where(evicted, fetched_total, totals[1:2])
    flag = jnp.broadcast_to(eviction[0].astype(F32), (1, HDIM))
    told = send(jnp.concatenate([chosen_total, query_gain, key_gain, flag], axis=1), prior)
    factor = factor_of(told[:, :tokens])
    gain_q = told[:, tokens : tokens + width]
    gain_k = told[:, tokens + width : tokens + 2 * width]
    after_evicted = told[0, tokens + 2 * width] == 1.0

    output = forward(current, factor_of(totals[0:1]), query_gain, key_gain, heads)

    mode = jnp.where(is_special, 3, jnp.where(evicted, jnp.where(me % 2 == 1, 1, 2), 0)).astype(jnp.int32)[None]
    crossed = jnp.logical_or(me == half - 1, me == n - 1)
    take = word(jnp.bool_(True), crossed)
    xs = []
    a, inner = None, 0.0
    for c in range(chunks):
        coming = min(c + 2, chunks - 1)
        sent, following = choose(mode, stashed, near[c], far, c, step, coming)
        if c + 2 < chunks:
            near[c + 2] = send(following, near_pairs)
        xs.append(send(sent, within))
    each = chunks // pieces
    for c in range(chunks):
        a, share = backward(
            take, xs[c], arrived, slots[c // each], factor, gain_q, gain_k, heads, 1, (0, c, c % each, c), a
        )
        inner = inner + share
    inner = lax.psum(inner, "tensor")
    done = word(jnp.logical_and(me == half - 1, jnp.logical_not(after_evicted)))
    result = finish(done, a, factor**3 * inner / width_all, xs, slots)
    return (output[None], result[None])


def solution(mesh):
    placed = (
        P("section", None, "tensor"),
        P("section", None, "tensor"),
        P("section", None, None, "tensor"),
        P("section"),
        P("section", "tensor"),
        P("section", "tensor"),
    )

    def whole(layer_input, *others):
        return jax.shard_map(
            functools.partial(local, layer_input.shape[-1]),
            mesh=mesh,
            in_specs=placed,
            out_specs=(P("section", None, "tensor"), P("section", None, "tensor")),
            check_vma=False,
        )(layer_input, *others)

    return whole
```

```python
import functools
import math

import jax
import jax.numpy as jnp
from jax import lax
from jax.experimental import pallas as pl
from jax.experimental.pallas import tpu as pltpu
from jax.sharding import PartitionSpec as P

HDIM = 128
EPSILON = 1e-05
SCALE = 1.0 / math.sqrt(HDIM)
LOG2E = math.log2(math.e)
VMEM = 32 * 1024 * 1024

F32 = jnp.float32
BF16 = jnp.bfloat16


def dot(a, b, contract):
    return lax.dot_general(a, b, ((contract[0], contract[1]), ((), ())), preferred_element_type=F32)


def nt(a, b):
    return dot(a, b, ((1,), (1,)))


def nn(a, b):
    return dot(a, b, ((1,), (0,)))


def block_of(tokens):
    return 256 if tokens % 256 == 0 else tokens


def masked(block, kept):
    return jnp.where(kept, block, -1e30)


def kept_keys(size):
    keys = lax.broadcasted_iota(jnp.int32, (size, size), 0)
    return keys <= lax.broadcasted_iota(jnp.int32, (size, size), 1)


def scores_of(keys, queries, j, size, kept):
    mine = queries[j * size : (j + 1) * size]
    diagonal = masked(nt(keys[j * size : (j + 1) * size], mine), kept)
    if j == 0:
        return [diagonal]
    return [nt(keys[: j * size], mine), diagonal]


def exponents(parts):
    top = functools.reduce(jnp.maximum, [jnp.max(p, axis=0, keepdims=True) for p in parts])
    exps = [jnp.exp2((p - top) * (SCALE * LOG2E)) for p in parts]
    total = sum(jnp.sum(e, axis=0, keepdims=True) for e in exps)
    return exps, total


def stacked(parts):
    return parts[0] if len(parts) == 1 else jnp.concatenate(parts, axis=0)


def normed_head(x, factor, gain_q, gain_k):
    wide = x.astype(F32)
    normed = wide * factor
    return wide, (normed * gain_q).astype(BF16), (normed * gain_k).astype(BF16), normed.astype(BF16)


def column_of(row):
    return jnp.broadcast_to(row, (HDIM, row.shape[1])).T[:, 0:1]


def forward_kernel(heads, x_ref, f_ref, gq_ref, gk_ref, *rest):
    o_ref = rest[-1]
    tokens = x_ref.shape[0]
    size = block_of(tokens)
    kept = kept_keys(size)
    factor = column_of(f_ref[...])
    for h in range(heads):
        lanes = slice(h * HDIM, (h + 1) * HDIM)
        wide, q, k, v = normed_head(x_ref[:, lanes], factor, gq_ref[:, lanes], gk_ref[:, lanes])
        vt = v.T
        for j in range(tokens // size):
            exps, total = exponents(scores_of(k, q, j, size, kept))
            mixed = nn(vt[:, : (j + 1) * size], stacked(exps).astype(BF16)) * (1.0 / total)
            rows = slice(j * size, (j + 1) * size)
            o_ref[rows, lanes] = (wide[rows] + mixed.T).astype(BF16)


def forward(x, factor, gain_q, gain_k, heads, after=()):
    tokens, width = x.shape
    lanes = heads * HDIM
    block = pl.BlockSpec((tokens, lanes), lambda i: (0, i))
    gain = pl.BlockSpec((1, lanes), lambda i: (0, i))
    return pl.pallas_call(
        functools.partial(forward_kernel, heads),
        out_shape=jax.ShapeDtypeStruct(x.shape, BF16),
        grid=(width // lanes,),
        in_specs=[block, pl.BlockSpec((1, tokens), lambda i: (0, 0)), gain, gain]
        + [pl.BlockSpec(memory_space=pl.ANY)] * len(after),
        out_specs=block,
        compiler_params=pltpu.CompilerParams(vmem_limit_bytes=VMEM),
        name="forward",
    )(x, factor, gain_q, gain_k, *after)


def backward_head(x, g, factor, gain_q, gain_k):
    tokens = x.shape[0]
    size = block_of(tokens)
    kept = kept_keys(size)
    wide, q, k, v = normed_head(x, factor, gain_q, gain_k)
    kt = k.T
    blocks = tokens // size
    d_q = []
    d_k = [None] * blocks
    d_v = [None] * blocks
    for j in range(blocks):
        rows = slice(j * size, (j + 1) * size)
        exps, total = exponents(scores_of(k, q, j, size, kept))
        inverse = 1.0 / total
        weights = [e * inverse for e in exps]
        grads = [nt(v[: j * size], g[rows])] if j else []
        grads.append(nt(v[rows], g[rows]))
        delta = sum(jnp.sum(w * d, axis=0, keepdims=True) for w, d in zip(weights, grads))
        scores = stacked([(w * ((d - delta) * SCALE)).astype(BF16) for w, d in zip(weights, grads)])
        rounded = stacked([w.astype(BF16) for w in weights])
        d_q.append(nn(kt[:, : (j + 1) * size], scores).T)
        part_k = nn(scores, q[rows])
        part_v = nn(rounded, g[rows])
        for i in range(j + 1):
            mine = slice(i * size, (i + 1) * size)
            d_k[i] = part_k[mine] if d_k[i] is None else d_k[i] + part_k[mine]
            d_v[i] = part_v[mine] if d_v[i] is None else d_v[i] + part_v[mine]
    d_normed = stacked(d_q) * gain_q + stacked(d_k) * gain_k + stacked(d_v)
    return wide, d_normed


def chosen(index, refs, at):
    value = refs[0][at]
    for i, ref in enumerate(refs[1:]):
        value = jnp.where(index == i + 1, ref[at], value)
    return value


def backward_kernel(heads, n_x, n_g, pick_ref, *refs):
    x_refs, g_refs = refs[:n_x], refs[n_x : n_x + n_g]
    f_ref, gq_ref, gk_ref = refs[n_x + n_g : n_x + n_g + 3]
    a_ref, x_ref, inner_ref = refs[-3:]
    first = pl.program_id(0) == 0

    @pl.when(jnp.logical_and(first, pick_ref[0] == 0))
    def _():
        inner_ref[...] = jnp.zeros_like(inner_ref)

    @pl.when(pick_ref[0] == 1)
    def _():
        factor = column_of(f_ref[...])
        part = None
        for h in range(heads):
            lanes = slice(h * HDIM, (h + 1) * HDIM)
            here = (slice(None), lanes)
            x = chosen(pick_ref[1], x_refs, here)
            g = chosen(pick_ref[2], g_refs, here)
            wide, d_normed = backward_head(x, g, factor, gq_ref[:, lanes], gk_ref[:, lanes])
            a_ref[:, lanes] = g.astype(F32) + factor * d_normed
            x_ref[:, lanes] = x
            product = d_normed * wide
            part = product if part is None else part + product
        inner = jnp.sum(part.T, axis=0, keepdims=True)

        @pl.when(first)
        def _():
            inner_ref[...] = inner

        @pl.when(jnp.logical_not(first))
        def _():
            inner_ref[...] += inner


def backward(pick, xs, gs, factor, gain_q, gain_k, heads, steps, first, sofar=(), after=()):
    tokens = xs[0][0].shape[0]
    width = gain_q.shape[1]
    lanes = heads * HDIM
    at = lambda start: pl.BlockSpec((tokens, lanes), lambda i, pick: (0, start + i))
    gain = pl.BlockSpec((1, lanes), lambda i, pick: (0, first + i))
    row = pl.BlockSpec((1, tokens), lambda i, pick: (0, 0))
    extra = tuple(sofar) + tuple(after)
    before = 1 + len(xs) + len(gs) + 3
    return pl.pallas_call(
        functools.partial(backward_kernel, heads, len(xs), len(gs)),
        out_shape=(
            jax.ShapeDtypeStruct((tokens, width), F32),
            jax.ShapeDtypeStruct((tokens, width), BF16),
            jax.ShapeDtypeStruct((1, tokens), F32),
        ),
        grid_spec=pltpu.PrefetchScalarGridSpec(
            num_scalar_prefetch=1,
            grid=(steps,),
            in_specs=[at(b) for _, b in (*xs, *gs)] + [row, gain, gain]
            + [pl.BlockSpec(memory_space=pl.ANY)] * len(extra),
            out_specs=(at(first), at(first), row),
        ),
        input_output_aliases={before: 0, before + 1: 1} if sofar else {},
        compiler_params=pltpu.CompilerParams(vmem_limit_bytes=VMEM),
        name="backward",
    )(pick, *[x for x, _ in xs], *[g for g, _ in gs], factor, gain_q, gain_k, *extra)


def choose_kernel(mode_ref, *refs):
    for m, ref in enumerate(refs[:2]):

        @pl.when(mode_ref[0] == m)
        def _():
            refs[-2][...] = ref[...]

    refs[-1][...] = refs[2][...]


def choose(mode, stash, fetched, start, step, coming, after=()):
    tokens = fetched.shape[0]
    block = (tokens, step)
    whole = lambda at: pl.BlockSpec(block, lambda i, mode: (0, at))
    of_stash = lambda which, at: pl.BlockSpec((None, None, tokens, step), lambda i, mode: (0, which, 0, at))
    return pl.pallas_call(
        choose_kernel,
        out_shape=[jax.ShapeDtypeStruct(block, BF16)] * 2,
        grid_spec=pltpu.PrefetchScalarGridSpec(
            num_scalar_prefetch=1,
            grid=(1,),
            in_specs=[of_stash(0, start), whole(start), of_stash(1, coming)]
            + [pl.BlockSpec(memory_space=pl.ANY)] * len(after),
            out_specs=[whole(0)] * 2,
        ),
        compiler_params=pltpu.CompilerParams(vmem_limit_bytes=VMEM),
        name="choose",
    )(mode, stash, fetched, stash, *after)


def finish_kernel(pick_ref, a_ref, x_ref, row_ref, other_ref, o_ref):
    row = column_of(row_ref[...])

    @pl.when(pick_ref[0] == 0)
    def _():
        o_ref[...] = (a_ref[...] - x_ref[...].astype(F32) * row).astype(BF16)

    @pl.when(pick_ref[0] == 1)
    def _():
        o_ref[...] = other_ref[...]


def finish(pick, a, x, row, other, lanes):
    tokens, width = a.shape
    block = pl.BlockSpec((tokens, lanes), lambda i, pick: (0, i))
    return pl.pallas_call(
        finish_kernel,
        out_shape=jax.ShapeDtypeStruct(a.shape, BF16),
        grid_spec=pltpu.PrefetchScalarGridSpec(
            num_scalar_prefetch=1,
            grid=(width // lanes,),
            in_specs=[block, block, pl.BlockSpec((1, tokens), lambda i, pick: (0, 0)), block],
            out_specs=block,
        ),
        compiler_params=pltpu.CompilerParams(vmem_limit_bytes=VMEM),
        name="finish",
    )(pick, a, x, row, other)


def squares_kernel(current_ref, stash_ref, o_ref):
    def total(x):
        wide = x.astype(F32)
        square = wide * wide
        sums = sum(square[:, i : i + HDIM] for i in range(0, square.shape[1], HDIM))
        return jnp.sum(sums.T, axis=0, keepdims=True)

    rows = jnp.concatenate([total(current_ref[...]), total(stash_ref[0]), total(stash_ref[1])], axis=0)

    @pl.when(pl.program_id(0) == 0)
    def _():
        o_ref[...] = rows

    @pl.when(pl.program_id(0) > 0)
    def _():
        o_ref[...] += rows


def squares(current, stash, lanes):
    tokens, width = current.shape
    return pl.pallas_call(
        squares_kernel,
        out_shape=jax.ShapeDtypeStruct((3, tokens), F32),
        grid=(width // lanes,),
        in_specs=[
            pl.BlockSpec((tokens, lanes), lambda i: (0, i)),
            pl.BlockSpec((None, 2, tokens, lanes), lambda i: (0, 0, 0, i)),
        ],
        out_specs=pl.BlockSpec((3, tokens), lambda i: (0, 0)),
        compiler_params=pltpu.CompilerParams(vmem_limit_bytes=VMEM),
        name="squares",
    )(current, stash)


def send(x, pairs):
    return lax.ppermute(x, "section", pairs)


def local(width_all, layer_input, grad_input, stashed, eviction, query_gain, key_gain):
    n = lax.axis_size("section")
    half = n // 2
    special = (0, half)
    me = lax.axis_index("section")
    evicted = eviction[0] == 1
    word = lambda *flags: jnp.stack([jnp.asarray(f).astype(jnp.int32) for f in flags])

    prior = [(s, (s - 1) % n) for s in range(n)]
    inside = [(s, s - 1) for s in range(n) if s not in special]
    partner = [(s, (s + half) % n) for s in range(n)]
    to_partner = [p for p in partner if p[0] not in special]
    within = inside + [(half, n - 1), (0, half - 1)]
    direct = [((s + half) % n, s - 1) for s in range(n) if s not in special]

    current = layer_input[0]
    upstream = grad_input[0]
    tokens, width = current.shape
    heads_here = width // HDIM
    step = width // 3
    heads = heads_here // 3
    own, held = stashed[0, 0], stashed[0, 1]
    piece = lambda x, c: x[:, c * step : (c + 1) * step]

    is_special = jnp.logical_or(me == 0, me == half)
    fetched = send(held[:, : 2 * step], to_partner)
    early = send(jnp.where(is_special, held, upstream), within)
    kept = send(piece(own, 2), inside)
    upward = send(upstream, [(0, n - 1)])

    totals = lax.psum(squares(current, stashed, step), "tensor")
    factor_of = lambda total: lax.rsqrt(total / width_all + EPSILON)

    kept_here = jnp.logical_and(me == half, jnp.logical_not(evicted))
    own_factor = factor_of(totals[1:2])
    own_a, own_x, own_inner = backward(
        word(kept_here, 0, 0), [(own, 0)], [(upstream, 0)], own_factor, query_gain, key_gain, heads, 3, 0,
    )
    own_inner = lax.psum(own_inner, "tensor")
    slot = finish(
        word(jnp.logical_not(kept_here)), own_a, own_x, own_factor**3 * own_inner / width_all, upstream, step
    )
    downward = send(slot, [(half, half - 1)])

    fetched_total = send(totals[2:3], partner)
    chosen_total = jnp.where(evicted, fetched_total, totals[1:2])
    flag = jnp.broadcast_to(eviction[0].astype(F32), (1, HDIM))
    told = send(jnp.concatenate([chosen_total, query_gain, key_gain, flag], axis=1), prior)
    factor = factor_of(told[:, :tokens])
    gain_q = told[:, tokens : tokens + width]
    gain_k = told[:, tokens + width : tokens + 2 * width]
    after_evicted = told[0, tokens + 2 * width] == 1.0

    mode = eviction
    sent, last = choose(mode, stashed, fetched, 0, step, 2, (slot,))
    passed = [send(sent, inside)]
    straight = send(last, direct)
    sent, _ = choose(mode, stashed, fetched, 1, step, 2, (slot,))
    passed.append(send(sent, inside))

    output = forward(current, factor_of(totals[0:1]), query_gain, key_gain, heads, (sent,))

    crossed = jnp.logical_or(me == half - 1, me == n - 1)
    which_g = jnp.where(me == half - 1, 1, jnp.where(me == n - 1, 2, 0))
    take = word(1, jnp.where(crossed, 1, 0), which_g)
    take_last = word(1, jnp.where(crossed, 2, jnp.where(after_evicted, 0, 1)), which_g)
    gs = lambda c: [(early, c), (downward, c), (upward, c)]
    a, x, inner = backward(take, [(passed[0], 0), (early, 0)], gs(0), factor, gain_q, gain_k, heads, 1, 0)
    a, x, part = backward(
        take_last, [(straight, 0), (kept, 0), (early, 2)], gs(2), factor, gain_q, gain_k, heads, 1, 2, (a, x)
    )
    inner = inner + part
    a, x, part = backward(
        take, [(passed[1], 0), (early, 1)], gs(1), factor, gain_q, gain_k, heads, 1, 1, (a, x)
    )
    inner = lax.psum(inner + part, "tensor")
    done = word(jnp.logical_and(me == half - 1, jnp.logical_not(after_evicted)))
    result = finish(done, a, x, factor**3 * inner / width_all, downward, step)
    return (output[None], result[None])


def solution(mesh):
    placed = (
        P("section", None, "tensor"),
        P("section", None, "tensor"),
        P("section", None, None, "tensor"),
        P("section"),
        P("section", "tensor"),
        P("section", "tensor"),
    )

    def whole(layer_input, *others):
        return jax.shard_map(
            functools.partial(local, layer_input.shape[-1]),
            mesh=mesh,
            in_specs=placed,
            out_specs=(P("section", None, "tensor"), P("section", None, "tensor")),
            check_vma=False,
        )(layer_input, *others)

    return whole
```

```python
import functools
import math

import jax
import jax.numpy as jnp
from jax import lax
from jax.experimental import pallas as pl
from jax.experimental.pallas import tpu as pltpu
from jax.sharding import PartitionSpec as P

HDIM = 128
EPSILON = 1e-05
SCALE = 1.0 / math.sqrt(HDIM)
LOG2E = math.log2(math.e)
VMEM = 32 * 1024 * 1024

F32 = jnp.float32
BF16 = jnp.bfloat16


def dot(a, b, contract):
    return lax.dot_general(a, b, ((contract[0], contract[1]), ((), ())), preferred_element_type=F32)


def nt(a, b):
    return dot(a, b, ((1,), (1,)))


def nn(a, b):
    return dot(a, b, ((1,), (0,)))


def block_of(tokens):
    return 256 if tokens % 256 == 0 else tokens


def masked(block, kept):
    return jnp.where(kept, block, -1e30)


def kept_keys(size):
    keys = lax.broadcasted_iota(jnp.int32, (size, size), 0)
    return keys <= lax.broadcasted_iota(jnp.int32, (size, size), 1)


def scores_of(keys, queries, j, size, kept):
    mine = queries[j * size : (j + 1) * size]
    diagonal = masked(nt(keys[j * size : (j + 1) * size], mine), kept)
    if j == 0:
        return [diagonal]
    return [nt(keys[: j * size], mine), diagonal]


def exponents(parts):
    top = functools.reduce(jnp.maximum, [jnp.max(p, axis=0, keepdims=True) for p in parts])
    exps = [jnp.exp2((p - top) * (SCALE * LOG2E)) for p in parts]
    total = sum(jnp.sum(e, axis=0, keepdims=True) for e in exps)
    return exps, total


def stacked(parts):
    return parts[0] if len(parts) == 1 else jnp.concatenate(parts, axis=0)


def normed_head(x, factor, gain_q, gain_k):
    wide = x.astype(F32)
    normed = wide * factor
    return wide, (normed * gain_q).astype(BF16), (normed * gain_k).astype(BF16), normed.astype(BF16)


def column_of(row):
    return jnp.broadcast_to(row, (HDIM, row.shape[1])).T[:, 0:1]


def forward_kernel(heads, x_ref, f_ref, gq_ref, gk_ref, *rest):
    o_ref = rest[-1]
    tokens = x_ref.shape[0]
    size = block_of(tokens)
    kept = kept_keys(size)
    factor = column_of(f_ref[...])
    for h in range(heads):
        lanes = slice(h * HDIM, (h + 1) * HDIM)
        wide, q, k, v = normed_head(x_ref[:, lanes], factor, gq_ref[:, lanes], gk_ref[:, lanes])
        vt = v.T
        for j in range(tokens // size):
            exps, total = exponents(scores_of(k, q, j, size, kept))
            mixed = nn(vt[:, : (j + 1) * size], stacked(exps).astype(BF16)) * (1.0 / total)
            rows = slice(j * size, (j + 1) * size)
            o_ref[rows, lanes] = (wide[rows] + mixed.T).astype(BF16)


def forward(x, factor, gain_q, gain_k, heads, after=()):
    tokens, width = x.shape
    lanes = heads * HDIM
    block = pl.BlockSpec((tokens, lanes), lambda i: (0, i))
    gain = pl.BlockSpec((1, lanes), lambda i: (0, i))
    return pl.pallas_call(
        functools.partial(forward_kernel, heads),
        out_shape=jax.ShapeDtypeStruct(x.shape, BF16),
        grid=(width // lanes,),
        in_specs=[block, pl.BlockSpec((1, tokens), lambda i: (0, 0)), gain, gain]
        + [pl.BlockSpec(memory_space=pl.ANY)] * len(after),
        out_specs=block,
        compiler_params=pltpu.CompilerParams(vmem_limit_bytes=VMEM),
        name="forward",
    )(x, factor, gain_q, gain_k, *after)


def backward_head(x, g, factor, gain_q, gain_k):
    tokens = x.shape[0]
    size = block_of(tokens)
    kept = kept_keys(size)
    wide, q, k, v = normed_head(x, factor, gain_q, gain_k)
    kt = k.T
    blocks = tokens // size
    d_q = []
    d_k = [None] * blocks
    d_v = [None] * blocks
    for j in range(blocks):
        rows = slice(j * size, (j + 1) * size)
        exps, total = exponents(scores_of(k, q, j, size, kept))
        inverse = 1.0 / total
        weights = [e * inverse for e in exps]
        grads = [nt(v[: j * size], g[rows])] if j else []
        grads.append(nt(v[rows], g[rows]))
        delta = sum(jnp.sum(w * d, axis=0, keepdims=True) for w, d in zip(weights, grads))
        scores = stacked([(w * ((d - delta) * SCALE)).astype(BF16) for w, d in zip(weights, grads)])
        rounded = stacked([w.astype(BF16) for w in weights])
        d_q.append(nn(kt[:, : (j + 1) * size], scores).T)
        part_k = nn(scores, q[rows])
        part_v = nn(rounded, g[rows])
        for i in range(j + 1):
            mine = slice(i * size, (i + 1) * size)
            d_k[i] = part_k[mine] if d_k[i] is None else d_k[i] + part_k[mine]
            d_v[i] = part_v[mine] if d_v[i] is None else d_v[i] + part_v[mine]
    d_normed = stacked(d_q) * gain_q + stacked(d_k) * gain_k + stacked(d_v)
    return wide, d_normed


def chosen(index, refs, at):
    value = refs[0][at]
    for i, ref in enumerate(refs[1:]):
        value = jnp.where(index == i + 1, ref[at], value)
    return value


def backward_kernel(heads, n_x, n_g, pick_ref, *refs):
    x_refs, g_refs = refs[:n_x], refs[n_x : n_x + n_g]
    f_ref, gq_ref, gk_ref = refs[n_x + n_g : n_x + n_g + 3]
    a_ref, x_ref, inner_ref = refs[-3:]
    first = pl.program_id(0) == 0

    @pl.when(jnp.logical_and(first, pick_ref[0] == 0))
    def _():
        inner_ref[...] = jnp.zeros_like(inner_ref)

    @pl.when(pick_ref[0] == 1)
    def _():
        factor = column_of(f_ref[...])
        part = None
        for h in range(heads):
            lanes = slice(h * HDIM, (h + 1) * HDIM)
            here = (slice(None), lanes)
            x = chosen(pick_ref[1], x_refs, here)
            g = chosen(pick_ref[2], g_refs, here)
            wide, d_normed = backward_head(x, g, factor, gq_ref[:, lanes], gk_ref[:, lanes])
            a_ref[:, lanes] = g.astype(F32) + jnp.where(pick_ref[3] == 1, 0.0, factor * d_normed)
            x_ref[:, lanes] = x
            product = d_normed * wide
            part = product if part is None else part + product
        inner = jnp.sum(part.T, axis=0, keepdims=True)

        @pl.when(first)
        def _():
            inner_ref[...] = inner

        @pl.when(jnp.logical_not(first))
        def _():
            inner_ref[...] += inner


def backward(pick, xs, gs, factor, gain_q, gain_k, heads, steps, first, sofar=(), after=()):
    tokens = xs[0][0].shape[0]
    width = gain_q.shape[1]
    lanes = heads * HDIM
    at = lambda start: pl.BlockSpec((tokens, lanes), lambda i, pick: (0, start + i))
    gain = pl.BlockSpec((1, lanes), lambda i, pick: (0, first + i))
    row = pl.BlockSpec((1, tokens), lambda i, pick: (0, 0))
    extra = tuple(sofar) + tuple(after)
    before = 1 + len(xs) + len(gs) + 3
    return pl.pallas_call(
        functools.partial(backward_kernel, heads, len(xs), len(gs)),
        out_shape=(
            jax.ShapeDtypeStruct((tokens, width), F32),
            jax.ShapeDtypeStruct((tokens, width), BF16),
            jax.ShapeDtypeStruct((1, tokens), F32),
        ),
        grid_spec=pltpu.PrefetchScalarGridSpec(
            num_scalar_prefetch=1,
            grid=(steps,),
            in_specs=[at(b) for _, b in (*xs, *gs)] + [row, gain, gain]
            + [pl.BlockSpec(memory_space=pl.ANY)] * len(extra),
            out_specs=(at(first), at(first), row),
        ),
        input_output_aliases={before: 0, before + 1: 1} if sofar else {},
        compiler_params=pltpu.CompilerParams(vmem_limit_bytes=VMEM),
        name="backward",
    )(pick, *[x for x, _ in xs], *[g for g, _ in gs], factor, gain_q, gain_k, *extra)


def choose_kernel(mode_ref, *refs):
    for m, ref in enumerate(refs[:3]):

        @pl.when(mode_ref[0] == m)
        def _():
            refs[-2][...] = ref[...]

    refs[-1][...] = refs[3][...]


def choose(mode, stash, fetched, slot, start, step, coming, after=()):
    tokens = fetched.shape[0]
    block = (tokens, step)
    whole = lambda at: pl.BlockSpec(block, lambda i, mode: (0, at))
    of_stash = lambda which, at: pl.BlockSpec((None, None, tokens, step), lambda i, mode: (0, which, 0, at))
    return pl.pallas_call(
        choose_kernel,
        out_shape=[jax.ShapeDtypeStruct(block, BF16)] * 2,
        grid_spec=pltpu.PrefetchScalarGridSpec(
            num_scalar_prefetch=1,
            grid=(1,),
            in_specs=[of_stash(0, start), whole(start), whole(start), of_stash(1, coming)]
            + [pl.BlockSpec(memory_space=pl.ANY)] * len(after),
            out_specs=[whole(0)] * 2,
        ),
        compiler_params=pltpu.CompilerParams(vmem_limit_bytes=VMEM),
        name="choose",
    )(mode, stash, fetched, slot, stash, *after)


def finish_kernel(pick_ref, a_ref, x_ref, row_ref, other_ref, o_ref):
    row = column_of(row_ref[...])

    @pl.when(pick_ref[0] == 0)
    def _():
        o_ref[...] = (a_ref[...] - x_ref[...].astype(F32) * row).astype(BF16)

    @pl.when(pick_ref[0] == 1)
    def _():
        o_ref[...] = other_ref[...]


def finish(pick, a, x, row, other, lanes):
    tokens, width = a.shape
    block = pl.BlockSpec((tokens, lanes), lambda i, pick: (0, i))
    return pl.pallas_call(
        finish_kernel,
        out_shape=jax.ShapeDtypeStruct(a.shape, BF16),
        grid_spec=pltpu.PrefetchScalarGridSpec(
            num_scalar_prefetch=1,
            grid=(width // lanes,),
            in_specs=[block, block, pl.BlockSpec((1, tokens), lambda i, pick: (0, 0)), block],
            out_specs=block,
        ),
        compiler_params=pltpu.CompilerParams(vmem_limit_bytes=VMEM),
        name="finish",
    )(pick, a, x, row, other)


def squares_kernel(current_ref, stash_ref, o_ref):
    def total(x):
        wide = x.astype(F32)
        square = wide * wide
        sums = sum(square[:, i : i + HDIM] for i in range(0, square.shape[1], HDIM))
        return jnp.sum(sums.T, axis=0, keepdims=True)

    rows = jnp.concatenate([total(current_ref[...]), total(stash_ref[0]), total(stash_ref[1])], axis=0)

    @pl.when(pl.program_id(0) == 0)
    def _():
        o_ref[...] = rows

    @pl.when(pl.program_id(0) > 0)
    def _():
        o_ref[...] += rows


def squares(current, stash, lanes):
    tokens, width = current.shape
    return pl.pallas_call(
        squares_kernel,
        out_shape=jax.ShapeDtypeStruct((3, tokens), F32),
        grid=(width // lanes,),
        in_specs=[
            pl.BlockSpec((tokens, lanes), lambda i: (0, i)),
            pl.BlockSpec((None, 2, tokens, lanes), lambda i: (0, 0, 0, i)),
        ],
        out_specs=pl.BlockSpec((3, tokens), lambda i: (0, 0)),
        compiler_params=pltpu.CompilerParams(vmem_limit_bytes=VMEM),
        name="squares",
    )(current, stash)


def send(x, pairs):
    return lax.ppermute(x, "section", pairs)


def local(width_all, layer_input, grad_input, stashed, eviction, query_gain, key_gain):
    n = lax.axis_size("section")
    half = n // 2
    special = (0, half)
    me = lax.axis_index("section")
    evicted = eviction[0] == 1
    word = lambda *flags: jnp.stack([jnp.asarray(f).astype(jnp.int32) for f in flags])

    inside = [(s, s - 1) for s in range(n) if s not in special]
    partner = [(s, (s + half) % n) for s in range(n)]
    to_partner = [p for p in partner if p[0] not in special]
    prior = [(s, (s - 1) % n) for s in range(n)]
    within = inside + [(half, n - 1), (0, half - 1)]
    direct = [((s + half) % n, s - 1) for s in range(n) if s not in special]

    current = layer_input[0]
    upstream = grad_input[0]
    tokens, width = current.shape
    heads_here = width // HDIM
    step = width // 3
    heads = heads_here // 3
    own, held = stashed[0, 0], stashed[0, 1]
    piece = lambda x, c: x[:, c * step : (c + 1) * step]

    is_special = jnp.logical_or(me == 0, me == half)
    fetched = send(held[:, : 2 * step], to_partner)
    early = send(jnp.where(is_special, held, upstream), within)

    totals = lax.psum(squares(current, stashed, step), "tensor")
    factor_of = lambda total: lax.rsqrt(total / width_all + EPSILON)

    kept_here = jnp.logical_and(me == half, jnp.logical_not(evicted))
    own_factor = factor_of(totals[1:2])
    own_a, own_x, own_inner = backward(
        word(kept_here, 0, 0, 0), [(own, 0)], [(upstream, 0)], own_factor, query_gain, key_gain, heads, 3, 0,
    )
    own_inner = lax.psum(own_inner, "tensor")
    slot = finish(
        word(jnp.logical_not(kept_here)), own_a, own_x, own_factor**3 * own_inner / width_all, upstream, step
    )
    kept = send(jnp.where(is_special, piece(slot, 2), piece(own, 2)), prior)

    flag = jnp.broadcast_to(eviction[0].astype(F32), (1, HDIM))
    facts = lax.all_gather(
        jnp.concatenate([totals[1:2], totals[2:3], query_gain, key_gain, flag], axis=1), "section", axis=0, tiled=True
    )
    mode = jnp.where(is_special, 2, eviction)
    sent, last = choose(mode, stashed, fetched, slot, 0, step, 2)
    straight = send(last, direct)
    passed = [send(sent, prior)]
    sent, _ = choose(mode, stashed, fetched, slot, 1, step, 2)
    passed.append(send(sent, prior))

    output = forward(current, factor_of(totals[0:1]), query_gain, key_gain, heads, (sent,))

    facts, _ = lax.optimization_barrier((facts, sent))
    told = lax.dynamic_slice_in_dim(facts, lax.rem(me + 1, n), 1, axis=0)
    held_total = lax.dynamic_slice_in_dim(facts, lax.rem(me + 1 + half, n), 1, axis=0)[:, tokens : 2 * tokens]
    gain_q = told[:, 2 * tokens : 2 * tokens + width]
    gain_k = told[:, 2 * tokens + width : 2 * tokens + 2 * width]
    after_evicted = told[0, 2 * tokens + 2 * width] == 1.0
    factor = factor_of(jnp.where(after_evicted, held_total, told[:, :tokens]))

    crossed = jnp.logical_or(me == half - 1, me == n - 1)
    done = jnp.logical_and(me == half - 1, jnp.logical_not(after_evicted))
    take = word(1, crossed, crossed, done)
    take_last = word(1, jnp.where(crossed, 2, jnp.where(after_evicted, 0, 1)), crossed, done)
    a, x, inner = backward(
        take, [(passed[0], 0), (early, 0)], [(early, 0), (passed[0], 0)], factor, gain_q, gain_k, heads, 1, 0
    )
    a, x, part = backward(
        take_last, [(straight, 0), (kept, 0), (early, 2)], [(early, 2), (kept, 0)],
        factor, gain_q, gain_k, heads, 1, 2, (a, x),
    )
    inner = inner + part
    a, x, part = backward(
        take, [(passed[1], 0), (early, 1)], [(early, 1), (passed[1], 0)], factor, gain_q, gain_k, heads, 1, 1, (a, x)
    )
    inner = lax.psum(inner + part, "tensor")
    row = jnp.where(done, 0.0, factor**3 * inner / width_all)
    result = finish(word(0), a, x, row, early, step)
    return (output[None], result[None])


def solution(mesh):
    placed = (
        P("section", None, "tensor"),
        P("section", None, "tensor"),
        P("section", None, None, "tensor"),
        P("section"),
        P("section", "tensor"),
        P("section", "tensor"),
    )

    def whole(layer_input, *others):
        return jax.shard_map(
            functools.partial(local, layer_input.shape[-1]),
            mesh=mesh,
            in_specs=placed,
            out_specs=(P("section", None, "tensor"), P("section", None, "tensor")),
            check_vma=False,
        )(layer_input, *others)

    return whole
```

```python
import functools
import math

import jax
import jax.numpy as jnp
from jax import lax
from jax.experimental import pallas as pl
from jax.experimental.pallas import tpu as pltpu
from jax.sharding import PartitionSpec as P

HDIM = 128
EPSILON = 1e-05
SCALE = 1.0 / math.sqrt(HDIM)
LOG2E = math.log2(math.e)
VMEM = 32 * 1024 * 1024
MOST = 60 * 1024 * 1024

F32 = jnp.float32
BF16 = jnp.bfloat16


def dot(a, b, contract):
    return lax.dot_general(a, b, ((contract[0], contract[1]), ((), ())), preferred_element_type=F32)


def nt(a, b):
    return dot(a, b, ((1,), (1,)))


def nn(a, b):
    return dot(a, b, ((1,), (0,)))


def block_of(tokens):
    return 256 if tokens % 256 == 0 else tokens


def masked(block, kept):
    return jnp.where(kept, block, -1e30)


def kept_keys(size):
    keys = lax.broadcasted_iota(jnp.int32, (size, size), 0)
    return keys <= lax.broadcasted_iota(jnp.int32, (size, size), 1)


def scores_of(keys, queries, j, size, kept):
    mine = queries[j * size : (j + 1) * size]
    diagonal = masked(nt(keys[j * size : (j + 1) * size], mine), kept)
    if j == 0:
        return [diagonal]
    return [nt(keys[: j * size], mine), diagonal]


def exponents(parts):
    top = functools.reduce(jnp.maximum, [jnp.max(p, axis=0, keepdims=True) for p in parts])
    exps = [jnp.exp2((p - top) * (SCALE * LOG2E)) for p in parts]
    total = sum(jnp.sum(e, axis=0, keepdims=True) for e in exps)
    return exps, total


def stacked(parts):
    return parts[0] if len(parts) == 1 else jnp.concatenate(parts, axis=0)


def normed_head(x, factor, gain_q, gain_k):
    wide = x.astype(F32)
    normed = wide * factor
    return wide, (normed * gain_q).astype(BF16), (normed * gain_k).astype(BF16), normed.astype(BF16)


def column_of(row):
    return jnp.broadcast_to(row, (HDIM, row.shape[1])).T[:, 0:1]


def forward_kernel(heads, x_ref, f_ref, gq_ref, gk_ref, *rest):
    o_ref = rest[-1]
    tokens = x_ref.shape[0]
    size = block_of(tokens)
    kept = kept_keys(size)
    factor = column_of(f_ref[...])
    for h in range(heads):
        lanes = slice(h * HDIM, (h + 1) * HDIM)
        wide, q, k, v = normed_head(x_ref[:, lanes], factor, gq_ref[:, lanes], gk_ref[:, lanes])
        vt = v.T
        for j in range(tokens // size):
            exps, total = exponents(scores_of(k, q, j, size, kept))
            mixed = nn(vt[:, : (j + 1) * size], stacked(exps).astype(BF16)) * (1.0 / total)
            rows = slice(j * size, (j + 1) * size)
            o_ref[rows, lanes] = (wide[rows] + mixed.T).astype(BF16)


def forward(x, factor, gain_q, gain_k, heads, after=()):
    tokens, width = x.shape
    lanes = heads * HDIM
    block = pl.BlockSpec((tokens, lanes), lambda i: (0, i))
    gain = pl.BlockSpec((1, lanes), lambda i: (0, i))
    return pl.pallas_call(
        functools.partial(forward_kernel, heads),
        out_shape=jax.ShapeDtypeStruct(x.shape, BF16),
        grid=(width // lanes,),
        in_specs=[block, pl.BlockSpec((1, tokens), lambda i: (0, 0)), gain, gain]
        + [pl.BlockSpec(memory_space=pl.ANY)] * len(after),
        out_specs=block,
        compiler_params=pltpu.CompilerParams(vmem_limit_bytes=VMEM),
        name="forward",
    )(x, factor, gain_q, gain_k, *after)


def backward_head(x, g, factor, gain_q, gain_k):
    tokens = x.shape[0]
    size = block_of(tokens)
    kept = kept_keys(size)
    wide, q, k, v = normed_head(x, factor, gain_q, gain_k)
    kt = k.T
    blocks = tokens // size
    d_q = []
    d_k = [None] * blocks
    d_v = [None] * blocks
    for j in range(blocks):
        rows = slice(j * size, (j + 1) * size)
        exps, total = exponents(scores_of(k, q, j, size, kept))
        inverse = 1.0 / total
        weights = [e * inverse for e in exps]
        grads = [nt(v[: j * size], g[rows])] if j else []
        grads.append(nt(v[rows], g[rows]))
        delta = sum(jnp.sum(w * d, axis=0, keepdims=True) for w, d in zip(weights, grads))
        scores = stacked([(w * ((d - delta) * SCALE)).astype(BF16) for w, d in zip(weights, grads)])
        rounded = stacked([w.astype(BF16) for w in weights])
        d_q.append(nn(kt[:, : (j + 1) * size], scores).T)
        part_k = nn(scores, q[rows])
        part_v = nn(rounded, g[rows])
        for i in range(j + 1):
            mine = slice(i * size, (i + 1) * size)
            d_k[i] = part_k[mine] if d_k[i] is None else d_k[i] + part_k[mine]
            d_v[i] = part_v[mine] if d_v[i] is None else d_v[i] + part_v[mine]
    d_normed = stacked(d_q) * gain_q + stacked(d_k) * gain_k + stacked(d_v)
    return wide, d_normed


def selected(which, refs, at):
    values = [ref[lanes_of(start + at, HDIM)] for ref, start in refs]
    value = values[0]
    for i, other in enumerate(values[1:]):
        value = jnp.where(which == i + 1, other, value)
    return value


def lanes_of(start, size):
    return (slice(None), slice(start, start + size))


def backward_piece(pick_ref, xs, gs, f_ref, gq_ref, gk_ref, a_ref, x_ref, heads, first):
    factor = column_of(f_ref[...])
    part = None
    for h in range(heads):
        mine = lanes_of(first + h * HDIM, HDIM)
        x = selected(pick_ref[1], xs, h * HDIM)
        g = selected(pick_ref[2], gs, h * HDIM)
        wide, d_normed = backward_head(x, g, factor, gq_ref[mine], gk_ref[mine])
        a_ref[mine] = g.astype(F32) + jnp.where(pick_ref[3] == 1, 0.0, factor * d_normed)
        x_ref[mine] = x
        product = d_normed * wide
        part = product if part is None else part + product
    return jnp.sum(part.T, axis=0, keepdims=True)


def backward_kernel(heads, first, x_at, g_at, pick_ref, *refs):
    n_x, n_g = len(x_at), len(g_at)
    xs = list(zip(refs[:n_x], x_at))
    gs = list(zip(refs[n_x : n_x + n_g], g_at))
    a_ref, x_ref, inner_ref = refs[-3:]
    inner_ref[...] = backward_piece(pick_ref, xs, gs, *refs[n_x + n_g : n_x + n_g + 3], a_ref, x_ref, heads, first)


IN_VMEM = pl.BlockSpec(memory_space=pltpu.VMEM)


def backward(pick, xs, gs, factor, gain_q, gain_k, heads, first, sofar=(), after=()):
    tokens = xs[0][0].shape[0]
    width = gain_q.shape[1]
    before = 1 + len(xs) + len(gs) + 3
    return pl.pallas_call(
        functools.partial(backward_kernel, heads, first, tuple(at for _, at in xs), tuple(at for _, at in gs)),
        out_shape=(
            jax.ShapeDtypeStruct((tokens, width), F32),
            jax.ShapeDtypeStruct((tokens, width), BF16),
            jax.ShapeDtypeStruct((1, tokens), F32),
        ),
        in_specs=[pl.BlockSpec(memory_space=pltpu.SMEM)] + [IN_VMEM] * (before - 1 + len(sofar))
        + [pl.BlockSpec(memory_space=pl.ANY)] * len(after),
        out_specs=(IN_VMEM, IN_VMEM, IN_VMEM),
        input_output_aliases={before: 0, before + 1: 1} if sofar else {},
        compiler_params=pltpu.CompilerParams(vmem_limit_bytes=VMEM),
        name="backward",
    )(pick, *[x for x, _ in xs], *[g for g, _ in gs], factor, gain_q, gain_k, *sofar, *after)


def early_kernel(heads, pick_ref, x_ref, g_ref, f_ref, gq_ref, gk_ref, a_ref, inner_ref, x_scratch):
    first = pl.program_id(0) == 0

    @pl.when(first)
    def _():
        inner_ref[...] = jnp.zeros_like(inner_ref)

    @pl.when(pick_ref[0] == 1)
    def _():
        inner_ref[...] += backward_piece(
            pick_ref, [(x_ref, 0)], [(g_ref, 0)], f_ref, gq_ref, gk_ref, a_ref, x_scratch, heads, 0
        )


def early_backward(pick, stash, g, factor, gain_q, gain_k, heads):
    tokens, width = g.shape
    lanes = heads * HDIM
    at = lambda i, pick: (0, i * pick[0])
    block = pl.BlockSpec((tokens, lanes), at)
    row = pl.BlockSpec((1, tokens), lambda i, pick: (0, 0))
    gain = pl.BlockSpec((1, lanes), at)
    return pl.pallas_call(
        functools.partial(early_kernel, heads),
        out_shape=(jax.ShapeDtypeStruct((tokens, width), F32), jax.ShapeDtypeStruct((1, tokens), F32)),
        grid_spec=pltpu.PrefetchScalarGridSpec(
            num_scalar_prefetch=1,
            grid=(width // lanes,),
            in_specs=[
                pl.BlockSpec((None, None, tokens, lanes), lambda i, pick: (0, 0, 0, i * pick[0])),
                block, row, gain, gain,
            ],
            out_specs=(block, row),
            scratch_shapes=[pltpu.VMEM((tokens, lanes), BF16)],
        ),
        compiler_params=pltpu.CompilerParams(vmem_limit_bytes=MOST),
        name="early_backward",
    )(pick, stash, g, factor, gain_q, gain_k)


def choose_kernel(mode_ref, *refs):
    for m, ref in enumerate(refs[:3]):

        @pl.when(mode_ref[0] == m)
        def _():
            refs[-2][...] = ref[...]

    refs[-1][...] = refs[3][...]


def choose(mode, stash, fetched, slot, start, step, coming, after=()):
    tokens = fetched.shape[0]
    block = (tokens, step)
    whole = lambda at: pl.BlockSpec(block, lambda i, mode: (0, at))
    of_stash = lambda which, at: pl.BlockSpec((None, None, tokens, step), lambda i, mode: (0, which, 0, at))
    return pl.pallas_call(
        choose_kernel,
        out_shape=[jax.ShapeDtypeStruct(block, BF16)] * 2,
        grid_spec=pltpu.PrefetchScalarGridSpec(
            num_scalar_prefetch=1,
            grid=(1,),
            in_specs=[of_stash(0, start), whole(start), whole(start), of_stash(1, coming)]
            + [pl.BlockSpec(memory_space=pl.ANY)] * len(after),
            out_specs=[whole(0)] * 2,
        ),
        compiler_params=pltpu.CompilerParams(vmem_limit_bytes=VMEM),
        name="choose",
    )(mode, stash, fetched, slot, stash, *after)


def finish_kernel(lanes, a_ref, x_ref, row_ref, o_ref):
    row = column_of(row_ref[...])
    at = (slice(None), pl.ds(pl.program_id(0) * lanes, lanes))
    o_ref[...] = (a_ref[at] - x_ref[at].astype(F32) * row).astype(BF16)


def finish(a, x, row, lanes):
    tokens, width = a.shape
    return pl.pallas_call(
        functools.partial(finish_kernel, lanes),
        out_shape=jax.ShapeDtypeStruct(a.shape, BF16),
        grid=(width // lanes,),
        in_specs=[IN_VMEM] * 3,
        out_specs=pl.BlockSpec((tokens, lanes), lambda i: (0, i)),
        compiler_params=pltpu.CompilerParams(vmem_limit_bytes=VMEM),
        name="finish",
    )(a, x, row)


def slot_kernel(pick_ref, a_ref, x_ref, g_ref, row_ref, o_ref):
    @pl.when(pick_ref[0] == 1)
    def _():
        row = column_of(row_ref[...])
        o_ref[...] = (a_ref[...] - x_ref[...].astype(F32) * row).astype(BF16)

    @pl.when(pick_ref[0] == 0)
    def _():
        o_ref[...] = g_ref[...]


def kept_kernel(last, pick_ref, a_ref, x_ref, g_ref, row_ref, o_ref, kept_ref):
    slot_kernel(pick_ref, a_ref, x_ref, g_ref, row_ref, o_ref)

    @pl.when(jnp.logical_and(pl.program_id(0) == last, pick_ref[1] == 1))
    def _():
        kept_ref[...] = o_ref[...]

    @pl.when(jnp.logical_and(pl.program_id(0) == last, pick_ref[1] == 0))
    def _():
        kept_ref[...] = x_ref[...]


def slot_of(pick, a, stash, g, row, lanes):
    tokens, width = g.shape
    last = width // lanes - 1
    block = pl.BlockSpec((tokens, lanes), lambda i, pick: (0, i))
    return pl.pallas_call(
        functools.partial(kept_kernel, last),
        out_shape=(jax.ShapeDtypeStruct((tokens, width), BF16), jax.ShapeDtypeStruct((tokens, lanes), BF16)),
        grid_spec=pltpu.PrefetchScalarGridSpec(
            num_scalar_prefetch=1,
            grid=(width // lanes,),
            in_specs=[
                pl.BlockSpec((tokens, lanes), lambda i, pick: (0, i * pick[0])),
                pl.BlockSpec((None, None, tokens, lanes), lambda i, pick: (0, 0, 0, i)),
                block,
                pl.BlockSpec((1, tokens), lambda i, pick: (0, 0)),
            ],
            out_specs=(block, pl.BlockSpec((tokens, lanes), lambda i, pick: (0, 0))),
        ),
        compiler_params=pltpu.CompilerParams(vmem_limit_bytes=MOST),
        name="slot",
    )(pick, a, stash, g, row)


def open_kernel(pieces, pick_ref, current_ref, stash_ref, g_ref, gq_ref, gk_ref, rows_ref, told_ref, away_ref, early_ref):
    step = pl.program_id(0)
    tokens, lanes = current_ref.shape

    def total(x):
        wide = x.astype(F32)
        square = wide * wide
        sums = sum(square[:, i : i + HDIM] for i in range(0, square.shape[1], HDIM))
        return jnp.sum(sums.T, axis=0, keepdims=True)

    rows = jnp.concatenate([total(current_ref[...]), total(stash_ref[0]), total(stash_ref[1])], axis=0)

    @pl.when(step == 0)
    def _():
        rows_ref[...] = rows

    @pl.when(step > 0)
    def _():
        rows_ref[...] += rows

    @pl.when(step < pieces - 1)
    def _():
        away_ref[...] = stash_ref[1]

    @pl.when(pick_ref[0] == 1)
    def _():
        early_ref[...] = stash_ref[1]

    @pl.when(pick_ref[0] == 0)
    def _():
        early_ref[...] = g_ref[...]

    @pl.when(step == pieces - 1)
    def _():
        width = gq_ref.shape[1]
        told_ref[:, :tokens] = rows_ref[1:2, :]
        told_ref[:, tokens : tokens + width] = gq_ref[...]
        told_ref[:, tokens + width : tokens + 2 * width] = gk_ref[...]
        told_ref[:, tokens + 2 * width :] = jnp.full((1, HDIM), pick_ref[1].astype(F32))


def opened(pick, current, stash, g, gain_q, gain_k, lanes):
    tokens, width = current.shape
    pieces = width // lanes
    block = pl.BlockSpec((tokens, lanes), lambda i, pick: (0, i))
    still = lambda *shape: pl.BlockSpec(shape, lambda i, pick: (0, 0))
    told = tokens + 2 * width + HDIM
    return pl.pallas_call(
        functools.partial(open_kernel, pieces),
        out_shape=(
            jax.ShapeDtypeStruct((3, tokens), F32),
            jax.ShapeDtypeStruct((1, told), F32),
            jax.ShapeDtypeStruct((tokens, width - lanes), BF16),
            jax.ShapeDtypeStruct((tokens, width), BF16),
        ),
        grid_spec=pltpu.PrefetchScalarGridSpec(
            num_scalar_prefetch=1,
            grid=(pieces,),
            in_specs=[
                block,
                pl.BlockSpec((None, 2, tokens, lanes), lambda i, pick: (0, 0, 0, i)),
                block,
                still(1, width),
                still(1, width),
            ],
            out_specs=(
                still(3, tokens),
                still(1, told),
                pl.BlockSpec((tokens, lanes), lambda i, pick: (0, jnp.minimum(i, pieces - 2))),
                block,
            ),
        ),
        compiler_params=pltpu.CompilerParams(vmem_limit_bytes=MOST),
        name="opened",
    )(pick, current, stash, g, gain_q, gain_k)


def send(x, pairs):
    return lax.ppermute(x, "section", pairs)


def local(width_all, layer_input, grad_input, stashed, eviction, query_gain, key_gain):
    n = lax.axis_size("section")
    half = n // 2
    special = (0, half)
    me = lax.axis_index("section")
    evicted = eviction[0] == 1
    word = lambda *flags: jnp.stack([jnp.asarray(f).astype(jnp.int32) for f in flags])

    inside = [(s, s - 1) for s in range(n) if s not in special]
    partner = [(s, (s + half) % n) for s in range(n)]
    to_partner = [p for p in partner if p[0] not in special]
    prior = [(s, (s - 1) % n) for s in range(n)]
    within = inside + [(half, n - 1), (0, half - 1)]
    direct = [((s + half) % n, s - 1) for s in range(n) if s not in special]

    current = layer_input[0]
    upstream = grad_input[0]
    tokens, width = current.shape
    heads_here = width // HDIM
    step = width // 3
    heads = heads_here // 3

    is_special = jnp.logical_or(me == 0, me == half)
    rows, told, away, first = opened(
        word(is_special, evicted), current, stashed, upstream, query_gain, key_gain, step
    )
    told = send(told, prior)
    held_row = send(rows[2:3], [((s + half) % n, (s - 1) % n) for s in range(n)])
    fetched = send(away, to_partner)
    early = send(first, within)

    gain_q = told[:, tokens : tokens + width]
    gain_k = told[:, tokens + width : tokens + 2 * width]
    after_evicted = told[0, tokens + 2 * width] == 1.0
    chosen_row = jnp.where(after_evicted, held_row, told[:, :tokens])
    totals = lax.psum(jnp.concatenate([rows[:2], chosen_row], axis=0), "tensor")
    factors = lax.rsqrt(totals / width_all + EPSILON)
    forward_factor, own_factor, factor = factors[0:1], factors[1:2], factors[2:3]

    kept_here = jnp.logical_and(me == half, jnp.logical_not(evicted))
    own_a, own_inner = early_backward(
        word(kept_here, 0, 0, 0), stashed, upstream, own_factor, query_gain, key_gain, heads
    )
    own_inner = lax.psum(own_inner, "tensor")
    slot, last = slot_of(
        word(kept_here, is_special), own_a, stashed, upstream, own_factor**3 * own_inner / width_all, step
    )
    kept = send(last, prior)

    mode = jnp.where(is_special, 2, eviction)
    sent, last = choose(mode, stashed, fetched, slot, 0, step, 2)
    straight = send(last, direct)
    passed = [send(sent, prior)]
    sent, _ = choose(mode, stashed, fetched, slot, 1, step, 2)
    passed.append(send(sent, prior))

    output = forward(current, forward_factor, query_gain, key_gain, heads, (sent,))

    crossed = jnp.logical_or(me == half - 1, me == n - 1)
    done = jnp.logical_and(me == half - 1, jnp.logical_not(after_evicted))
    take = word(1, crossed, crossed, done)
    take_last = word(1, jnp.where(crossed, 2, jnp.where(after_evicted, 0, 1)), crossed, done)
    facts = (factor, gain_q, gain_k)
    a, x, inner = backward(
        take, [(passed[0], 0), (early, 0)], [(early, 0), (passed[0], 0)], *facts, heads, 0,
        after=(output,),
    )
    a, x, part = backward(
        take_last, [(straight, 0), (kept, 0), (early, 2 * step)], [(early, 2 * step), (kept, 0)], *facts, heads,
        2 * step, (a, x),
    )
    inner = inner + part
    a, x, part = backward(
        take, [(passed[1], 0), (early, step)], [(early, step), (passed[1], 0)], *facts, heads, step, (a, x)
    )
    inner = lax.psum(inner + part, "tensor")
    result = finish(a, x, jnp.where(done, 0.0, factor**3 * inner / width_all), step)
    return (output[None], result[None])


def solution(mesh):
    placed = (
        P("section", None, "tensor"),
        P("section", None, "tensor"),
        P("section", None, None, "tensor"),
        P("section"),
        P("section", "tensor"),
        P("section", "tensor"),
    )

    def whole(layer_input, *others):
        return jax.shard_map(
            functools.partial(local, layer_input.shape[-1]),
            mesh=mesh,
            in_specs=placed,
            out_specs=(P("section", None, "tensor"), P("section", None, "tensor")),
            check_vma=False,
        )(layer_input, *others)

    return whole
```

```python
import functools
import math

import jax
import jax.numpy as jnp
from jax import lax
from jax.experimental import pallas as pl
from jax.experimental.pallas import tpu as pltpu
from jax.sharding import PartitionSpec as P

HDIM = 128
EPSILON = 1e-05
SCALE = 1.0 / math.sqrt(HDIM)
LOG2E = math.log2(math.e)
VMEM = 32 * 1024 * 1024
MOST = 60 * 1024 * 1024

F32 = jnp.float32
BF16 = jnp.bfloat16


def dot(a, b, contract):
    return lax.dot_general(a, b, ((contract[0], contract[1]), ((), ())), preferred_element_type=F32)


def nt(a, b):
    return dot(a, b, ((1,), (1,)))


def nn(a, b):
    return dot(a, b, ((1,), (0,)))


def block_of(tokens):
    return 256 if tokens % 256 == 0 else tokens


def masked(block, kept):
    return jnp.where(kept, block, -1e30)


def kept_keys(size):
    keys = lax.broadcasted_iota(jnp.int32, (size, size), 0)
    return keys <= lax.broadcasted_iota(jnp.int32, (size, size), 1)


def scores_of(keys, queries, j, size, kept):
    mine = queries[j * size : (j + 1) * size]
    diagonal = masked(nt(keys[j * size : (j + 1) * size], mine), kept)
    if j == 0:
        return [diagonal]
    return [nt(keys[: j * size], mine), diagonal]


def exponents(parts):
    top = functools.reduce(jnp.maximum, [jnp.max(p, axis=0, keepdims=True) for p in parts])
    exps = [jnp.exp2((p - top) * (SCALE * LOG2E)) for p in parts]
    total = sum(jnp.sum(e, axis=0, keepdims=True) for e in exps)
    return exps, total


def stacked(parts):
    return parts[0] if len(parts) == 1 else jnp.concatenate(parts, axis=0)


def normed_head(x, factor, gain_q, gain_k):
    wide = x.astype(F32)
    normed = wide * factor
    return wide, (normed * gain_q).astype(BF16), (normed * gain_k).astype(BF16), normed.astype(BF16)


def column_of(row):
    return jnp.broadcast_to(row, (HDIM, row.shape[1])).T[:, 0:1]


def forward_kernel(heads, x_ref, f_ref, gq_ref, gk_ref, *rest):
    o_ref = rest[-1]
    tokens = x_ref.shape[0]
    size = block_of(tokens)
    kept = kept_keys(size)
    factor = column_of(f_ref[...])
    for h in range(heads):
        lanes = slice(h * HDIM, (h + 1) * HDIM)
        wide, q, k, v = normed_head(x_ref[:, lanes], factor, gq_ref[:, lanes], gk_ref[:, lanes])
        vt = v.T
        for j in range(tokens // size):
            exps, total = exponents(scores_of(k, q, j, size, kept))
            mixed = nn(vt[:, : (j + 1) * size], stacked(exps).astype(BF16)) * (1.0 / total)
            rows = slice(j * size, (j + 1) * size)
            o_ref[rows, lanes] = (wide[rows] + mixed.T).astype(BF16)


def forward(x, factor, gain_q, gain_k, heads, after=()):
    tokens, width = x.shape
    lanes = heads * HDIM
    block = pl.BlockSpec((tokens, lanes), lambda i: (0, i))
    gain = pl.BlockSpec((1, lanes), lambda i: (0, i))
    return pl.pallas_call(
        functools.partial(forward_kernel, heads),
        out_shape=jax.ShapeDtypeStruct(x.shape, BF16),
        grid=(width // lanes,),
        in_specs=[block, pl.BlockSpec((1, tokens), lambda i: (0, 0)), gain, gain]
        + [pl.BlockSpec(memory_space=pl.ANY)] * len(after),
        out_specs=block,
        compiler_params=pltpu.CompilerParams(vmem_limit_bytes=VMEM),
        name="forward",
    )(x, factor, gain_q, gain_k, *after)


def backward_head(x, g, factor, gain_q, gain_k):
    tokens = x.shape[0]
    size = block_of(tokens)
    kept = kept_keys(size)
    wide, q, k, v = normed_head(x, factor, gain_q, gain_k)
    kt = k.T
    blocks = tokens // size
    d_q = []
    d_k = [None] * blocks
    d_v = [None] * blocks
    for j in range(blocks):
        rows = slice(j * size, (j + 1) * size)
        exps, total = exponents(scores_of(k, q, j, size, kept))
        inverse = 1.0 / total
        weights = [e * inverse for e in exps]
        grads = [nt(v[: j * size], g[rows])] if j else []
        grads.append(nt(v[rows], g[rows]))
        delta = sum(jnp.sum(w * d, axis=0, keepdims=True) for w, d in zip(weights, grads))
        scores = stacked([(w * ((d - delta) * SCALE)).astype(BF16) for w, d in zip(weights, grads)])
        rounded = stacked([w.astype(BF16) for w in weights])
        d_q.append(nn(kt[:, : (j + 1) * size], scores).T)
        part_k = nn(scores, q[rows])
        part_v = nn(rounded, g[rows])
        for i in range(j + 1):
            mine = slice(i * size, (i + 1) * size)
            d_k[i] = part_k[mine] if d_k[i] is None else d_k[i] + part_k[mine]
            d_v[i] = part_v[mine] if d_v[i] is None else d_v[i] + part_v[mine]
    d_normed = stacked(d_q) * gain_q + stacked(d_k) * gain_k + stacked(d_v)
    return wide, d_normed


def selected(which, refs, at):
    values = [ref[lanes_of(start + at, HDIM)] for ref, start in refs]
    value = values[0]
    for i, other in enumerate(values[1:]):
        value = jnp.where(which == i + 1, other, value)
    return value


def lanes_of(start, size):
    return (slice(None), slice(start, start + size))


def backward_piece(pick_ref, xs, gs, f_ref, gq_ref, gk_ref, a_ref, x_ref, heads, first):
    factor = column_of(f_ref[...])
    part = None
    for h in range(heads):
        mine = lanes_of(first + h * HDIM, HDIM)
        x = selected(pick_ref[1], xs, h * HDIM)
        g = selected(pick_ref[2], gs, h * HDIM)
        wide, d_normed = backward_head(x, g, factor, gq_ref[mine], gk_ref[mine])
        a_ref[mine] = g.astype(F32) + jnp.where(pick_ref[3] == 1, 0.0, factor * d_normed)
        x_ref[mine] = x
        product = d_normed * wide
        part = product if part is None else part + product
    return jnp.sum(part.T, axis=0, keepdims=True)


def backward_kernel(heads, first, x_at, g_at, pick_ref, *refs):
    n_x, n_g = len(x_at), len(g_at)
    xs = list(zip(refs[:n_x], x_at))
    gs = list(zip(refs[n_x : n_x + n_g], g_at))
    a_ref, x_ref, inner_ref = refs[-3:]
    inner_ref[...] = backward_piece(pick_ref, xs, gs, *refs[n_x + n_g : n_x + n_g + 3], a_ref, x_ref, heads, first)


IN_VMEM = pl.BlockSpec(memory_space=pltpu.VMEM)


def backward(pick, xs, gs, factor, gain_q, gain_k, heads, first, sofar=(), after=()):
    tokens = xs[0][0].shape[0]
    width = gain_q.shape[1]
    before = 1 + len(xs) + len(gs) + 3
    return pl.pallas_call(
        functools.partial(backward_kernel, heads, first, tuple(at for _, at in xs), tuple(at for _, at in gs)),
        out_shape=(
            jax.ShapeDtypeStruct((tokens, width), F32),
            jax.ShapeDtypeStruct((tokens, width), BF16),
            jax.ShapeDtypeStruct((1, tokens), F32),
        ),
        in_specs=[pl.BlockSpec(memory_space=pltpu.SMEM)] + [IN_VMEM] * (before - 1 + len(sofar))
        + [pl.BlockSpec(memory_space=pl.ANY)] * len(after),
        out_specs=(IN_VMEM, IN_VMEM, IN_VMEM),
        input_output_aliases={before: 0, before + 1: 1} if sofar else {},
        compiler_params=pltpu.CompilerParams(vmem_limit_bytes=VMEM),
        name="backward",
    )(pick, *[x for x, _ in xs], *[g for g, _ in gs], factor, gain_q, gain_k, *sofar, *after)


def finish_kernel(lanes, a_ref, x_ref, row_ref, o_ref):
    row = column_of(row_ref[...])
    at = (slice(None), pl.ds(pl.program_id(0) * lanes, lanes))
    o_ref[...] = (a_ref[at] - x_ref[at].astype(F32) * row).astype(BF16)


def finish(a, x, row, lanes):
    tokens, width = a.shape
    return pl.pallas_call(
        functools.partial(finish_kernel, lanes),
        out_shape=jax.ShapeDtypeStruct(a.shape, BF16),
        grid=(width // lanes,),
        in_specs=[IN_VMEM] * 3,
        out_specs=pl.BlockSpec((tokens, lanes), lambda i: (0, i)),
        compiler_params=pltpu.CompilerParams(vmem_limit_bytes=VMEM),
        name="finish",
    )(a, x, row)


def open_kernel(pieces, current_ref, stash_ref, rows_ref, *out_refs):
    step = pl.program_id(0)

    def total(x):
        wide = x.astype(F32)
        square = wide * wide
        sums = sum(square[:, i : i + HDIM] for i in range(0, square.shape[1], HDIM))
        return jnp.sum(sums.T, axis=0, keepdims=True)

    rows = jnp.concatenate([total(current_ref[...]), total(stash_ref[0]), total(stash_ref[1])], axis=0)

    @pl.when(step == 0)
    def _():
        rows_ref[...] = rows

    @pl.when(step > 0)
    def _():
        rows_ref[...] += rows

    for p in range(pieces):

        @pl.when(step == p)
        def _():
            out_refs[p][...] = stash_ref[1]


def opened(current, stash, lanes):
    tokens, width = current.shape
    pieces = width // lanes
    still = lambda *shape: pl.BlockSpec(shape, lambda i: (0, 0))
    return pl.pallas_call(
        functools.partial(open_kernel, pieces),
        out_shape=[jax.ShapeDtypeStruct((3, tokens), F32)] + [jax.ShapeDtypeStruct((tokens, lanes), BF16)] * pieces,
        grid=(pieces,),
        in_specs=[
            pl.BlockSpec((tokens, lanes), lambda i: (0, i)),
            pl.BlockSpec((None, 2, tokens, lanes), lambda i: (0, 0, 0, i)),
        ],
        out_specs=[still(3, tokens)] + [still(tokens, lanes)] * pieces,
        compiler_params=pltpu.CompilerParams(vmem_limit_bytes=MOST),
        name="opened",
    )(current, stash)


def send(x, pairs):
    return lax.ppermute(x, "section", pairs)


def local(width_all, layer_input, grad_input, stashed, eviction, query_gain, key_gain):
    n = lax.axis_size("section")
    half = n // 2
    word = lambda *flags: jnp.stack([jnp.asarray(f).astype(jnp.int32) for f in flags])
    partner = [(s, (s + half) % n) for s in range(n)]
    prior = [(s, (s - 1) % n) for s in range(n)]

    current = layer_input[0]
    upstream = grad_input[0]
    tokens, width = current.shape
    heads = width // HDIM // 3
    step = heads * HDIM

    rows, *held = opened(current, stashed, step)
    held_row = send(rows[2:3], partner)
    fetched = [send(h, partner) for h in held]
    chosen_row = jnp.where(eviction[0] == 1, held_row, rows[1:2])
    totals = lax.psum(jnp.concatenate([rows[:1], chosen_row], axis=0), "tensor")
    factors = lax.rsqrt(totals / width_all + EPSILON)
    output = forward(current, factors[0:1], query_gain, key_gain, heads)
    facts = (factors[1:2], query_gain, key_gain)
    take = word(1, eviction[0], 0, 0)
    sofar, inner, after = (), 0.0, (output,)
    own = stashed[0, 0]
    for p, f in enumerate(fetched):
        a, x, part = backward(
            take, [(own, p * step), (f, 0)], [(upstream, p * step)], *facts, heads, p * step, sofar, after
        )
        sofar, inner, after = (a, x), inner + part, ()
    inner = lax.psum(inner, "tensor")
    result = finish(a, x, factors[1:2] ** 3 * inner / width_all, step)
    return (output[None], send(result, prior)[None])


def solution(mesh):
    placed = (
        P("section", None, "tensor"),
        P("section", None, "tensor"),
        P("section", None, None, "tensor"),
        P("section"),
        P("section", "tensor"),
        P("section", "tensor"),
    )

    def whole(layer_input, *others):
        return jax.shard_map(
            functools.partial(local, layer_input.shape[-1]),
            mesh=mesh,
            in_specs=placed,
            out_specs=(P("section", None, "tensor"), P("section", None, "tensor")),
            check_vma=False,
        )(layer_input, *others)

    return whole
```

```python
import functools
import math

import jax
import jax.numpy as jnp
from jax import lax
from jax.experimental import pallas as pl
from jax.experimental.pallas import tpu as pltpu
from jax.sharding import PartitionSpec as P

HDIM = 128
EPSILON = 1e-05
SCALE = 1.0 / math.sqrt(HDIM)
LOG2E = math.log2(math.e)
VMEM = 32 * 1024 * 1024
MOST = 60 * 1024 * 1024

F32 = jnp.float32
BF16 = jnp.bfloat16


def dot(a, b, contract):
    return lax.dot_general(a, b, ((contract[0], contract[1]), ((), ())), preferred_element_type=F32)


def nt(a, b):
    return dot(a, b, ((1,), (1,)))


def nn(a, b):
    return dot(a, b, ((1,), (0,)))


def block_of(tokens):
    return 256 if tokens % 256 == 0 else tokens


def masked(block, kept):
    return jnp.where(kept, block, -1e30)


def kept_keys(size):
    keys = lax.broadcasted_iota(jnp.int32, (size, size), 0)
    return keys <= lax.broadcasted_iota(jnp.int32, (size, size), 1)


def scores_of(keys, queries, j, size, kept):
    mine = queries[j * size : (j + 1) * size]
    diagonal = masked(nt(keys[j * size : (j + 1) * size], mine), kept)
    if j == 0:
        return [diagonal]
    return [nt(keys[: j * size], mine), diagonal]


def exponents(parts):
    top = functools.reduce(jnp.maximum, [jnp.max(p, axis=0, keepdims=True) for p in parts])
    exps = [jnp.exp2((p - top) * (SCALE * LOG2E)) for p in parts]
    total = sum(jnp.sum(e, axis=0, keepdims=True) for e in exps)
    return exps, total


def stacked(parts):
    return parts[0] if len(parts) == 1 else jnp.concatenate(parts, axis=0)


def normed_head(x, factor, gain_q, gain_k):
    wide = x.astype(F32)
    normed = wide * factor
    return wide, (normed * gain_q).astype(BF16), (normed * gain_k).astype(BF16), normed.astype(BF16)


def column_of(row):
    return jnp.broadcast_to(row, (HDIM, row.shape[1])).T[:, 0:1]


def inverse_rms(total, width_all):
    return lax.rsqrt(total / width_all + EPSILON)


def lanes_of(start, size):
    return (slice(None), slice(start, start + size))


def compiler(limit):
    return pltpu.CompilerParams(vmem_limit_bytes=limit)


IN_VMEM = pl.BlockSpec(memory_space=pltpu.VMEM)
ANYWHERE = pl.BlockSpec(memory_space=pl.ANY)


def forward_kernel(heads, width_all, x_ref, t_ref, gq_ref, gk_ref, *rest):
    o_ref = rest[-1]
    tokens = x_ref.shape[0]
    size = block_of(tokens)
    kept = kept_keys(size)
    factor = column_of(inverse_rms(t_ref[0:1, :], width_all))
    for h in range(heads):
        lanes = slice(h * HDIM, (h + 1) * HDIM)
        wide, q, k, v = normed_head(x_ref[:, lanes], factor, gq_ref[:, lanes], gk_ref[:, lanes])
        vt = v.T
        for j in range(tokens // size):
            exps, total = exponents(scores_of(k, q, j, size, kept))
            mixed = nn(vt[:, : (j + 1) * size], stacked(exps).astype(BF16)) * (1.0 / total)
            rows = slice(j * size, (j + 1) * size)
            o_ref[rows, lanes] = (wide[rows] + mixed.T).astype(BF16)


def forward(width_all, x, totals, gain_q, gain_k, heads, after=()):
    tokens, width = x.shape
    lanes = heads * HDIM
    block = pl.BlockSpec((tokens, lanes), lambda i: (0, i))
    gain = pl.BlockSpec((1, lanes), lambda i: (0, i))
    return pl.pallas_call(
        functools.partial(forward_kernel, heads, width_all),
        out_shape=jax.ShapeDtypeStruct(x.shape, BF16),
        grid=(width // lanes,),
        in_specs=[block, pl.BlockSpec(totals.shape, lambda i: (0, 0)), gain, gain] + [ANYWHERE] * len(after),
        out_specs=block,
        compiler_params=compiler(VMEM),
        name="forward",
    )(x, totals, gain_q, gain_k, *after)


def backward_head(x, g, factor, gain_q, gain_k):
    tokens = x.shape[0]
    size = block_of(tokens)
    kept = kept_keys(size)
    wide, q, k, v = normed_head(x, factor, gain_q, gain_k)
    kt = k.T
    blocks = tokens // size
    d_q = []
    d_k = [None] * blocks
    d_v = [None] * blocks
    for j in range(blocks):
        rows = slice(j * size, (j + 1) * size)
        exps, total = exponents(scores_of(k, q, j, size, kept))
        inverse = 1.0 / total
        weights = [e * inverse for e in exps]
        grads = [nt(v[: j * size], g[rows])] if j else []
        grads.append(nt(v[rows], g[rows]))
        delta = sum(jnp.sum(w * d, axis=0, keepdims=True) for w, d in zip(weights, grads))
        scores = stacked([(w * ((d - delta) * SCALE)).astype(BF16) for w, d in zip(weights, grads)])
        rounded = stacked([w.astype(BF16) for w in weights])
        d_q.append(nn(kt[:, : (j + 1) * size], scores).T)
        part_k = nn(scores, q[rows])
        part_v = nn(rounded, g[rows])
        for i in range(j + 1):
            mine = slice(i * size, (i + 1) * size)
            d_k[i] = part_k[mine] if d_k[i] is None else d_k[i] + part_k[mine]
            d_v[i] = part_v[mine] if d_v[i] is None else d_v[i] + part_v[mine]
    d_normed = stacked(d_q) * gain_q + stacked(d_k) * gain_k + stacked(d_v)
    return wide, d_normed


def selected(which, refs, at):
    values = [ref[lanes_of(start + at, HDIM)] for ref, start in refs]
    value = values[0]
    for i, other in enumerate(values[1:]):
        value = jnp.where(which == i + 1, other, value)
    return value


def backward_kernel(first, heads, width_all, x_at, g_at, pick_ref, *refs):
    n_x, n_g = len(x_at), len(g_at)
    unevicted = x_at[-1] is None
    xs = list(zip(refs[:n_x], [at or 0 for at in x_at]))
    gs = list(zip(refs[n_x : n_x + n_g], g_at))
    t_ref, told_ref, past_ref = refs[n_x + n_g : n_x + n_g + 3]
    a_ref, x_ref, inner_ref = refs[-3:]
    tokens, width = a_ref.shape
    factor = column_of(inverse_rms(t_ref[2:3, :], width_all))
    evicted = told_ref[:, tokens + 2 * width :] == 1.0
    ready = jnp.logical_and(pick_ref[2] == 1, jnp.logical_not(evicted))
    part = None
    for h in range(heads):
        at = h * HDIM
        mine = lanes_of(first + at, HDIM)
        gain_q = told_ref[lanes_of(tokens + first + at, HDIM)]
        gain_k = told_ref[lanes_of(tokens + width + first + at, HDIM)]
        if unevicted:
            straight, start = xs[0]
            own, own_start = xs[-1]
            x = jnp.where(evicted, straight[lanes_of(start + at, HDIM)].astype(F32), own[lanes_of(own_start + at, HDIM)].astype(F32))
            x = x.astype(BF16)
            for i, (ref, start) in enumerate(xs[1:-1]):
                x = jnp.where(pick_ref[0] == i + 1, ref[lanes_of(start + at, HDIM)], x)
        else:
            x = selected(pick_ref[0], xs, at)
        g = selected(pick_ref[1], gs, at)
        wide, d_normed = backward_head(x, g, factor, gain_q, gain_k)
        a_ref[mine] = g.astype(F32) + jnp.where(ready, 0.0, factor * d_normed)
        x_ref[mine] = x
        product = d_normed * wide
        part = product if part is None else part + product
    inner = jnp.sum(part.T, axis=0, keepdims=True)
    inner_ref[...] = inner if past_ref is None else inner + past_ref[...]


def backward(width_all, width, pick, xs, gs, totals, told, past, heads, first, sofar=(), after=()):
    tokens = totals.shape[1]
    before = 1 + len(xs) + len(gs) + 3
    return pl.pallas_call(
        functools.partial(
            backward_kernel, first, heads, width_all, tuple(at for _, at in xs), tuple(at for _, at in gs)
        ),
        out_shape=(
            jax.ShapeDtypeStruct((tokens, width), F32),
            jax.ShapeDtypeStruct((tokens, width), BF16),
            jax.ShapeDtypeStruct((1, tokens), F32),
        ),
        in_specs=[pl.BlockSpec(memory_space=pltpu.SMEM)] + [IN_VMEM] * (before - 1 + len(sofar))
        + [ANYWHERE] * len(after),
        out_specs=(IN_VMEM, IN_VMEM, IN_VMEM),
        input_output_aliases={before: 0, before + 1: 1} if sofar else {},
        compiler_params=compiler(VMEM),
        name="backward",
    )(pick, *[x for x, _ in xs], *[g for g, _ in gs], totals, told, past, *sofar, *after)


def early_kernel(heads, width_all, pick_ref, x_ref, g_ref, t_ref, gq_ref, gk_ref, a_ref, inner_ref):
    @pl.when(pl.program_id(0) == 0)
    def _():
        inner_ref[...] = jnp.zeros_like(inner_ref)

    @pl.when(pick_ref[0] == 1)
    def _():
        factor = column_of(inverse_rms(t_ref[1:2, :], width_all))
        part = None
        for h in range(heads):
            mine = lanes_of(h * HDIM, HDIM)
            g = g_ref[mine]
            wide, d_normed = backward_head(x_ref[mine], g, factor, gq_ref[mine], gk_ref[mine])
            a_ref[mine] = g.astype(F32) + factor * d_normed
            product = d_normed * wide
            part = product if part is None else part + product
        inner_ref[...] += jnp.sum(part.T, axis=0, keepdims=True)


def early_backward(width_all, pick, stash, g, totals, gain_q, gain_k, heads):
    tokens, width = g.shape
    lanes = heads * HDIM
    at = lambda i, pick: (0, i * pick[0])
    block = pl.BlockSpec((tokens, lanes), at)
    still = lambda shape: pl.BlockSpec(shape, lambda i, pick: (0, 0))
    gain = pl.BlockSpec((1, lanes), at)
    return pl.pallas_call(
        functools.partial(early_kernel, heads, width_all),
        out_shape=(jax.ShapeDtypeStruct((tokens, width), F32), jax.ShapeDtypeStruct((1, tokens), F32)),
        grid_spec=pltpu.PrefetchScalarGridSpec(
            num_scalar_prefetch=1,
            grid=(width // lanes,),
            in_specs=[
                pl.BlockSpec((None, None, tokens, lanes), lambda i, pick: (0, 0, 0, i * pick[0])),
                block, still(totals.shape), gain, gain,
            ],
            out_specs=(block, still((1, tokens))),
        ),
        compiler_params=compiler(MOST),
        name="early_backward",
    )(pick, stash, g, totals, gain_q, gain_k)


def row_of(total, inner, width_all):
    return inverse_rms(total, width_all) ** 3 * inner / width_all


def finish_kernel(lanes, width_all, pick_ref, a_ref, x_ref, t_ref, told_ref, inner_ref, o_ref):
    tokens, width = a_ref.shape
    evicted = told_ref[:, tokens + 2 * width : tokens + 2 * width + 1] == 1.0
    ready = jnp.logical_and(pick_ref[2] == 1, jnp.logical_not(evicted))
    row = jnp.where(ready, 0.0, row_of(t_ref[2:3, :], inner_ref[...], width_all))
    at = (slice(None), pl.ds(pl.program_id(0) * lanes, lanes))
    o_ref[...] = (a_ref[at] - x_ref[at].astype(F32) * column_of(row)).astype(BF16)


def finish(width_all, pick, a, x, totals, told, inner, lanes):
    tokens, width = a.shape
    return pl.pallas_call(
        functools.partial(finish_kernel, lanes, width_all),
        out_shape=jax.ShapeDtypeStruct(a.shape, BF16),
        grid=(width // lanes,),
        in_specs=[pl.BlockSpec(memory_space=pltpu.SMEM)] + [IN_VMEM] * 5,
        out_specs=pl.BlockSpec((tokens, lanes), lambda i: (0, i)),
        compiler_params=compiler(VMEM),
        name="finish",
    )(pick, a, x, totals, told, inner)


def slot_kernel(width_all, last, pick_ref, a_ref, x_ref, g_ref, t_ref, inner_ref, o_ref, kept_ref):
    special = pick_ref[1] == 1
    step = pl.program_id(0)

    @pl.when(jnp.logical_and(special, pick_ref[0] == 1))
    def _():
        row = column_of(row_of(t_ref[1:2, :], inner_ref[...], width_all))
        o_ref[...] = (a_ref[...] - x_ref[...].astype(F32) * row).astype(BF16)

    @pl.when(jnp.logical_and(special, pick_ref[0] == 0))
    def _():
        o_ref[...] = g_ref[...]

    @pl.when(jnp.logical_and(special, step == 0))
    def _():
        kept_ref[...] = o_ref[...]

    @pl.when(jnp.logical_and(jnp.logical_not(special), step == last))
    def _():
        kept_ref[...] = x_ref[...]


def slot_of(width_all, pick, a, stash, g, totals, inner, lanes):
    tokens, width = g.shape
    last = width // lanes - 1
    block = pl.BlockSpec((tokens, lanes), lambda i, pick: (0, i * pick[1]))
    still = lambda shape: pl.BlockSpec(shape, lambda i, pick: (0, 0))
    return pl.pallas_call(
        functools.partial(slot_kernel, width_all, last),
        out_shape=(jax.ShapeDtypeStruct((tokens, width), BF16), jax.ShapeDtypeStruct((tokens, lanes), BF16)),
        grid_spec=pltpu.PrefetchScalarGridSpec(
            num_scalar_prefetch=1,
            grid=(width // lanes,),
            in_specs=[
                pl.BlockSpec((tokens, lanes), lambda i, pick: (0, i * pick[0])),
                pl.BlockSpec(
                    (None, None, tokens, lanes), lambda i, pick: (0, 0, 0, jnp.where(pick[1] == 1, i, last))
                ),
                block,
                still(totals.shape),
                still(inner.shape),
            ],
            out_specs=(block, still((tokens, lanes))),
        ),
        compiler_params=compiler(MOST),
        name="slot",
    )(pick, a, stash, g, totals, inner)


def choose_kernel(n, mode_ref, *refs):
    outs = refs[-2:]
    sets = (refs[:n], refs[n:-2])
    for i, (out, options) in enumerate(zip(outs, sets)):
        for m, ref in enumerate(options):

            @pl.when(mode_ref[i] == m)
            def _():
                out[...] = ref[...]


def choose(mode, first, second, tokens, step, after=()):
    def spec(array, at):
        if isinstance(at, tuple):
            return pl.BlockSpec((None, None, tokens, step), lambda i, mode: (0, at[0], 0, at[1]))
        return pl.BlockSpec((tokens, step), lambda i, mode: (0, at))

    piece = pl.BlockSpec((tokens, step), lambda i, mode: (0, 0))

    def kernel(mode_ref, *refs):
        used = len(first) + len(second)
        choose_kernel(len(first), mode_ref, *refs[:used], *refs[-2:])

    return pl.pallas_call(
        kernel,
        out_shape=[jax.ShapeDtypeStruct((tokens, step), BF16)] * 2,
        grid_spec=pltpu.PrefetchScalarGridSpec(
            num_scalar_prefetch=1,
            grid=(1,),
            in_specs=[spec(*o) for o in (*first, *second)] + [ANYWHERE] * len(after),
            out_specs=[piece] * 2,
        ),
        compiler_params=compiler(VMEM),
        name="choose",
    )(mode, *[array for array, _ in (*first, *second)], *after)


def sums_kernel(pieces, pick_ref, current_ref, stash_ref, gq_ref, gk_ref, rows_ref, told_ref):
    step = pl.program_id(0)
    tokens = current_ref.shape[0]

    def total(x):
        wide = x.astype(F32)
        square = wide * wide
        sums = sum(square[:, i : i + HDIM] for i in range(0, square.shape[1], HDIM))
        return jnp.sum(sums.T, axis=0, keepdims=True)

    rows = jnp.concatenate([total(current_ref[...]), total(stash_ref[0]), total(stash_ref[1])], axis=0)

    @pl.when(step == 0)
    def _():
        rows_ref[...] = rows

    @pl.when(step > 0)
    def _():
        rows_ref[...] += rows

    @pl.when(step == pieces - 1)
    def _():
        width = gq_ref.shape[1]
        told_ref[:, :tokens] = rows_ref[1:2, :]
        told_ref[:, tokens : tokens + width] = gq_ref[...]
        told_ref[:, tokens + width : tokens + 2 * width] = gk_ref[...]
        told_ref[:, tokens + 2 * width :] = jnp.full((1, HDIM), pick_ref[2].astype(F32))


def sums_of(pick, current, stash, gain_q, gain_k, lanes):
    tokens, width = current.shape
    pieces = width // lanes
    still = lambda *shape: pl.BlockSpec(shape, lambda i, pick: (0, 0))
    told = tokens + 2 * width + HDIM
    return pl.pallas_call(
        functools.partial(sums_kernel, pieces),
        out_shape=(jax.ShapeDtypeStruct((3, tokens), F32), jax.ShapeDtypeStruct((1, told), F32)),
        grid_spec=pltpu.PrefetchScalarGridSpec(
            num_scalar_prefetch=1,
            grid=(pieces,),
            in_specs=[
                pl.BlockSpec((tokens, lanes), lambda i, pick: (0, i)),
                pl.BlockSpec((None, 2, tokens, lanes), lambda i, pick: (0, 0, 0, i)),
                still(1, width),
                still(1, width),
            ],
            out_specs=(still(3, tokens), still(1, told)),
        ),
        compiler_params=compiler(MOST),
        name="sums",
    )(pick, current, stash, gain_q, gain_k)


def pack_kernel(pieces, pick_ref, stash_ref, g_ref, *refs):
    away_ref, first_ref, last_ref = refs[-3:]
    step = pl.program_id(0)

    @pl.when(step == 0)
    def _():
        away_ref[...] = stash_ref[...]

    for mine, out in ((step < pieces - 1, first_ref), (step == pieces - 1, last_ref)):

        @pl.when(jnp.logical_and(mine, pick_ref[1] == 1))
        def _():
            out[...] = stash_ref[...]

        @pl.when(jnp.logical_and(mine, pick_ref[1] == 0))
        def _():
            out[...] = g_ref[...]


def pack(pick, stash, g, lanes, after=()):
    tokens, width = g.shape
    pieces = width // lanes
    piece = pl.BlockSpec((tokens, lanes), lambda i, pick: (0, 0))
    return pl.pallas_call(
        functools.partial(pack_kernel, pieces),
        out_shape=[jax.ShapeDtypeStruct((tokens, w), BF16) for w in (lanes, width - lanes, lanes)],
        grid_spec=pltpu.PrefetchScalarGridSpec(
            num_scalar_prefetch=1,
            grid=(pieces,),
            in_specs=[
                pl.BlockSpec((None, None, tokens, lanes), lambda i, pick: (0, 1, 0, i * pick[1])),
                pl.BlockSpec((tokens, lanes), lambda i, pick: (0, i)),
            ]
            + [ANYWHERE] * len(after),
            out_specs=[
                piece, pl.BlockSpec((tokens, lanes), lambda i, pick: (0, jnp.minimum(i, pieces - 2))), piece
            ],
        ),
        compiler_params=compiler(MOST),
        name="pack",
    )(pick, stash, g, *after)


def join_kernel(rows_ref, told_ref, held_ref, o_ref):
    tokens = rows_ref.shape[1]
    o_ref[0:2, :] = rows_ref[0:2, :]
    evicted = told_ref[:, told_ref.shape[1] - 1 :] == 1.0
    o_ref[2:3, :] = jnp.where(evicted, held_ref[2:3, :], told_ref[:, :tokens])


def join(rows, told, held):
    return pl.pallas_call(
        join_kernel,
        out_shape=jax.ShapeDtypeStruct(rows.shape, F32),
        in_specs=[IN_VMEM] * 3,
        out_specs=IN_VMEM,
        compiler_params=compiler(VMEM),
        name="join",
    )(rows, told, held)


def send(x, pairs):
    return lax.ppermute(x, "section", pairs)


def local(width_all, layer_input, grad_input, stashed, eviction, query_gain, key_gain):
    n = lax.axis_size("section")
    half = n // 2
    special = (0, half)
    me = lax.axis_index("section")

    prior = [(s, (s - 1) % n) for s in range(n)]
    inside = [(s, s - 1) for s in range(n) if s not in special]
    within = inside + [(half, n - 1), (0, half - 1)]
    around = [p for p in within if p[0] not in (half, n - 2)] + [(half, n - 3), (n - 2, n - 1)]
    back = [(n - 1, n - 3), (n - 3, n - 1)]
    to_partner = [(s, (s + half) % n) for s in range(n) if s not in special]
    holder = [((s + half) % n, (s - 1) % n) for s in range(n)]
    direct = [p for p in holder if p[0] not in special] + [(half, half - 1), (0, n - 1)]

    current = layer_input[0]
    upstream = grad_input[0]
    tokens, width = current.shape
    heads = width // HDIM // 3
    step = heads * HDIM

    flag = lambda f: jnp.asarray(f).astype(jnp.int32)
    is_special = jnp.logical_or(me == 0, me == half)
    kept_here = jnp.logical_and(me == half, eviction[0] == 0)
    crossed = jnp.logical_or(me == half - 1, me == n - 1)
    early_pick = jnp.stack([flag(kept_here), flag(is_special), eviction[0]])
    mode = jnp.stack([jnp.where(is_special, 2, eviction[0]), flag(is_special)])
    mode_first = jnp.stack([eviction[0], flag(False)])
    final = flag(me == half - 1)
    take = jnp.stack([
        jnp.where(crossed, jnp.where(me == n - 1, 2, 1), 0),
        jnp.where(crossed, 2, jnp.where(me == n - 3, 1, 0)),
        final,
    ])
    take_first = jnp.stack([flag(crossed), flag(crossed), final])

    rows, told = sums_of(early_pick, current, stashed, query_gain, key_gain, step)
    told = send(told, prior)
    held_rows = send(rows, holder)
    away, early_first, early_last = pack(early_pick, stashed, upstream, step, (told, held_rows))
    fetched = send(away, to_partner)
    early_first = send(early_first, within)
    early_last = send(early_last, around)
    totals = lax.psum(join(rows, told, held_rows), "tensor")

    own_a, own_inner = early_backward(width_all, early_pick, stashed, upstream, totals, query_gain, key_gain, heads)
    sent, away = choose(
        mode_first, [(stashed, (0, 0)), (fetched, 0)], [(stashed, (1, 1))], tokens, step, (own_inner,)
    )
    fetched = send(away, to_partner)
    passed = [send(sent, inside)]
    last_back = send(early_last, back)
    own_inner = lax.psum(own_inner, "tensor")
    slot, last = slot_of(width_all, early_pick, own_a, stashed, upstream, totals, own_inner, step)
    kept = send(last, prior)
    sent, last = choose(
        mode, [(stashed, (0, 1)), (fetched, 0), (slot, 1)], [(stashed, (1, 2)), (slot, 2)], tokens, step
    )
    straight = send(last, direct)
    passed.append(send(sent, prior))
    output = forward(width_all, current, totals, query_gain, key_gain, heads, (sent,))

    share = functools.partial(backward, width_all, width)
    a, x, inner = share(
        take_first, [(passed[0], 0), (early_first, 0)], [(early_first, 0), (kept, 0)], totals, told,
        jnp.zeros((1, tokens), F32), heads, 0, (), (output,),
    )
    a, x, inner = share(
        take_first, [(passed[1], 0), (early_first, step)], [(early_first, step), (passed[1], 0)],
        totals, told, inner, heads, step, (a, x),
    )
    a, x, inner = share(
        take, [(straight, 0), (early_last, 0), (last_back, 0), (kept, None)],
        [(early_last, 0), (last_back, 0), (straight, 0)], totals, told, inner, heads, 2 * step, (a, x),
    )
    inner = lax.psum(inner, "tensor")
    result = finish(width_all, take, a, x, totals, told, inner, step)
    return (output[None], result[None])


def solution(mesh):
    placed = (
        P("section", None, "tensor"),
        P("section", None, "tensor"),
        P("section", None, None, "tensor"),
        P("section"),
        P("section", "tensor"),
        P("section", "tensor"),
    )

    def whole(layer_input, *others):
        return jax.shard_map(
            functools.partial(local, layer_input.shape[-1]),
            mesh=mesh,
            in_specs=placed,
            out_specs=(P("section", None, "tensor"), P("section", None, "tensor")),
            check_vma=False,
        )(layer_input, *others)

    return whole
```

```python
import functools
import math

import jax
import jax.numpy as jnp
from jax import lax
from jax.experimental import pallas as pl
from jax.experimental.pallas import tpu as pltpu
from jax.sharding import PartitionSpec as P

HDIM = 128
EPSILON = 1e-05
SCALE = 1.0 / math.sqrt(HDIM)
LOG2E = math.log2(math.e)
VMEM = 32 * 1024 * 1024
MOST = 60 * 1024 * 1024

F32 = jnp.float32
BF16 = jnp.bfloat16


def dot(a, b, contract):
    return lax.dot_general(a, b, ((contract[0], contract[1]), ((), ())), preferred_element_type=F32)


def nt(a, b):
    return dot(a, b, ((1,), (1,)))


def nn(a, b):
    return dot(a, b, ((1,), (0,)))


def block_of(tokens):
    return 256 if tokens % 256 == 0 else tokens


def masked(block, kept):
    return jnp.where(kept, block, -1e30)


def kept_keys(size):
    keys = lax.broadcasted_iota(jnp.int32, (size, size), 0)
    return keys <= lax.broadcasted_iota(jnp.int32, (size, size), 1)


def scores_of(keys, queries, j, size, kept):
    mine = queries[j * size : (j + 1) * size]
    diagonal = masked(nt(keys[j * size : (j + 1) * size], mine), kept)
    if j == 0:
        return [diagonal]
    return [nt(keys[: j * size], mine), diagonal]


def exponents(parts):
    top = functools.reduce(jnp.maximum, [jnp.max(p, axis=0, keepdims=True) for p in parts])
    exps = [jnp.exp2((p - top) * (SCALE * LOG2E)) for p in parts]
    total = sum(jnp.sum(e, axis=0, keepdims=True) for e in exps)
    return exps, total


def stacked(parts):
    return parts[0] if len(parts) == 1 else jnp.concatenate(parts, axis=0)


def normed_head(x, factor, gain_q, gain_k):
    wide = x.astype(F32)
    normed = wide * factor
    return wide, (normed * gain_q).astype(BF16), (normed * gain_k).astype(BF16), normed.astype(BF16)


def column_of(row):
    return jnp.broadcast_to(row, (HDIM, row.shape[1])).T[:, 0:1]


def inverse_rms(total, width_all):
    return lax.rsqrt(total / width_all + EPSILON)


def lanes_of(start, size):
    return (slice(None), slice(start, start + size))


def compiler(limit):
    return pltpu.CompilerParams(vmem_limit_bytes=limit)


IN_VMEM = pl.BlockSpec(memory_space=pltpu.VMEM)
ANYWHERE = pl.BlockSpec(memory_space=pl.ANY)


def forward_kernel(heads, width_all, x_ref, t_ref, gq_ref, gk_ref, *rest):
    o_ref = rest[-1]
    tokens = x_ref.shape[0]
    size = block_of(tokens)
    kept = kept_keys(size)
    factor = column_of(inverse_rms(t_ref[0:1, :], width_all))
    for h in range(heads):
        lanes = slice(h * HDIM, (h + 1) * HDIM)
        wide, q, k, v = normed_head(x_ref[:, lanes], factor, gq_ref[:, lanes], gk_ref[:, lanes])
        vt = v.T
        for j in range(tokens // size):
            exps, total = exponents(scores_of(k, q, j, size, kept))
            mixed = nn(vt[:, : (j + 1) * size], stacked(exps).astype(BF16)) * (1.0 / total)
            rows = slice(j * size, (j + 1) * size)
            o_ref[rows, lanes] = (wide[rows] + mixed.T).astype(BF16)


def forward(width_all, x, totals, gain_q, gain_k, heads, after=()):
    tokens, width = x.shape
    lanes = heads * HDIM
    block = pl.BlockSpec((tokens, lanes), lambda i: (0, i))
    gain = pl.BlockSpec((1, lanes), lambda i: (0, i))
    return pl.pallas_call(
        functools.partial(forward_kernel, heads, width_all),
        out_shape=jax.ShapeDtypeStruct(x.shape, BF16),
        grid=(width // lanes,),
        in_specs=[block, pl.BlockSpec(totals.shape, lambda i: (0, 0)), gain, gain] + [ANYWHERE] * len(after),
        out_specs=block,
        compiler_params=compiler(VMEM),
        name="forward",
    )(x, totals, gain_q, gain_k, *after)


def backward_head(x, g, factor, gain_q, gain_k):
    tokens = x.shape[0]
    size = block_of(tokens)
    kept = kept_keys(size)
    wide, q, k, v = normed_head(x, factor, gain_q, gain_k)
    kt = k.T
    blocks = tokens // size
    d_q = []
    d_k = [None] * blocks
    d_v = [None] * blocks
    for j in range(blocks):
        rows = slice(j * size, (j + 1) * size)
        exps, total = exponents(scores_of(k, q, j, size, kept))
        inverse = 1.0 / total
        weights = [e * inverse for e in exps]
        grads = [nt(v[: j * size], g[rows])] if j else []
        grads.append(nt(v[rows], g[rows]))
        delta = sum(jnp.sum(w * d, axis=0, keepdims=True) for w, d in zip(weights, grads))
        scores = stacked([(w * ((d - delta) * SCALE)).astype(BF16) for w, d in zip(weights, grads)])
        rounded = stacked([w.astype(BF16) for w in weights])
        d_q.append(nn(kt[:, : (j + 1) * size], scores).T)
        part_k = nn(scores, q[rows])
        part_v = nn(rounded, g[rows])
        for i in range(j + 1):
            mine = slice(i * size, (i + 1) * size)
            d_k[i] = part_k[mine] if d_k[i] is None else d_k[i] + part_k[mine]
            d_v[i] = part_v[mine] if d_v[i] is None else d_v[i] + part_v[mine]
    d_normed = stacked(d_q) * gain_q + stacked(d_k) * gain_k + stacked(d_v)
    return wide, d_normed


def selected(which, refs, at):
    values = [ref[lanes_of(start + at, HDIM)] for ref, start in refs]
    value = values[0]
    for i, other in enumerate(values[1:]):
        value = jnp.where(which == i + 1, other, value)
    return value


def backward_kernel(first, heads, width_all, x_at, g_at, pick_ref, *refs):
    n_x, n_g = len(x_at), len(g_at)
    unevicted = x_at[-1] is None
    xs = list(zip(refs[:n_x], [at or 0 for at in x_at]))
    gs = list(zip(refs[n_x : n_x + n_g], g_at))
    t_ref, told_ref, past_ref = refs[n_x + n_g : n_x + n_g + 3]
    a_ref, x_ref, inner_ref = refs[-3:]
    tokens, width = a_ref.shape
    factor = column_of(inverse_rms(t_ref[...], width_all))
    evicted = told_ref[:, tokens + 2 * width :] == 1.0
    ready = jnp.logical_and(pick_ref[2] == 1, jnp.logical_not(evicted))
    part = None
    for h in range(heads):
        at = h * HDIM
        mine = lanes_of(first + at, HDIM)
        gain_q = told_ref[lanes_of(tokens + first + at, HDIM)]
        gain_k = told_ref[lanes_of(tokens + width + first + at, HDIM)]
        if unevicted:
            straight, start = xs[0]
            own, own_start = xs[-1]
            x = jnp.where(evicted, straight[lanes_of(start + at, HDIM)].astype(F32), own[lanes_of(own_start + at, HDIM)].astype(F32))
            x = x.astype(BF16)
            for i, (ref, start) in enumerate(xs[1:-1]):
                x = jnp.where(pick_ref[0] == i + 1, ref[lanes_of(start + at, HDIM)], x)
        else:
            x = selected(pick_ref[0], xs, at)
        g = selected(pick_ref[1], gs, at)
        wide, d_normed = backward_head(x, g, factor, gain_q, gain_k)
        a_ref[mine] = g.astype(F32) + jnp.where(ready, 0.0, factor * d_normed)
        x_ref[mine] = x
        product = d_normed * wide
        part = product if part is None else part + product
    inner = jnp.sum(part.T, axis=0, keepdims=True)
    inner_ref[...] = inner if past_ref is None else inner + past_ref[...]


def backward(width_all, width, pick, xs, gs, totals, told, past, heads, first, sofar=(), after=()):
    tokens = totals.shape[1]
    before = 1 + len(xs) + len(gs) + 3
    return pl.pallas_call(
        functools.partial(
            backward_kernel, first, heads, width_all, tuple(at for _, at in xs), tuple(at for _, at in gs)
        ),
        out_shape=(
            jax.ShapeDtypeStruct((tokens, width), F32),
            jax.ShapeDtypeStruct((tokens, width), BF16),
            jax.ShapeDtypeStruct((1, tokens), F32),
        ),
        in_specs=[pl.BlockSpec(memory_space=pltpu.SMEM)] + [IN_VMEM] * (before - 1 + len(sofar))
        + [ANYWHERE] * len(after),
        out_specs=(IN_VMEM, IN_VMEM, IN_VMEM),
        input_output_aliases={before: 0, before + 1: 1} if sofar else {},
        compiler_params=compiler(VMEM),
        name="backward",
    )(pick, *[x for x, _ in xs], *[g for g, _ in gs], totals, told, past, *sofar, *after)


def early_kernel(heads, width_all, pick_ref, x_ref, g_ref, t_ref, gq_ref, gk_ref, a_ref, inner_ref):
    @pl.when(pl.program_id(0) == 0)
    def _():
        inner_ref[...] = jnp.zeros_like(inner_ref)

    @pl.when(pick_ref[0] == 1)
    def _():
        factor = column_of(inverse_rms(t_ref[1:2, :], width_all))
        part = None
        for h in range(heads):
            mine = lanes_of(h * HDIM, HDIM)
            g = g_ref[mine]
            wide, d_normed = backward_head(x_ref[mine], g, factor, gq_ref[mine], gk_ref[mine])
            a_ref[mine] = g.astype(F32) + factor * d_normed
            product = d_normed * wide
            part = product if part is None else part + product
        inner_ref[...] += jnp.sum(part.T, axis=0, keepdims=True)


def early_backward(width_all, pick, stash, g, totals, gain_q, gain_k, heads):
    tokens, width = g.shape
    lanes = heads * HDIM
    at = lambda i, pick: (0, i * pick[0])
    block = pl.BlockSpec((tokens, lanes), at)
    still = lambda shape: pl.BlockSpec(shape, lambda i, pick: (0, 0))
    gain = pl.BlockSpec((1, lanes), at)
    return pl.pallas_call(
        functools.partial(early_kernel, heads, width_all),
        out_shape=(jax.ShapeDtypeStruct((tokens, width), F32), jax.ShapeDtypeStruct((1, tokens), F32)),
        grid_spec=pltpu.PrefetchScalarGridSpec(
            num_scalar_prefetch=1,
            grid=(width // lanes,),
            in_specs=[
                pl.BlockSpec((None, None, tokens, lanes), lambda i, pick: (0, 0, 0, i * pick[0])),
                block, still(totals.shape), gain, gain,
            ],
            out_specs=(block, still((1, tokens))),
        ),
        compiler_params=compiler(MOST),
        name="early_backward",
    )(pick, stash, g, totals, gain_q, gain_k)


def row_of(total, inner, width_all):
    return inverse_rms(total, width_all) ** 3 * inner / width_all


def finish_kernel(lanes, width_all, pick_ref, a_ref, x_ref, t_ref, told_ref, inner_ref, o_ref):
    tokens, width = a_ref.shape
    evicted = told_ref[:, tokens + 2 * width : tokens + 2 * width + 1] == 1.0
    ready = jnp.logical_and(pick_ref[2] == 1, jnp.logical_not(evicted))
    row = jnp.where(ready, 0.0, row_of(t_ref[...], inner_ref[...], width_all))
    at = (slice(None), pl.ds(pl.program_id(0) * lanes, lanes))
    o_ref[...] = (a_ref[at] - x_ref[at].astype(F32) * column_of(row)).astype(BF16)


def finish(width_all, pick, a, x, totals, told, inner, lanes):
    tokens, width = a.shape
    return pl.pallas_call(
        functools.partial(finish_kernel, lanes, width_all),
        out_shape=jax.ShapeDtypeStruct(a.shape, BF16),
        grid=(width // lanes,),
        in_specs=[pl.BlockSpec(memory_space=pltpu.SMEM)] + [IN_VMEM] * 5,
        out_specs=pl.BlockSpec((tokens, lanes), lambda i: (0, i)),
        compiler_params=compiler(VMEM),
        name="finish",
    )(pick, a, x, totals, told, inner)


def slot_kernel(width_all, last, pick_ref, a_ref, x_ref, g_ref, t_ref, inner_ref, o_ref, kept_ref):
    special = pick_ref[1] == 1
    step = pl.program_id(0)

    @pl.when(jnp.logical_and(special, pick_ref[0] == 1))
    def _():
        row = column_of(row_of(t_ref[1:2, :], inner_ref[...], width_all))
        o_ref[...] = (a_ref[...] - x_ref[...].astype(F32) * row).astype(BF16)

    @pl.when(jnp.logical_and(special, pick_ref[0] == 0))
    def _():
        o_ref[...] = g_ref[...]

    @pl.when(jnp.logical_and(special, step == 0))
    def _():
        kept_ref[...] = o_ref[...]

    @pl.when(jnp.logical_and(jnp.logical_not(special), step == last))
    def _():
        kept_ref[...] = x_ref[...]


def slot_of(width_all, pick, a, stash, g, totals, inner, lanes):
    tokens, width = g.shape
    last = width // lanes - 1
    block = pl.BlockSpec((tokens, lanes), lambda i, pick: (0, i * pick[1]))
    still = lambda shape: pl.BlockSpec(shape, lambda i, pick: (0, 0))
    return pl.pallas_call(
        functools.partial(slot_kernel, width_all, last),
        out_shape=(jax.ShapeDtypeStruct((tokens, width), BF16), jax.ShapeDtypeStruct((tokens, lanes), BF16)),
        grid_spec=pltpu.PrefetchScalarGridSpec(
            num_scalar_prefetch=1,
            grid=(width // lanes,),
            in_specs=[
                pl.BlockSpec((tokens, lanes), lambda i, pick: (0, i * pick[0])),
                pl.BlockSpec(
                    (None, None, tokens, lanes), lambda i, pick: (0, 0, 0, jnp.where(pick[1] == 1, i, last))
                ),
                block,
                still(totals.shape),
                still(inner.shape),
            ],
            out_specs=(block, still((tokens, lanes))),
        ),
        compiler_params=compiler(MOST),
        name="slot",
    )(pick, a, stash, g, totals, inner)


def choose_kernel(n, mode_ref, *refs):
    outs = refs[-2:]
    sets = (refs[:n], refs[n:-2])
    for i, (out, options) in enumerate(zip(outs, sets)):
        for m, ref in enumerate(options):

            @pl.when(mode_ref[i] == m)
            def _():
                out[...] = ref[...]


def choose(mode, first, second, tokens, step, after=()):
    def spec(array, at):
        if isinstance(at, tuple):
            return pl.BlockSpec((None, None, tokens, step), lambda i, mode: (0, at[0], 0, at[1]))
        return pl.BlockSpec((tokens, step), lambda i, mode: (0, at))

    piece = pl.BlockSpec((tokens, step), lambda i, mode: (0, 0))

    def kernel(mode_ref, *refs):
        used = len(first) + len(second)
        choose_kernel(len(first), mode_ref, *refs[:used], *refs[-2:])

    return pl.pallas_call(
        kernel,
        out_shape=[jax.ShapeDtypeStruct((tokens, step), BF16)] * 2,
        grid_spec=pltpu.PrefetchScalarGridSpec(
            num_scalar_prefetch=1,
            grid=(1,),
            in_specs=[spec(*o) for o in (*first, *second)] + [ANYWHERE] * len(after),
            out_specs=[piece] * 2,
        ),
        compiler_params=compiler(VMEM),
        name="choose",
    )(mode, *[array for array, _ in (*first, *second)], *after)


def open_kernel(pieces, pick_ref, current_ref, stash_ref, g_ref, gq_ref, gk_ref, rows_ref, held_ref, told_ref, away_ref, early_ref):
    step = pl.program_id(0)
    tokens, lanes = current_ref.shape

    def total(x):
        wide = x.astype(F32)
        square = wide * wide
        sums = sum(square[:, i : i + HDIM] for i in range(0, square.shape[1], HDIM))
        return jnp.sum(sums.T, axis=0, keepdims=True)

    rows = jnp.concatenate([total(current_ref[...]), total(stash_ref[0])], axis=0)
    held = total(stash_ref[1])

    @pl.when(step == 0)
    def _():
        rows_ref[...] = rows
        held_ref[...] = held
        away_ref[...] = stash_ref[1]

    @pl.when(step > 0)
    def _():
        rows_ref[...] += rows
        held_ref[...] += held

    @pl.when(pick_ref[1] == 1)
    def _():
        early_ref[...] = stash_ref[1]

    @pl.when(pick_ref[1] == 0)
    def _():
        early_ref[...] = g_ref[...]

    @pl.when(step == pieces - 1)
    def _():
        width = gq_ref.shape[1]
        told_ref[:, :tokens] = rows_ref[1:2, :]
        told_ref[:, tokens : tokens + width] = gq_ref[...]
        told_ref[:, tokens + width : tokens + 2 * width] = gk_ref[...]
        told_ref[:, tokens + 2 * width :] = jnp.full((1, HDIM), pick_ref[2].astype(F32))


def opened(pick, current, stash, g, gain_q, gain_k, lanes):
    tokens, width = current.shape
    pieces = width // lanes
    block = pl.BlockSpec((tokens, lanes), lambda i, pick: (0, i))
    still = lambda *shape: pl.BlockSpec(shape, lambda i, pick: (0, 0))
    told = tokens + 2 * width + HDIM
    return pl.pallas_call(
        functools.partial(open_kernel, pieces),
        out_shape=(
            jax.ShapeDtypeStruct((2, tokens), F32),
            jax.ShapeDtypeStruct((1, tokens), F32),
            jax.ShapeDtypeStruct((1, told), F32),
            jax.ShapeDtypeStruct((tokens, lanes), BF16),
            jax.ShapeDtypeStruct((tokens, width), BF16),
        ),
        grid_spec=pltpu.PrefetchScalarGridSpec(
            num_scalar_prefetch=1,
            grid=(pieces,),
            in_specs=[
                block,
                pl.BlockSpec((None, 2, tokens, lanes), lambda i, pick: (0, 0, 0, i)),
                block,
                still(1, width),
                still(1, width),
            ],
            out_specs=(still(2, tokens), still(1, tokens), still(1, told), still(tokens, lanes), block),
        ),
        compiler_params=compiler(MOST),
        name="opened",
    )(pick, current, stash, g, gain_q, gain_k)


def join_kernel(told_ref, held_ref, *rest):
    tokens = held_ref.shape[1]
    evicted = told_ref[:, told_ref.shape[1] - 1 :] == 1.0
    rest[-1][...] = jnp.where(evicted, held_ref[...], told_ref[:, :tokens])


def join(told, held, after):
    return pl.pallas_call(
        join_kernel,
        out_shape=jax.ShapeDtypeStruct(held.shape, F32),
        in_specs=[IN_VMEM] * 2 + [ANYWHERE] * len(after),
        out_specs=IN_VMEM,
        compiler_params=compiler(VMEM),
        name="join",
    )(told, held, *after)


def send(x, pairs):
    return lax.ppermute(x, "section", pairs)


def local(width_all, layer_input, grad_input, stashed, eviction, query_gain, key_gain):
    n = lax.axis_size("section")
    half = n // 2
    special = (0, half)
    me = lax.axis_index("section")

    prior = [(s, (s - 1) % n) for s in range(n)]
    inside = [(s, s - 1) for s in range(n) if s not in special]
    within = inside + [(half, n - 1), (0, half - 1)]
    to_partner = [(s, (s + half) % n) for s in range(n) if s not in special]
    holder = [((s + half) % n, (s - 1) % n) for s in range(n)]
    direct = [p for p in holder if p[0] not in special] + [(half, half - 1), (0, n - 1)]

    current = layer_input[0]
    upstream = grad_input[0]
    tokens, width = current.shape
    heads = width // HDIM // 3
    step = heads * HDIM

    flag = lambda f: jnp.asarray(f).astype(jnp.int32)
    is_special = jnp.logical_or(me == 0, me == half)
    kept_here = jnp.logical_and(me == half, eviction[0] == 0)
    crossed = jnp.logical_or(me == half - 1, me == n - 1)
    early_pick = jnp.stack([flag(kept_here), flag(is_special), eviction[0]])
    mode = jnp.stack([jnp.where(is_special, 2, eviction[0]), flag(is_special)])
    mode_first = jnp.stack([eviction[0], flag(False)])
    final = flag(me == half - 1)
    take = jnp.stack([flag(crossed), flag(crossed), final])

    rows, held, told, away, early = opened(early_pick, current, stashed, upstream, query_gain, key_gain, step)
    told = send(told, prior)
    held = send(held, holder)
    fetched = send(away, to_partner)
    early = send(early, within)
    totals = lax.psum(rows, "tensor")

    own_a, own_inner = early_backward(width_all, early_pick, stashed, upstream, totals, query_gain, key_gain, heads)
    sent, away = choose(
        mode_first, [(stashed, (0, 0)), (fetched, 0)], [(stashed, (1, 1))], tokens, step, (own_inner, told, held)
    )
    fetched = send(away, to_partner)
    passed = [send(sent, inside)]
    own_inner = lax.psum(own_inner, "tensor")
    slot, last = slot_of(width_all, early_pick, own_a, stashed, upstream, totals, own_inner, step)
    kept = send(last, prior)
    output = forward(width_all, current, totals, query_gain, key_gain, heads, (last,))

    sent, last = choose(
        mode, [(stashed, (0, 1)), (fetched, 0), (slot, 1)], [(stashed, (1, 2)), (slot, 2)], tokens, step,
        (output, passed[0]),
    )
    straight = send(last, direct)
    passed.append(send(sent, prior))

    total = lax.psum(join(told, held, (sent,)), "tensor")

    share = functools.partial(backward, width_all, width)
    a, x, inner = share(
        take, [(passed[0], 0), (early, 0)], [(early, 0), (kept, 0)], total, told,
        jnp.zeros((1, tokens), F32), heads, 0,
    )
    a, x, inner = share(
        take, [(passed[1], 0), (early, step)], [(early, step), (passed[1], 0)],
        total, told, inner, heads, step, (a, x),
    )
    a, x, inner = share(
        take, [(straight, 0), (early, 2 * step), (kept, None)], [(early, 2 * step), (straight, 0)],
        total, told, inner, heads, 2 * step, (a, x),
    )
    inner = lax.psum(inner, "tensor")
    result = finish(width_all, take, a, x, total, told, inner, step)
    return (output[None], result[None])


def solution(mesh):
    placed = (
        P("section", None, "tensor"),
        P("section", None, "tensor"),
        P("section", None, None, "tensor"),
        P("section"),
        P("section", "tensor"),
        P("section", "tensor"),
    )

    def whole(layer_input, *others):
        return jax.shard_map(
            functools.partial(local, layer_input.shape[-1]),
            mesh=mesh,
            in_specs=placed,
            out_specs=(P("section", None, "tensor"), P("section", None, "tensor")),
            check_vma=False,
        )(layer_input, *others)

    return whole
```

```python
import functools
import math

import jax
import jax.numpy as jnp
from jax import lax
from jax.experimental import pallas as pl
from jax.experimental.pallas import tpu as pltpu
from jax.sharding import PartitionSpec as P

HDIM = 128
EPSILON = 1e-05
SCALE = 1.0 / math.sqrt(HDIM)
LOG2E = math.log2(math.e)
VMEM = 32 * 1024 * 1024
MOST = 60 * 1024 * 1024

F32 = jnp.float32
BF16 = jnp.bfloat16


def dot(a, b, contract):
    return lax.dot_general(a, b, ((contract[0], contract[1]), ((), ())), preferred_element_type=F32)


def nt(a, b):
    return dot(a, b, ((1,), (1,)))


def nn(a, b):
    return dot(a, b, ((1,), (0,)))


def block_of(tokens):
    return 256 if tokens % 256 == 0 else tokens


def masked(block, kept):
    return jnp.where(kept, block, -1e30)


def kept_keys(size):
    keys = lax.broadcasted_iota(jnp.int32, (size, size), 0)
    return keys <= lax.broadcasted_iota(jnp.int32, (size, size), 1)


def scores_of(keys, queries, j, size, kept):
    mine = queries[j * size : (j + 1) * size]
    diagonal = masked(nt(keys[j * size : (j + 1) * size], mine), kept)
    if j == 0:
        return [diagonal]
    return [nt(keys[: j * size], mine), diagonal]


def exponents(parts):
    top = functools.reduce(jnp.maximum, [jnp.max(p, axis=0, keepdims=True) for p in parts])
    exps = [jnp.exp2((p - top) * (SCALE * LOG2E)) for p in parts]
    total = sum(jnp.sum(e, axis=0, keepdims=True) for e in exps)
    return exps, total


def stacked(parts):
    return parts[0] if len(parts) == 1 else jnp.concatenate(parts, axis=0)


def normed_head(x, factor, gain_q, gain_k):
    wide = x.astype(F32)
    normed = wide * factor
    return wide, (normed * gain_q).astype(BF16), (normed * gain_k).astype(BF16), normed.astype(BF16)


def column_of(row):
    return jnp.broadcast_to(row, (HDIM, row.shape[1])).T[:, 0:1]


def inverse_rms(total, width_all):
    return lax.rsqrt(total / width_all + EPSILON)


def lanes_of(start, size):
    return (slice(None), slice(start, start + size))


def compiler(limit):
    return pltpu.CompilerParams(vmem_limit_bytes=limit)


IN_VMEM = pl.BlockSpec(memory_space=pltpu.VMEM)
ANYWHERE = pl.BlockSpec(memory_space=pl.ANY)
IN_HBM = pl.BlockSpec(memory_space=pltpu.HBM)


def in_hbm(x):
    return pltpu.with_memory_space_constraint(x, pltpu.HBM)


def forward_kernel(heads, width_all, x_ref, t_ref, gq_ref, gk_ref, *rest):
    o_ref = rest[-1]
    tokens = x_ref.shape[0]
    size = block_of(tokens)
    kept = kept_keys(size)
    factor = column_of(inverse_rms(t_ref[0:1, :], width_all))
    for h in range(heads):
        lanes = slice(h * HDIM, (h + 1) * HDIM)
        wide, q, k, v = normed_head(x_ref[:, lanes], factor, gq_ref[:, lanes], gk_ref[:, lanes])
        vt = v.T
        for j in range(tokens // size):
            exps, total = exponents(scores_of(k, q, j, size, kept))
            mixed = nn(vt[:, : (j + 1) * size], stacked(exps).astype(BF16)) * (1.0 / total)
            rows = slice(j * size, (j + 1) * size)
            o_ref[rows, lanes] = (wide[rows] + mixed.T).astype(BF16)


def forward(width_all, x, totals, gain_q, gain_k, heads, after=()):
    tokens, width = x.shape
    lanes = heads * HDIM
    block = pl.BlockSpec((tokens, lanes), lambda i: (0, i))
    gain = pl.BlockSpec((1, lanes), lambda i: (0, i))
    return pl.pallas_call(
        functools.partial(forward_kernel, heads, width_all),
        out_shape=jax.ShapeDtypeStruct(x.shape, BF16),
        grid=(width // lanes,),
        in_specs=[block, pl.BlockSpec(totals.shape, lambda i: (0, 0)), gain, gain] + [IN_HBM] * len(after),
        out_specs=block,
        compiler_params=compiler(VMEM),
        name="forward",
    )(in_hbm(x), totals, gain_q, gain_k, *map(in_hbm, after))


def backward_head(x, g, factor, gain_q, gain_k):
    tokens = x.shape[0]
    size = block_of(tokens)
    kept = kept_keys(size)
    wide, q, k, v = normed_head(x, factor, gain_q, gain_k)
    kt = k.T
    blocks = tokens // size
    d_q = []
    d_k = [None] * blocks
    d_v = [None] * blocks
    for j in range(blocks):
        rows = slice(j * size, (j + 1) * size)
        exps, total = exponents(scores_of(k, q, j, size, kept))
        inverse = 1.0 / total
        weights = [e * inverse for e in exps]
        grads = [nt(v[: j * size], g[rows])] if j else []
        grads.append(nt(v[rows], g[rows]))
        delta = sum(jnp.sum(w * d, axis=0, keepdims=True) for w, d in zip(weights, grads))
        scores = stacked([(w * ((d - delta) * SCALE)).astype(BF16) for w, d in zip(weights, grads)])
        rounded = stacked([w.astype(BF16) for w in weights])
        d_q.append(nn(kt[:, : (j + 1) * size], scores).T)
        part_k = nn(scores, q[rows])
        part_v = nn(rounded, g[rows])
        for i in range(j + 1):
            mine = slice(i * size, (i + 1) * size)
            d_k[i] = part_k[mine] if d_k[i] is None else d_k[i] + part_k[mine]
            d_v[i] = part_v[mine] if d_v[i] is None else d_v[i] + part_v[mine]
    d_normed = stacked(d_q) * gain_q + stacked(d_k) * gain_k + stacked(d_v)
    return wide, d_normed


def selected(which, refs, at):
    values = [ref[lanes_of(start + at, HDIM)] for ref, start in refs]
    value = values[0]
    for i, other in enumerate(values[1:]):
        value = jnp.where(which == i + 1, other, value)
    return value


def backward_kernel(first, heads, width_all, x_at, g_at, pick_ref, *refs):
    n_x, n_g = len(x_at), len(g_at)
    unevicted = x_at[-1] is None
    xs = list(zip(refs[:n_x], [at or 0 for at in x_at]))
    gs = list(zip(refs[n_x : n_x + n_g], g_at))
    t_ref, told_ref, past_ref = refs[n_x + n_g : n_x + n_g + 3]
    a_ref, x_ref, inner_ref = refs[-3:]
    tokens, width = a_ref.shape
    factor = column_of(inverse_rms(t_ref[2:3, :], width_all))
    evicted = told_ref[:, tokens + 2 * width :] == 1.0
    ready = jnp.logical_and(pick_ref[2] == 1, jnp.logical_not(evicted))
    part = None
    for h in range(heads):
        at = h * HDIM
        mine = lanes_of(first + at, HDIM)
        gain_q = told_ref[lanes_of(tokens + first + at, HDIM)]
        gain_k = told_ref[lanes_of(tokens + width + first + at, HDIM)]
        if unevicted:
            straight, start = xs[0]
            own, own_start = xs[-1]
            x = jnp.where(evicted, straight[lanes_of(start + at, HDIM)].astype(F32), own[lanes_of(own_start + at, HDIM)].astype(F32))
            x = x.astype(BF16)
            for i, (ref, start) in enumerate(xs[1:-1]):
                x = jnp.where(pick_ref[0] == i + 1, ref[lanes_of(start + at, HDIM)], x)
        else:
            x = selected(pick_ref[0], xs, at)
        g = selected(pick_ref[1], gs, at)
        wide, d_normed = backward_head(x, g, factor, gain_q, gain_k)
        a_ref[mine] = g.astype(F32) + jnp.where(ready, 0.0, factor * d_normed)
        x_ref[mine] = x
        product = d_normed * wide
        part = product if part is None else part + product
    inner = jnp.sum(part.T, axis=0, keepdims=True)
    inner_ref[...] = inner if past_ref is None else inner + past_ref[...]


def backward(width_all, width, pick, xs, gs, totals, told, past, heads, first, sofar=(), after=()):
    tokens = totals.shape[1]
    before = 1 + len(xs) + len(gs) + 3
    return pl.pallas_call(
        functools.partial(
            backward_kernel, first, heads, width_all, tuple(at for _, at in xs), tuple(at for _, at in gs)
        ),
        out_shape=(
            jax.ShapeDtypeStruct((tokens, width), F32),
            jax.ShapeDtypeStruct((tokens, width), BF16),
            jax.ShapeDtypeStruct((1, tokens), F32),
        ),
        in_specs=[pl.BlockSpec(memory_space=pltpu.SMEM)] + [IN_VMEM] * (before - 1 + len(sofar))
        + [IN_HBM] * len(after),
        out_specs=(IN_VMEM, IN_VMEM, IN_VMEM),
        input_output_aliases={before: 0, before + 1: 1} if sofar else {},
        compiler_params=compiler(VMEM),
        name="backward",
    )(pick, *[x for x, _ in xs], *[g for g, _ in gs], totals, told, past, *sofar, *after)


def early_kernel(heads, width_all, pick_ref, x_ref, g_ref, t_ref, gq_ref, gk_ref, a_ref, inner_ref):
    @pl.when(pl.program_id(0) == 0)
    def _():
        inner_ref[...] = jnp.zeros_like(inner_ref)

    @pl.when(pick_ref[0] == 1)
    def _():
        factor = column_of(inverse_rms(t_ref[1:2, :], width_all))
        part = None
        for h in range(heads):
            mine = lanes_of(h * HDIM, HDIM)
            g = g_ref[mine]
            wide, d_normed = backward_head(x_ref[mine], g, factor, gq_ref[mine], gk_ref[mine])
            a_ref[mine] = g.astype(F32) + factor * d_normed
            product = d_normed * wide
            part = product if part is None else part + product
        inner_ref[...] += jnp.sum(part.T, axis=0, keepdims=True)


def early_backward(width_all, pick, stash, g, totals, gain_q, gain_k, heads):
    tokens, width = g.shape
    lanes = heads * HDIM
    at = lambda i, pick: (0, i * pick[0])
    block = pl.BlockSpec((tokens, lanes), at)
    still = lambda shape: pl.BlockSpec(shape, lambda i, pick: (0, 0))
    gain = pl.BlockSpec((1, lanes), at)
    return pl.pallas_call(
        functools.partial(early_kernel, heads, width_all),
        out_shape=(jax.ShapeDtypeStruct((tokens, width), F32), jax.ShapeDtypeStruct((1, tokens), F32)),
        grid_spec=pltpu.PrefetchScalarGridSpec(
            num_scalar_prefetch=1,
            grid=(width // lanes,),
            in_specs=[
                pl.BlockSpec((None, None, tokens, lanes), lambda i, pick: (0, 0, 0, i * pick[0])),
                block, still(totals.shape), gain, gain,
            ],
            out_specs=(block, still((1, tokens))),
        ),
        compiler_params=compiler(MOST),
        name="early_backward",
    )(pick, in_hbm(stash), in_hbm(g), totals, gain_q, gain_k)


def row_of(total, inner, width_all):
    return inverse_rms(total, width_all) ** 3 * inner / width_all


def finish_kernel(lanes, width_all, pick_ref, a_ref, x_ref, t_ref, told_ref, inner_ref, o_ref):
    tokens, width = a_ref.shape
    evicted = told_ref[:, tokens + 2 * width : tokens + 2 * width + 1] == 1.0
    ready = jnp.logical_and(pick_ref[2] == 1, jnp.logical_not(evicted))
    row = jnp.where(ready, 0.0, row_of(t_ref[2:3, :], inner_ref[...], width_all))
    at = (slice(None), pl.ds(pl.program_id(0) * lanes, lanes))
    o_ref[...] = (a_ref[at] - x_ref[...].astype(F32) * column_of(row)).astype(BF16)


def finish(width_all, pick, a, x, totals, told, inner, lanes):
    tokens, width = a.shape
    block = pl.BlockSpec((tokens, lanes), lambda i: (0, i))
    return pl.pallas_call(
        functools.partial(finish_kernel, lanes, width_all),
        out_shape=jax.ShapeDtypeStruct(a.shape, BF16),
        grid=(width // lanes,),
        in_specs=[pl.BlockSpec(memory_space=pltpu.SMEM), IN_VMEM, block] + [IN_VMEM] * 3,
        out_specs=block,
        compiler_params=compiler(VMEM),
        name="finish",
    )(pick, a, in_hbm(x), totals, told, inner)


def slot_kernel(width_all, last, pick_ref, a_ref, x_ref, g_ref, t_ref, inner_ref, o_ref, kept_ref):
    special = pick_ref[1] == 1
    step = pl.program_id(0)

    @pl.when(jnp.logical_and(special, pick_ref[0] == 1))
    def _():
        row = column_of(row_of(t_ref[1:2, :], inner_ref[...], width_all))
        o_ref[...] = (a_ref[...] - x_ref[...].astype(F32) * row).astype(BF16)

    @pl.when(jnp.logical_and(special, pick_ref[0] == 0))
    def _():
        o_ref[...] = g_ref[...]

    @pl.when(jnp.logical_and(special, step == 0))
    def _():
        kept_ref[...] = o_ref[...]

    @pl.when(jnp.logical_and(jnp.logical_not(special), step == last))
    def _():
        kept_ref[...] = x_ref[...]


def slot_of(width_all, pick, a, stash, g, totals, inner, lanes):
    tokens, width = g.shape
    last = width // lanes - 1
    block = pl.BlockSpec((tokens, lanes), lambda i, pick: (0, i * pick[1]))
    still = lambda shape: pl.BlockSpec(shape, lambda i, pick: (0, 0))
    return pl.pallas_call(
        functools.partial(slot_kernel, width_all, last),
        out_shape=(jax.ShapeDtypeStruct((tokens, width), BF16), jax.ShapeDtypeStruct((tokens, lanes), BF16)),
        grid_spec=pltpu.PrefetchScalarGridSpec(
            num_scalar_prefetch=1,
            grid=(width // lanes,),
            in_specs=[
                pl.BlockSpec((tokens, lanes), lambda i, pick: (0, i * pick[0])),
                pl.BlockSpec(
                    (None, None, tokens, lanes), lambda i, pick: (0, 0, 0, jnp.where(pick[1] == 1, i, last))
                ),
                block,
                still(totals.shape),
                still(inner.shape),
            ],
            out_specs=(block, still((tokens, lanes))),
        ),
        compiler_params=compiler(MOST),
        name="slot",
    )(pick, a, in_hbm(stash), in_hbm(g), totals, inner)


def choose(mode, first, second, tokens, step, after=()):
    options = (first, second)
    count = len(first) + len(second)

    def kernel(mode_ref, *refs):
        sems = refs[-1]
        outs = refs[-3:-1]
        ins = iter(refs[:count])
        copies = []
        for i, (out, chosen) in enumerate(zip(outs, options)):
            for m, (_, at) in enumerate(chosen):
                ref = next(ins)
                if isinstance(at, tuple):
                    ref = ref.at[0, at[0], :, at[1] * step : (at[1] + 1) * step]
                else:
                    ref = ref.at[:, at * step : (at + 1) * step]
                copies.append((mode_ref[i] == m, pltpu.make_async_copy(ref, out, sems.at[i])))
        for wanted, copy in copies:
            pl.when(wanted)(copy.start)
        for wanted, copy in copies:
            pl.when(wanted)(copy.wait)

    return pl.pallas_call(
        kernel,
        out_shape=[jax.ShapeDtypeStruct((tokens, step), BF16)] * 2,
        in_specs=[pl.BlockSpec(memory_space=pltpu.SMEM)]
        + [IN_HBM if isinstance(at, tuple) else ANYWHERE for _, at in (*first, *second)]
        + [ANYWHERE] * len(after),
        out_specs=[ANYWHERE] * 2,
        scratch_shapes=[pltpu.SemaphoreType.DMA((2,))],
        compiler_params=compiler(VMEM),
        name="choose",
    )(mode, *[array for array, _ in (*first, *second)], *after)


def hold(arrays, after):
    n = len(arrays)
    return pl.pallas_call(
        lambda *refs: None,
        out_shape=[jax.ShapeDtypeStruct(x.shape, x.dtype) for x in arrays],
        in_specs=[IN_HBM] * n + [ANYWHERE] * len(after),
        out_specs=[IN_HBM] * n,
        input_output_aliases={i: i for i in range(n)},
        name="hold",
    )(*arrays, *after)


def open_kernel(
    pieces, pick_ref, current_ref, stash_ref, g_ref, gq_ref, gk_ref, rows_ref, told_ref, away_ref, early_ref, sums
):
    step = pl.program_id(0)
    tokens, lanes = current_ref.shape

    def total(x):
        wide = x.astype(F32)
        square = wide * wide
        return sum(square[:, i : i + HDIM] for i in range(0, square.shape[1], HDIM))

    @pl.when(step == 0)
    def _():
        away_ref[...] = stash_ref[1]

    for i, x in enumerate((current_ref[...], stash_ref[0], stash_ref[1])):
        part = total(x)

        @pl.when(step == 0)
        def _():
            sums[i] = part

        @pl.when(step > 0)
        def _():
            sums[i] += part

    @pl.when(pick_ref[1] == 1)
    def _():
        early_ref[...] = stash_ref[1]

    @pl.when(pick_ref[1] == 0)
    def _():
        early_ref[...] = g_ref[...]

    @pl.when(step == pieces - 1)
    def _():
        for i in range(3):
            rows_ref[i : i + 1, :] = jnp.sum(sums[i].T, axis=0, keepdims=True)
        width = gq_ref.shape[1]
        told_ref[:, :tokens] = rows_ref[1:2, :]
        told_ref[:, tokens : tokens + width] = gq_ref[...]
        told_ref[:, tokens + width : tokens + 2 * width] = gk_ref[...]
        told_ref[:, tokens + 2 * width :] = jnp.full((1, HDIM), pick_ref[2].astype(F32))


def opened(pick, current, stash, g, gain_q, gain_k, lanes):
    tokens, width = current.shape
    pieces = width // lanes
    block = pl.BlockSpec((tokens, lanes), lambda i, pick: (0, i))
    still = lambda *shape: pl.BlockSpec(shape, lambda i, pick: (0, 0))
    told = tokens + 2 * width + HDIM
    return pl.pallas_call(
        functools.partial(open_kernel, pieces),
        out_shape=(
            jax.ShapeDtypeStruct((3, tokens), F32),
            jax.ShapeDtypeStruct((1, told), F32),
            jax.ShapeDtypeStruct((tokens, lanes), BF16),
            jax.ShapeDtypeStruct((tokens, width), BF16),
        ),
        grid_spec=pltpu.PrefetchScalarGridSpec(
            num_scalar_prefetch=1,
            grid=(pieces,),
            in_specs=[
                block,
                pl.BlockSpec((None, 2, tokens, lanes), lambda i, pick: (0, 0, 0, i)),
                block,
                still(1, width),
                still(1, width),
            ],
            out_specs=(still(3, tokens), still(1, told), still(tokens, lanes), block),
            scratch_shapes=[pltpu.VMEM((3, tokens, HDIM), F32)],
        ),
        compiler_params=compiler(MOST),
        name="opened",
    )(pick, in_hbm(current), in_hbm(stash), in_hbm(g), gain_q, gain_k)


def join_kernel(rows_ref, told_ref, held_ref, o_ref):
    tokens = rows_ref.shape[1]
    evicted = told_ref[:, told_ref.shape[1] - 1 :] == 1.0
    o_ref[0:2, :] = rows_ref[0:2, :]
    o_ref[2:3, :] = jnp.where(evicted, held_ref[2:3, :], told_ref[:, :tokens])


def join(rows, told, held):
    return pl.pallas_call(
        join_kernel,
        out_shape=jax.ShapeDtypeStruct(rows.shape, F32),
        in_specs=[IN_VMEM] * 3,
        out_specs=IN_VMEM,
        compiler_params=compiler(VMEM),
        name="join",
    )(rows, told, held)


def send(x, pairs):
    return lax.ppermute(x, "section", pairs)


def local(width_all, layer_input, grad_input, stashed, eviction, query_gain, key_gain):
    n = lax.axis_size("section")
    half = n // 2
    special = (0, half)
    me = lax.axis_index("section")

    prior = [(s, (s - 1) % n) for s in range(n)]
    inside = [(s, s - 1) for s in range(n) if s not in special]
    within = inside + [(half, n - 1), (0, half - 1)]
    to_partner = [(s, (s + half) % n) for s in range(n) if s not in special]
    holder = [((s + half) % n, (s - 1) % n) for s in range(n)]
    direct = [p for p in holder if p[0] not in special] + [(half, half - 1), (0, n - 1)]

    current = layer_input[0]
    upstream = grad_input[0]
    tokens, width = current.shape
    heads = width // HDIM // 3
    step = heads * HDIM

    flag = lambda f: jnp.asarray(f).astype(jnp.int32)
    is_special = jnp.logical_or(me == 0, me == half)
    kept_here = jnp.logical_and(me == half, eviction[0] == 0)
    crossed = jnp.logical_or(me == half - 1, me == n - 1)
    early_pick = jnp.stack([flag(kept_here), flag(is_special), eviction[0]])
    mode = jnp.stack([jnp.where(is_special, 2, eviction[0]), flag(is_special)])
    mode_first = jnp.stack([eviction[0], flag(False)])
    final = flag(me == half - 1)
    take = jnp.stack([flag(crossed), flag(crossed), final])

    stash = in_hbm(stashed)
    rows, told, away, early = opened(early_pick, current, stashed, upstream, query_gain, key_gain, step)
    told = send(told, prior)
    held = send(rows, holder)
    away, early = hold((away, early), (told, held))
    fetched = send(away, to_partner)
    early = send(early, within)
    total = lax.psum(join(rows, told, held), "tensor")

    own_a, own_inner = early_backward(width_all, early_pick, stashed, upstream, total, query_gain, key_gain, heads)
    sent, away = choose(
        mode_first, [(stash, (0, 0)), (fetched, 0)], [(stash, (1, 1))], tokens, step, (in_hbm(own_inner),)
    )
    fetched = send(away, to_partner)
    passed = [send(sent, inside)]
    own_inner = lax.psum(own_inner, "tensor")
    slot, last = slot_of(width_all, early_pick, own_a, stashed, upstream, total, own_inner, step)
    kept = send(last, prior)
    slot = in_hbm(slot)
    output = forward(width_all, current, total, query_gain, key_gain, heads, (last,))

    sent, last = choose(
        mode, [(stash, (0, 1)), (fetched, 0), (slot, 1)], [(stash, (1, 2)), (slot, 2)], tokens, step,
        (in_hbm(output), passed[0]),
    )
    straight = send(last, direct)
    passed.append(send(sent, prior))

    share = functools.partial(backward, width_all, width)
    a, x, inner = share(
        take, [(passed[0], 0), (early, 0)], [(early, 0), (kept, 0)], total, told,
        jnp.zeros((1, tokens), F32), heads, 0,
    )
    a, x, inner = share(
        take, [(passed[1], 0), (early, step)], [(early, step), (passed[1], 0)],
        total, told, inner, heads, step, (a, x),
    )
    a, x, inner = share(
        take, [(straight, 0), (early, 2 * step), (kept, None)], [(early, 2 * step), (straight, 0)],
        total, told, inner, heads, 2 * step, (a, x),
    )
    inner = lax.psum(inner, "tensor")
    result = finish(width_all, take, a, x, total, told, inner, step)
    return (output[None], result[None])


def solution(mesh):
    placed = (
        P("section", None, "tensor"),
        P("section", None, "tensor"),
        P("section", None, None, "tensor"),
        P("section"),
        P("section", "tensor"),
        P("section", "tensor"),
    )

    def whole(layer_input, *others):
        return jax.shard_map(
            functools.partial(local, layer_input.shape[-1]),
            mesh=mesh,
            in_specs=placed,
            out_specs=(P("section", None, "tensor"), P("section", None, "tensor")),
            check_vma=False,
        )(layer_input, *others)

    return whole
```

```python
import functools
import math

import jax
import jax.numpy as jnp
from jax import lax
from jax.experimental import pallas as pl
from jax.experimental.pallas import tpu as pltpu
from jax.sharding import PartitionSpec as P

HDIM = 128
EPSILON = 1e-05
SCALE = 1.0 / math.sqrt(HDIM)
LOG2E = math.log2(math.e)
VMEM = 32 * 1024 * 1024
MOST = 60 * 1024 * 1024

F32 = jnp.float32
BF16 = jnp.bfloat16


def dot(a, b, contract):
    return lax.dot_general(a, b, ((contract[0], contract[1]), ((), ())), preferred_element_type=F32)


def nt(a, b):
    return dot(a, b, ((1,), (1,)))


def nn(a, b):
    return dot(a, b, ((1,), (0,)))


def block_of(tokens):
    return 256 if tokens % 256 == 0 else tokens


def masked(block, kept):
    return jnp.where(kept, block, -1e30)


def kept_keys(size):
    keys = lax.broadcasted_iota(jnp.int32, (size, size), 0)
    return keys <= lax.broadcasted_iota(jnp.int32, (size, size), 1)


def scores_of(keys, queries, j, size, kept):
    mine = queries[j * size : (j + 1) * size]
    diagonal = masked(nt(keys[j * size : (j + 1) * size], mine), kept)
    if j == 0:
        return [diagonal]
    return [nt(keys[: j * size], mine), diagonal]


def exponents(parts):
    top = functools.reduce(jnp.maximum, [jnp.max(p, axis=0, keepdims=True) for p in parts])
    exps = [jnp.exp2((p - top) * (SCALE * LOG2E)) for p in parts]
    total = sum(jnp.sum(e, axis=0, keepdims=True) for e in exps)
    return exps, total


def stacked(parts):
    return parts[0] if len(parts) == 1 else jnp.concatenate(parts, axis=0)


def normed_head(x, factor, gain_q, gain_k):
    wide = x.astype(F32)
    normed = wide * factor
    return wide, (normed * gain_q).astype(BF16), (normed * gain_k).astype(BF16), normed.astype(BF16)


def column_of(row):
    return jnp.broadcast_to(row, (HDIM, row.shape[1])).T[:, 0:1]


def inverse_rms(total, width_all):
    return lax.rsqrt(total / width_all + EPSILON)


def lanes_of(start, size):
    return (slice(None), slice(start, start + size))


def compiler(limit):
    return pltpu.CompilerParams(vmem_limit_bytes=limit)


IN_VMEM = pl.BlockSpec(memory_space=pltpu.VMEM)
ANYWHERE = pl.BlockSpec(memory_space=pl.ANY)
IN_HBM = pl.BlockSpec(memory_space=pltpu.HBM)


def in_hbm(x):
    return pltpu.with_memory_space_constraint(x, pltpu.HBM)


def forward_kernel(heads, width_all, x_ref, t_ref, gq_ref, gk_ref, *rest):
    o_ref = rest[-1]
    tokens = x_ref.shape[0]
    size = block_of(tokens)
    kept = kept_keys(size)
    factor = column_of(inverse_rms(t_ref[0:1, :], width_all))
    for h in range(heads):
        lanes = slice(h * HDIM, (h + 1) * HDIM)
        wide, q, k, v = normed_head(x_ref[:, lanes], factor, gq_ref[:, lanes], gk_ref[:, lanes])
        vt = v.T
        for j in range(tokens // size):
            exps, total = exponents(scores_of(k, q, j, size, kept))
            mixed = nn(vt[:, : (j + 1) * size], stacked(exps).astype(BF16)) * (1.0 / total)
            rows = slice(j * size, (j + 1) * size)
            o_ref[rows, lanes] = (wide[rows] + mixed.T).astype(BF16)


def forward(width_all, x, totals, gain_q, gain_k, heads, after=()):
    tokens, width = x.shape
    lanes = heads * HDIM
    block = pl.BlockSpec((tokens, lanes), lambda i: (0, i))
    gain = pl.BlockSpec((1, lanes), lambda i: (0, i))
    return pl.pallas_call(
        functools.partial(forward_kernel, heads, width_all),
        out_shape=jax.ShapeDtypeStruct(x.shape, BF16),
        grid=(width // lanes,),
        in_specs=[block, pl.BlockSpec(totals.shape, lambda i: (0, 0)), gain, gain] + [IN_HBM] * len(after),
        out_specs=block,
        compiler_params=compiler(VMEM),
        name="forward",
    )(in_hbm(x), totals, gain_q, gain_k, *map(in_hbm, after))


def backward_head(x, g, factor, gain_q, gain_k):
    tokens = x.shape[0]
    size = block_of(tokens)
    kept = kept_keys(size)
    wide, q, k, v = normed_head(x, factor, gain_q, gain_k)
    kt = k.T
    blocks = tokens // size
    d_q = []
    d_k = [None] * blocks
    d_v = [None] * blocks
    for j in range(blocks):
        rows = slice(j * size, (j + 1) * size)
        exps, total = exponents(scores_of(k, q, j, size, kept))
        inverse = 1.0 / total
        weights = [e * inverse for e in exps]
        grads = [nt(v[: j * size], g[rows])] if j else []
        grads.append(nt(v[rows], g[rows]))
        delta = sum(jnp.sum(w * d, axis=0, keepdims=True) for w, d in zip(weights, grads))
        scores = stacked([(w * ((d - delta) * SCALE)).astype(BF16) for w, d in zip(weights, grads)])
        rounded = stacked([w.astype(BF16) for w in weights])
        d_q.append(nn(kt[:, : (j + 1) * size], scores).T)
        part_k = nn(scores, q[rows])
        part_v = nn(rounded, g[rows])
        for i in range(j + 1):
            mine = slice(i * size, (i + 1) * size)
            d_k[i] = part_k[mine] if d_k[i] is None else d_k[i] + part_k[mine]
            d_v[i] = part_v[mine] if d_v[i] is None else d_v[i] + part_v[mine]
    d_normed = stacked(d_q) * gain_q + stacked(d_k) * gain_k + stacked(d_v)
    return wide, d_normed


def selected(which, refs, at):
    values = [ref[lanes_of(start + at, HDIM)] for ref, start in refs]
    value = values[0]
    for i, other in enumerate(values[1:]):
        value = jnp.where(which == i + 1, other, value)
    return value


def backward_kernel(first, heads, width_all, x_at, g_at, pick_ref, *refs):
    n_x, n_g = len(x_at), len(g_at)
    unevicted = x_at[-1] is None
    xs = list(zip(refs[:n_x], [at or 0 for at in x_at]))
    gs = list(zip(refs[n_x : n_x + n_g], g_at))
    t_ref, told_ref, past_ref = refs[n_x + n_g : n_x + n_g + 3]
    a_ref, x_ref, inner_ref = refs[-3:]
    tokens, width = a_ref.shape
    factor = column_of(inverse_rms(t_ref[2:3, :], width_all))
    evicted = told_ref[:, tokens + 2 * width :] == 1.0
    ready = jnp.logical_and(pick_ref[2] == 1, jnp.logical_not(evicted))
    part = None
    for h in range(heads):
        at = h * HDIM
        mine = lanes_of(first + at, HDIM)
        gain_q = told_ref[lanes_of(tokens + first + at, HDIM)]
        gain_k = told_ref[lanes_of(tokens + width + first + at, HDIM)]
        if unevicted:
            straight, start = xs[0]
            own, own_start = xs[-1]
            x = jnp.where(evicted, straight[lanes_of(start + at, HDIM)].astype(F32), own[lanes_of(own_start + at, HDIM)].astype(F32))
            x = x.astype(BF16)
            for i, (ref, start) in enumerate(xs[1:-1]):
                x = jnp.where(pick_ref[0] == i + 1, ref[lanes_of(start + at, HDIM)], x)
        else:
            x = selected(pick_ref[0], xs, at)
        g = selected(pick_ref[1], gs, at)
        wide, d_normed = backward_head(x, g, factor, gain_q, gain_k)
        a_ref[mine] = g.astype(F32) + jnp.where(ready, 0.0, factor * d_normed)
        x_ref[mine] = x
        product = d_normed * wide
        part = product if part is None else part + product
    inner = jnp.sum(part.T, axis=0, keepdims=True)
    inner_ref[...] = inner if past_ref is None else inner + past_ref[...]


def backward(width_all, width, pick, xs, gs, totals, told, past, heads, first, sofar=(), after=()):
    tokens = totals.shape[1]
    before = 1 + len(xs) + len(gs) + 3
    return pl.pallas_call(
        functools.partial(
            backward_kernel, first, heads, width_all, tuple(at for _, at in xs), tuple(at for _, at in gs)
        ),
        out_shape=(
            jax.ShapeDtypeStruct((tokens, width), F32),
            jax.ShapeDtypeStruct((tokens, width), BF16),
            jax.ShapeDtypeStruct((1, tokens), F32),
        ),
        in_specs=[pl.BlockSpec(memory_space=pltpu.SMEM)] + [IN_VMEM] * (before - 1 + len(sofar))
        + [IN_HBM] * len(after),
        out_specs=(IN_VMEM, IN_VMEM, IN_VMEM),
        input_output_aliases={before: 0, before + 1: 1} if sofar else {},
        compiler_params=compiler(VMEM),
        name="backward",
    )(pick, *[x for x, _ in xs], *[g for g, _ in gs], totals, told, past, *sofar, *after)


def early_kernel(heads, width_all, pick_ref, x_ref, g_ref, t_ref, gq_ref, gk_ref, a_ref, inner_ref):
    @pl.when(pl.program_id(0) == 0)
    def _():
        inner_ref[...] = jnp.zeros_like(inner_ref)

    @pl.when(pick_ref[0] == 1)
    def _():
        factor = column_of(inverse_rms(t_ref[1:2, :], width_all))
        part = None
        for h in range(heads):
            mine = lanes_of(h * HDIM, HDIM)
            g = g_ref[mine]
            wide, d_normed = backward_head(x_ref[mine], g, factor, gq_ref[mine], gk_ref[mine])
            a_ref[mine] = g.astype(F32) + factor * d_normed
            product = d_normed * wide
            part = product if part is None else part + product
        inner_ref[...] += jnp.sum(part.T, axis=0, keepdims=True)


def early_backward(width_all, pick, stash, g, totals, gain_q, gain_k, heads):
    tokens, width = g.shape
    lanes = heads * HDIM
    at = lambda i, pick: (0, i * pick[0])
    block = pl.BlockSpec((tokens, lanes), at)
    still = lambda shape: pl.BlockSpec(shape, lambda i, pick: (0, 0))
    gain = pl.BlockSpec((1, lanes), at)
    return pl.pallas_call(
        functools.partial(early_kernel, heads, width_all),
        out_shape=(jax.ShapeDtypeStruct((tokens, width), F32), jax.ShapeDtypeStruct((1, tokens), F32)),
        grid_spec=pltpu.PrefetchScalarGridSpec(
            num_scalar_prefetch=1,
            grid=(width // lanes,),
            in_specs=[
                pl.BlockSpec((None, None, tokens, lanes), lambda i, pick: (0, 0, 0, i * pick[0])),
                block, still(totals.shape), gain, gain,
            ],
            out_specs=(block, still((1, tokens))),
        ),
        compiler_params=compiler(MOST),
        name="early_backward",
    )(pick, in_hbm(stash), in_hbm(g), totals, gain_q, gain_k)


def row_of(total, inner, width_all):
    return inverse_rms(total, width_all) ** 3 * inner / width_all


def finish_kernel(lanes, width_all, pick_ref, a_ref, x_ref, t_ref, told_ref, inner_ref, o_ref):
    tokens, width = a_ref.shape
    evicted = told_ref[:, tokens + 2 * width : tokens + 2 * width + 1] == 1.0
    ready = jnp.logical_and(pick_ref[2] == 1, jnp.logical_not(evicted))
    row = jnp.where(ready, 0.0, row_of(t_ref[2:3, :], inner_ref[...], width_all))
    at = (slice(None), pl.ds(pl.program_id(0) * lanes, lanes))
    o_ref[...] = (a_ref[at] - x_ref[...].astype(F32) * column_of(row)).astype(BF16)


def finish(width_all, pick, a, x, totals, told, inner, lanes):
    tokens, width = a.shape
    block = pl.BlockSpec((tokens, lanes), lambda i: (0, i))
    return pl.pallas_call(
        functools.partial(finish_kernel, lanes, width_all),
        out_shape=jax.ShapeDtypeStruct(a.shape, BF16),
        grid=(width // lanes,),
        in_specs=[pl.BlockSpec(memory_space=pltpu.SMEM), IN_VMEM, block] + [IN_VMEM] * 3,
        out_specs=block,
        compiler_params=compiler(VMEM),
        name="finish",
    )(pick, a, in_hbm(x), totals, told, inner)


def slot_kernel(width_all, last, pick_ref, a_ref, x_ref, g_ref, t_ref, inner_ref, o_ref, kept_ref):
    special = pick_ref[1] == 1
    step = pl.program_id(0)

    @pl.when(jnp.logical_and(special, pick_ref[0] == 1))
    def _():
        row = column_of(row_of(t_ref[1:2, :], inner_ref[...], width_all))
        o_ref[...] = (a_ref[...] - x_ref[...].astype(F32) * row).astype(BF16)

    @pl.when(jnp.logical_and(special, pick_ref[0] == 0))
    def _():
        o_ref[...] = g_ref[...]

    @pl.when(jnp.logical_and(special, step == 0))
    def _():
        kept_ref[...] = o_ref[...]

    @pl.when(jnp.logical_and(jnp.logical_not(special), step == last))
    def _():
        kept_ref[...] = x_ref[...]


def slot_of(width_all, pick, a, stash, g, totals, inner, lanes):
    tokens, width = g.shape
    last = width // lanes - 1
    block = pl.BlockSpec((tokens, lanes), lambda i, pick: (0, i * pick[1]))
    still = lambda shape: pl.BlockSpec(shape, lambda i, pick: (0, 0))
    return pl.pallas_call(
        functools.partial(slot_kernel, width_all, last),
        out_shape=(jax.ShapeDtypeStruct((tokens, width), BF16), jax.ShapeDtypeStruct((tokens, lanes), BF16)),
        grid_spec=pltpu.PrefetchScalarGridSpec(
            num_scalar_prefetch=1,
            grid=(width // lanes,),
            in_specs=[
                pl.BlockSpec((tokens, lanes), lambda i, pick: (0, i * pick[0])),
                pl.BlockSpec(
                    (None, None, tokens, lanes), lambda i, pick: (0, 0, 0, jnp.where(pick[1] == 1, i, last))
                ),
                block,
                still(totals.shape),
                still(inner.shape),
            ],
            out_specs=(block, still((tokens, lanes))),
        ),
        compiler_params=compiler(MOST),
        name="slot",
    )(pick, a, in_hbm(stash), in_hbm(g), totals, inner)


def choose(mode, first, second, tokens, step, after=()):
    options = (first, second)
    count = len(first) + len(second)

    def kernel(mode_ref, *refs):
        sems = refs[-1]
        outs = refs[-3:-1]
        ins = iter(refs[:count])
        copies = []
        for i, (out, chosen) in enumerate(zip(outs, options)):
            for m, (_, at) in enumerate(chosen):
                ref = next(ins)
                if isinstance(at, tuple):
                    ref = ref.at[0, at[0], :, at[1] * step : (at[1] + 1) * step]
                else:
                    ref = ref.at[:, at * step : (at + 1) * step]
                copies.append((mode_ref[i] == m, pltpu.make_async_copy(ref, out, sems.at[i])))
        for wanted, copy in copies:
            pl.when(wanted)(copy.start)
        for wanted, copy in copies:
            pl.when(wanted)(copy.wait)

    return pl.pallas_call(
        kernel,
        out_shape=[jax.ShapeDtypeStruct((tokens, step), BF16)] * 2,
        in_specs=[pl.BlockSpec(memory_space=pltpu.SMEM)]
        + [IN_HBM if isinstance(at, tuple) else ANYWHERE for _, at in (*first, *second)]
        + [ANYWHERE] * len(after),
        out_specs=[IN_VMEM] * 2,
        scratch_shapes=[pltpu.SemaphoreType.DMA((2,))],
        compiler_params=compiler(VMEM),
        name="choose",
    )(mode, *[array for array, _ in (*first, *second)], *after)


def hold(arrays, after):
    n = len(arrays)
    return pl.pallas_call(
        lambda *refs: None,
        out_shape=[jax.ShapeDtypeStruct(x.shape, x.dtype) for x in arrays],
        in_specs=[IN_HBM] * n + [ANYWHERE] * len(after),
        out_specs=[IN_HBM] * n,
        input_output_aliases={i: i for i in range(n)},
        name="hold",
    )(*arrays, *after)


def open_kernel(
    pieces, pick_ref, current_ref, stash_ref, g_ref, gq_ref, gk_ref, rows_ref, told_ref, away_ref, early_ref, sums
):
    step = pl.program_id(0)
    tokens, lanes = current_ref.shape

    def total(x):
        wide = x.astype(F32)
        square = wide * wide
        return sum(square[:, i : i + HDIM] for i in range(0, square.shape[1], HDIM))

    @pl.when(step == 0)
    def _():
        away_ref[...] = stash_ref[1]

    for i, x in enumerate((current_ref[...], stash_ref[0], stash_ref[1])):
        part = total(x)

        @pl.when(step == 0)
        def _():
            sums[i] = part

        @pl.when(step > 0)
        def _():
            sums[i] += part

    @pl.when(pick_ref[1] == 1)
    def _():
        early_ref[...] = stash_ref[1]

    @pl.when(pick_ref[1] == 0)
    def _():
        early_ref[...] = g_ref[...]

    @pl.when(step == pieces - 1)
    def _():
        for i in range(3):
            rows_ref[i : i + 1, :] = jnp.sum(sums[i].T, axis=0, keepdims=True)
        width = gq_ref.shape[1]
        told_ref[:, :tokens] = rows_ref[1:2, :]
        told_ref[:, tokens : tokens + width] = gq_ref[...]
        told_ref[:, tokens + width : tokens + 2 * width] = gk_ref[...]
        told_ref[:, tokens + 2 * width :] = jnp.full((1, HDIM), pick_ref[2].astype(F32))


def opened(pick, current, stash, g, gain_q, gain_k, lanes):
    tokens, width = current.shape
    pieces = width // lanes
    block = pl.BlockSpec((tokens, lanes), lambda i, pick: (0, i))
    still = lambda *shape: pl.BlockSpec(shape, lambda i, pick: (0, 0))
    told = tokens + 2 * width + HDIM
    return pl.pallas_call(
        functools.partial(open_kernel, pieces),
        out_shape=(
            jax.ShapeDtypeStruct((3, tokens), F32),
            jax.ShapeDtypeStruct((1, told), F32),
            jax.ShapeDtypeStruct((tokens, lanes), BF16),
            jax.ShapeDtypeStruct((tokens, width), BF16),
        ),
        grid_spec=pltpu.PrefetchScalarGridSpec(
            num_scalar_prefetch=1,
            grid=(pieces,),
            in_specs=[
                block,
                pl.BlockSpec((None, 2, tokens, lanes), lambda i, pick: (0, 0, 0, i)),
                block,
                still(1, width),
                still(1, width),
            ],
            out_specs=(still(3, tokens), still(1, told), still(tokens, lanes), block),
            scratch_shapes=[pltpu.VMEM((3, tokens, HDIM), F32)],
        ),
        compiler_params=compiler(MOST),
        name="opened",
    )(pick, in_hbm(current), in_hbm(stash), in_hbm(g), gain_q, gain_k)


def join_kernel(rows_ref, told_ref, held_ref, o_ref):
    tokens = rows_ref.shape[1]
    evicted = told_ref[:, told_ref.shape[1] - 1 :] == 1.0
    o_ref[0:2, :] = rows_ref[0:2, :]
    o_ref[2:3, :] = jnp.where(evicted, held_ref[2:3, :], told_ref[:, :tokens])


def join(rows, told, held):
    return pl.pallas_call(
        join_kernel,
        out_shape=jax.ShapeDtypeStruct(rows.shape, F32),
        in_specs=[IN_VMEM] * 3,
        out_specs=IN_VMEM,
        compiler_params=compiler(VMEM),
        name="join",
    )(rows, told, held)


def send(x, pairs):
    return lax.ppermute(x, "section", pairs)


def local(width_all, layer_input, grad_input, stashed, eviction, query_gain, key_gain):
    n = lax.axis_size("section")
    half = n // 2
    special = (0, half)
    me = lax.axis_index("section")

    prior = [(s, (s - 1) % n) for s in range(n)]
    inside = [(s, s - 1) for s in range(n) if s not in special]
    within = inside + [(half, n - 1), (0, half - 1)]
    to_partner = [(s, (s + half) % n) for s in range(n) if s not in special]
    holder = [((s + half) % n, (s - 1) % n) for s in range(n)]
    direct = [p for p in holder if p[0] not in special] + [(half, half - 1), (0, n - 1)]

    current = layer_input[0]
    upstream = grad_input[0]
    tokens, width = current.shape
    heads = width // HDIM // 3
    step = heads * HDIM

    flag = lambda f: jnp.asarray(f).astype(jnp.int32)
    is_special = jnp.logical_or(me == 0, me == half)
    kept_here = jnp.logical_and(me == half, eviction[0] == 0)
    crossed = jnp.logical_or(me == half - 1, me == n - 1)
    early_pick = jnp.stack([flag(kept_here), flag(is_special), eviction[0]])
    mode = jnp.stack([jnp.where(is_special, 2, eviction[0]), flag(is_special)])
    mode_first = jnp.stack([eviction[0], flag(False)])
    final = flag(me == half - 1)
    take = jnp.stack([flag(crossed), flag(crossed), final])

    stash = in_hbm(stashed)
    rows, told, away, early = opened(early_pick, current, stashed, upstream, query_gain, key_gain, step)
    told = send(told, prior)
    held = send(rows, holder)
    away, early = hold((away, early), (told, held))
    fetched = send(away, to_partner)
    early = send(early, within)
    total = lax.psum(join(rows, told, held), "tensor")

    own_a, own_inner = early_backward(width_all, early_pick, stashed, upstream, total, query_gain, key_gain, heads)
    sent, away = choose(
        mode_first, [(stash, (0, 0)), (fetched, 0)], [(stash, (1, 1))], tokens, step, (in_hbm(own_inner),)
    )
    fetched = send(away, to_partner)
    passed = [send(sent, inside)]
    own_inner = lax.psum(own_inner, "tensor")
    slot, last = slot_of(width_all, early_pick, own_a, stashed, upstream, total, own_inner, step)
    kept = send(last, prior)
    slot = in_hbm(slot)
    output = forward(width_all, current, total, query_gain, key_gain, heads, (last,))

    sent, last = choose(
        mode, [(stash, (0, 1)), (fetched, 0), (slot, 1)], [(stash, (1, 2)), (slot, 2)], tokens, step,
        (in_hbm(output), passed[0]),
    )
    straight = send(last, direct)
    passed.append(send(sent, prior))

    share = functools.partial(backward, width_all, width)
    a, x, inner = share(
        take, [(passed[0], 0), (early, 0)], [(early, 0), (kept, 0)], total, told,
        jnp.zeros((1, tokens), F32), heads, 0,
    )
    a, x, inner = share(
        take, [(passed[1], 0), (early, step)], [(early, step), (passed[1], 0)],
        total, told, inner, heads, step, (a, x),
    )
    a, x, inner = share(
        take, [(straight, 0), (early, 2 * step), (kept, None)], [(early, 2 * step), (straight, 0)],
        total, told, inner, heads, 2 * step, (a, x),
    )
    inner = lax.psum(inner, "tensor")
    result = finish(width_all, take, a, x, total, told, inner, step)
    return (output[None], result[None])


def solution(mesh):
    placed = (
        P("section", None, "tensor"),
        P("section", None, "tensor"),
        P("section", None, None, "tensor"),
        P("section"),
        P("section", "tensor"),
        P("section", "tensor"),
    )

    def whole(layer_input, *others):
        return jax.shard_map(
            functools.partial(local, layer_input.shape[-1]),
            mesh=mesh,
            in_specs=placed,
            out_specs=(P("section", None, "tensor"), P("section", None, "tensor")),
            check_vma=False,
        )(layer_input, *others)

    return whole
```

```python
import functools
import math

import jax
import jax.numpy as jnp
from jax import lax
from jax.experimental import pallas as pl
from jax.experimental.pallas import tpu as pltpu
from jax.sharding import PartitionSpec as P

HDIM = 128
EPSILON = 1e-05
SCALE = 1.0 / math.sqrt(HDIM)
LOG2E = math.log2(math.e)
VMEM = 32 * 1024 * 1024
MOST = 60 * 1024 * 1024

F32 = jnp.float32
BF16 = jnp.bfloat16


def dot(a, b, contract):
    return lax.dot_general(a, b, ((contract[0], contract[1]), ((), ())), preferred_element_type=F32)


def nt(a, b):
    return dot(a, b, ((1,), (1,)))


def nn(a, b):
    return dot(a, b, ((1,), (0,)))


def block_of(tokens):
    return 256 if tokens % 256 == 0 else tokens


def masked(block, kept):
    return jnp.where(kept, block, -1e30)


def kept_keys(size):
    keys = lax.broadcasted_iota(jnp.int32, (size, size), 0)
    return keys <= lax.broadcasted_iota(jnp.int32, (size, size), 1)


def scores_of(keys, queries, j, size, kept):
    mine = queries[j * size : (j + 1) * size]
    diagonal = masked(nt(keys[j * size : (j + 1) * size], mine), kept)
    if j == 0:
        return [diagonal]
    return [nt(keys[: j * size], mine), diagonal]


def exponents(parts):
    top = functools.reduce(jnp.maximum, [jnp.max(p, axis=0, keepdims=True) for p in parts])
    exps = [jnp.exp2((p - top) * (SCALE * LOG2E)) for p in parts]
    total = sum(jnp.sum(e, axis=0, keepdims=True) for e in exps)
    return exps, total


def stacked(parts):
    return parts[0] if len(parts) == 1 else jnp.concatenate(parts, axis=0)


def normed_head(x, factor, gain_q, gain_k):
    wide = x.astype(F32)
    normed = wide * factor
    return wide, (normed * gain_q).astype(BF16), (normed * gain_k).astype(BF16), normed.astype(BF16)


def column_of(row):
    return jnp.broadcast_to(row, (HDIM, row.shape[1])).T[:, 0:1]


def inverse_rms(total, width_all):
    return lax.rsqrt(total / width_all + EPSILON)


def lanes_of(start, size):
    return (slice(None), slice(start, start + size))


def compiler(limit):
    return pltpu.CompilerParams(vmem_limit_bytes=limit)


IN_VMEM = pl.BlockSpec(memory_space=pltpu.VMEM)
ANYWHERE = pl.BlockSpec(memory_space=pl.ANY)
IN_HBM = pl.BlockSpec(memory_space=pltpu.HBM)


def in_hbm(x):
    return pltpu.with_memory_space_constraint(x, pltpu.HBM)


def forward_kernel(heads, width_all, x_ref, t_ref, gq_ref, gk_ref, *rest):
    o_ref = rest[-1]
    tokens = x_ref.shape[0]
    size = block_of(tokens)
    kept = kept_keys(size)
    factor = column_of(inverse_rms(t_ref[0:1, :], width_all))
    for h in range(heads):
        lanes = slice(h * HDIM, (h + 1) * HDIM)
        wide, q, k, v = normed_head(x_ref[:, lanes], factor, gq_ref[:, lanes], gk_ref[:, lanes])
        vt = v.T
        for j in range(tokens // size):
            exps, total = exponents(scores_of(k, q, j, size, kept))
            mixed = nn(vt[:, : (j + 1) * size], stacked(exps).astype(BF16)) * (1.0 / total)
            rows = slice(j * size, (j + 1) * size)
            o_ref[rows, lanes] = (wide[rows] + mixed.T).astype(BF16)


def forward(width_all, x, totals, gain_q, gain_k, heads, after=()):
    tokens, width = x.shape
    lanes = heads * HDIM
    block = pl.BlockSpec((tokens, lanes), lambda i: (0, i))
    gain = pl.BlockSpec((1, lanes), lambda i: (0, i))
    return pl.pallas_call(
        functools.partial(forward_kernel, heads, width_all),
        out_shape=jax.ShapeDtypeStruct(x.shape, BF16),
        grid=(width // lanes,),
        in_specs=[block, pl.BlockSpec(totals.shape, lambda i: (0, 0)), gain, gain] + [IN_HBM] * len(after),
        out_specs=block,
        compiler_params=compiler(VMEM),
        name="forward",
    )(in_hbm(x), totals, gain_q, gain_k, *map(in_hbm, after))


def backward_head(x, g, factor, gain_q, gain_k):
    tokens = x.shape[0]
    size = block_of(tokens)
    kept = kept_keys(size)
    wide, q, k, v = normed_head(x, factor, gain_q, gain_k)
    kt = k.T
    blocks = tokens // size
    d_q = []
    d_k = [None] * blocks
    d_v = [None] * blocks
    for j in range(blocks):
        rows = slice(j * size, (j + 1) * size)
        exps, total = exponents(scores_of(k, q, j, size, kept))
        inverse = 1.0 / total
        weights = [e * inverse for e in exps]
        grads = [nt(v[: j * size], g[rows])] if j else []
        grads.append(nt(v[rows], g[rows]))
        delta = sum(jnp.sum(w * d, axis=0, keepdims=True) for w, d in zip(weights, grads))
        scores = stacked([(w * ((d - delta) * SCALE)).astype(BF16) for w, d in zip(weights, grads)])
        rounded = stacked([w.astype(BF16) for w in weights])
        d_q.append(nn(kt[:, : (j + 1) * size], scores).T)
        part_k = nn(scores, q[rows])
        part_v = nn(rounded, g[rows])
        for i in range(j + 1):
            mine = slice(i * size, (i + 1) * size)
            d_k[i] = part_k[mine] if d_k[i] is None else d_k[i] + part_k[mine]
            d_v[i] = part_v[mine] if d_v[i] is None else d_v[i] + part_v[mine]
    d_normed = stacked(d_q) * gain_q + stacked(d_k) * gain_k + stacked(d_v)
    return wide, d_normed


def backward_kernel(first, heads, width_all, x_at, g_at, odd, pick_ref, *refs):
    n_x, n_g = len(x_at), len(g_at)
    x_refs, g_refs = refs[:n_x], refs[n_x : n_x + n_g]
    t_ref, told_ref, past_ref = refs[n_x + n_g : n_x + n_g + 3]
    a_out, x_out, inner_ref, xs, gs, owns, outs, x_sem, g_sem, own_sem, a_sem, out_sem = refs[-12:]
    tokens, width = a_out.shape

    def piece(ref, start, h):
        return ref.at[lanes_of(start + h * HDIM, HDIM)]

    copies = {}
    for h in range(heads):
        to = lanes_of(h * HDIM, HDIM)
        copies[h] = [
            (which == i, pltpu.make_async_copy(piece(ref, at, h), into.at[to], sem.at[h]))
            for which, sources, starts, into, sem in (
                (pick_ref[0], x_refs[: n_x - odd], x_at, xs, x_sem),
                (pick_ref[1], g_refs, g_at, gs, g_sem),
            )
            for i, (ref, at) in enumerate(zip(sources, starts))
        ]
        for wanted, copy in copies[h]:
            pl.when(wanted)(copy.start)
        if odd:
            own = pltpu.make_async_copy(piece(x_refs[-1], x_at[-1], h), owns.at[to], own_sem.at[h])
            own.start()
            copies[h].append((None, own))

    evicted = told_ref[:, tokens + 2 * width :] == 1.0
    factor = column_of(inverse_rms(t_ref[2:3, :], width_all))
    ready = jnp.logical_and(pick_ref[2] == 1, jnp.logical_not(evicted))
    part = None
    sent = []
    for h in range(heads):
        for wanted, copy in copies[h]:
            if wanted is None:
                copy.wait()
            else:
                pl.when(wanted)(copy.wait)
        at = h * HDIM
        mine = lanes_of(at, HDIM)
        gain_q = told_ref[lanes_of(tokens + first + at, HDIM)]
        gain_k = told_ref[lanes_of(tokens + width + first + at, HDIM)]
        x, g = xs[mine], gs[mine]
        if odd:
            stays = jnp.logical_or(evicted, pick_ref[0] > 0)
            x = jnp.where(stays, x.astype(F32), owns[mine].astype(F32)).astype(BF16)
            xs[mine] = x
        wide, d_normed = backward_head(x, g, factor, gain_q, gain_k)
        outs[mine] = g.astype(F32) + jnp.where(ready, 0.0, factor * d_normed)
        to = lanes_of(first + at, HDIM)
        sent.append(pltpu.make_async_copy(outs.at[mine], a_out.at[to], a_sem.at[h]))
        sent.append(pltpu.make_async_copy(xs.at[mine], x_out.at[to], out_sem.at[h]))
        for copy in sent[-2:]:
            copy.start()
        product = d_normed * wide
        part = product if part is None else part + product
    inner_ref[...] = jnp.sum(part.T, axis=0, keepdims=True) + past_ref[...]
    for copy in sent:
        copy.wait()


def backward(width_all, width, pick, xs, gs, totals, told, past, heads, first, sofar=(), after=(), odd=False):
    tokens = totals.shape[1]
    lanes = heads * HDIM
    count = 1 + len(xs) + len(gs) + 3
    dma = pltpu.SemaphoreType.DMA((heads,))
    small = (tokens, lanes)
    return pl.pallas_call(
        functools.partial(
            backward_kernel, first, heads, width_all, tuple(at for _, at in xs), tuple(at for _, at in gs), int(odd)
        ),
        out_shape=(
            pltpu.HBM((tokens, width), F32),
            pltpu.HBM((tokens, width), BF16),
            jax.ShapeDtypeStruct((1, tokens), F32),
        ),
        in_specs=[pl.BlockSpec(memory_space=pltpu.SMEM)] + [ANYWHERE] * (len(xs) + len(gs)) + [IN_VMEM] * 3
        + [IN_HBM] * len(sofar) + [ANYWHERE] * len(after),
        out_specs=(IN_HBM, IN_HBM, IN_VMEM),
        input_output_aliases={count: 0, count + 1: 1} if sofar else {},
        scratch_shapes=[pltpu.VMEM(small, BF16)] * 3 + [pltpu.VMEM(small, F32)] + [dma] * 5,
        compiler_params=compiler(VMEM),
        name="backward",
    )(pick, *[x for x, _ in xs], *[g for g, _ in gs], totals, told, past, *sofar, *after)


def early_kernel(heads, width_all, pick_ref, x_ref, g_ref, t_ref, gq_ref, gk_ref, a_ref, inner_ref):
    @pl.when(pl.program_id(0) == 0)
    def _():
        inner_ref[...] = jnp.zeros_like(inner_ref)

    @pl.when(pick_ref[0] == 1)
    def _():
        factor = column_of(inverse_rms(t_ref[1:2, :], width_all))
        part = None
        for h in range(heads):
            mine = lanes_of(h * HDIM, HDIM)
            g = g_ref[mine]
            wide, d_normed = backward_head(x_ref[mine], g, factor, gq_ref[mine], gk_ref[mine])
            a_ref[mine] = g.astype(F32) + factor * d_normed
            product = d_normed * wide
            part = product if part is None else part + product
        inner_ref[...] += jnp.sum(part.T, axis=0, keepdims=True)


def early_backward(width_all, pick, stash, g, totals, gain_q, gain_k, heads):
    tokens, width = g.shape
    lanes = heads * HDIM
    at = lambda i, pick: (0, i * pick[0])
    block = pl.BlockSpec((tokens, lanes), at)
    still = lambda shape: pl.BlockSpec(shape, lambda i, pick: (0, 0))
    gain = pl.BlockSpec((1, lanes), at)
    return pl.pallas_call(
        functools.partial(early_kernel, heads, width_all),
        out_shape=(jax.ShapeDtypeStruct((tokens, width), F32), jax.ShapeDtypeStruct((1, tokens), F32)),
        grid_spec=pltpu.PrefetchScalarGridSpec(
            num_scalar_prefetch=1,
            grid=(width // lanes,),
            in_specs=[
                pl.BlockSpec((None, None, tokens, lanes), lambda i, pick: (0, 0, 0, i * pick[0])),
                block, still(totals.shape), gain, gain,
            ],
            out_specs=(block, still((1, tokens))),
        ),
        compiler_params=compiler(MOST),
        name="early_backward",
    )(pick, in_hbm(stash), in_hbm(g), totals, gain_q, gain_k)


def row_of(total, inner, width_all):
    return inverse_rms(total, width_all) ** 3 * inner / width_all


def finish_kernel(width_all, pick_ref, a_ref, x_ref, t_ref, told_ref, inner_ref, o_ref):
    evicted = told_ref[:, told_ref.shape[1] - 1 :] == 1.0
    ready = jnp.logical_and(pick_ref[2] == 1, jnp.logical_not(evicted))
    row = jnp.where(ready, 0.0, row_of(t_ref[2:3, :], inner_ref[...], width_all))
    o_ref[...] = (a_ref[...] - x_ref[...].astype(F32) * column_of(row)).astype(BF16)


def finish(width_all, pick, a, x, totals, told, inner, lanes):
    tokens, width = a.shape
    block = pl.BlockSpec((tokens, lanes), lambda i: (0, i))
    return pl.pallas_call(
        functools.partial(finish_kernel, width_all),
        out_shape=jax.ShapeDtypeStruct(a.shape, BF16),
        grid=(width // lanes,),
        in_specs=[pl.BlockSpec(memory_space=pltpu.SMEM), block, block] + [IN_VMEM] * 3,
        out_specs=block,
        compiler_params=compiler(VMEM),
        name="finish",
    )(pick, in_hbm(a), in_hbm(x), totals, told, inner)


def slot_kernel(width_all, last, pick_ref, a_ref, x_ref, g_ref, t_ref, inner_ref, o_ref, kept_ref):
    special = pick_ref[1] == 1
    step = pl.program_id(0)

    @pl.when(jnp.logical_and(special, pick_ref[0] == 1))
    def _():
        row = column_of(row_of(t_ref[1:2, :], inner_ref[...], width_all))
        o_ref[...] = (a_ref[...] - x_ref[...].astype(F32) * row).astype(BF16)

    @pl.when(jnp.logical_and(special, pick_ref[0] == 0))
    def _():
        o_ref[...] = g_ref[...]

    @pl.when(jnp.logical_and(special, step == 0))
    def _():
        kept_ref[...] = o_ref[...]

    @pl.when(jnp.logical_and(jnp.logical_not(special), step == last))
    def _():
        kept_ref[...] = x_ref[...]


def slot_of(width_all, pick, a, stash, g, totals, inner, lanes):
    tokens, width = g.shape
    last = width // lanes - 1
    block = pl.BlockSpec((tokens, lanes), lambda i, pick: (0, i * pick[1]))
    still = lambda shape: pl.BlockSpec(shape, lambda i, pick: (0, 0))
    return pl.pallas_call(
        functools.partial(slot_kernel, width_all, last),
        out_shape=(jax.ShapeDtypeStruct((tokens, width), BF16), jax.ShapeDtypeStruct((tokens, lanes), BF16)),
        grid_spec=pltpu.PrefetchScalarGridSpec(
            num_scalar_prefetch=1,
            grid=(width // lanes,),
            in_specs=[
                pl.BlockSpec((tokens, lanes), lambda i, pick: (0, i * pick[0])),
                pl.BlockSpec(
                    (None, None, tokens, lanes), lambda i, pick: (0, 0, 0, jnp.where(pick[1] == 1, i, last))
                ),
                block,
                still(totals.shape),
                still(inner.shape),
            ],
            out_specs=(block, still((tokens, lanes))),
        ),
        compiler_params=compiler(MOST),
        name="slot",
    )(pick, a, in_hbm(stash), in_hbm(g), totals, inner)


def choose(mode, first, second, tokens, step, after=()):
    options = (first, second)
    count = len(first) + len(second)

    def kernel(mode_ref, *refs):
        sems = refs[-1]
        outs = refs[-3:-1]
        ins = iter(refs[:count])
        copies = []
        for i, (out, chosen) in enumerate(zip(outs, options)):
            for m, (_, at) in enumerate(chosen):
                ref = next(ins)
                if isinstance(at, tuple):
                    ref = ref.at[0, at[0], :, at[1] * step : (at[1] + 1) * step]
                else:
                    ref = ref.at[:, at * step : (at + 1) * step]
                copies.append((mode_ref[i] == m, pltpu.make_async_copy(ref, out, sems.at[i])))
        for wanted, copy in copies:
            pl.when(wanted)(copy.start)
        for wanted, copy in copies:
            pl.when(wanted)(copy.wait)

    return pl.pallas_call(
        kernel,
        out_shape=[jax.ShapeDtypeStruct((tokens, step), BF16)] * 2,
        in_specs=[pl.BlockSpec(memory_space=pltpu.SMEM)]
        + [IN_HBM if isinstance(at, tuple) else ANYWHERE for _, at in (*first, *second)]
        + [ANYWHERE] * len(after),
        out_specs=[IN_VMEM] * 2,
        scratch_shapes=[pltpu.SemaphoreType.DMA((2,))],
        compiler_params=compiler(VMEM),
        name="choose",
    )(mode, *[array for array, _ in (*first, *second)], *after)


def hold(arrays, after):
    n = len(arrays)
    return pl.pallas_call(
        lambda *refs: None,
        out_shape=[jax.ShapeDtypeStruct(x.shape, x.dtype) for x in arrays],
        in_specs=[IN_HBM] * n + [ANYWHERE] * len(after),
        out_specs=[IN_HBM] * n,
        input_output_aliases={i: i for i in range(n)},
        name="hold",
    )(*arrays, *after)


def open_kernel(
    pieces, pick_ref, current_ref, stash_ref, g_ref, gq_ref, gk_ref, rows_ref, told_ref, away_ref, early_ref, sums
):
    step = pl.program_id(0)
    tokens, lanes = current_ref.shape

    def total(x):
        wide = x.astype(F32)
        square = wide * wide
        return sum(square[:, i : i + HDIM] for i in range(0, square.shape[1], HDIM))

    @pl.when(step == 0)
    def _():
        away_ref[...] = stash_ref[1]

    for i, x in enumerate((current_ref[...], stash_ref[0], stash_ref[1])):
        part = total(x)

        @pl.when(step == 0)
        def _():
            sums[i] = part

        @pl.when(step > 0)
        def _():
            sums[i] += part

    @pl.when(pick_ref[1] == 1)
    def _():
        early_ref[...] = stash_ref[1]

    @pl.when(pick_ref[1] == 0)
    def _():
        early_ref[...] = g_ref[...]

    @pl.when(step == pieces - 1)
    def _():
        for i in range(3):
            rows_ref[i : i + 1, :] = jnp.sum(sums[i].T, axis=0, keepdims=True)
        width = gq_ref.shape[1]
        told_ref[:, :tokens] = rows_ref[1:2, :]
        told_ref[:, tokens : tokens + width] = gq_ref[...]
        told_ref[:, tokens + width : tokens + 2 * width] = gk_ref[...]
        told_ref[:, tokens + 2 * width :] = jnp.full((1, HDIM), pick_ref[2].astype(F32))


def opened(pick, current, stash, g, gain_q, gain_k, lanes):
    tokens, width = current.shape
    pieces = width // lanes
    block = pl.BlockSpec((tokens, lanes), lambda i, pick: (0, i))
    still = lambda *shape: pl.BlockSpec(shape, lambda i, pick: (0, 0))
    told = tokens + 2 * width + HDIM
    return pl.pallas_call(
        functools.partial(open_kernel, pieces),
        out_shape=(
            jax.ShapeDtypeStruct((3, tokens), F32),
            jax.ShapeDtypeStruct((1, told), F32),
            jax.ShapeDtypeStruct((tokens, lanes), BF16),
            jax.ShapeDtypeStruct((tokens, width), BF16),
        ),
        grid_spec=pltpu.PrefetchScalarGridSpec(
            num_scalar_prefetch=1,
            grid=(pieces,),
            in_specs=[
                block,
                pl.BlockSpec((None, 2, tokens, lanes), lambda i, pick: (0, 0, 0, i)),
                block,
                still(1, width),
                still(1, width),
            ],
            out_specs=(still(3, tokens), still(1, told), still(tokens, lanes), block),
            scratch_shapes=[pltpu.VMEM((3, tokens, HDIM), F32)],
        ),
        compiler_params=compiler(MOST),
        name="opened",
    )(pick, in_hbm(current), in_hbm(stash), in_hbm(g), gain_q, gain_k)


def join_kernel(rows_ref, told_ref, held_ref, o_ref):
    tokens = rows_ref.shape[1]
    evicted = told_ref[:, told_ref.shape[1] - 1 :] == 1.0
    o_ref[0:2, :] = rows_ref[0:2, :]
    o_ref[2:3, :] = jnp.where(evicted, held_ref[2:3, :], told_ref[:, :tokens])


def join(rows, told, held):
    return pl.pallas_call(
        join_kernel,
        out_shape=jax.ShapeDtypeStruct(rows.shape, F32),
        in_specs=[IN_VMEM] * 3,
        out_specs=IN_VMEM,
        compiler_params=compiler(VMEM),
        name="join",
    )(rows, told, held)


def send(x, pairs):
    return lax.ppermute(x, "section", pairs)


def local(width_all, layer_input, grad_input, stashed, eviction, query_gain, key_gain):
    n = lax.axis_size("section")
    half = n // 2
    special = (0, half)
    me = lax.axis_index("section")

    prior = [(s, (s - 1) % n) for s in range(n)]
    inside = [(s, s - 1) for s in range(n) if s not in special]
    within = inside + [(half, n - 1), (0, half - 1)]
    to_partner = [(s, (s + half) % n) for s in range(n) if s not in special]
    holder = [((s + half) % n, (s - 1) % n) for s in range(n)]
    direct = [p for p in holder if p[0] not in special] + [(half, half - 1), (0, n - 1)]

    current = layer_input[0]
    upstream = grad_input[0]
    tokens, width = current.shape
    heads = width // HDIM // 3
    step = heads * HDIM

    flag = lambda f: jnp.asarray(f).astype(jnp.int32)
    is_special = jnp.logical_or(me == 0, me == half)
    kept_here = jnp.logical_and(me == half, eviction[0] == 0)
    crossed = jnp.logical_or(me == half - 1, me == n - 1)
    early_pick = jnp.stack([flag(kept_here), flag(is_special), eviction[0]])
    mode = jnp.stack([jnp.where(is_special, 2, eviction[0]), flag(is_special)])
    mode_first = jnp.stack([eviction[0], flag(False)])
    final = flag(me == half - 1)
    take = jnp.stack([flag(crossed), flag(crossed), final])

    stash = in_hbm(stashed)
    rows, told, away, early = opened(early_pick, current, stashed, upstream, query_gain, key_gain, step)
    told = send(told, prior)
    held = send(rows, holder)
    away, early = hold((away, early), (told, held))
    fetched = send(away, to_partner)
    early = send(early, within)
    total = lax.psum(join(rows, told, held), "tensor")

    own_a, own_inner = early_backward(width_all, early_pick, stashed, upstream, total, query_gain, key_gain, heads)
    sent, away = choose(
        mode_first, [(stash, (0, 0)), (fetched, 0)], [(stash, (1, 1))], tokens, step, (in_hbm(own_inner),)
    )
    fetched = send(away, to_partner)
    passed = [send(sent, inside)]
    own_inner = lax.psum(own_inner, "tensor")
    slot, last = slot_of(width_all, early_pick, own_a, stashed, upstream, total, own_inner, step)
    kept = send(last, prior)
    slot = in_hbm(slot)
    sent, last = choose(
        mode, [(stash, (0, 1)), (fetched, 0), (slot, 1)], [(stash, (1, 2)), (slot, 2)], tokens, step,
    )
    straight = send(last, direct)
    passed.append(send(sent, prior))

    output = forward(width_all, current, total, query_gain, key_gain, heads, (sent,))

    share = functools.partial(backward, width_all, width)
    a, x, inner = share(
        take, [(passed[0], 0), (early, 0)], [(early, 0), (kept, 0)], total, told, jnp.zeros((1, tokens), F32), heads, 0,
        after=(in_hbm(output),),
    )
    a, x, inner = share(
        take, [(passed[1], 0), (early, step)], [(early, step), (passed[1], 0)], total, told, inner, heads, step, (a, x),
    )
    a, x, inner = share(
        take, [(straight, 0), (early, 2 * step), (kept, 0)], [(early, 2 * step), (straight, 0)],
        total, told, inner, heads, 2 * step, (a, x), odd=True,
    )
    inner = lax.psum(inner, "tensor")
    result = finish(width_all, take, a, x, total, told, inner, step)
    return (output[None], result[None])


def solution(mesh):
    placed = (
        P("section", None, "tensor"),
        P("section", None, "tensor"),
        P("section", None, None, "tensor"),
        P("section"),
        P("section", "tensor"),
        P("section", "tensor"),
    )

    def whole(layer_input, *others):
        return jax.shard_map(
            functools.partial(local, layer_input.shape[-1]),
            mesh=mesh,
            in_specs=placed,
            out_specs=(P("section", None, "tensor"), P("section", None, "tensor")),
            check_vma=False,
        )(layer_input, *others)

    return whole
```

```python
import functools
import math

import jax
import jax.numpy as jnp
from jax import lax
from jax.experimental import pallas as pl
from jax.experimental.pallas import tpu as pltpu
from jax.sharding import PartitionSpec as P

HDIM = 128
EPSILON = 1e-05
SCALE = 1.0 / math.sqrt(HDIM)
LOG2E = math.log2(math.e)
VMEM = 32 * 1024 * 1024
MOST = 60 * 1024 * 1024

F32 = jnp.float32
BF16 = jnp.bfloat16


def dot(a, b, contract):
    return lax.dot_general(a, b, ((contract[0], contract[1]), ((), ())), preferred_element_type=F32)


def nt(a, b):
    return dot(a, b, ((1,), (1,)))


def nn(a, b):
    return dot(a, b, ((1,), (0,)))


def block_of(tokens):
    return 256 if tokens % 256 == 0 else tokens


def masked(block, kept):
    return jnp.where(kept, block, -1e30)


def kept_keys(size):
    keys = lax.broadcasted_iota(jnp.int32, (size, size), 0)
    return keys <= lax.broadcasted_iota(jnp.int32, (size, size), 1)


def scores_of(keys, queries, j, size, kept):
    mine = queries[j * size : (j + 1) * size]
    diagonal = masked(nt(keys[j * size : (j + 1) * size], mine), kept)
    if j == 0:
        return [diagonal]
    return [nt(keys[: j * size], mine), diagonal]


def exponents(parts):
    top = functools.reduce(jnp.maximum, [jnp.max(p, axis=0, keepdims=True) for p in parts])
    exps = [jnp.exp2((p - top) * (SCALE * LOG2E)) for p in parts]
    total = sum(jnp.sum(e, axis=0, keepdims=True) for e in exps)
    return exps, total


def stacked(parts):
    return parts[0] if len(parts) == 1 else jnp.concatenate(parts, axis=0)


def normed_head(x, factor, gain_q, gain_k):
    wide = x.astype(F32)
    normed = wide * factor
    return wide, (normed * gain_q).astype(BF16), (normed * gain_k).astype(BF16), normed.astype(BF16)


def column_of(row):
    return jnp.broadcast_to(row, (HDIM, row.shape[1])).T[:, 0:1]


def inverse_rms(total, width_all):
    return lax.rsqrt(total / width_all + EPSILON)


def lanes_of(start, size):
    return (slice(None), slice(start, start + size))


def compiler(limit):
    return pltpu.CompilerParams(vmem_limit_bytes=limit)


IN_VMEM = pl.BlockSpec(memory_space=pltpu.VMEM)
ANYWHERE = pl.BlockSpec(memory_space=pl.ANY)
IN_HBM = pl.BlockSpec(memory_space=pltpu.HBM)


def in_hbm(x):
    return pltpu.with_memory_space_constraint(x, pltpu.HBM)


def forward_kernel(heads, width_all, x_ref, t_ref, gq_ref, gk_ref, *rest):
    o_ref = rest[-1]
    tokens = x_ref.shape[0]
    size = block_of(tokens)
    kept = kept_keys(size)
    factor = column_of(inverse_rms(t_ref[0:1, :], width_all))
    for h in range(heads):
        lanes = slice(h * HDIM, (h + 1) * HDIM)
        wide, q, k, v = normed_head(x_ref[:, lanes], factor, gq_ref[:, lanes], gk_ref[:, lanes])
        vt = v.T
        for j in range(tokens // size):
            exps, total = exponents(scores_of(k, q, j, size, kept))
            mixed = nn(vt[:, : (j + 1) * size], stacked(exps).astype(BF16)) * (1.0 / total)
            rows = slice(j * size, (j + 1) * size)
            o_ref[rows, lanes] = (wide[rows] + mixed.T).astype(BF16)


def forward(width_all, x, totals, gain_q, gain_k, heads, after=()):
    tokens, width = x.shape
    lanes = heads * HDIM
    block = pl.BlockSpec((tokens, lanes), lambda i: (0, i))
    gain = pl.BlockSpec((1, lanes), lambda i: (0, i))
    return pl.pallas_call(
        functools.partial(forward_kernel, heads, width_all),
        out_shape=jax.ShapeDtypeStruct(x.shape, BF16),
        grid=(width // lanes,),
        in_specs=[block, pl.BlockSpec(totals.shape, lambda i: (0, 0)), gain, gain] + [IN_HBM] * len(after),
        out_specs=block,
        compiler_params=compiler(VMEM),
        name="forward",
    )(in_hbm(x), totals, gain_q, gain_k, *map(in_hbm, after))


def backward_head(x, g, factor, gain_q, gain_k):
    tokens = x.shape[0]
    size = block_of(tokens)
    kept = kept_keys(size)
    wide, q, k, v = normed_head(x, factor, gain_q, gain_k)
    kt = k.T
    blocks = tokens // size
    d_q = []
    d_k = [None] * blocks
    d_v = [None] * blocks
    for j in range(blocks):
        rows = slice(j * size, (j + 1) * size)
        exps, total = exponents(scores_of(k, q, j, size, kept))
        inverse = 1.0 / total
        weights = [e * inverse for e in exps]
        grads = [nt(v[: j * size], g[rows])] if j else []
        grads.append(nt(v[rows], g[rows]))
        delta = sum(jnp.sum(w * d, axis=0, keepdims=True) for w, d in zip(weights, grads))
        scores = stacked([(w * ((d - delta) * SCALE)).astype(BF16) for w, d in zip(weights, grads)])
        rounded = stacked([w.astype(BF16) for w in weights])
        d_q.append(nn(kt[:, : (j + 1) * size], scores).T)
        part_k = nn(scores, q[rows])
        part_v = nn(rounded, g[rows])
        for i in range(j + 1):
            mine = slice(i * size, (i + 1) * size)
            d_k[i] = part_k[mine] if d_k[i] is None else d_k[i] + part_k[mine]
            d_v[i] = part_v[mine] if d_v[i] is None else d_v[i] + part_v[mine]
    d_normed = stacked(d_q) * gain_q + stacked(d_k) * gain_k + stacked(d_v)
    return wide, d_normed


def backward_kernel(first, heads, width_all, evicted_ref, own_ref, far_ref, g_ref, t_ref, held_ref, gq_ref, gk_ref, past_ref, *refs):
    a_out, x_out, inner_ref, xs, gs, outs, x_sem, g_sem, a_sem, out_sem = refs[-10:]
    evicted = evicted_ref[0] == 1
    copies = []
    for h in range(heads):
        to = lanes_of(h * HDIM, HDIM)
        there = lanes_of(first + h * HDIM, HDIM)
        far = pltpu.make_async_copy(far_ref.at[to], xs.at[to], x_sem.at[h])
        near = pltpu.make_async_copy(own_ref.at[(0, 0) + there], xs.at[to], x_sem.at[h])
        g = pltpu.make_async_copy(g_ref.at[(0,) + there], gs.at[to], g_sem.at[h])
        pl.when(evicted)(far.start)
        pl.when(jnp.logical_not(evicted))(near.start)
        g.start()
        copies.append((far, near, g))
    factor = column_of(inverse_rms(total_of(evicted_ref, t_ref, held_ref), width_all))
    part = None
    sent = []
    for h in range(heads):
        far, near, copy = copies[h]
        pl.when(evicted)(far.wait)
        pl.when(jnp.logical_not(evicted))(near.wait)
        copy.wait()
        mine = lanes_of(h * HDIM, HDIM)
        there = lanes_of(first + h * HDIM, HDIM)
        g = gs[mine]
        wide, d_normed = backward_head(xs[mine], g, factor, gq_ref[there], gk_ref[there])
        outs[mine] = g.astype(F32) + factor * d_normed
        sent.append(pltpu.make_async_copy(outs.at[mine], a_out.at[there], a_sem.at[h]))
        sent.append(pltpu.make_async_copy(xs.at[mine], x_out.at[there], out_sem.at[h]))
        for copy in sent[-2:]:
            copy.start()
        product = d_normed * wide
        part = product if part is None else part + product
    inner_ref[...] = jnp.sum(part.T, axis=0, keepdims=True) + past_ref[...]
    for copy in sent:
        copy.wait()


def total_of(evicted_ref, t_ref, held_ref):
    return jnp.where(evicted_ref[0] == 1, held_ref[2:3, :], t_ref[1:2, :])


def backward(width_all, evicted, stash, far, g, totals, held, gain_q, gain_k, past, heads, first, sofar=(), after=()):
    tokens, width = totals.shape[1], gain_q.shape[1]
    small = (tokens, heads * HDIM)
    dma = pltpu.SemaphoreType.DMA((heads,))
    return pl.pallas_call(
        functools.partial(backward_kernel, first, heads, width_all),
        out_shape=(
            pltpu.HBM((tokens, width), F32),
            pltpu.HBM((tokens, width), BF16),
            jax.ShapeDtypeStruct((1, tokens), F32),
        ),
        in_specs=[pl.BlockSpec(memory_space=pltpu.SMEM)] + [ANYWHERE] * 3 + [IN_VMEM] * 5
        + [IN_HBM] * len(sofar) + [ANYWHERE] * len(after),
        out_specs=(IN_HBM, IN_HBM, IN_VMEM),
        input_output_aliases={9: 0, 10: 1} if sofar else {},
        scratch_shapes=[pltpu.VMEM(small, BF16)] * 2 + [pltpu.VMEM(small, F32)] + [dma] * 4,
        compiler_params=compiler(VMEM),
        name="backward",
    )(evicted, in_hbm(stash), far, in_hbm(g), totals, held, gain_q, gain_k, past, *sofar, *after)


def row_of(total, inner, width_all):
    return inverse_rms(total, width_all) ** 3 * inner / width_all


def finish_kernel(width_all, evicted_ref, a_ref, x_ref, t_ref, held_ref, inner_ref, o_ref):
    row = row_of(total_of(evicted_ref, t_ref, held_ref), inner_ref[...], width_all)
    o_ref[...] = (a_ref[...] - x_ref[...].astype(F32) * column_of(row)).astype(BF16)


def finish(width_all, evicted, a, x, totals, held, inner, lanes):
    tokens, width = a.shape
    block = pl.BlockSpec((tokens, lanes), lambda i: (0, i))
    return pl.pallas_call(
        functools.partial(finish_kernel, width_all),
        out_shape=jax.ShapeDtypeStruct(a.shape, BF16),
        grid=(width // lanes,),
        in_specs=[pl.BlockSpec(memory_space=pltpu.SMEM), block, block] + [IN_VMEM] * 3,
        out_specs=block,
        compiler_params=compiler(VMEM),
        name="finish",
    )(evicted, in_hbm(a), in_hbm(x), totals, held, inner)


def squares_kernel(current_ref, stash_ref, *rest):
    rows_ref, sums = rest[-2:]
    step = pl.program_id(0)

    def total(x):
        wide = x.astype(F32)
        square = wide * wide
        return sum(square[:, i : i + HDIM] for i in range(0, square.shape[1], HDIM))

    for i, x in enumerate((current_ref[...], stash_ref[0], stash_ref[1])):
        part = total(x)

        @pl.when(step == 0)
        def _():
            sums[i] = part

        @pl.when(step > 0)
        def _():
            sums[i] += part

    @pl.when(step == pl.num_programs(0) - 1)
    def _():
        for i in range(3):
            rows_ref[i : i + 1, :] = jnp.sum(sums[i].T, axis=0, keepdims=True)


def squares(current, stash, lanes, after=()):
    tokens, width = current.shape
    return pl.pallas_call(
        squares_kernel,
        out_shape=jax.ShapeDtypeStruct((3, tokens), F32),
        grid=(width // lanes,),
        in_specs=[
            pl.BlockSpec((tokens, lanes), lambda i: (0, i)),
            pl.BlockSpec((None, 2, tokens, lanes), lambda i: (0, 0, 0, i)),
        ] + [ANYWHERE] * len(after),
        out_specs=pl.BlockSpec((3, tokens), lambda i: (0, 0)),
        scratch_shapes=[pltpu.VMEM((3, tokens, HDIM), F32)],
        compiler_params=compiler(MOST),
        name="squares",
    )(in_hbm(current), in_hbm(stash), *after)


def piece_kernel(starts, sizes, stash_ref, *rest):
    outs, mark, sems = rest[-2 - len(sizes) : -2], rest[-2], rest[-1]
    mark[...] = jnp.zeros_like(mark)
    copies = [
        pltpu.make_async_copy(stash_ref.at[(0, 1) + lanes_of(start, size)], out, sems.at[i])
        for i, (start, size, out) in enumerate(zip(starts, sizes, outs))
    ]
    for copy in copies:
        copy.start()
    for copy in copies:
        copy.wait()


def pieces_of(stash, starts, sizes, after=()):
    tokens = stash.shape[2]
    return pl.pallas_call(
        functools.partial(piece_kernel, starts, sizes),
        out_shape=[jax.ShapeDtypeStruct((tokens, size), BF16) for size in sizes] + [jax.ShapeDtypeStruct((8, HDIM), F32)],
        in_specs=[IN_HBM] + [ANYWHERE] * len(after),
        out_specs=[IN_VMEM] * (len(sizes) + 1),
        scratch_shapes=[pltpu.SemaphoreType.DMA((len(sizes),))],
        compiler_params=compiler(VMEM),
        name="pieces",
    )(in_hbm(stash), *after)


def send(x, pairs):
    return lax.ppermute(x, "section", pairs)


def local(width_all, layer_input, grad_input, stashed, eviction, query_gain, key_gain):
    n = lax.axis_size("section")
    partner = [(s, (s + n // 2) % n) for s in range(n)]
    prior = [(s, (s - 1) % n) for s in range(n)]
    current = layer_input[0]
    tokens, width = current.shape
    count = width // HDIM
    heads = (max(1, count // 3), count - max(1, count // 3) - max(1, count // 4), max(1, count // 4))
    sizes = [h * HDIM for h in heads]
    starts = [sum(sizes[:i]) for i in range(3)]
    third = count // 3 * HDIM

    *away, mark = pieces_of(stashed, starts[:2], sizes[:2])
    fetched = [send(x, partner) for x in away]
    totals = lax.psum(squares(current, stashed, third, (mark,)), "tensor")
    held = send(totals, partner)
    output = forward(width_all, current, totals, query_gain, key_gain, third // HDIM)
    fetched.append(send(pieces_of(stashed, starts[2:], sizes[2:], (fetched[0], in_hbm(output)))[0], partner))

    sofar, inner, after = (), jnp.zeros((1, tokens), F32), (in_hbm(output),)
    for h, start, far in zip(heads, starts, fetched):
        *sofar, inner = backward(
            width_all, eviction, stashed, far, grad_input, totals, held, query_gain, key_gain, inner, h, start,
            tuple(sofar), after,
        )
        after = ()
    inner = lax.psum(inner, "tensor")
    result = finish(width_all, eviction, *sofar, totals, held, inner, third)
    return (output[None], send(result, prior)[None])


def solution(mesh):
    placed = (
        P("section", None, "tensor"),
        P("section", None, "tensor"),
        P("section", None, None, "tensor"),
        P("section"),
        P("section", "tensor"),
        P("section", "tensor"),
    )

    def whole(layer_input, *others):
        return jax.shard_map(
            functools.partial(local, layer_input.shape[-1]),
            mesh=mesh,
            in_specs=placed,
            out_specs=(P("section", None, "tensor"), P("section", None, "tensor")),
            check_vma=False,
        )(layer_input, *others)

    return whole
```

```python
import functools
import math

import jax
import jax.numpy as jnp
from jax import lax
from jax.experimental import pallas as pl
from jax.experimental.pallas import tpu as pltpu
from jax.sharding import PartitionSpec as P

HDIM = 128
EPSILON = 1e-05
SCALE = 1.0 / math.sqrt(HDIM)
LOG2E = math.log2(math.e)
VMEM = 32 * 1024 * 1024
MOST = 60 * 1024 * 1024

F32 = jnp.float32
BF16 = jnp.bfloat16


def dot(a, b, contract):
    return lax.dot_general(a, b, ((contract[0], contract[1]), ((), ())), preferred_element_type=F32)


def nt(a, b):
    return dot(a, b, ((1,), (1,)))


def nn(a, b):
    return dot(a, b, ((1,), (0,)))


def block_of(tokens):
    return 256 if tokens % 256 == 0 else tokens


def masked(block, kept):
    return jnp.where(kept, block, -1e30)


def kept_keys(size):
    keys = lax.broadcasted_iota(jnp.int32, (size, size), 0)
    return keys <= lax.broadcasted_iota(jnp.int32, (size, size), 1)


def scores_of(keys, queries, j, size, kept):
    mine = queries[j * size : (j + 1) * size]
    diagonal = masked(nt(keys[j * size : (j + 1) * size], mine), kept)
    if j == 0:
        return [diagonal]
    return [nt(keys[: j * size], mine), diagonal]


def exponents(parts):
    top = functools.reduce(jnp.maximum, [jnp.max(p, axis=0, keepdims=True) for p in parts])
    exps = [jnp.exp2((p - top) * (SCALE * LOG2E)) for p in parts]
    total = sum(jnp.sum(e, axis=0, keepdims=True) for e in exps)
    return exps, total


def stacked(parts):
    return parts[0] if len(parts) == 1 else jnp.concatenate(parts, axis=0)


def normed_head(x, factor, gain_q, gain_k):
    wide = x.astype(F32)
    normed = wide * factor
    return wide, (normed * gain_q).astype(BF16), (normed * gain_k).astype(BF16), normed.astype(BF16)


def column_of(row):
    return jnp.broadcast_to(row, (HDIM, row.shape[1])).T[:, 0:1]


def inverse_rms(total, width_all):
    return lax.rsqrt(total / width_all + EPSILON)


def lanes_of(start, size):
    return (slice(None), slice(start, start + size))


def compiler(limit):
    return pltpu.CompilerParams(vmem_limit_bytes=limit)


IN_VMEM = pl.BlockSpec(memory_space=pltpu.VMEM)
ANYWHERE = pl.BlockSpec(memory_space=pl.ANY)
IN_HBM = pl.BlockSpec(memory_space=pltpu.HBM)


def in_hbm(x):
    return pltpu.with_memory_space_constraint(x, pltpu.HBM)


def forward_kernel(heads, width_all, x_ref, t_ref, gq_ref, gk_ref, *rest):
    o_ref = rest[-1]
    tokens = x_ref.shape[0]
    size = block_of(tokens)
    kept = kept_keys(size)
    factor = column_of(inverse_rms(t_ref[0:1, :], width_all))
    for h in range(heads):
        lanes = slice(h * HDIM, (h + 1) * HDIM)
        wide, q, k, v = normed_head(x_ref[:, lanes], factor, gq_ref[:, lanes], gk_ref[:, lanes])
        vt = v.T
        for j in range(tokens // size):
            exps, total = exponents(scores_of(k, q, j, size, kept))
            mixed = nn(vt[:, : (j + 1) * size], stacked(exps).astype(BF16)) * (1.0 / total)
            rows = slice(j * size, (j + 1) * size)
            o_ref[rows, lanes] = (wide[rows] + mixed.T).astype(BF16)


def forward(width_all, x, totals, gain_q, gain_k, heads, after=()):
    tokens, width = x.shape
    lanes = heads * HDIM
    block = pl.BlockSpec((tokens, lanes), lambda i: (0, i))
    gain = pl.BlockSpec((1, lanes), lambda i: (0, i))
    return pl.pallas_call(
        functools.partial(forward_kernel, heads, width_all),
        out_shape=jax.ShapeDtypeStruct(x.shape, BF16),
        grid=(width // lanes,),
        in_specs=[block, pl.BlockSpec(totals.shape, lambda i: (0, 0)), gain, gain] + [IN_HBM] * len(after),
        out_specs=block,
        compiler_params=compiler(VMEM),
        name="forward",
    )(in_hbm(x), totals, gain_q, gain_k, *map(in_hbm, after))


def backward_head(x, g, factor, gain_q, gain_k):
    tokens = x.shape[0]
    size = block_of(tokens)
    kept = kept_keys(size)
    wide, q, k, v = normed_head(x, factor, gain_q, gain_k)
    kt = k.T
    blocks = tokens // size
    d_q = []
    d_k = [None] * blocks
    d_v = [None] * blocks
    for j in range(blocks):
        rows = slice(j * size, (j + 1) * size)
        exps, total = exponents(scores_of(k, q, j, size, kept))
        inverse = 1.0 / total
        weights = [e * inverse for e in exps]
        grads = [nt(v[: j * size], g[rows])] if j else []
        grads.append(nt(v[rows], g[rows]))
        delta = sum(jnp.sum(w * d, axis=0, keepdims=True) for w, d in zip(weights, grads))
        scores = stacked([(w * ((d - delta) * SCALE)).astype(BF16) for w, d in zip(weights, grads)])
        rounded = stacked([w.astype(BF16) for w in weights])
        d_q.append(nn(kt[:, : (j + 1) * size], scores).T)
        part_k = nn(scores, q[rows])
        part_v = nn(rounded, g[rows])
        for i in range(j + 1):
            mine = slice(i * size, (i + 1) * size)
            d_k[i] = part_k[mine] if d_k[i] is None else d_k[i] + part_k[mine]
            d_v[i] = part_v[mine] if d_v[i] is None else d_v[i] + part_v[mine]
    d_normed = stacked(d_q) * gain_q + stacked(d_k) * gain_k + stacked(d_v)
    return wide, d_normed


def backward_kernel(first, heads, width_all, evicted_ref, own_ref, far_ref, g_ref, t_ref, held_ref, gq_ref, gk_ref, past_ref, *refs):
    a_out, x_out, inner_ref, xs, gs, outs, x_sem, g_sem, a_sem, out_sem = refs[-10:]
    evicted = evicted_ref[0] == 1
    copies = []
    for h in range(heads):
        to = lanes_of(h * HDIM, HDIM)
        there = lanes_of(first + h * HDIM, HDIM)
        far = pltpu.make_async_copy(far_ref.at[to], xs.at[to], x_sem.at[h])
        near = pltpu.make_async_copy(own_ref.at[(0, 0) + there], xs.at[to], x_sem.at[h])
        g = pltpu.make_async_copy(g_ref.at[(0,) + there], gs.at[to], g_sem.at[h])
        pl.when(evicted)(far.start)
        pl.when(jnp.logical_not(evicted))(near.start)
        g.start()
        copies.append((far, near, g))
    factor = column_of(inverse_rms(total_of(evicted_ref, t_ref, held_ref), width_all))
    part = None
    sent = []
    for h in range(heads):
        far, near, copy = copies[h]
        pl.when(evicted)(far.wait)
        pl.when(jnp.logical_not(evicted))(near.wait)
        copy.wait()
        mine = lanes_of(h * HDIM, HDIM)
        there = lanes_of(first + h * HDIM, HDIM)
        g = gs[mine]
        wide, d_normed = backward_head(xs[mine], g, factor, gq_ref[there], gk_ref[there])
        outs[mine] = g.astype(F32) + factor * d_normed
        sent.append(pltpu.make_async_copy(outs.at[mine], a_out.at[there], a_sem.at[h]))
        sent.append(pltpu.make_async_copy(xs.at[mine], x_out.at[there], out_sem.at[h]))
        for copy in sent[-2:]:
            copy.start()
        product = d_normed * wide
        part = product if part is None else part + product
    inner_ref[...] = jnp.sum(part.T, axis=0, keepdims=True) + past_ref[...]
    for copy in sent:
        copy.wait()


def total_of(evicted_ref, t_ref, held_ref):
    return jnp.where(evicted_ref[0] == 1, held_ref[2:3, :], t_ref[1:2, :])


def backward(width_all, evicted, stash, far, g, totals, held, gain_q, gain_k, past, heads, first, sofar=(), after=()):
    tokens, width = totals.shape[1], gain_q.shape[1]
    small = (tokens, heads * HDIM)
    dma = pltpu.SemaphoreType.DMA((heads,))
    return pl.pallas_call(
        functools.partial(backward_kernel, first, heads, width_all),
        out_shape=(
            pltpu.HBM((tokens, width), F32),
            pltpu.HBM((tokens, width), BF16),
            jax.ShapeDtypeStruct((1, tokens), F32),
        ),
        in_specs=[pl.BlockSpec(memory_space=pltpu.SMEM)] + [ANYWHERE] * 3 + [IN_VMEM] * 5
        + [IN_HBM] * len(sofar) + [ANYWHERE] * len(after),
        out_specs=(IN_HBM, IN_HBM, IN_VMEM),
        input_output_aliases={9: 0, 10: 1} if sofar else {},
        scratch_shapes=[pltpu.VMEM(small, BF16)] * 2 + [pltpu.VMEM(small, F32)] + [dma] * 4,
        compiler_params=compiler(VMEM),
        name="backward",
    )(evicted, in_hbm(stash), far, in_hbm(g), totals, held, gain_q, gain_k, past, *sofar, *after)


def row_of(total, inner, width_all):
    return inverse_rms(total, width_all) ** 3 * inner / width_all


def finish_kernel(width_all, evicted_ref, a_ref, x_ref, t_ref, held_ref, inner_ref, o_ref):
    row = row_of(total_of(evicted_ref, t_ref, held_ref), inner_ref[...], width_all)
    o_ref[...] = (a_ref[...] - x_ref[...].astype(F32) * column_of(row)).astype(BF16)


def finish(width_all, evicted, a, x, totals, held, inner, lanes):
    tokens, width = a.shape
    block = pl.BlockSpec((tokens, lanes), lambda i: (0, i))
    return pl.pallas_call(
        functools.partial(finish_kernel, width_all),
        out_shape=jax.ShapeDtypeStruct(a.shape, BF16),
        grid=(width // lanes,),
        in_specs=[pl.BlockSpec(memory_space=pltpu.SMEM), block, block] + [IN_VMEM] * 3,
        out_specs=block,
        compiler_params=compiler(VMEM),
        name="finish",
    )(evicted, in_hbm(a), in_hbm(x), totals, held, inner)


def squares_kernel(current_ref, stash_ref, *rest):
    rows_ref, sums = rest[-2:]
    step = pl.program_id(0)

    def total(x):
        wide = x.astype(F32)
        square = wide * wide
        return sum(square[:, i : i + HDIM] for i in range(0, square.shape[1], HDIM))

    for i, x in enumerate((current_ref[...], stash_ref[0], stash_ref[1])):
        part = total(x)

        @pl.when(step == 0)
        def _():
            sums[i] = part

        @pl.when(step > 0)
        def _():
            sums[i] += part

    @pl.when(step == pl.num_programs(0) - 1)
    def _():
        for i in range(3):
            rows_ref[i : i + 1, :] = jnp.sum(sums[i].T, axis=0, keepdims=True)


def squares(current, stash, lanes, after=()):
    tokens, width = current.shape
    return pl.pallas_call(
        squares_kernel,
        out_shape=jax.ShapeDtypeStruct((3, tokens), F32),
        grid=(width // lanes,),
        in_specs=[
            pl.BlockSpec((tokens, lanes), lambda i: (0, i)),
            pl.BlockSpec((None, 2, tokens, lanes), lambda i: (0, 0, 0, i)),
        ] + [ANYWHERE] * len(after),
        out_specs=pl.BlockSpec((3, tokens), lambda i: (0, 0)),
        scratch_shapes=[pltpu.VMEM((3, tokens, HDIM), F32)],
        compiler_params=compiler(MOST),
        name="squares",
    )(in_hbm(current), in_hbm(stash), *after)


def piece_kernel(starts, sizes, stash_ref, *rest):
    outs, mark, sems = rest[-2 - len(sizes) : -2], rest[-2], rest[-1]
    mark[...] = jnp.zeros_like(mark)
    copies = [
        pltpu.make_async_copy(stash_ref.at[(0, 1) + lanes_of(start, size)], out, sems.at[i])
        for i, (start, size, out) in enumerate(zip(starts, sizes, outs))
    ]
    for copy in copies:
        copy.start()
    for copy in copies:
        copy.wait()


def pieces_of(stash, starts, sizes, after=()):
    tokens = stash.shape[2]
    return pl.pallas_call(
        functools.partial(piece_kernel, starts, sizes),
        out_shape=[jax.ShapeDtypeStruct((tokens, size), BF16) for size in sizes] + [jax.ShapeDtypeStruct((8, HDIM), F32)],
        in_specs=[IN_HBM] + [ANYWHERE] * len(after),
        out_specs=[IN_VMEM] * (len(sizes) + 1),
        scratch_shapes=[pltpu.SemaphoreType.DMA((len(sizes),))],
        compiler_params=compiler(VMEM),
        name="pieces",
    )(in_hbm(stash), *after)


def send(x, pairs):
    return lax.ppermute(x, "section", pairs)


def local(width_all, layer_input, grad_input, stashed, eviction, query_gain, key_gain):
    n = lax.axis_size("section")
    partner = [(s, (s + n // 2) % n) for s in range(n)]
    prior = [(s, (s - 1) % n) for s in range(n)]
    current = layer_input[0]
    tokens, width = current.shape
    count = width // HDIM
    heads = (max(1, count // 3), count - max(1, count // 3) - max(1, count // 4), max(1, count // 4))
    sizes = [h * HDIM for h in heads]
    starts = [sum(sizes[:i]) for i in range(3)]
    third = count // 3 * HDIM

    *away, mark = pieces_of(stashed, starts[:2], sizes[:2])
    fetched = [send(x, partner) for x in away]
    totals = lax.psum(squares(current, stashed, third, (mark,)), "tensor")
    held = send(totals, partner)
    output = forward(width_all, current, totals, query_gain, key_gain, third // HDIM)
    fetched.append(send(pieces_of(stashed, starts[2:], sizes[2:], (fetched[0], held, in_hbm(output)))[0], partner))

    sofar, inner, after = (), jnp.zeros((1, tokens), F32), (in_hbm(output),)
    for h, start, far in zip(heads, starts, fetched):
        *sofar, inner = backward(
            width_all, eviction, stashed, far, grad_input, totals, held, query_gain, key_gain, inner, h, start,
            tuple(sofar), after,
        )
        after = ()
    inner = lax.psum(inner, "tensor")
    result = finish(width_all, eviction, *sofar, totals, held, inner, third)
    return (output[None], send(result, prior)[None])


def solution(mesh):
    placed = (
        P("section", None, "tensor"),
        P("section", None, "tensor"),
        P("section", None, None, "tensor"),
        P("section"),
        P("section", "tensor"),
        P("section", "tensor"),
    )

    def whole(layer_input, *others):
        return jax.shard_map(
            functools.partial(local, layer_input.shape[-1]),
            mesh=mesh,
            in_specs=placed,
            out_specs=(P("section", None, "tensor"), P("section", None, "tensor")),
            check_vma=False,
        )(layer_input, *others)

    return whole
```

```python
import functools
import math

import jax
import jax.numpy as jnp
from jax import lax
from jax.experimental import pallas as pl
from jax.experimental.pallas import tpu as pltpu
from jax.sharding import PartitionSpec as P

HDIM = 128
EPSILON = 1e-05
SCALE = 1.0 / math.sqrt(HDIM)
LOG2E = math.log2(math.e)
VMEM = 32 * 1024 * 1024
MOST = 60 * 1024 * 1024

F32 = jnp.float32
BF16 = jnp.bfloat16


def dot(a, b, contract):
    return lax.dot_general(a, b, ((contract[0], contract[1]), ((), ())), preferred_element_type=F32)


def nt(a, b):
    return dot(a, b, ((1,), (1,)))


def nn(a, b):
    return dot(a, b, ((1,), (0,)))


def block_of(tokens):
    return 256 if tokens % 256 == 0 else tokens


def masked(block, kept):
    return jnp.where(kept, block, -1e30)


def kept_keys(size):
    keys = lax.broadcasted_iota(jnp.int32, (size, size), 0)
    return keys <= lax.broadcasted_iota(jnp.int32, (size, size), 1)


def scores_of(keys, queries, j, size, kept):
    mine = queries[j * size : (j + 1) * size]
    diagonal = masked(nt(keys[j * size : (j + 1) * size], mine), kept)
    if j == 0:
        return [diagonal]
    return [nt(keys[: j * size], mine), diagonal]


def exponents(parts):
    top = functools.reduce(jnp.maximum, [jnp.max(p, axis=0, keepdims=True) for p in parts])
    exps = [jnp.exp2((p - top) * (SCALE * LOG2E)) for p in parts]
    total = sum(jnp.sum(e, axis=0, keepdims=True) for e in exps)
    return exps, total


def stacked(parts):
    return parts[0] if len(parts) == 1 else jnp.concatenate(parts, axis=0)


def normed_head(x, factor, gain_q, gain_k):
    wide = x.astype(F32)
    normed = wide * factor
    return wide, (normed * gain_q).astype(BF16), (normed * gain_k).astype(BF16), normed.astype(BF16)


def column_of(row):
    return jnp.broadcast_to(row, (HDIM, row.shape[1])).T[:, 0:1]


def inverse_rms(total, width_all):
    return lax.rsqrt(total / width_all + EPSILON)


def lanes_of(start, size):
    return (slice(None), slice(start, start + size))


def compiler(limit):
    return pltpu.CompilerParams(vmem_limit_bytes=limit)


IN_VMEM = pl.BlockSpec(memory_space=pltpu.VMEM)
ANYWHERE = pl.BlockSpec(memory_space=pl.ANY)
IN_HBM = pl.BlockSpec(memory_space=pltpu.HBM)


def in_hbm(x):
    return pltpu.with_memory_space_constraint(x, pltpu.HBM)


def forward_kernel(heads, width_all, x_ref, t_ref, gq_ref, gk_ref, *rest):
    o_ref = rest[-1]
    tokens = x_ref.shape[0]
    size = block_of(tokens)
    kept = kept_keys(size)
    factor = column_of(inverse_rms(t_ref[0:1, :], width_all))
    for h in range(heads):
        lanes = slice(h * HDIM, (h + 1) * HDIM)
        wide, q, k, v = normed_head(x_ref[:, lanes], factor, gq_ref[:, lanes], gk_ref[:, lanes])
        vt = v.T
        for j in range(tokens // size):
            exps, total = exponents(scores_of(k, q, j, size, kept))
            mixed = nn(vt[:, : (j + 1) * size], stacked(exps).astype(BF16)) * (1.0 / total)
            rows = slice(j * size, (j + 1) * size)
            o_ref[rows, lanes] = (wide[rows] + mixed.T).astype(BF16)


def forward(width_all, x, totals, gain_q, gain_k, heads, after=()):
    tokens, width = x.shape
    lanes = heads * HDIM
    block = pl.BlockSpec((tokens, lanes), lambda i: (0, i))
    gain = pl.BlockSpec((1, lanes), lambda i: (0, i))
    return pl.pallas_call(
        functools.partial(forward_kernel, heads, width_all),
        out_shape=jax.ShapeDtypeStruct(x.shape, BF16),
        grid=(width // lanes,),
        in_specs=[block, pl.BlockSpec(totals.shape, lambda i: (0, 0)), gain, gain] + [IN_HBM] * len(after),
        out_specs=block,
        compiler_params=compiler(VMEM),
        name="forward",
    )(in_hbm(x), totals, gain_q, gain_k, *map(in_hbm, after))


def backward_head(x, g, factor, gain_q, gain_k):
    tokens = x.shape[0]
    size = block_of(tokens)
    kept = kept_keys(size)
    wide, q, k, v = normed_head(x, factor, gain_q, gain_k)
    kt = k.T
    blocks = tokens // size
    d_q = []
    d_k = [None] * blocks
    d_v = [None] * blocks
    for j in range(blocks):
        rows = slice(j * size, (j + 1) * size)
        exps, total = exponents(scores_of(k, q, j, size, kept))
        inverse = 1.0 / total
        weights = [e * inverse for e in exps]
        grads = [nt(v[: j * size], g[rows])] if j else []
        grads.append(nt(v[rows], g[rows]))
        delta = sum(jnp.sum(w * d, axis=0, keepdims=True) for w, d in zip(weights, grads))
        scores = stacked([(w * ((d - delta) * SCALE)).astype(BF16) for w, d in zip(weights, grads)])
        rounded = stacked([w.astype(BF16) for w in weights])
        d_q.append(nn(kt[:, : (j + 1) * size], scores).T)
        part_k = nn(scores, q[rows])
        part_v = nn(rounded, g[rows])
        for i in range(j + 1):
            mine = slice(i * size, (i + 1) * size)
            d_k[i] = part_k[mine] if d_k[i] is None else d_k[i] + part_k[mine]
            d_v[i] = part_v[mine] if d_v[i] is None else d_v[i] + part_v[mine]
    d_normed = stacked(d_q) * gain_q + stacked(d_k) * gain_k + stacked(d_v)
    return wide, d_normed


def backward_kernel(
    first, base, heads, ahead, width_all,
    evicted_ref, own_ref, far_ref, g_ref, t_ref, held_ref, gq_ref, gk_ref, past_ref, *refs,
):
    evicted = evicted_ref[0] == 1
    if ahead:
        pair, inner_ref, xs, gs, x_sem, g_sem = refs[-6:]
    else:
        a_out, x_out, inner_ref, xs, gs, outs, x_sem, g_sem, a_sem, out_sem = refs[-10:]
    copies = []
    for h in range(heads):
        to = lanes_of(h * HDIM, HDIM)
        there = lanes_of(first + h * HDIM, HDIM)
        far = pltpu.make_async_copy(far_ref.at[to], xs.at[to], x_sem.at[h])
        near = pltpu.make_async_copy(own_ref.at[(0, 0) + there], xs.at[to], x_sem.at[h])
        g = pltpu.make_async_copy(g_ref.at[(0,) + there], gs.at[to], g_sem.at[h])
        pl.when(evicted)(far.start)
        pl.when(jnp.logical_not(evicted))(near.start)
        g.start()
        copies.append((far, near, g))
    factor = column_of(inverse_rms(total_of(evicted_ref, t_ref, held_ref), width_all))
    part = None
    sent = []
    for h in range(heads):
        far, near, copy = copies[h]
        pl.when(evicted)(far.wait)
        pl.when(jnp.logical_not(evicted))(near.wait)
        copy.wait()
        mine = lanes_of(h * HDIM, HDIM)
        there = lanes_of(first + h * HDIM, HDIM)
        g = gs[mine]
        wide, d_normed = backward_head(xs[mine], g, factor, gq_ref[there], gk_ref[there])
        term = g.astype(F32) + factor * d_normed
        if ahead:
            pair[mine] = term.astype(BF16)
            pair[lanes_of((heads + h) * HDIM, HDIM)] = xs[mine]
        else:
            outs[mine] = term
            to = lanes_of(first - base + h * HDIM, HDIM)
            sent.append(pltpu.make_async_copy(outs.at[mine], a_out.at[to], a_sem.at[h]))
            sent.append(pltpu.make_async_copy(xs.at[mine], x_out.at[to], out_sem.at[h]))
            for copy in sent[-2:]:
                copy.start()
        product = d_normed * wide
        part = product if part is None else part + product
    inner_ref[...] = jnp.sum(part.T, axis=0, keepdims=True) + past_ref[...]
    for copy in sent:
        copy.wait()


def total_of(evicted_ref, t_ref, held_ref):
    return jnp.where(evicted_ref[0] == 1, held_ref[2:3, :], t_ref[1:2, :])


def backward(
    width_all, evicted, stash, far, g, totals, held, gain_q, gain_k, past, heads, first, base, sofar=(), after=()
):
    tokens, width = totals.shape[1], gain_q.shape[1]
    ahead = first < base
    small = (tokens, heads * HDIM)
    dma = pltpu.SemaphoreType.DMA((heads,))
    inner = jax.ShapeDtypeStruct((1, tokens), F32)
    if ahead:
        shapes = (jax.ShapeDtypeStruct((tokens, 2 * heads * HDIM), BF16), inner)
        scratch = [pltpu.VMEM(small, BF16)] * 2 + [dma] * 2
    else:
        shapes = (pltpu.HBM((tokens, width - base), F32), pltpu.HBM((tokens, width - base), BF16), inner)
        scratch = [pltpu.VMEM(small, BF16)] * 2 + [pltpu.VMEM(small, F32)] + [dma] * 4
    return pl.pallas_call(
        functools.partial(backward_kernel, first, base, heads, ahead, width_all),
        out_shape=shapes,
        in_specs=[pl.BlockSpec(memory_space=pltpu.SMEM)] + [ANYWHERE] * 3 + [IN_VMEM] * 5
        + [IN_HBM] * len(sofar) + [ANYWHERE] * len(after),
        out_specs=(IN_VMEM, IN_VMEM) if ahead else (IN_HBM, IN_HBM, IN_VMEM),
        input_output_aliases={9: 0, 10: 1} if sofar else {},
        scratch_shapes=scratch,
        compiler_params=compiler(VMEM),
        name="backward",
    )(evicted, in_hbm(stash), far, in_hbm(g), totals, held, gain_q, gain_k, past, *sofar, *after)


def row_of(total, inner, width_all):
    return inverse_rms(total, width_all) ** 3 * inner / width_all


def finish_kernel(width_all, evicted_ref, a_ref, x_ref, t_ref, held_ref, inner_ref, o_ref, row_ref):
    row = row_of(total_of(evicted_ref, t_ref, held_ref), inner_ref[...], width_all)
    row_ref[...] = row
    o_ref[...] = (a_ref[...] - x_ref[...].astype(F32) * column_of(row)).astype(BF16)


def finish(width_all, evicted, a, x, totals, held, inner, lanes):
    tokens, width = a.shape
    block = pl.BlockSpec((tokens, lanes), lambda i: (0, i))
    return pl.pallas_call(
        functools.partial(finish_kernel, width_all),
        out_shape=(jax.ShapeDtypeStruct(a.shape, BF16), jax.ShapeDtypeStruct((1, tokens), F32)),
        grid=(width // lanes,),
        in_specs=[pl.BlockSpec(memory_space=pltpu.SMEM), block, block] + [IN_VMEM] * 3,
        out_specs=(block, pl.BlockSpec((1, tokens), lambda i: (0, 0))),
        compiler_params=compiler(VMEM),
        name="finish",
    )(evicted, in_hbm(a), in_hbm(x), totals, held, inner)


def place_kernel(ahead, pair_ref, row_ref, rest_ref, o_ref):
    step = pl.program_id(0)

    @pl.when(step < ahead)
    def _():
        at = pl.multiple_of(step * HDIM, HDIM)
        term = pair_ref[:, pl.ds(at, HDIM)]
        x = pair_ref[:, pl.ds(at + ahead * HDIM, HDIM)]
        o_ref[...] = (term.astype(F32) - x.astype(F32) * column_of(row_ref[...])).astype(BF16)

    @pl.when(step >= ahead)
    def _():
        o_ref[...] = rest_ref[:, pl.ds(pl.multiple_of((step - ahead) * HDIM, HDIM), HDIM)]


def place(pair, row, rest):
    tokens = rest.shape[0]
    ahead = pair.shape[1] // HDIM // 2
    width = rest.shape[1] + ahead * HDIM
    return pl.pallas_call(
        functools.partial(place_kernel, ahead),
        out_shape=jax.ShapeDtypeStruct((tokens, width), BF16),
        grid=(width // HDIM,),
        in_specs=[IN_VMEM] * 3,
        out_specs=pl.BlockSpec((tokens, HDIM), lambda i: (0, i)),
        compiler_params=compiler(VMEM),
        name="place",
    )(pair, row, rest)


def squares_kernel(current_ref, stash_ref, *rest):
    rows_ref, sums = rest[-2:]
    step = pl.program_id(0)

    def total(x):
        wide = x.astype(F32)
        square = wide * wide
        return sum(square[:, i : i + HDIM] for i in range(0, square.shape[1], HDIM))

    for i, x in enumerate((current_ref[...], stash_ref[0], stash_ref[1])):
        part = total(x)

        @pl.when(step == 0)
        def _():
            sums[i] = part

        @pl.when(step > 0)
        def _():
            sums[i] += part

    @pl.when(step == pl.num_programs(0) - 1)
    def _():
        for i in range(3):
            rows_ref[i : i + 1, :] = jnp.sum(sums[i].T, axis=0, keepdims=True)


def squares(current, stash, lanes, after=()):
    tokens, width = current.shape
    return pl.pallas_call(
        squares_kernel,
        out_shape=jax.ShapeDtypeStruct((3, tokens), F32),
        grid=(width // lanes,),
        in_specs=[
            pl.BlockSpec((tokens, lanes), lambda i: (0, i)),
            pl.BlockSpec((None, 2, tokens, lanes), lambda i: (0, 0, 0, i)),
        ] + [ANYWHERE] * len(after),
        out_specs=pl.BlockSpec((3, tokens), lambda i: (0, 0)),
        scratch_shapes=[pltpu.VMEM((3, tokens, HDIM), F32)],
        compiler_params=compiler(MOST),
        name="squares",
    )(in_hbm(current), in_hbm(stash), *after)


def piece_kernel(starts, sizes, stash_ref, *rest):
    outs, mark, sems = rest[-2 - len(sizes) : -2], rest[-2], rest[-1]
    mark[...] = jnp.zeros_like(mark)
    copies = [
        pltpu.make_async_copy(stash_ref.at[(0, 1) + lanes_of(start, size)], out, sems.at[i])
        for i, (start, size, out) in enumerate(zip(starts, sizes, outs))
    ]
    for copy in copies:
        copy.start()
    for copy in copies:
        copy.wait()


def pieces_of(stash, starts, sizes, after=()):
    tokens = stash.shape[2]
    return pl.pallas_call(
        functools.partial(piece_kernel, starts, sizes),
        out_shape=[jax.ShapeDtypeStruct((tokens, size), BF16) for size in sizes] + [jax.ShapeDtypeStruct((8, HDIM), F32)],
        in_specs=[IN_HBM] + [ANYWHERE] * len(after),
        out_specs=[IN_VMEM] * (len(sizes) + 1),
        scratch_shapes=[pltpu.SemaphoreType.DMA((len(sizes),))],
        compiler_params=compiler(VMEM),
        name="pieces",
    )(in_hbm(stash), *after)


def send(x, pairs):
    return lax.ppermute(x, "section", pairs)


def local(width_all, layer_input, grad_input, stashed, eviction, query_gain, key_gain):
    n = lax.axis_size("section")
    partner = [(s, (s + n // 2) % n) for s in range(n)]
    prior = [(s, (s - 1) % n) for s in range(n)]
    current = layer_input[0]
    tokens, width = current.shape
    count = width // HDIM
    heads = (max(1, count // 3), count - max(1, count // 3) - max(1, count // 6), max(1, count // 6))
    sizes = [h * HDIM for h in heads]
    starts = [sum(sizes[:i]) for i in range(3)]
    third = count // 3 * HDIM

    *away, mark = pieces_of(stashed, starts[:2], sizes[:2])
    fetched = [send(x, partner) for x in away]
    totals = lax.psum(squares(current, stashed, third, (mark,)), "tensor")
    held = send(totals, partner)
    output = forward(width_all, current, totals, query_gain, key_gain, third // HDIM)
    fetched.append(send(pieces_of(stashed, starts[2:], sizes[2:], (fetched[0], held, in_hbm(output)))[0], partner))

    share = functools.partial(backward, width_all, eviction, stashed)
    facts = (grad_input, totals, held, query_gain, key_gain)
    base = starts[1]
    pair, inner = share(
        fetched[0], *facts, jnp.zeros((1, tokens), F32), heads[0], 0, base, (), (in_hbm(output),)
    )
    pair = send(pair, prior)
    sofar = ()
    for h, start, far in zip(heads[1:], starts[1:], fetched[1:]):
        *sofar, inner = share(far, *facts, inner, h, start, base, tuple(sofar))
    inner = lax.psum(inner, "tensor")
    lanes = next(c for c in (2, 1) if (width - base) % (c * HDIM) == 0) * HDIM
    result, row = finish(width_all, eviction, *sofar, totals, held, inner, lanes)
    result = place(pair, send(row, prior), send(result, prior))
    return (output[None], result[None])


def solution(mesh):
    placed = (
        P("section", None, "tensor"),
        P("section", None, "tensor"),
        P("section", None, None, "tensor"),
        P("section"),
        P("section", "tensor"),
        P("section", "tensor"),
    )

    def whole(layer_input, *others):
        return jax.shard_map(
            functools.partial(local, layer_input.shape[-1]),
            mesh=mesh,
            in_specs=placed,
            out_specs=(P("section", None, "tensor"), P("section", None, "tensor")),
            check_vma=False,
        )(layer_input, *others)

    return whole
```

```python
import functools
import math

import jax
import jax.numpy as jnp
from jax import lax
from jax.experimental import pallas as pl
from jax.experimental.pallas import tpu as pltpu
from jax.sharding import PartitionSpec as P

HDIM = 128
EPSILON = 1e-05
SCALE = 1.0 / math.sqrt(HDIM)
LOG2E = math.log2(math.e)
VMEM = 32 * 1024 * 1024
MOST = 60 * 1024 * 1024

F32 = jnp.float32
BF16 = jnp.bfloat16


def dot(a, b, contract):
    return lax.dot_general(a, b, ((contract[0], contract[1]), ((), ())), preferred_element_type=F32)


def nt(a, b):
    return dot(a, b, ((1,), (1,)))


def nn(a, b):
    return dot(a, b, ((1,), (0,)))


def block_of(tokens):
    return 256 if tokens % 256 == 0 else tokens


def masked(block, kept):
    return jnp.where(kept, block, -1e30)


def kept_keys(size):
    keys = lax.broadcasted_iota(jnp.int32, (size, size), 0)
    return keys <= lax.broadcasted_iota(jnp.int32, (size, size), 1)


def scores_of(keys, queries, j, size, kept):
    mine = queries[j * size : (j + 1) * size]
    diagonal = masked(nt(keys[j * size : (j + 1) * size], mine), kept)
    if j == 0:
        return [diagonal]
    return [nt(keys[: j * size], mine), diagonal]


def exponents(parts):
    top = functools.reduce(jnp.maximum, [jnp.max(p, axis=0, keepdims=True) for p in parts])
    exps = [jnp.exp2((p - top) * (SCALE * LOG2E)) for p in parts]
    total = sum(jnp.sum(e, axis=0, keepdims=True) for e in exps)
    return exps, total


def stacked(parts):
    return parts[0] if len(parts) == 1 else jnp.concatenate(parts, axis=0)


def normed_head(x, factor, gain_q, gain_k):
    wide = x.astype(F32)
    normed = wide * factor
    return wide, (normed * gain_q).astype(BF16), (normed * gain_k).astype(BF16), normed.astype(BF16)


def column_of(row):
    return jnp.broadcast_to(row, (HDIM, row.shape[1])).T[:, 0:1]


def inverse_rms(total, width_all):
    return lax.rsqrt(total / width_all + EPSILON)


def lanes_of(start, size):
    return (slice(None), slice(start, start + size))


def compiler(limit):
    return pltpu.CompilerParams(vmem_limit_bytes=limit)


IN_VMEM = pl.BlockSpec(memory_space=pltpu.VMEM)
ANYWHERE = pl.BlockSpec(memory_space=pl.ANY)
IN_HBM = pl.BlockSpec(memory_space=pltpu.HBM)


def in_hbm(x):
    return pltpu.with_memory_space_constraint(x, pltpu.HBM)


def forward_kernel(heads, width_all, x_ref, t_ref, gq_ref, gk_ref, *rest):
    o_ref = rest[-1]
    tokens = x_ref.shape[0]
    size = block_of(tokens)
    kept = kept_keys(size)
    factor = column_of(inverse_rms(t_ref[0:1, :], width_all))
    for h in range(heads):
        lanes = slice(h * HDIM, (h + 1) * HDIM)
        wide, q, k, v = normed_head(x_ref[:, lanes], factor, gq_ref[:, lanes], gk_ref[:, lanes])
        vt = v.T
        for j in range(tokens // size):
            exps, total = exponents(scores_of(k, q, j, size, kept))
            mixed = nn(vt[:, : (j + 1) * size], stacked(exps).astype(BF16)) * (1.0 / total)
            rows = slice(j * size, (j + 1) * size)
            o_ref[rows, lanes] = (wide[rows] + mixed.T).astype(BF16)


def forward(width_all, x, totals, gain_q, gain_k, heads, after=()):
    tokens, width = x.shape
    lanes = heads * HDIM
    block = pl.BlockSpec((tokens, lanes), lambda i: (0, i))
    gain = pl.BlockSpec((1, lanes), lambda i: (0, i))
    return pl.pallas_call(
        functools.partial(forward_kernel, heads, width_all),
        out_shape=jax.ShapeDtypeStruct(x.shape, BF16),
        grid=(width // lanes,),
        in_specs=[block, pl.BlockSpec(totals.shape, lambda i: (0, 0)), gain, gain] + [IN_HBM] * len(after),
        out_specs=block,
        compiler_params=compiler(VMEM),
        name="forward",
    )(in_hbm(x), totals, gain_q, gain_k, *map(in_hbm, after))


def backward_head(x, g, factor, gain_q, gain_k):
    tokens = x.shape[0]
    size = block_of(tokens)
    kept = kept_keys(size)
    wide, q, k, v = normed_head(x, factor, gain_q, gain_k)
    kt = k.T
    blocks = tokens // size
    d_q = []
    d_k = [None] * blocks
    d_v = [None] * blocks
    for j in range(blocks):
        rows = slice(j * size, (j + 1) * size)
        exps, total = exponents(scores_of(k, q, j, size, kept))
        inverse = 1.0 / total
        weights = [e * inverse for e in exps]
        grads = [nt(v[: j * size], g[rows])] if j else []
        grads.append(nt(v[rows], g[rows]))
        delta = sum(jnp.sum(w * d, axis=0, keepdims=True) for w, d in zip(weights, grads))
        scores = stacked([(w * ((d - delta) * SCALE)).astype(BF16) for w, d in zip(weights, grads)])
        rounded = stacked([w.astype(BF16) for w in weights])
        d_q.append(nn(kt[:, : (j + 1) * size], scores).T)
        part_k = nn(scores, q[rows])
        part_v = nn(rounded, g[rows])
        for i in range(j + 1):
            mine = slice(i * size, (i + 1) * size)
            d_k[i] = part_k[mine] if d_k[i] is None else d_k[i] + part_k[mine]
            d_v[i] = part_v[mine] if d_v[i] is None else d_v[i] + part_v[mine]
    d_normed = stacked(d_q) * gain_q + stacked(d_k) * gain_k + stacked(d_v)
    return wide, d_normed


def backward_kernel(
    first, base, heads, ahead, pieces, width_all, evicted_ref, own_ref, g_ref, t_ref, held_ref, gq_ref, gk_ref, past_ref, *refs
):
    evicted = evicted_ref[0] == 1
    far_refs, each = refs[:pieces], heads // pieces
    if ahead:
        pair, inner_ref, xs, gs, x_sem, g_sem = refs[-6:]
    else:
        a_out, x_out, inner_ref, xs, gs, outs, x_sem, g_sem, a_sem, out_sem = refs[-10:]
    copies = []
    for h in range(heads):
        to = lanes_of(h * HDIM, HDIM)
        there = lanes_of(first + h * HDIM, HDIM)
        far_ref = far_refs[h // each].at[: t_ref.shape[1], h % each * HDIM : (h % each + 1) * HDIM]
        far = pltpu.make_async_copy(far_ref, xs.at[to], x_sem.at[h])
        near = pltpu.make_async_copy(own_ref.at[(0, 0) + there], xs.at[to], x_sem.at[h])
        g = pltpu.make_async_copy(g_ref.at[(0,) + there], gs.at[to], g_sem.at[h])
        pl.when(evicted)(far.start)
        pl.when(jnp.logical_not(evicted))(near.start)
        g.start()
        copies.append((far, near, g))
    factor = column_of(inverse_rms(total_of(evicted_ref, t_ref, held_ref), width_all))
    part = None
    sent = []
    for h in range(heads):
        far, near, copy = copies[h]
        pl.when(evicted)(far.wait)
        pl.when(jnp.logical_not(evicted))(near.wait)
        copy.wait()
        mine = lanes_of(h * HDIM, HDIM)
        there = lanes_of(first + h * HDIM, HDIM)
        g = gs[mine]
        wide, d_normed = backward_head(xs[mine], g, factor, gq_ref[there], gk_ref[there])
        term = g.astype(F32) + factor * d_normed
        if ahead:
            pair[mine] = term.astype(BF16)
            pair[lanes_of((heads + h) * HDIM, HDIM)] = xs[mine]
        else:
            outs[mine] = term
            to = lanes_of(first - base + h * HDIM, HDIM)
            sent.append(pltpu.make_async_copy(outs.at[mine], a_out.at[to], a_sem.at[h]))
            sent.append(pltpu.make_async_copy(xs.at[mine], x_out.at[to], out_sem.at[h]))
            for copy in sent[-2:]:
                copy.start()
        product = d_normed * wide
        part = product if part is None else part + product
    inner_ref[...] = jnp.sum(part.T, axis=0, keepdims=True) + past_ref[...]
    for copy in sent:
        copy.wait()


def total_of(evicted_ref, t_ref, held_ref):
    return jnp.where(evicted_ref[0] == 1, held_ref[...], t_ref[1:2, :])


def backward(
    width_all, evicted, stash, far, g, totals, held, gain_q, gain_k, past, heads, first, base, sofar=(), after=()
):
    tokens, width = totals.shape[1], gain_q.shape[1]
    ahead = first < base
    small = (tokens, heads * HDIM)
    dma = pltpu.SemaphoreType.DMA((heads,))
    inner = jax.ShapeDtypeStruct((1, tokens), F32)
    if ahead:
        shapes = (jax.ShapeDtypeStruct((tokens, 2 * heads * HDIM), BF16), inner)
        scratch = [pltpu.VMEM(small, BF16)] * 2 + [dma] * 2
    else:
        shapes = (pltpu.HBM((tokens, width - base), F32), pltpu.HBM((tokens, width - base), BF16), inner)
        scratch = [pltpu.VMEM(small, BF16)] * 2 + [pltpu.VMEM(small, F32)] + [dma] * 4
    return pl.pallas_call(
        functools.partial(backward_kernel, first, base, heads, ahead, len(far), width_all),
        out_shape=shapes,
        in_specs=[pl.BlockSpec(memory_space=pltpu.SMEM)] + [ANYWHERE] * 2 + [IN_VMEM] * 5
        + [ANYWHERE] * len(far) + [IN_HBM] * len(sofar) + [ANYWHERE] * len(after),
        out_specs=(IN_VMEM, IN_VMEM) if ahead else (IN_HBM, IN_HBM, IN_VMEM),
        input_output_aliases={8 + len(far): 0, 9 + len(far): 1} if sofar else {},
        scratch_shapes=scratch,
        compiler_params=compiler(VMEM),
        name="backward",
    )(evicted, in_hbm(stash), in_hbm(g), totals, held, gain_q, gain_k, past, *far, *sofar, *after)


def row_of(total, inner, width_all):
    return inverse_rms(total, width_all) ** 3 * inner / width_all


def finish_kernel(width_all, evicted_ref, a_ref, x_ref, t_ref, held_ref, inner_ref, o_ref, row_ref):
    row = row_of(total_of(evicted_ref, t_ref, held_ref), inner_ref[...], width_all)
    row_ref[...] = row
    o_ref[...] = (a_ref[...] - x_ref[...].astype(F32) * column_of(row)).astype(BF16)


def finish(width_all, evicted, a, x, totals, held, inner, lanes):
    tokens, width = a.shape
    block = pl.BlockSpec((tokens, lanes), lambda i: (0, i))
    return pl.pallas_call(
        functools.partial(finish_kernel, width_all),
        out_shape=(jax.ShapeDtypeStruct(a.shape, BF16), jax.ShapeDtypeStruct((1, tokens), F32)),
        grid=(width // lanes,),
        in_specs=[pl.BlockSpec(memory_space=pltpu.SMEM), block, block] + [IN_VMEM] * 3,
        out_specs=(block, pl.BlockSpec((1, tokens), lambda i: (0, 0))),
        compiler_params=compiler(VMEM),
        name="finish",
    )(evicted, in_hbm(a), in_hbm(x), totals, held, inner)


def place_kernel(ahead, pair_ref, row_ref, rest_ref, o_ref, outs, sems):
    lanes = ahead * HDIM
    width = o_ref.shape[1]
    rest = pltpu.make_async_copy(rest_ref, o_ref.at[lanes_of(lanes, width - lanes)], sems.at[ahead])
    rest.start()
    row = column_of(row_ref[...])
    copies = [rest]
    for h in range(ahead):
        mine = lanes_of(h * HDIM, HDIM)
        x = pair_ref[lanes_of(lanes + h * HDIM, HDIM)]
        outs[mine] = (pair_ref[mine].astype(F32) - x.astype(F32) * row).astype(BF16)
        copies.append(pltpu.make_async_copy(outs.at[mine], o_ref.at[mine], sems.at[h]))
        copies[-1].start()
    for copy in copies:
        copy.wait()


def place(pair, row, rest):
    tokens = rest.shape[0]
    ahead = pair.shape[1] // HDIM // 2
    return pl.pallas_call(
        functools.partial(place_kernel, ahead),
        out_shape=jax.ShapeDtypeStruct((tokens, rest.shape[1] + ahead * HDIM), BF16),
        in_specs=[IN_VMEM] * 3,
        out_specs=ANYWHERE,
        scratch_shapes=[pltpu.VMEM((tokens, ahead * HDIM), BF16), pltpu.SemaphoreType.DMA((ahead + 1,))],
        compiler_params=compiler(VMEM),
        name="place",
    )(pair, row, rest)


def hold_kernel(x_ref, *rest):
    pass


def hold(x, after):
    return pl.pallas_call(
        hold_kernel,
        out_shape=jax.ShapeDtypeStruct(x.shape, x.dtype),
        in_specs=[IN_VMEM] + [ANYWHERE] * len(after),
        out_specs=IN_VMEM,
        input_output_aliases={0: 0},
        compiler_params=compiler(VMEM),
        name="hold",
    )(x, *after)


def squares_kernel(current_ref, stash_ref, *rest):
    rows_ref, sums = rest[-2:]
    step = pl.program_id(0)

    def total(x):
        wide = x.astype(F32)
        square = wide * wide
        return sum(square[:, i : i + HDIM] for i in range(0, square.shape[1], HDIM))

    for i, x in enumerate((current_ref[...], stash_ref[0], stash_ref[1])):
        part = total(x)

        @pl.when(step == 0)
        def _():
            sums[i] = part

        @pl.when(step > 0)
        def _():
            sums[i] += part

    @pl.when(step == pl.num_programs(0) - 1)
    def _():
        for i in range(3):
            rows_ref[i : i + 1, :] = jnp.sum(sums[i].T, axis=0, keepdims=True)


def squares(current, stash, lanes, after=()):
    tokens, width = current.shape
    return pl.pallas_call(
        squares_kernel,
        out_shape=jax.ShapeDtypeStruct((3, tokens), F32),
        grid=(width // lanes,),
        in_specs=[
            pl.BlockSpec((tokens, lanes), lambda i: (0, i)),
            pl.BlockSpec((None, 2, tokens, lanes), lambda i: (0, 0, 0, i)),
        ] + [ANYWHERE] * len(after),
        out_specs=pl.BlockSpec((3, tokens), lambda i: (0, 0)),
        scratch_shapes=[pltpu.VMEM((3, tokens, HDIM), F32)],
        compiler_params=compiler(MOST),
        name="squares",
    )(in_hbm(current), in_hbm(stash), *after)


def piece_kernel(starts, sizes, stash_ref, *rest):
    outs, mark, sems = rest[-2 - len(sizes) : -2], rest[-2], rest[-1]
    mark[...] = jnp.zeros_like(mark)
    copies = [
        pltpu.make_async_copy(stash_ref.at[(0, 1) + lanes_of(start, size)], out, sems.at[i])
        for i, (start, size, out) in enumerate(zip(starts, sizes, outs))
    ]
    for copy in copies:
        copy.start()
    for copy in copies:
        copy.wait()


def pieces_of(stash, starts, sizes, after=()):
    tokens = stash.shape[2]
    return pl.pallas_call(
        functools.partial(piece_kernel, starts, sizes),
        out_shape=[jax.ShapeDtypeStruct((tokens, size), BF16) for size in sizes] + [jax.ShapeDtypeStruct((8, HDIM), F32)],
        in_specs=[IN_HBM] + [ANYWHERE] * len(after),
        out_specs=[IN_VMEM] * (len(sizes) + 1),
        scratch_shapes=[pltpu.SemaphoreType.DMA((len(sizes),))],
        compiler_params=compiler(VMEM),
        name="pieces",
    )(in_hbm(stash), *after)


def in_rows(row, size):
    tokens = row.shape[1]
    rows = []
    for _ in range(3):
        term = row.astype(BF16)
        row = row - term.astype(F32)
        rows += [term[:, i : i + size] for i in range(0, tokens, size)]
    fill = -len(rows) % 16
    return jnp.concatenate(rows + [jnp.zeros((fill, size), BF16)] * (fill > 0), axis=0)


def row_kernel(extra_ref, o_ref):
    tokens, size = o_ref.shape[1], extra_ref.shape[1]
    each = tokens // size
    extra = extra_ref[...].astype(F32)
    for i in range(each):
        o_ref[:, i * size : (i + 1) * size] = sum(extra[p * each + i : p * each + i + 1] for p in range(3))


def row_from(piece, tokens):
    extra = piece.shape[0] - tokens
    size = piece.shape[1]
    return pl.pallas_call(
        row_kernel,
        out_shape=jax.ShapeDtypeStruct((1, tokens), F32),
        grid=(1,),
        in_specs=[pl.BlockSpec((extra, size), lambda i: (tokens // extra, 0))],
        out_specs=pl.BlockSpec((1, tokens), lambda i: (0, 0)),
        compiler_params=compiler(VMEM),
        name="row",
    )(piece)


def piece_and_row_kernel(start, stash_ref, t_ref, *rest):
    out, sem = rest[-2:]
    tokens, size = stash_ref.shape[2], out.shape[1]
    copy = pltpu.make_async_copy(stash_ref.at[(0, 1) + lanes_of(start, size)], out.at[:tokens, :], sem.at[0])
    copy.start()
    out[tokens:, :] = in_rows(t_ref[2:3, :], size)
    copy.wait()


def piece_and_row(stash, totals, start, size, after):
    tokens = stash.shape[2]
    extra = -(-3 * tokens // size // 16) * 16
    return pl.pallas_call(
        functools.partial(piece_and_row_kernel, start),
        out_shape=jax.ShapeDtypeStruct((tokens + extra, size), BF16),
        in_specs=[IN_HBM, IN_VMEM] + [ANYWHERE] * len(after),
        out_specs=IN_VMEM,
        scratch_shapes=[pltpu.SemaphoreType.DMA((1,))],
        compiler_params=compiler(VMEM),
        name="piece_and_row",
    )(in_hbm(stash), totals, *after)


def send(x, pairs):
    return lax.ppermute(x, "section", pairs)


def local(width_all, layer_input, grad_input, stashed, eviction, query_gain, key_gain):
    n = lax.axis_size("section")
    partner = [(s, (s + n // 2) % n) for s in range(n)]
    prior = [(s, (s - 1) % n) for s in range(n)]
    current = layer_input[0]
    tokens, width = current.shape
    count = width // HDIM
    each = max(1, count // 6)
    pieces = count // each
    size = each * HDIM
    third = count // 3 * HDIM

    *away, mark = pieces_of(stashed, (0, size), (size, size))
    fetched = [send(x, partner) for x in away]
    totals = lax.psum(squares(current, stashed, third, (mark,)), "tensor")
    output = forward(width_all, current, totals, query_gain, key_gain, third // HDIM)

    def fetch(p, after):
        away, mark = pieces_of(stashed, (p * size,), (size,), (fetched[p - 2], after))
        fetched.append(send(away, partner))
        return mark

    fetched.append(send(piece_and_row(stashed, totals, 2 * size, size, (fetched[0],)), partner))
    held = row_from(fetched[2], tokens)
    marks = [fetch(p, in_hbm(output)) for p in range(3, min(5, pieces))]
    share = functools.partial(backward, width_all, eviction, stashed)
    facts = (grad_input, totals, held, query_gain, key_gain)
    group = max(1, pieces // 3)
    base = group * size
    pair, inner = share(
        fetched[:group], *facts, jnp.zeros((1, tokens), F32), group * each, 0, base, (), (in_hbm(output), *marks)
    )
    marks = [fetch(p, inner) for p in range(len(fetched), pieces)]
    pair = send(hold(pair, (fetched[-1],)), prior)
    sofar = ()
    for first, last in [(group, 2 * group)] + [(p, p + 1) for p in range(2 * group, pieces)]:
        *sofar, inner = share(
            fetched[first:last], *facts, inner, (last - first) * each, first * size, base, tuple(sofar), tuple(marks)
        )
        marks = []
    inner = lax.psum(inner, "tensor")
    lanes = next(c for c in (2, 1) if (width - base) % (c * HDIM) == 0) * HDIM
    result, row = finish(width_all, eviction, *sofar, totals, held, inner, lanes)
    result = place(pair, send(row, prior), send(result, prior))
    return (output[None], result[None])


def solution(mesh):
    placed = (
        P("section", None, "tensor"),
        P("section", None, "tensor"),
        P("section", None, None, "tensor"),
        P("section"),
        P("section", "tensor"),
        P("section", "tensor"),
    )

    def whole(layer_input, *others):
        return jax.shard_map(
            functools.partial(local, layer_input.shape[-1]),
            mesh=mesh,
            in_specs=placed,
            out_specs=(P("section", None, "tensor"), P("section", None, "tensor")),
            check_vma=False,
        )(layer_input, *others)

    return whole
```

```python
import functools
import math

import jax
import jax.numpy as jnp
from jax import lax
from jax.experimental import pallas as pl
from jax.experimental.pallas import tpu as pltpu
from jax.sharding import PartitionSpec as P

HDIM = 128
EPSILON = 1e-05
SCALE = 1.0 / math.sqrt(HDIM)
LOG2E = math.log2(math.e)
VMEM = 32 * 1024 * 1024
MOST = 60 * 1024 * 1024

F32 = jnp.float32
BF16 = jnp.bfloat16


def dot(a, b, contract):
    return lax.dot_general(a, b, ((contract[0], contract[1]), ((), ())), preferred_element_type=F32)


def nt(a, b):
    return dot(a, b, ((1,), (1,)))


def nn(a, b):
    return dot(a, b, ((1,), (0,)))


def block_of(tokens):
    return 256 if tokens % 256 == 0 else tokens


def masked(block, kept):
    return jnp.where(kept, block, -1e30)


def kept_keys(size):
    keys = lax.broadcasted_iota(jnp.int32, (size, size), 0)
    return keys <= lax.broadcasted_iota(jnp.int32, (size, size), 1)


def scores_of(keys, queries, j, size, kept):
    mine = queries[j * size : (j + 1) * size]
    diagonal = masked(nt(keys[j * size : (j + 1) * size], mine), kept)
    if j == 0:
        return [diagonal]
    return [nt(keys[: j * size], mine), diagonal]


def exponents(parts):
    top = functools.reduce(jnp.maximum, [jnp.max(p, axis=0, keepdims=True) for p in parts])
    exps = [jnp.exp2((p - top) * (SCALE * LOG2E)) for p in parts]
    total = sum(jnp.sum(e, axis=0, keepdims=True) for e in exps)
    return exps, total


def stacked(parts):
    return parts[0] if len(parts) == 1 else jnp.concatenate(parts, axis=0)


def normed_head(x, factor, gain_q, gain_k):
    wide = x.astype(F32)
    normed = wide * factor
    return wide, (normed * gain_q).astype(BF16), (normed * gain_k).astype(BF16), normed.astype(BF16)


def column_of(row):
    return jnp.broadcast_to(row, (HDIM, row.shape[1])).T[:, 0:1]


def inverse_rms(total, width_all):
    return lax.rsqrt(total / width_all + EPSILON)


def lanes_of(start, size):
    return (slice(None), slice(start, start + size))


def compiler(limit):
    return pltpu.CompilerParams(vmem_limit_bytes=limit)


IN_VMEM = pl.BlockSpec(memory_space=pltpu.VMEM)
ANYWHERE = pl.BlockSpec(memory_space=pl.ANY)
IN_HBM = pl.BlockSpec(memory_space=pltpu.HBM)


def in_hbm(x):
    return pltpu.with_memory_space_constraint(x, pltpu.HBM)


def forward_kernel(heads, width_all, x_ref, t_ref, gq_ref, gk_ref, *rest):
    o_ref = rest[-1]
    tokens = x_ref.shape[0]
    size = block_of(tokens)
    kept = kept_keys(size)
    factor = column_of(inverse_rms(t_ref[0:1, :], width_all))
    for h in range(heads):
        lanes = slice(h * HDIM, (h + 1) * HDIM)
        wide, q, k, v = normed_head(x_ref[:, lanes], factor, gq_ref[:, lanes], gk_ref[:, lanes])
        vt = v.T
        for j in range(tokens // size):
            exps, total = exponents(scores_of(k, q, j, size, kept))
            mixed = nn(vt[:, : (j + 1) * size], stacked(exps).astype(BF16)) * (1.0 / total)
            rows = slice(j * size, (j + 1) * size)
            o_ref[rows, lanes] = (wide[rows] + mixed.T).astype(BF16)


def forward(width_all, x, totals, gain_q, gain_k, heads, after=()):
    tokens, width = x.shape
    lanes = heads * HDIM
    block = pl.BlockSpec((tokens, lanes), lambda i: (0, i))
    gain = pl.BlockSpec((1, lanes), lambda i: (0, i))
    return pl.pallas_call(
        functools.partial(forward_kernel, heads, width_all),
        out_shape=jax.ShapeDtypeStruct(x.shape, BF16),
        grid=(width // lanes,),
        in_specs=[block, pl.BlockSpec(totals.shape, lambda i: (0, 0)), gain, gain] + [IN_HBM] * len(after),
        out_specs=block,
        compiler_params=compiler(VMEM),
        name="forward",
    )(in_hbm(x), totals, gain_q, gain_k, *map(in_hbm, after))


def backward_head(x, g, factor, gain_q, gain_k):
    tokens = x.shape[0]
    size = block_of(tokens)
    kept = kept_keys(size)
    wide, q, k, v = normed_head(x, factor, gain_q, gain_k)
    kt = k.T
    blocks = tokens // size
    d_q = []
    d_k = [None] * blocks
    d_v = [None] * blocks
    for j in range(blocks):
        rows = slice(j * size, (j + 1) * size)
        exps, total = exponents(scores_of(k, q, j, size, kept))
        inverse = 1.0 / total
        weights = [e * inverse for e in exps]
        grads = [nt(v[: j * size], g[rows])] if j else []
        grads.append(nt(v[rows], g[rows]))
        delta = sum(jnp.sum(w * d, axis=0, keepdims=True) for w, d in zip(weights, grads))
        scores = stacked([(w * ((d - delta) * SCALE)).astype(BF16) for w, d in zip(weights, grads)])
        rounded = stacked([w.astype(BF16) for w in weights])
        d_q.append(nn(kt[:, : (j + 1) * size], scores).T)
        part_k = nn(scores, q[rows])
        part_v = nn(rounded, g[rows])
        for i in range(j + 1):
            mine = slice(i * size, (i + 1) * size)
            d_k[i] = part_k[mine] if d_k[i] is None else d_k[i] + part_k[mine]
            d_v[i] = part_v[mine] if d_v[i] is None else d_v[i] + part_v[mine]
    d_normed = stacked(d_q) * gain_q + stacked(d_k) * gain_k + stacked(d_v)
    return wide, d_normed


def backward_kernel(
    first, base, heads, ahead, pieces, width_all, evicted_ref, own_ref, g_ref, t_ref, held_ref, gq_ref, gk_ref, past_ref, *refs
):
    evicted = evicted_ref[0] == 1
    far_refs, each = refs[:pieces], heads // pieces
    if ahead:
        pair, inner_ref, xs, gs, x_sem, g_sem = refs[-6:]
    else:
        a_out, x_out, inner_ref, xs, gs, outs, x_sem, g_sem, a_sem, out_sem = refs[-10:]
    copies = []
    for h in range(heads):
        to = lanes_of(h * HDIM, HDIM)
        there = lanes_of(first + h * HDIM, HDIM)
        far_ref = far_refs[h // each].at[: t_ref.shape[1], h % each * HDIM : (h % each + 1) * HDIM]
        far = pltpu.make_async_copy(far_ref, xs.at[to], x_sem.at[h])
        near = pltpu.make_async_copy(own_ref.at[(0, 0) + there], xs.at[to], x_sem.at[h])
        g = pltpu.make_async_copy(g_ref.at[(0,) + there], gs.at[to], g_sem.at[h])
        pl.when(evicted)(far.start)
        pl.when(jnp.logical_not(evicted))(near.start)
        g.start()
        copies.append((far, near, g))
    factor = column_of(inverse_rms(total_of(evicted_ref, t_ref, held_ref), width_all))
    part = None
    sent = []
    for h in range(heads):
        far, near, copy = copies[h]
        pl.when(evicted)(far.wait)
        pl.when(jnp.logical_not(evicted))(near.wait)
        copy.wait()
        mine = lanes_of(h * HDIM, HDIM)
        there = lanes_of(first + h * HDIM, HDIM)
        g = gs[mine]
        wide, d_normed = backward_head(xs[mine], g, factor, gq_ref[there], gk_ref[there])
        term = g.astype(F32) + factor * d_normed
        if ahead:
            pair[mine] = term.astype(BF16)
            pair[lanes_of((heads + h) * HDIM, HDIM)] = xs[mine]
        else:
            outs[mine] = term
            to = lanes_of(first - base + h * HDIM, HDIM)
            sent.append(pltpu.make_async_copy(outs.at[mine], a_out.at[to], a_sem.at[h]))
            sent.append(pltpu.make_async_copy(xs.at[mine], x_out.at[to], out_sem.at[h]))
            for copy in sent[-2:]:
                copy.start()
        product = d_normed * wide
        part = product if part is None else part + product
    inner_ref[...] = jnp.sum(part.T, axis=0, keepdims=True) + past_ref[...]
    for copy in sent:
        copy.wait()


def total_of(evicted_ref, t_ref, held_ref):
    return jnp.where(evicted_ref[0] == 1, held_ref[...], t_ref[1:2, :])


def backward(
    width_all, evicted, stash, far, g, totals, held, gain_q, gain_k, past, heads, first, base, sofar=(), after=()
):
    tokens, width = totals.shape[1], gain_q.shape[1]
    ahead = first < base
    small = (tokens, heads * HDIM)
    dma = pltpu.SemaphoreType.DMA((heads,))
    inner = jax.ShapeDtypeStruct((1, tokens), F32)
    if ahead:
        shapes = (jax.ShapeDtypeStruct((tokens, 2 * heads * HDIM), BF16), inner)
        scratch = [pltpu.VMEM(small, BF16)] * 2 + [dma] * 2
    else:
        shapes = (pltpu.HBM((tokens, width - base), F32), pltpu.HBM((tokens, width - base), BF16), inner)
        scratch = [pltpu.VMEM(small, BF16)] * 2 + [pltpu.VMEM(small, F32)] + [dma] * 4
    return pl.pallas_call(
        functools.partial(backward_kernel, first, base, heads, ahead, len(far), width_all),
        out_shape=shapes,
        in_specs=[pl.BlockSpec(memory_space=pltpu.SMEM)] + [ANYWHERE] * 2 + [IN_VMEM] * 5
        + [ANYWHERE] * len(far) + [IN_HBM] * len(sofar) + [ANYWHERE] * len(after),
        out_specs=(IN_VMEM, IN_VMEM) if ahead else (IN_HBM, IN_HBM, IN_VMEM),
        input_output_aliases={8 + len(far): 0, 9 + len(far): 1} if sofar else {},
        scratch_shapes=scratch,
        compiler_params=compiler(VMEM),
        name="backward",
    )(evicted, in_hbm(stash), in_hbm(g), totals, held, gain_q, gain_k, past, *far, *sofar, *after)


def row_of(total, inner, width_all):
    return inverse_rms(total, width_all) ** 3 * inner / width_all


def finish_kernel(width_all, evicted_ref, a_ref, x_ref, t_ref, held_ref, inner_ref, o_ref, row_ref):
    row = row_of(total_of(evicted_ref, t_ref, held_ref), inner_ref[...], width_all)
    row_ref[...] = row
    o_ref[...] = (a_ref[...] - x_ref[...].astype(F32) * column_of(row)).astype(BF16)


def finish(width_all, evicted, a, x, totals, held, inner, lanes):
    tokens, width = a.shape
    block = pl.BlockSpec((tokens, lanes), lambda i: (0, i))
    return pl.pallas_call(
        functools.partial(finish_kernel, width_all),
        out_shape=(jax.ShapeDtypeStruct(a.shape, BF16), jax.ShapeDtypeStruct((1, tokens), F32)),
        grid=(width // lanes,),
        in_specs=[pl.BlockSpec(memory_space=pltpu.SMEM), block, block] + [IN_VMEM] * 3,
        out_specs=(block, pl.BlockSpec((1, tokens), lambda i: (0, 0))),
        compiler_params=compiler(VMEM),
        name="finish",
    )(evicted, in_hbm(a), in_hbm(x), totals, held, inner)


def place_kernel(ahead, pair_ref, row_ref, rest_ref, o_ref, outs, sems):
    lanes = ahead * HDIM
    width = o_ref.shape[1]
    rest = pltpu.make_async_copy(rest_ref, o_ref.at[lanes_of(lanes, width - lanes)], sems.at[ahead])
    rest.start()
    row = column_of(row_ref[...])
    copies = [rest]
    for h in range(ahead):
        mine = lanes_of(h * HDIM, HDIM)
        x = pair_ref[lanes_of(lanes + h * HDIM, HDIM)]
        outs[mine] = (pair_ref[mine].astype(F32) - x.astype(F32) * row).astype(BF16)
        copies.append(pltpu.make_async_copy(outs.at[mine], o_ref.at[mine], sems.at[h]))
        copies[-1].start()
    for copy in copies:
        copy.wait()


def place(pair, row, rest):
    tokens = rest.shape[0]
    ahead = pair.shape[1] // HDIM // 2
    return pl.pallas_call(
        functools.partial(place_kernel, ahead),
        out_shape=jax.ShapeDtypeStruct((tokens, rest.shape[1] + ahead * HDIM), BF16),
        in_specs=[IN_VMEM] * 3,
        out_specs=ANYWHERE,
        scratch_shapes=[pltpu.VMEM((tokens, ahead * HDIM), BF16), pltpu.SemaphoreType.DMA((ahead + 1,))],
        compiler_params=compiler(VMEM),
        name="place",
    )(pair, row, rest)


def hold_kernel(x_ref, *rest):
    pass


def hold(x, after):
    return pl.pallas_call(
        hold_kernel,
        out_shape=jax.ShapeDtypeStruct(x.shape, x.dtype),
        in_specs=[IN_VMEM] + [ANYWHERE] * len(after),
        out_specs=IN_VMEM,
        input_output_aliases={0: 0},
        compiler_params=compiler(VMEM),
        name="hold",
    )(x, *after)


def squares_kernel(current_ref, stash_ref, *rest):
    rows_ref, sums = rest[-2:]
    step = pl.program_id(0)

    def total(x):
        wide = x.astype(F32)
        square = wide * wide
        return sum(square[:, i : i + HDIM] for i in range(0, square.shape[1], HDIM))

    for i, x in enumerate((current_ref[...], stash_ref[0], stash_ref[1])):
        part = total(x)

        @pl.when(step == 0)
        def _():
            sums[i] = part

        @pl.when(step > 0)
        def _():
            sums[i] += part

    @pl.when(step == pl.num_programs(0) - 1)
    def _():
        for i in range(3):
            rows_ref[i : i + 1, :] = jnp.sum(sums[i].T, axis=0, keepdims=True)


def squares(current, stash, lanes, after=()):
    tokens, width = current.shape
    return pl.pallas_call(
        squares_kernel,
        out_shape=jax.ShapeDtypeStruct((3, tokens), F32),
        grid=(width // lanes,),
        in_specs=[
            pl.BlockSpec((tokens, lanes), lambda i: (0, i)),
            pl.BlockSpec((None, 2, tokens, lanes), lambda i: (0, 0, 0, i)),
        ] + [ANYWHERE] * len(after),
        out_specs=pl.BlockSpec((3, tokens), lambda i: (0, 0)),
        scratch_shapes=[pltpu.VMEM((3, tokens, HDIM), F32)],
        compiler_params=compiler(MOST),
        name="squares",
    )(in_hbm(current), in_hbm(stash), *after)


def piece_kernel(starts, sizes, stash_ref, *rest):
    outs, mark, sems = rest[-2 - len(sizes) : -2], rest[-2], rest[-1]
    mark[...] = jnp.zeros_like(mark)
    copies = [
        pltpu.make_async_copy(stash_ref.at[(0, 1) + lanes_of(start, size)], out, sems.at[i])
        for i, (start, size, out) in enumerate(zip(starts, sizes, outs))
    ]
    for copy in copies:
        copy.start()
    for copy in copies:
        copy.wait()


def pieces_of(stash, starts, sizes, after=()):
    tokens = stash.shape[2]
    return pl.pallas_call(
        functools.partial(piece_kernel, starts, sizes),
        out_shape=[jax.ShapeDtypeStruct((tokens, size), BF16) for size in sizes] + [jax.ShapeDtypeStruct((8, HDIM), F32)],
        in_specs=[IN_HBM] + [ANYWHERE] * len(after),
        out_specs=[IN_VMEM] * (len(sizes) + 1),
        scratch_shapes=[pltpu.SemaphoreType.DMA((len(sizes),))],
        compiler_params=compiler(VMEM),
        name="pieces",
    )(in_hbm(stash), *after)


def in_rows(row, size):
    tokens = row.shape[1]
    rows = []
    for _ in range(3):
        term = row.astype(BF16)
        row = row - term.astype(F32)
        rows += [term[:, i : i + size] for i in range(0, tokens, size)]
    fill = -len(rows) % 16
    return jnp.concatenate(rows + [jnp.zeros((fill, size), BF16)] * (fill > 0), axis=0)


def row_kernel(extra_ref, o_ref):
    tokens, size = o_ref.shape[1], extra_ref.shape[1]
    each = tokens // size
    extra = extra_ref[...].astype(F32)
    for i in range(each):
        o_ref[:, i * size : (i + 1) * size] = sum(extra[p * each + i : p * each + i + 1] for p in range(3))


def row_from(piece, tokens):
    extra = piece.shape[0] - tokens
    size = piece.shape[1]
    return pl.pallas_call(
        row_kernel,
        out_shape=jax.ShapeDtypeStruct((1, tokens), F32),
        grid=(1,),
        in_specs=[pl.BlockSpec((extra, size), lambda i: (tokens // extra, 0))],
        out_specs=pl.BlockSpec((1, tokens), lambda i: (0, 0)),
        compiler_params=compiler(VMEM),
        name="row",
    )(piece)


def piece_and_row_kernel(start, stash_ref, t_ref, *rest):
    out, sem = rest[-2:]
    tokens, size = stash_ref.shape[2], out.shape[1]
    copy = pltpu.make_async_copy(stash_ref.at[(0, 1) + lanes_of(start, size)], out.at[:tokens, :], sem.at[0])
    copy.start()
    out[tokens:, :] = in_rows(t_ref[2:3, :], size)
    copy.wait()


def piece_and_row(stash, totals, start, size, after):
    tokens = stash.shape[2]
    extra = -(-3 * tokens // size // 16) * 16
    return pl.pallas_call(
        functools.partial(piece_and_row_kernel, start),
        out_shape=jax.ShapeDtypeStruct((tokens + extra, size), BF16),
        in_specs=[IN_HBM, IN_VMEM] + [ANYWHERE] * len(after),
        out_specs=IN_VMEM,
        scratch_shapes=[pltpu.SemaphoreType.DMA((1,))],
        compiler_params=compiler(VMEM),
        name="piece_and_row",
    )(in_hbm(stash), totals, *after)


def send(x, pairs):
    return lax.ppermute(x, "section", pairs)


def local(width_all, layer_input, grad_input, stashed, eviction, query_gain, key_gain):
    n = lax.axis_size("section")
    partner = [(s, (s + n // 2) % n) for s in range(n)]
    prior = [(s, (s - 1) % n) for s in range(n)]
    current = layer_input[0]
    tokens, width = current.shape
    count = width // HDIM
    each = max(1, count // 6)
    pieces = count // each
    size = each * HDIM
    third = count // 3 * HDIM

    *away, mark = pieces_of(stashed, (0, size), (size, size))
    fetched = [send(x, partner) for x in away]
    totals = lax.psum(squares(current, stashed, third, (mark,)), "tensor")
    output = forward(width_all, current, totals, query_gain, key_gain, third // HDIM)

    def fetch(p, after):
        away, mark = pieces_of(stashed, (p * size,), (size,), (fetched[p - 2], after))
        fetched.append(send(away, partner))
        return mark

    fetched.append(send(piece_and_row(stashed, totals, 2 * size, size, (fetched[0],)), partner))
    held = row_from(fetched[2], tokens)
    marks = [fetch(p, in_hbm(output)) for p in range(3, min(5, pieces))]
    share = functools.partial(backward, width_all, eviction, stashed)
    facts = (grad_input, totals, held, query_gain, key_gain)
    group = max(1, pieces // 3)
    base = group * size
    pair, inner = share(
        fetched[:group], *facts, jnp.zeros((1, tokens), F32), group * each, 0, base, (), (in_hbm(output), *marks)
    )
    marks = [fetch(p, inner) for p in range(len(fetched), pieces)]
    pair = send(hold(pair, tuple(fetched[-2:])), prior)
    sofar = ()
    for first, last in [(group, 2 * group)] + [(p, p + 1) for p in range(2 * group, pieces)]:
        *sofar, inner = share(
            fetched[first:last], *facts, inner, (last - first) * each, first * size, base, tuple(sofar), tuple(marks)
        )
        marks = []
    inner = lax.psum(inner, "tensor")
    lanes = next(c for c in (2, 1) if (width - base) % (c * HDIM) == 0) * HDIM
    result, row = finish(width_all, eviction, *sofar, totals, held, inner, lanes)
    result = place(pair, send(row, prior), send(result, prior))
    return (output[None], result[None])


def solution(mesh):
    placed = (
        P("section", None, "tensor"),
        P("section", None, "tensor"),
        P("section", None, None, "tensor"),
        P("section"),
        P("section", "tensor"),
        P("section", "tensor"),
    )

    def whole(layer_input, *others):
        return jax.shard_map(
            functools.partial(local, layer_input.shape[-1]),
            mesh=mesh,
            in_specs=placed,
            out_specs=(P("section", None, "tensor"), P("section", None, "tensor")),
            check_vma=False,
        )(layer_input, *others)

    return whole
```

```python
import functools
import math

import jax
import jax.numpy as jnp
from jax import lax
from jax.experimental import pallas as pl
from jax.experimental.pallas import tpu as pltpu
from jax.sharding import PartitionSpec as P

HDIM = 128
EPSILON = 1e-05
SCALE = 1.0 / math.sqrt(HDIM)
LOG2E = math.log2(math.e)
VMEM = 32 * 1024 * 1024
MOST = 60 * 1024 * 1024

F32 = jnp.float32
BF16 = jnp.bfloat16


def dot(a, b, contract):
    return lax.dot_general(a, b, ((contract[0], contract[1]), ((), ())), preferred_element_type=F32)


def nt(a, b):
    return dot(a, b, ((1,), (1,)))


def nn(a, b):
    return dot(a, b, ((1,), (0,)))


def block_of(tokens):
    return 256 if tokens % 256 == 0 else tokens


def masked(block, kept):
    return jnp.where(kept, block, -1e30)


def kept_keys(size):
    keys = lax.broadcasted_iota(jnp.int32, (size, size), 0)
    return keys <= lax.broadcasted_iota(jnp.int32, (size, size), 1)


def scores_of(keys, queries, j, size, kept):
    mine = queries[j * size : (j + 1) * size]
    diagonal = masked(nt(keys[j * size : (j + 1) * size], mine), kept)
    if j == 0:
        return [diagonal]
    return [nt(keys[: j * size], mine), diagonal]


def exponents(parts):
    top = functools.reduce(jnp.maximum, [jnp.max(p, axis=0, keepdims=True) for p in parts])
    exps = [jnp.exp2((p - top) * (SCALE * LOG2E)) for p in parts]
    total = sum(jnp.sum(e, axis=0, keepdims=True) for e in exps)
    return exps, total


def stacked(parts):
    return parts[0] if len(parts) == 1 else jnp.concatenate(parts, axis=0)


def normed_head(x, factor, gain_q, gain_k):
    wide = x.astype(F32)
    normed = wide * factor
    return wide, (normed * gain_q).astype(BF16), (normed * gain_k).astype(BF16), normed.astype(BF16)


def column_of(row):
    return jnp.broadcast_to(row, (HDIM, row.shape[1])).T[:, 0:1]


def inverse_rms(total, width_all):
    return lax.rsqrt(total / width_all + EPSILON)


def lanes_of(start, size):
    return (slice(None), slice(start, start + size))


def compiler(limit):
    return pltpu.CompilerParams(vmem_limit_bytes=limit)


IN_VMEM = pl.BlockSpec(memory_space=pltpu.VMEM)
ANYWHERE = pl.BlockSpec(memory_space=pl.ANY)
IN_HBM = pl.BlockSpec(memory_space=pltpu.HBM)


def in_hbm(x):
    return pltpu.with_memory_space_constraint(x, pltpu.HBM)


def forward_kernel(heads, width_all, x_ref, t_ref, gq_ref, gk_ref, *rest):
    o_ref = rest[-1]
    tokens = x_ref.shape[0]
    size = block_of(tokens)
    kept = kept_keys(size)
    factor = column_of(inverse_rms(t_ref[0:1, :], width_all))
    for h in range(heads):
        lanes = slice(h * HDIM, (h + 1) * HDIM)
        wide, q, k, v = normed_head(x_ref[:, lanes], factor, gq_ref[:, lanes], gk_ref[:, lanes])
        vt = v.T
        for j in range(tokens // size):
            exps, total = exponents(scores_of(k, q, j, size, kept))
            mixed = nn(vt[:, : (j + 1) * size], stacked(exps).astype(BF16)) * (1.0 / total)
            rows = slice(j * size, (j + 1) * size)
            o_ref[rows, lanes] = (wide[rows] + mixed.T).astype(BF16)


def forward(width_all, x, totals, gain_q, gain_k, heads, after=()):
    tokens, width = x.shape
    lanes = heads * HDIM
    block = pl.BlockSpec((tokens, lanes), lambda i: (0, i))
    gain = pl.BlockSpec((1, lanes), lambda i: (0, i))
    return pl.pallas_call(
        functools.partial(forward_kernel, heads, width_all),
        out_shape=jax.ShapeDtypeStruct(x.shape, BF16),
        grid=(width // lanes,),
        in_specs=[block, pl.BlockSpec(totals.shape, lambda i: (0, 0)), gain, gain] + [IN_HBM] * len(after),
        out_specs=block,
        compiler_params=compiler(VMEM),
        name="forward",
    )(in_hbm(x), totals, gain_q, gain_k, *map(in_hbm, after))


def backward_head(x, g, factor, gain_q, gain_k):
    tokens = x.shape[0]
    size = block_of(tokens)
    kept = kept_keys(size)
    wide, q, k, v = normed_head(x, factor, gain_q, gain_k)
    kt = k.T
    blocks = tokens // size
    d_q = []
    d_k = [None] * blocks
    d_v = [None] * blocks
    for j in range(blocks):
        rows = slice(j * size, (j + 1) * size)
        exps, total = exponents(scores_of(k, q, j, size, kept))
        inverse = 1.0 / total
        weights = [e * inverse for e in exps]
        grads = [nt(v[: j * size], g[rows])] if j else []
        grads.append(nt(v[rows], g[rows]))
        delta = sum(jnp.sum(w * d, axis=0, keepdims=True) for w, d in zip(weights, grads))
        scores = stacked([(w * ((d - delta) * SCALE)).astype(BF16) for w, d in zip(weights, grads)])
        rounded = stacked([w.astype(BF16) for w in weights])
        d_q.append(nn(kt[:, : (j + 1) * size], scores).T)
        part_k = nn(scores, q[rows])
        part_v = nn(rounded, g[rows])
        for i in range(j + 1):
            mine = slice(i * size, (i + 1) * size)
            d_k[i] = part_k[mine] if d_k[i] is None else d_k[i] + part_k[mine]
            d_v[i] = part_v[mine] if d_v[i] is None else d_v[i] + part_v[mine]
    d_normed = stacked(d_q) * gain_q + stacked(d_k) * gain_k + stacked(d_v)
    return wide, d_normed


def backward_kernel(
    first, base, found, width_all, evicted_ref, own_ref, g_ref, t_ref, held_ref, gq_ref, gk_ref, past_ref, *refs
):
    evicted = evicted_ref[0] == 1
    heads = len(found)
    ahead = first < base
    if ahead:
        outs, inner_ref, xs, gs, x_sem, g_sem = refs[-6:]
    else:
        a_out, x_out, inner_ref, xs, gs, outs, x_sem, g_sem, a_sem, out_sem = refs[-10:]
    copies = []
    for h, (p, lane) in enumerate(found):
        to = lanes_of(h * HDIM, HDIM)
        there = lanes_of(first + h * HDIM, HDIM)
        far = pltpu.make_async_copy(refs[p].at[: t_ref.shape[1], lane : lane + HDIM], xs.at[to], x_sem.at[h])
        near = pltpu.make_async_copy(own_ref.at[(0, 0) + there], xs.at[to], x_sem.at[h])
        g = pltpu.make_async_copy(g_ref.at[(0,) + there], gs.at[to], g_sem.at[h])
        pl.when(evicted)(far.start)
        pl.when(jnp.logical_not(evicted))(near.start)
        g.start()
        copies.append((far, near, g))
    factor = column_of(inverse_rms(total_of(evicted_ref, t_ref, held_ref), width_all))
    part = None
    sent = []
    for h in range(heads):
        far, near, copy = copies[h]
        pl.when(evicted)(far.wait)
        pl.when(jnp.logical_not(evicted))(near.wait)
        copy.wait()
        mine = lanes_of(h * HDIM, HDIM)
        there = lanes_of(first + h * HDIM, HDIM)
        g = gs[mine]
        wide, d_normed = backward_head(xs[mine], g, factor, gq_ref[there], gk_ref[there])
        outs[mine] = (g.astype(F32) + factor * d_normed).astype(outs.dtype)
        if not ahead:
            to = lanes_of(first - base + h * HDIM, HDIM)
            sent.append(pltpu.make_async_copy(outs.at[mine], a_out.at[to], a_sem.at[h]))
            sent.append(pltpu.make_async_copy(xs.at[mine], x_out.at[to], out_sem.at[h]))
            for copy in sent[-2:]:
                copy.start()
        product = d_normed * wide
        part = product if part is None else part + product
    inner_ref[...] = jnp.sum(part.T, axis=0, keepdims=True) + past_ref[...]
    for copy in sent:
        copy.wait()


def total_of(evicted_ref, t_ref, held_ref):
    return jnp.where(evicted_ref[0] == 1, held_ref[...], t_ref[1:2, :])


def backward(width_all, evicted, stash, g, totals, held, gain_q, gain_k, past, far, first, base, sofar=(), after=()):
    tokens, width = totals.shape[1], gain_q.shape[1]
    found = tuple((p, lane) for p, piece in enumerate(far) for lane in range(0, piece.shape[1], HDIM))
    heads = len(found)
    small = (tokens, heads * HDIM)
    dma = pltpu.SemaphoreType.DMA((heads,))
    inner = jax.ShapeDtypeStruct((1, tokens), F32)
    if first < base:
        shapes = (jax.ShapeDtypeStruct(small, BF16), inner)
        scratch = [pltpu.VMEM(small, BF16)] * 2 + [dma] * 2
    else:
        shapes = (pltpu.HBM((tokens, width - base), F32), pltpu.HBM((tokens, width - base), BF16), inner)
        scratch = [pltpu.VMEM(small, BF16)] * 2 + [pltpu.VMEM(small, F32)] + [dma] * 4
    return pl.pallas_call(
        functools.partial(backward_kernel, first, base, found, width_all),
        out_shape=shapes,
        in_specs=[pl.BlockSpec(memory_space=pltpu.SMEM)] + [ANYWHERE] * 2 + [IN_VMEM] * 5
        + [ANYWHERE] * len(far) + [IN_HBM] * len(sofar) + [ANYWHERE] * len(after),
        out_specs=(IN_VMEM,) * 2 if first < base else (IN_HBM, IN_HBM, IN_VMEM),
        input_output_aliases={8 + len(far): 0, 9 + len(far): 1} if sofar else {},
        scratch_shapes=scratch,
        compiler_params=compiler(VMEM),
        name="backward",
    )(evicted, in_hbm(stash), in_hbm(g), totals, held, gain_q, gain_k, past, *far, *sofar, *after)


def row_of(total, inner, width_all):
    return inverse_rms(total, width_all) ** 3 * inner / width_all


def finish_kernel(width_all, evicted_ref, a_ref, x_ref, t_ref, held_ref, inner_ref, o_ref, row_ref):
    row = row_of(total_of(evicted_ref, t_ref, held_ref), inner_ref[...], width_all)
    row_ref[...] = row
    o_ref[...] = (a_ref[...] - x_ref[...].astype(F32) * column_of(row)).astype(BF16)


def finish(width_all, evicted, a, x, totals, held, inner, lanes):
    tokens, width = a.shape
    block = pl.BlockSpec((tokens, lanes), lambda i: (0, i))
    return pl.pallas_call(
        functools.partial(finish_kernel, width_all),
        out_shape=(jax.ShapeDtypeStruct(a.shape, BF16), jax.ShapeDtypeStruct((1, tokens), F32)),
        grid=(width // lanes,),
        in_specs=[pl.BlockSpec(memory_space=pltpu.SMEM), block, block] + [IN_VMEM] * 3,
        out_specs=(block, pl.BlockSpec((1, tokens), lambda i: (0, 0))),
        compiler_params=compiler(VMEM),
        name="finish",
    )(evicted, in_hbm(a), in_hbm(x), totals, held, inner)


def place_ahead_kernel(crossed_ref, a_ref, x_ref, y_ref, row_ref, o_ref, outs, sems):
    row = column_of(row_ref[...])
    copies = []
    for h in range(a_ref.shape[1] // HDIM):
        mine = lanes_of(h * HDIM, HDIM)
        x = jnp.where(crossed_ref[0] == 1, y_ref[mine], x_ref[mine])
        outs[mine] = (a_ref[mine].astype(F32) - x.astype(F32) * row).astype(BF16)
        copies.append(pltpu.make_async_copy(outs.at[mine], o_ref.at[mine], sems.at[h]))
        copies[-1].start()
    for copy in copies:
        copy.wait()


def place_ahead(crossed, a, x, y, row, width):
    tokens, lanes = a.shape
    return pl.pallas_call(
        place_ahead_kernel,
        out_shape=pltpu.HBM((tokens, width), BF16),
        in_specs=[pl.BlockSpec(memory_space=pltpu.SMEM)] + [IN_VMEM] * 4,
        out_specs=IN_HBM,
        scratch_shapes=[pltpu.VMEM((tokens, lanes), BF16), pltpu.SemaphoreType.DMA((lanes // HDIM,))],
        compiler_params=compiler(VMEM),
        name="place_ahead",
    )(crossed, a, x, y, row)


def place_rest_kernel(rest_ref, front_ref, o_ref, sem):
    size = rest_ref.shape[1]
    copy = pltpu.make_async_copy(rest_ref, o_ref.at[lanes_of(o_ref.shape[1] - size, size)], sem.at[0])
    copy.start()
    copy.wait()


def place_rest(rest, front):
    return pl.pallas_call(
        place_rest_kernel,
        out_shape=pltpu.HBM(front.shape, BF16),
        in_specs=[IN_VMEM, IN_HBM],
        out_specs=IN_HBM,
        input_output_aliases={1: 0},
        scratch_shapes=[pltpu.SemaphoreType.DMA((1,))],
        compiler_params=compiler(VMEM),
        name="place_rest",
    )(rest, front)


def hold_kernel(x_ref, *rest):
    pass


def hold(x, after):
    return pl.pallas_call(
        hold_kernel,
        out_shape=jax.ShapeDtypeStruct(x.shape, x.dtype),
        in_specs=[IN_VMEM] + [ANYWHERE] * len(after),
        out_specs=IN_VMEM,
        input_output_aliases={0: 0},
        compiler_params=compiler(VMEM),
        name="hold",
    )(x, *after)


def squares_kernel(current_ref, stash_ref, *rest):
    rows_ref, sums = rest[-2:]
    step = pl.program_id(0)

    def total(x):
        wide = x.astype(F32)
        square = wide * wide
        return sum(square[:, i : i + HDIM] for i in range(0, square.shape[1], HDIM))

    for i, x in enumerate((current_ref[...], stash_ref[0], stash_ref[1])):
        part = total(x)

        @pl.when(step == 0)
        def _():
            sums[i] = part

        @pl.when(step > 0)
        def _():
            sums[i] += part

    @pl.when(step == pl.num_programs(0) - 1)
    def _():
        for i in range(3):
            rows_ref[i : i + 1, :] = jnp.sum(sums[i].T, axis=0, keepdims=True)


def squares(current, stash, lanes, after=()):
    tokens, width = current.shape
    return pl.pallas_call(
        squares_kernel,
        out_shape=jax.ShapeDtypeStruct((3, tokens), F32),
        grid=(width // lanes,),
        in_specs=[
            pl.BlockSpec((tokens, lanes), lambda i: (0, i)),
            pl.BlockSpec((None, 2, tokens, lanes), lambda i: (0, 0, 0, i)),
        ] + [ANYWHERE] * len(after),
        out_specs=pl.BlockSpec((3, tokens), lambda i: (0, 0)),
        scratch_shapes=[pltpu.VMEM((3, tokens, HDIM), F32)],
        compiler_params=compiler(MOST),
        name="squares",
    )(in_hbm(current), in_hbm(stash), *after)


def piece_kernel(starts, sizes, stash_ref, *rest):
    outs, mark, sems = rest[-2 - len(sizes) : -2], rest[-2], rest[-1]
    mark[...] = jnp.zeros_like(mark)
    copies = [
        pltpu.make_async_copy(stash_ref.at[(0, 1) + lanes_of(start, size)], out, sems.at[i])
        for i, (start, size, out) in enumerate(zip(starts, sizes, outs))
    ]
    for copy in copies:
        copy.start()
    for copy in copies:
        copy.wait()


def pieces_of(stash, starts, sizes, after=()):
    tokens = stash.shape[2]
    return pl.pallas_call(
        functools.partial(piece_kernel, starts, sizes),
        out_shape=[jax.ShapeDtypeStruct((tokens, size), BF16) for size in sizes] + [jax.ShapeDtypeStruct((8, HDIM), F32)],
        in_specs=[IN_HBM] + [ANYWHERE] * len(after),
        out_specs=[IN_VMEM] * (len(sizes) + 1),
        scratch_shapes=[pltpu.SemaphoreType.DMA((len(sizes),))],
        compiler_params=compiler(VMEM),
        name="pieces",
    )(in_hbm(stash), *after)


def in_rows(row, size):
    tokens = row.shape[1]
    rows = []
    for _ in range(3):
        term = row.astype(BF16)
        row = row - term.astype(F32)
        rows += [term[:, i : i + size] for i in range(0, tokens, size)]
    fill = -len(rows) % 16
    return jnp.concatenate(rows + [jnp.zeros((fill, size), BF16)] * (fill > 0), axis=0)


def row_kernel(extra_ref, o_ref):
    tokens, size = o_ref.shape[1], extra_ref.shape[1]
    each = tokens // size
    extra = extra_ref[...].astype(F32)
    for i in range(each):
        o_ref[:, i * size : (i + 1) * size] = sum(extra[p * each + i : p * each + i + 1] for p in range(3))


def row_from(piece, tokens):
    extra = piece.shape[0] - tokens
    size = piece.shape[1]
    return pl.pallas_call(
        row_kernel,
        out_shape=jax.ShapeDtypeStruct((1, tokens), F32),
        grid=(1,),
        in_specs=[pl.BlockSpec((extra, size), lambda i: (tokens // extra, 0))],
        out_specs=pl.BlockSpec((1, tokens), lambda i: (0, 0)),
        compiler_params=compiler(VMEM),
        name="row",
    )(piece)


def piece_and_row_kernel(start, stash_ref, t_ref, *rest):
    out, mark, sem = rest[-3:]
    mark[...] = jnp.zeros_like(mark)
    tokens, size = stash_ref.shape[2], out.shape[1]
    copy = pltpu.make_async_copy(stash_ref.at[(0, 1) + lanes_of(start, size)], out.at[:tokens, :], sem.at[0])
    copy.start()
    out[tokens:, :] = in_rows(t_ref[2:3, :], size)
    copy.wait()


def piece_and_row(stash, totals, start, size, after):
    tokens = stash.shape[2]
    extra = -(-3 * tokens // size // 16) * 16
    return pl.pallas_call(
        functools.partial(piece_and_row_kernel, start),
        out_shape=(jax.ShapeDtypeStruct((tokens + extra, size), BF16), jax.ShapeDtypeStruct((8, HDIM), F32)),
        in_specs=[IN_HBM, IN_VMEM] + [ANYWHERE] * len(after),
        out_specs=(IN_VMEM, IN_VMEM),
        scratch_shapes=[pltpu.SemaphoreType.DMA((1,))],
        compiler_params=compiler(VMEM),
        name="piece_and_row",
    )(in_hbm(stash), totals, *after)


def chosen_kernel(n, evicted_ref, own_ref, *refs):
    far_refs, out, sem = refs[:n], refs[-2], refs[-1]
    evicted = evicted_ref[0] == 1
    own = pltpu.make_async_copy(own_ref.at[(0, 0) + lanes_of(0, out.shape[1])], out, sem.at[0])
    copies, at = [], 0
    for i, ref in enumerate(far_refs):
        size = ref.shape[1]
        copies.append(pltpu.make_async_copy(ref, out.at[lanes_of(at, size)], sem.at[i + 1]))
        at += size

    @pl.when(evicted)
    def _():
        for copy in copies:
            copy.start()
        for copy in copies:
            copy.wait()

    @pl.when(jnp.logical_not(evicted))
    def _():
        own.start()
        own.wait()


def chosen_of(evicted, stash, far, after):
    shape = (stash.shape[2], sum(f.shape[1] for f in far))
    return pl.pallas_call(
        functools.partial(chosen_kernel, len(far)),
        out_shape=jax.ShapeDtypeStruct(shape, BF16),
        in_specs=[pl.BlockSpec(memory_space=pltpu.SMEM), IN_HBM] + [ANYWHERE] * (len(far) + len(after)),
        out_specs=IN_VMEM,
        scratch_shapes=[pltpu.SemaphoreType.DMA((len(far) + 1,))],
        compiler_params=compiler(VMEM),
        name="chosen",
    )(evicted, in_hbm(stash), *far, *after)


def send(x, pairs):
    return lax.ppermute(x, "section", pairs)


def local(width_all, layer_input, grad_input, stashed, eviction, query_gain, key_gain):
    n = lax.axis_size("section")
    half = n // 2
    me = lax.axis_index("section")
    partner = [(s, (s + half) % n) for s in range(n)]
    prior = [(s, (s - 1) % n) for s in range(n)]
    within = [(s, (s - 1) % half + s // half * half) for s in range(n)]
    beyond = [(half - 1, n - 1), (n - 1, half - 1)]
    crossed = jnp.logical_or(me == n - 1, me == half - 1).astype(jnp.int32)[None]

    current = layer_input[0]
    tokens, width = current.shape
    count = width // HDIM
    third = count // 3 * HDIM
    small, large = max(1, count // 6), max(1, count // 3)
    pieces, at = [(large, small), (0, large)], small + large
    while count - at > small:
        pieces.append((at, small))
        at += small
    left = count - at
    pieces += [(at, left // 2), (at + left // 2, left - left // 2)] if left > 1 else [(at, left)]
    pieces = [(first * HDIM, heads * HDIM) for first, heads in pieces]
    base = (small + large) * HDIM

    *away, mark = pieces_of(stashed, *zip(*pieces[:2]))
    fetched = [send(x, partner) for x in away]
    totals = lax.psum(squares(current, stashed, third, (mark,)), "tensor")

    def fetch(p, after):
        away, mark = pieces_of(stashed, *zip(pieces[p]), (fetched[p - 2], after))
        fetched.append(send(away, partner))
        return mark

    away, mark = piece_and_row(stashed, totals, *pieces[2], (fetched[0],))
    fetched.append(send(away, partner))
    output = forward(width_all, current, totals, query_gain, key_gain, third // HDIM, (mark,))
    held = row_from(fetched[2], tokens)
    marks = [fetch(p, in_hbm(output)) for p in range(3, min(5, len(pieces)))]
    share = functools.partial(
        backward, width_all, eviction, stashed, grad_input, totals, held, query_gain, key_gain
    )
    x = chosen_of(eviction, stashed, [fetched[1], fetched[0]], (in_hbm(output),))
    x_within = send(x, within)
    a, inner = share(jnp.zeros((1, tokens), F32), [x], 0, base, (), (in_hbm(output), *marks))
    marks = [fetch(p, inner) for p in range(len(fetched), len(pieces))]

    split = max(3, len(pieces) - 2)
    groups = [range(2, split)] + [[p] for p in range(split, len(pieces))]
    sofar, inners = (), []
    for group in groups:
        *sofar, inner = share(
            inner, [fetched[p] for p in group], pieces[group[0]][0], base, tuple(sofar), tuple(marks)
        )
        inners.append(inner)
        marks = []
    gone = (*fetched[-2:], inners[max(0, len(inners) - 2)])
    x_beyond = send(hold(x_within, gone), beyond)
    a = send(hold(a, gone), prior)
    inner = lax.psum(inner, "tensor")
    lanes = next(c for c in (2, 1) if (width - base) % (c * HDIM) == 0) * HDIM
    result, row = finish(width_all, eviction, *sofar, totals, held, inner, lanes)
    front = place_ahead(crossed, a, x_within, x_beyond, send(row, prior), width)
    result = place_rest(send(result, prior), front)
    return (output[None], result[None])


def solution(mesh):
    placed = (
        P("section", None, "tensor"),
        P("section", None, "tensor"),
        P("section", None, None, "tensor"),
        P("section"),
        P("section", "tensor"),
        P("section", "tensor"),
    )

    def whole(layer_input, *others):
        return jax.shard_map(
            functools.partial(local, layer_input.shape[-1]),
            mesh=mesh,
            in_specs=placed,
            out_specs=(P("section", None, "tensor"), P("section", None, "tensor")),
            check_vma=False,
        )(layer_input, *others)

    return whole
```

```python
import functools
import math

import jax
import jax.numpy as jnp
from jax import lax
from jax.experimental import pallas as pl
from jax.experimental.pallas import tpu as pltpu
from jax.sharding import PartitionSpec as P

HDIM = 128
EPSILON = 1e-05
SCALE = 1.0 / math.sqrt(HDIM)
LOG2E = math.log2(math.e)
VMEM = 32 * 1024 * 1024
MOST = 60 * 1024 * 1024

F32 = jnp.float32
BF16 = jnp.bfloat16


def dot(a, b, contract):
    return lax.dot_general(a, b, ((contract[0], contract[1]), ((), ())), preferred_element_type=F32)


def nt(a, b):
    return dot(a, b, ((1,), (1,)))


def nn(a, b):
    return dot(a, b, ((1,), (0,)))


def block_of(tokens):
    return 256 if tokens % 256 == 0 else tokens


def masked(block, kept):
    return jnp.where(kept, block, -1e30)


def kept_keys(size):
    keys = lax.broadcasted_iota(jnp.int32, (size, size), 0)
    return keys <= lax.broadcasted_iota(jnp.int32, (size, size), 1)


def scores_of(keys, queries, j, size, kept):
    mine = queries[j * size : (j + 1) * size]
    diagonal = masked(nt(keys[j * size : (j + 1) * size], mine), kept)
    if j == 0:
        return [diagonal]
    return [nt(keys[: j * size], mine), diagonal]


def exponents(parts):
    top = functools.reduce(jnp.maximum, [jnp.max(p, axis=0, keepdims=True) for p in parts])
    exps = [jnp.exp2((p - top) * (SCALE * LOG2E)) for p in parts]
    total = sum(jnp.sum(e, axis=0, keepdims=True) for e in exps)
    return exps, total


def stacked(parts):
    return parts[0] if len(parts) == 1 else jnp.concatenate(parts, axis=0)


def normed_head(x, factor, gain_q, gain_k):
    wide = x.astype(F32)
    normed = wide * factor
    return wide, (normed * gain_q).astype(BF16), (normed * gain_k).astype(BF16), normed.astype(BF16)


def column_of(row):
    return jnp.broadcast_to(row, (HDIM, row.shape[1])).T[:, 0:1]


def inverse_rms(total, width_all):
    return lax.rsqrt(total / width_all + EPSILON)


def lanes_of(start, size):
    return (slice(None), slice(start, start + size))


def compiler(limit):
    return pltpu.CompilerParams(vmem_limit_bytes=limit)


IN_VMEM = pl.BlockSpec(memory_space=pltpu.VMEM)
ANYWHERE = pl.BlockSpec(memory_space=pl.ANY)
IN_HBM = pl.BlockSpec(memory_space=pltpu.HBM)


def in_hbm(x):
    return pltpu.with_memory_space_constraint(x, pltpu.HBM)


def forward_kernel(heads, width_all, x_ref, t_ref, gq_ref, gk_ref, *rest):
    o_ref = rest[-1]
    tokens = x_ref.shape[0]
    size = block_of(tokens)
    kept = kept_keys(size)
    factor = column_of(inverse_rms(t_ref[0:1, :], width_all))
    for h in range(heads):
        lanes = slice(h * HDIM, (h + 1) * HDIM)
        wide, q, k, v = normed_head(x_ref[:, lanes], factor, gq_ref[:, lanes], gk_ref[:, lanes])
        vt = v.T
        for j in range(tokens // size):
            exps, total = exponents(scores_of(k, q, j, size, kept))
            mixed = nn(vt[:, : (j + 1) * size], stacked(exps).astype(BF16)) * (1.0 / total)
            rows = slice(j * size, (j + 1) * size)
            o_ref[rows, lanes] = (wide[rows] + mixed.T).astype(BF16)


def forward(width_all, x, totals, gain_q, gain_k, heads, after=()):
    tokens, width = x.shape
    lanes = heads * HDIM
    block = pl.BlockSpec((tokens, lanes), lambda i: (0, i))
    gain = pl.BlockSpec((1, lanes), lambda i: (0, i))
    return pl.pallas_call(
        functools.partial(forward_kernel, heads, width_all),
        out_shape=jax.ShapeDtypeStruct(x.shape, BF16),
        grid=(width // lanes,),
        in_specs=[block, pl.BlockSpec(totals.shape, lambda i: (0, 0)), gain, gain] + [IN_HBM] * len(after),
        out_specs=block,
        compiler_params=compiler(VMEM),
        name="forward",
    )(in_hbm(x), totals, gain_q, gain_k, *map(in_hbm, after))


def backward_head(x, g, factor, gain_q, gain_k):
    tokens = x.shape[0]
    size = block_of(tokens)
    kept = kept_keys(size)
    wide, q, k, v = normed_head(x, factor, gain_q, gain_k)
    kt = k.T
    blocks = tokens // size
    d_q = []
    d_k = [None] * blocks
    d_v = [None] * blocks
    for j in range(blocks):
        rows = slice(j * size, (j + 1) * size)
        exps, total = exponents(scores_of(k, q, j, size, kept))
        inverse = 1.0 / total
        weights = [e * inverse for e in exps]
        grads = [nt(v[: j * size], g[rows])] if j else []
        grads.append(nt(v[rows], g[rows]))
        delta = sum(jnp.sum(w * d, axis=0, keepdims=True) for w, d in zip(weights, grads))
        scores = stacked([(w * ((d - delta) * SCALE)).astype(BF16) for w, d in zip(weights, grads)])
        rounded = stacked([w.astype(BF16) for w in weights])
        d_q.append(nn(kt[:, : (j + 1) * size], scores).T)
        part_k = nn(scores, q[rows])
        part_v = nn(rounded, g[rows])
        for i in range(j + 1):
            mine = slice(i * size, (i + 1) * size)
            d_k[i] = part_k[mine] if d_k[i] is None else d_k[i] + part_k[mine]
            d_v[i] = part_v[mine] if d_v[i] is None else d_v[i] + part_v[mine]
    d_normed = stacked(d_q) * gain_q + stacked(d_k) * gain_k + stacked(d_v)
    return wide, d_normed


def backward_kernel(
    first, base, found, width_all, evicted_ref, own_ref, g_ref, t_ref, held_ref, gq_ref, gk_ref, past_ref, *refs
):
    evicted = evicted_ref[0] == 1
    heads = len(found)
    ahead = first < base
    if ahead:
        outs, inner_ref, xs, gs, x_sem, g_sem = refs[-6:]
    else:
        a_out, x_out, inner_ref, xs, gs, outs, x_sem, g_sem, a_sem, out_sem = refs[-10:]
    copies = []
    for h, (p, lane) in enumerate(found):
        to = lanes_of(h * HDIM, HDIM)
        there = lanes_of(first + h * HDIM, HDIM)
        far = pltpu.make_async_copy(refs[p].at[: t_ref.shape[1], lane : lane + HDIM], xs.at[to], x_sem.at[h])
        near = pltpu.make_async_copy(own_ref.at[(0, 0) + there], xs.at[to], x_sem.at[h])
        g = pltpu.make_async_copy(g_ref.at[(0,) + there], gs.at[to], g_sem.at[h])
        pl.when(evicted)(far.start)
        pl.when(jnp.logical_not(evicted))(near.start)
        g.start()
        copies.append((far, near, g))
    factor = column_of(inverse_rms(total_of(evicted_ref, t_ref, held_ref), width_all))
    part = None
    sent = []
    for h in range(heads):
        far, near, copy = copies[h]
        pl.when(evicted)(far.wait)
        pl.when(jnp.logical_not(evicted))(near.wait)
        copy.wait()
        mine = lanes_of(h * HDIM, HDIM)
        there = lanes_of(first + h * HDIM, HDIM)
        g = gs[mine]
        wide, d_normed = backward_head(xs[mine], g, factor, gq_ref[there], gk_ref[there])
        term = g.astype(F32) + factor * d_normed
        if ahead:
            outs[mine] = term.astype(BF16)
            outs[lanes_of((heads + h) * HDIM, HDIM)] = xs[mine]
        else:
            outs[mine] = term
            to = lanes_of(first - base + h * HDIM, HDIM)
            sent.append(pltpu.make_async_copy(outs.at[mine], a_out.at[to], a_sem.at[h]))
            sent.append(pltpu.make_async_copy(xs.at[mine], x_out.at[to], out_sem.at[h]))
            for copy in sent[-2:]:
                copy.start()
        product = d_normed * wide
        part = product if part is None else part + product
    inner_ref[...] = jnp.sum(part.T, axis=0, keepdims=True) + past_ref[...]
    for copy in sent:
        copy.wait()


def total_of(evicted_ref, t_ref, held_ref):
    return jnp.where(evicted_ref[0] == 1, held_ref[...], t_ref[1:2, :])


def backward(
    width_all, evicted, stash, g, totals, held, gain_q, gain_k, past, far, found, first, base, sofar=(), after=()
):
    tokens, width = totals.shape[1], gain_q.shape[1]
    heads = len(found)
    small = (tokens, heads * HDIM)
    dma = pltpu.SemaphoreType.DMA((heads,))
    inner = jax.ShapeDtypeStruct((1, tokens), F32)
    if first < base:
        shapes = (jax.ShapeDtypeStruct((tokens, 2 * heads * HDIM), BF16), inner)
        scratch = [pltpu.VMEM(small, BF16)] * 2 + [dma] * 2
    else:
        shapes = (pltpu.HBM((tokens, width - base), F32), pltpu.HBM((tokens, width - base), BF16), inner)
        scratch = [pltpu.VMEM(small, BF16)] * 2 + [pltpu.VMEM(small, F32)] + [dma] * 4
    return pl.pallas_call(
        functools.partial(backward_kernel, first, base, found, width_all),
        out_shape=shapes,
        in_specs=[pl.BlockSpec(memory_space=pltpu.SMEM)] + [ANYWHERE] * 2 + [IN_VMEM] * 5
        + [ANYWHERE] * len(far) + [IN_HBM] * len(sofar) + [ANYWHERE] * len(after),
        out_specs=(IN_VMEM,) * 2 if first < base else (IN_HBM, IN_HBM, IN_VMEM),
        input_output_aliases={8 + len(far): 0, 9 + len(far): 1} if sofar else {},
        scratch_shapes=scratch,
        compiler_params=compiler(VMEM),
        name="backward",
    )(evicted, in_hbm(stash), in_hbm(g), totals, held, gain_q, gain_k, past, *far, *sofar, *after)


def row_of(total, inner, width_all):
    return inverse_rms(total, width_all) ** 3 * inner / width_all


def finish_kernel(width_all, evicted_ref, a_ref, x_ref, t_ref, held_ref, inner_ref, o_ref, row_ref):
    row = row_of(total_of(evicted_ref, t_ref, held_ref), inner_ref[...], width_all)
    row_ref[...] = row
    o_ref[...] = (a_ref[...] - x_ref[...].astype(F32) * column_of(row)).astype(BF16)


def finish(width_all, evicted, a, x, totals, held, inner, first, last):
    tokens = a.shape[0]
    lanes = HDIM
    block = pl.BlockSpec((tokens, lanes), lambda i: (0, first // lanes + i))
    return pl.pallas_call(
        functools.partial(finish_kernel, width_all),
        out_shape=(jax.ShapeDtypeStruct((tokens, last - first), BF16), jax.ShapeDtypeStruct((1, tokens), F32)),
        grid=((last - first) // lanes,),
        in_specs=[pl.BlockSpec(memory_space=pltpu.SMEM), block, block] + [IN_VMEM] * 3,
        out_specs=(pl.BlockSpec((tokens, lanes), lambda i: (0, i)), pl.BlockSpec((1, tokens), lambda i: (0, 0))),
        compiler_params=compiler(VMEM),
        name="finish",
    )(evicted, in_hbm(a), in_hbm(x), totals, held, inner)


def place_kernel(pair_ref, row_ref, *refs):
    rest_refs, (o_ref, outs, sems) = refs[:-3], refs[-3:]
    lanes = outs.shape[1]
    ahead = lanes // HDIM
    copies, at = [], lanes
    for i, ref in enumerate(rest_refs):
        copies.append(pltpu.make_async_copy(ref, o_ref.at[lanes_of(at, ref.shape[1])], sems.at[ahead + i]))
        copies[-1].start()
        at += ref.shape[1]
    row = column_of(row_ref[...])
    for h in range(ahead):
        mine = lanes_of(h * HDIM, HDIM)
        x = pair_ref[lanes_of(lanes + h * HDIM, HDIM)]
        outs[mine] = (pair_ref[mine].astype(F32) - x.astype(F32) * row).astype(BF16)
        copies.append(pltpu.make_async_copy(outs.at[mine], o_ref.at[mine], sems.at[h]))
        copies[-1].start()
    for copy in copies:
        copy.wait()


def place(pair, row, *rest):
    tokens, lanes = pair.shape[0], pair.shape[1] // 2
    return pl.pallas_call(
        place_kernel,
        out_shape=jax.ShapeDtypeStruct((tokens, lanes + sum(r.shape[1] for r in rest)), BF16),
        in_specs=[IN_VMEM] * (2 + len(rest)),
        out_specs=ANYWHERE,
        scratch_shapes=[pltpu.VMEM((tokens, lanes), BF16), pltpu.SemaphoreType.DMA((lanes // HDIM + len(rest),))],
        compiler_params=compiler(VMEM),
        name="place",
    )(pair, row, *rest)


def hold_kernel(x_ref, *rest):
    pass


def hold(x, after):
    return pl.pallas_call(
        hold_kernel,
        out_shape=jax.ShapeDtypeStruct(x.shape, x.dtype),
        in_specs=[IN_VMEM] + [ANYWHERE] * len(after),
        out_specs=IN_VMEM,
        input_output_aliases={0: 0},
        compiler_params=compiler(VMEM),
        name="hold",
    )(x, *after)


def squares_kernel(current_ref, stash_ref, *rest):
    rows_ref, sums = rest[-2:]
    step = pl.program_id(0)

    def total(x):
        wide = x.astype(F32)
        square = wide * wide
        return sum(square[:, i : i + HDIM] for i in range(0, square.shape[1], HDIM))

    for i, x in enumerate((current_ref[...], stash_ref[0], stash_ref[1])):
        part = total(x)

        @pl.when(step == 0)
        def _():
            sums[i] = part

        @pl.when(step > 0)
        def _():
            sums[i] += part

    @pl.when(step == pl.num_programs(0) - 1)
    def _():
        for i in range(3):
            rows_ref[i : i + 1, :] = jnp.sum(sums[i].T, axis=0, keepdims=True)


def squares(current, stash, lanes, after=()):
    tokens, width = current.shape
    return pl.pallas_call(
        squares_kernel,
        out_shape=jax.ShapeDtypeStruct((3, tokens), F32),
        grid=(width // lanes,),
        in_specs=[
            pl.BlockSpec((tokens, lanes), lambda i: (0, i)),
            pl.BlockSpec((None, 2, tokens, lanes), lambda i: (0, 0, 0, i)),
        ] + [ANYWHERE] * len(after),
        out_specs=pl.BlockSpec((3, tokens), lambda i: (0, 0)),
        scratch_shapes=[pltpu.VMEM((3, tokens, HDIM), F32)],
        compiler_params=compiler(MOST),
        name="squares",
    )(in_hbm(current), in_hbm(stash), *after)


def piece_kernel(starts, sizes, stash_ref, *rest):
    outs, mark, sems = rest[-2 - len(sizes) : -2], rest[-2], rest[-1]
    mark[...] = jnp.zeros_like(mark)
    copies = [
        pltpu.make_async_copy(stash_ref.at[(0, 1) + lanes_of(start, size)], out, sems.at[i])
        for i, (start, size, out) in enumerate(zip(starts, sizes, outs))
    ]
    for copy in copies:
        copy.start()
    for copy in copies:
        copy.wait()


def pieces_of(stash, starts, sizes, after=()):
    tokens = stash.shape[2]
    return pl.pallas_call(
        functools.partial(piece_kernel, starts, sizes),
        out_shape=[jax.ShapeDtypeStruct((tokens, size), BF16) for size in sizes] + [jax.ShapeDtypeStruct((8, HDIM), F32)],
        in_specs=[IN_HBM] + [ANYWHERE] * len(after),
        out_specs=[IN_VMEM] * (len(sizes) + 1),
        scratch_shapes=[pltpu.SemaphoreType.DMA((len(sizes),))],
        compiler_params=compiler(VMEM),
        name="pieces",
    )(in_hbm(stash), *after)


def in_rows(row, size):
    tokens = row.shape[1]
    rows = []
    for _ in range(3):
        term = row.astype(BF16)
        row = row - term.astype(F32)
        rows += [term[:, i : i + size] for i in range(0, tokens, size)]
    fill = -len(rows) % 16
    return jnp.concatenate(rows + [jnp.zeros((fill, size), BF16)] * (fill > 0), axis=0)


def row_kernel(extra_ref, o_ref):
    tokens, size = o_ref.shape[1], extra_ref.shape[1]
    each = tokens // size
    extra = extra_ref[...].astype(F32)
    for i in range(each):
        o_ref[:, i * size : (i + 1) * size] = sum(extra[p * each + i : p * each + i + 1] for p in range(3))


def row_from(piece, tokens):
    extra = piece.shape[0] - tokens
    size = piece.shape[1]
    return pl.pallas_call(
        row_kernel,
        out_shape=jax.ShapeDtypeStruct((1, tokens), F32),
        grid=(1,),
        in_specs=[pl.BlockSpec((extra, size), lambda i: (tokens // extra, 0))],
        out_specs=pl.BlockSpec((1, tokens), lambda i: (0, 0)),
        compiler_params=compiler(VMEM),
        name="row",
    )(piece)


def piece_and_row_kernel(start, stash_ref, t_ref, *rest):
    out, sem = rest[-2:]
    tokens, size = stash_ref.shape[2], out.shape[1]
    copy = pltpu.make_async_copy(stash_ref.at[(0, 1) + lanes_of(start, size)], out.at[:tokens, :], sem.at[0])
    copy.start()
    out[tokens:, :] = in_rows(t_ref[2:3, :], size)
    copy.wait()


def piece_and_row(stash, totals, start, size, after):
    tokens = stash.shape[2]
    extra = -(-3 * tokens // size // 16) * 16
    return pl.pallas_call(
        functools.partial(piece_and_row_kernel, start),
        out_shape=jax.ShapeDtypeStruct((tokens + extra, size), BF16),
        in_specs=[IN_HBM, IN_VMEM] + [ANYWHERE] * len(after),
        out_specs=IN_VMEM,
        scratch_shapes=[pltpu.SemaphoreType.DMA((1,))],
        compiler_params=compiler(VMEM),
        name="piece_and_row",
    )(in_hbm(stash), totals, *after)


def send(x, pairs):
    return lax.ppermute(x, "section", pairs)


def local(width_all, layer_input, grad_input, stashed, eviction, query_gain, key_gain):
    n = lax.axis_size("section")
    partner = [(s, (s + n // 2) % n) for s in range(n)]
    prior = [(s, (s - 1) % n) for s in range(n)]
    current = layer_input[0]
    tokens, width = current.shape
    count = width // HDIM
    each = max(1, count // 6)
    pieces = count // each
    size = each * HDIM
    third = count // 3 * HDIM

    *away, mark = pieces_of(stashed, (0, size), (size, size))
    fetched = [send(x, partner) for x in away]
    totals = lax.psum(squares(current, stashed, third, (mark,)), "tensor")
    output = forward(width_all, current, totals, query_gain, key_gain, third // HDIM)

    def fetch(p, after):
        away, mark = pieces_of(stashed, (p * size,), (size,), (fetched[p - 2], after))
        fetched.append(send(away, partner))
        return mark

    fetched.append(send(piece_and_row(stashed, totals, 2 * size, size, (fetched[0],)), partner))
    held = row_from(fetched[2], tokens)
    marks = [fetch(p, in_hbm(output)) for p in range(3, min(5, pieces))]
    base = max(1, count // 4) * HDIM

    def share(inner, first, last, sofar, after):
        heads = range(first // HDIM, last // HDIM)
        used = sorted({h // each for h in heads})
        found = tuple((used.index(h // each), h % each * HDIM) for h in heads)
        return backward(
            width_all, eviction, stashed, grad_input, totals, held, query_gain, key_gain, inner,
            [fetched[p] for p in used], found, first, base, sofar, after,
        )

    pair, inner = share(jnp.zeros((1, tokens), F32), 0, base, (), (in_hbm(output), *marks))
    marks = [fetch(p, inner) for p in range(len(fetched), pieces)]
    sofar, inners = (), [inner]
    ends = [base, width - 2 * size, width - size, width]
    for first, last in zip(ends[:-1], ends[1:]):
        if first < last:
            *sofar, inner = share(inner, first, last, tuple(sofar), tuple(marks))
            inners.append(inner)
            marks = []
    pair = send(hold(pair, (*fetched[-2:], inners[-2])), prior)
    inner = lax.psum(inner, "tensor")
    left = width - base
    cut = (left // HDIM + 1) // 2 * HDIM
    ends = (*sofar, totals, held, inner)
    early, row = finish(width_all, eviction, *ends, 0, cut)
    early = send(early, prior)
    late, _ = finish(width_all, eviction, *ends, cut, left)
    result = place(pair, send(row, prior), early, send(late, prior))
    return (output[None], result[None])


def solution(mesh):
    placed = (
        P("section", None, "tensor"),
        P("section", None, "tensor"),
        P("section", None, None, "tensor"),
        P("section"),
        P("section", "tensor"),
        P("section", "tensor"),
    )

    def whole(layer_input, *others):
        return jax.shard_map(
            functools.partial(local, layer_input.shape[-1]),
            mesh=mesh,
            in_specs=placed,
            out_specs=(P("section", None, "tensor"), P("section", None, "tensor")),
            check_vma=False,
        )(layer_input, *others)

    return whole
```

```python
import functools
import math

import jax
import jax.numpy as jnp
from jax import lax
from jax.experimental import pallas as pl
from jax.experimental.pallas import tpu as pltpu
from jax.sharding import PartitionSpec as P

HDIM = 128
EPSILON = 1e-05
SCALE = 1.0 / math.sqrt(HDIM)
LOG2E = math.log2(math.e)
VMEM = 32 * 1024 * 1024
MOST = 60 * 1024 * 1024

F32 = jnp.float32
BF16 = jnp.bfloat16


def dot(a, b, contract):
    return lax.dot_general(a, b, ((contract[0], contract[1]), ((), ())), preferred_element_type=F32)


def nt(a, b):
    return dot(a, b, ((1,), (1,)))


def nn(a, b):
    return dot(a, b, ((1,), (0,)))


def block_of(tokens):
    return 256 if tokens % 256 == 0 else tokens


def masked(block, kept):
    return jnp.where(kept, block, -1e30)


def kept_keys(size):
    keys = lax.broadcasted_iota(jnp.int32, (size, size), 0)
    return keys <= lax.broadcasted_iota(jnp.int32, (size, size), 1)


def scores_of(keys, queries, j, size, kept):
    mine = queries[j * size : (j + 1) * size]
    diagonal = masked(nt(keys[j * size : (j + 1) * size], mine), kept)
    if j == 0:
        return [diagonal]
    return [nt(keys[: j * size], mine), diagonal]


def exponents(parts):
    top = functools.reduce(jnp.maximum, [jnp.max(p, axis=0, keepdims=True) for p in parts])
    exps = [jnp.exp2((p - top) * (SCALE * LOG2E)) for p in parts]
    total = sum(jnp.sum(e, axis=0, keepdims=True) for e in exps)
    return exps, total


def stacked(parts):
    return parts[0] if len(parts) == 1 else jnp.concatenate(parts, axis=0)


def normed_head(x, factor, gain_q, gain_k):
    wide = x.astype(F32)
    normed = wide * factor
    return wide, (normed * gain_q).astype(BF16), (normed * gain_k).astype(BF16), normed.astype(BF16)


def column_of(row):
    return jnp.broadcast_to(row, (HDIM, row.shape[1])).T[:, 0:1]


def inverse_rms(total, width_all):
    return lax.rsqrt(total / width_all + EPSILON)


def lanes_of(start, size):
    return (slice(None), slice(start, start + size))


def compiler(limit):
    return pltpu.CompilerParams(vmem_limit_bytes=limit)


IN_VMEM = pl.BlockSpec(memory_space=pltpu.VMEM)
ANYWHERE = pl.BlockSpec(memory_space=pl.ANY)
IN_HBM = pl.BlockSpec(memory_space=pltpu.HBM)


def in_hbm(x):
    return pltpu.with_memory_space_constraint(x, pltpu.HBM)


def forward_kernel(heads, width_all, x_ref, t_ref, gq_ref, gk_ref, *rest):
    o_ref = rest[-1]
    tokens = x_ref.shape[0]
    size = block_of(tokens)
    kept = kept_keys(size)
    factor = column_of(inverse_rms(t_ref[0:1, :], width_all))
    for h in range(heads):
        lanes = slice(h * HDIM, (h + 1) * HDIM)
        wide, q, k, v = normed_head(x_ref[:, lanes], factor, gq_ref[:, lanes], gk_ref[:, lanes])
        vt = v.T
        for j in range(tokens // size):
            exps, total = exponents(scores_of(k, q, j, size, kept))
            mixed = nn(vt[:, : (j + 1) * size], stacked(exps).astype(BF16)) * (1.0 / total)
            rows = slice(j * size, (j + 1) * size)
            o_ref[rows, lanes] = (wide[rows] + mixed.T).astype(BF16)


def forward(width_all, x, totals, gain_q, gain_k, heads, after=()):
    tokens, width = x.shape
    lanes = heads * HDIM
    block = pl.BlockSpec((tokens, lanes), lambda i: (0, i))
    gain = pl.BlockSpec((1, lanes), lambda i: (0, i))
    return pl.pallas_call(
        functools.partial(forward_kernel, heads, width_all),
        out_shape=jax.ShapeDtypeStruct(x.shape, BF16),
        grid=(width // lanes,),
        in_specs=[block, pl.BlockSpec(totals.shape, lambda i: (0, 0)), gain, gain] + [IN_HBM] * len(after),
        out_specs=block,
        compiler_params=compiler(VMEM),
        name="forward",
    )(in_hbm(x), totals, gain_q, gain_k, *map(in_hbm, after))


def backward_head(x, g, factor, gain_q, gain_k):
    tokens = x.shape[0]
    size = block_of(tokens)
    kept = kept_keys(size)
    wide, q, k, v = normed_head(x, factor, gain_q, gain_k)
    kt = k.T
    blocks = tokens // size
    d_q = []
    d_k = [None] * blocks
    d_v = [None] * blocks
    for j in range(blocks):
        rows = slice(j * size, (j + 1) * size)
        exps, total = exponents(scores_of(k, q, j, size, kept))
        inverse = 1.0 / total
        weights = [e * inverse for e in exps]
        grads = [nt(v[: j * size], g[rows])] if j else []
        grads.append(nt(v[rows], g[rows]))
        delta = sum(jnp.sum(w * d, axis=0, keepdims=True) for w, d in zip(weights, grads))
        scores = stacked([(w * ((d - delta) * SCALE)).astype(BF16) for w, d in zip(weights, grads)])
        rounded = stacked([w.astype(BF16) for w in weights])
        d_q.append(nn(kt[:, : (j + 1) * size], scores).T)
        part_k = nn(scores, q[rows])
        part_v = nn(rounded, g[rows])
        for i in range(j + 1):
            mine = slice(i * size, (i + 1) * size)
            d_k[i] = part_k[mine] if d_k[i] is None else d_k[i] + part_k[mine]
            d_v[i] = part_v[mine] if d_v[i] is None else d_v[i] + part_v[mine]
    d_normed = stacked(d_q) * gain_q + stacked(d_k) * gain_k + stacked(d_v)
    return wide, d_normed


def backward_kernel(
    first, base, found, width_all, evicted_ref, own_ref, g_ref, t_ref, held_ref, gq_ref, gk_ref, past_ref, *refs
):
    evicted = evicted_ref[0] == 1
    heads = len(found)
    ahead = first < base
    if ahead:
        outs, inner_ref, xs, gs, x_sem, g_sem = refs[-6:]
    else:
        a_out, x_out, inner_ref, xs, gs, outs, x_sem, g_sem, a_sem, out_sem = refs[-10:]
    copies = []
    for h, (p, lane) in enumerate(found):
        to = lanes_of(h * HDIM, HDIM)
        there = lanes_of(first + h * HDIM, HDIM)
        far = pltpu.make_async_copy(refs[p].at[: t_ref.shape[1], lane : lane + HDIM], xs.at[to], x_sem.at[h])
        near = pltpu.make_async_copy(own_ref.at[(0, 0) + there], xs.at[to], x_sem.at[h])
        g = pltpu.make_async_copy(g_ref.at[(0,) + there], gs.at[to], g_sem.at[h])
        pl.when(evicted)(far.start)
        pl.when(jnp.logical_not(evicted))(near.start)
        g.start()
        copies.append((far, near, g))
    factor = column_of(inverse_rms(total_of(evicted_ref, t_ref, held_ref), width_all))
    part = None
    sent = []
    for h in range(heads):
        far, near, copy = copies[h]
        pl.when(evicted)(far.wait)
        pl.when(jnp.logical_not(evicted))(near.wait)
        copy.wait()
        mine = lanes_of(h * HDIM, HDIM)
        there = lanes_of(first + h * HDIM, HDIM)
        g = gs[mine]
        wide, d_normed = backward_head(xs[mine], g, factor, gq_ref[there], gk_ref[there])
        term = g.astype(F32) + factor * d_normed
        if ahead:
            outs[mine] = term.astype(BF16)
            outs[lanes_of((heads + h) * HDIM, HDIM)] = xs[mine]
        else:
            outs[mine] = term
            to = lanes_of(first - base + h * HDIM, HDIM)
            sent.append(pltpu.make_async_copy(outs.at[mine], a_out.at[to], a_sem.at[h]))
            sent.append(pltpu.make_async_copy(xs.at[mine], x_out.at[to], out_sem.at[h]))
            for copy in sent[-2:]:
                copy.start()
        product = d_normed * wide
        part = product if part is None else part + product
    inner_ref[...] = jnp.sum(part.T, axis=0, keepdims=True) + past_ref[...]
    for copy in sent:
        copy.wait()


def total_of(evicted_ref, t_ref, held_ref):
    return jnp.where(evicted_ref[0] == 1, held_ref[...], t_ref[1:2, :])


def backward(
    width_all, evicted, stash, g, totals, held, gain_q, gain_k, past, far, found, first, base, sofar=(), after=()
):
    tokens, width = totals.shape[1], gain_q.shape[1]
    heads = len(found)
    small = (tokens, heads * HDIM)
    dma = pltpu.SemaphoreType.DMA((heads,))
    inner = jax.ShapeDtypeStruct((1, tokens), F32)
    if first < base:
        shapes = (jax.ShapeDtypeStruct((tokens, 2 * heads * HDIM), BF16), inner)
        scratch = [pltpu.VMEM(small, BF16)] * 2 + [dma] * 2
    else:
        shapes = (pltpu.HBM((tokens, width - base), F32), pltpu.HBM((tokens, width - base), BF16), inner)
        scratch = [pltpu.VMEM(small, BF16)] * 2 + [pltpu.VMEM(small, F32)] + [dma] * 4
    return pl.pallas_call(
        functools.partial(backward_kernel, first, base, found, width_all),
        out_shape=shapes,
        in_specs=[pl.BlockSpec(memory_space=pltpu.SMEM)] + [ANYWHERE] * 2 + [IN_VMEM] * 5
        + [ANYWHERE] * len(far) + [IN_HBM] * len(sofar) + [ANYWHERE] * len(after),
        out_specs=(IN_VMEM,) * 2 if first < base else (IN_HBM, IN_HBM, IN_VMEM),
        input_output_aliases={8 + len(far): 0, 9 + len(far): 1} if sofar else {},
        scratch_shapes=scratch,
        compiler_params=compiler(VMEM),
        name="backward",
    )(evicted, in_hbm(stash), in_hbm(g), totals, held, gain_q, gain_k, past, *far, *sofar, *after)


def row_of(total, inner, width_all):
    return inverse_rms(total, width_all) ** 3 * inner / width_all


def finish_kernel(
    first, width_all, evicted_ref, a_ref, x_ref, t_ref, held_ref, inner_ref, o_ref, row_ref, terms, xs, a_sem, x_sem
):
    heads = o_ref.shape[1] // HDIM
    copies = []
    for h in range(heads):
        mine = lanes_of(h * HDIM, HDIM)
        there = lanes_of(first + h * HDIM, HDIM)
        copies.append(
            (
                pltpu.make_async_copy(a_ref.at[there], terms.at[mine], a_sem.at[h]),
                pltpu.make_async_copy(x_ref.at[there], xs.at[mine], x_sem.at[h]),
            )
        )
        for copy in copies[-1]:
            copy.start()
    row = row_of(total_of(evicted_ref, t_ref, held_ref), inner_ref[...], width_all)
    row_ref[...] = row
    column = column_of(row)
    for h in range(heads):
        mine = lanes_of(h * HDIM, HDIM)
        for copy in copies[h]:
            copy.wait()
        o_ref[mine] = (terms[mine] - xs[mine].astype(F32) * column).astype(BF16)


def finish(width_all, evicted, a, x, totals, held, inner, first, last):
    shape = (a.shape[0], last - first)
    dma = pltpu.SemaphoreType.DMA(((last - first) // HDIM,))
    return pl.pallas_call(
        functools.partial(finish_kernel, first, width_all),
        out_shape=(jax.ShapeDtypeStruct(shape, BF16), jax.ShapeDtypeStruct((1, a.shape[0]), F32)),
        in_specs=[pl.BlockSpec(memory_space=pltpu.SMEM)] + [IN_HBM] * 2 + [IN_VMEM] * 3,
        out_specs=(IN_VMEM, IN_VMEM),
        scratch_shapes=[pltpu.VMEM(shape, F32), pltpu.VMEM(shape, BF16), dma, dma],
        compiler_params=compiler(VMEM),
        name="finish",
    )(evicted, in_hbm(a), in_hbm(x), totals, held, inner)


def place_kernel(pair_ref, row_ref, *refs):
    rest_refs, (o_ref, outs, sems) = refs[:-3], refs[-3:]
    lanes = outs.shape[1]
    ahead = lanes // HDIM
    copies, at = [], lanes
    for i, ref in enumerate(rest_refs):
        copies.append(pltpu.make_async_copy(ref, o_ref.at[lanes_of(at, ref.shape[1])], sems.at[ahead + i]))
        copies[-1].start()
        at += ref.shape[1]
    row = column_of(row_ref[...])
    for h in range(ahead):
        mine = lanes_of(h * HDIM, HDIM)
        x = pair_ref[lanes_of(lanes + h * HDIM, HDIM)]
        outs[mine] = (pair_ref[mine].astype(F32) - x.astype(F32) * row).astype(BF16)
        copies.append(pltpu.make_async_copy(outs.at[mine], o_ref.at[mine], sems.at[h]))
        copies[-1].start()
    for copy in copies:
        copy.wait()


def place(pair, row, *rest):
    tokens, lanes = pair.shape[0], pair.shape[1] // 2
    return pl.pallas_call(
        place_kernel,
        out_shape=jax.ShapeDtypeStruct((tokens, lanes + sum(r.shape[1] for r in rest)), BF16),
        in_specs=[IN_VMEM] * (2 + len(rest)),
        out_specs=ANYWHERE,
        scratch_shapes=[pltpu.VMEM((tokens, lanes), BF16), pltpu.SemaphoreType.DMA((lanes // HDIM + len(rest),))],
        compiler_params=compiler(VMEM),
        name="place",
    )(pair, row, *rest)


def hold_kernel(x_ref, *rest):
    pass


def hold(x, after):
    return pl.pallas_call(
        hold_kernel,
        out_shape=jax.ShapeDtypeStruct(x.shape, x.dtype),
        in_specs=[IN_VMEM] + [ANYWHERE] * len(after),
        out_specs=IN_VMEM,
        input_output_aliases={0: 0},
        compiler_params=compiler(VMEM),
        name="hold",
    )(x, *after)


def squares_kernel(current_ref, stash_ref, *rest):
    rows_ref, sums = rest[-2:]
    step = pl.program_id(0)

    def total(x):
        wide = x.astype(F32)
        square = wide * wide
        return sum(square[:, i : i + HDIM] for i in range(0, square.shape[1], HDIM))

    for i, x in enumerate((current_ref[...], stash_ref[0], stash_ref[1])):
        part = total(x)

        @pl.when(step == 0)
        def _():
            sums[i] = part

        @pl.when(step > 0)
        def _():
            sums[i] += part

    @pl.when(step == pl.num_programs(0) - 1)
    def _():
        for i in range(3):
            rows_ref[i : i + 1, :] = jnp.sum(sums[i].T, axis=0, keepdims=True)


def squares(current, stash, lanes, after=()):
    tokens, width = current.shape
    return pl.pallas_call(
        squares_kernel,
        out_shape=jax.ShapeDtypeStruct((3, tokens), F32),
        grid=(width // lanes,),
        in_specs=[
            pl.BlockSpec((tokens, lanes), lambda i: (0, i)),
            pl.BlockSpec((None, 2, tokens, lanes), lambda i: (0, 0, 0, i)),
        ] + [ANYWHERE] * len(after),
        out_specs=pl.BlockSpec((3, tokens), lambda i: (0, 0)),
        scratch_shapes=[pltpu.VMEM((3, tokens, HDIM), F32)],
        compiler_params=compiler(MOST),
        name="squares",
    )(in_hbm(current), in_hbm(stash), *after)


def piece_kernel(starts, sizes, stash_ref, *rest):
    outs, mark, sems = rest[-2 - len(sizes) : -2], rest[-2], rest[-1]
    mark[...] = jnp.zeros_like(mark)
    copies = [
        pltpu.make_async_copy(stash_ref.at[(0, 1) + lanes_of(start, size)], out, sems.at[i])
        for i, (start, size, out) in enumerate(zip(starts, sizes, outs))
    ]
    for copy in copies:
        copy.start()
    for copy in copies:
        copy.wait()


def pieces_of(stash, starts, sizes, after=()):
    tokens = stash.shape[2]
    return pl.pallas_call(
        functools.partial(piece_kernel, starts, sizes),
        out_shape=[jax.ShapeDtypeStruct((tokens, size), BF16) for size in sizes] + [jax.ShapeDtypeStruct((8, HDIM), F32)],
        in_specs=[IN_HBM] + [ANYWHERE] * len(after),
        out_specs=[IN_VMEM] * (len(sizes) + 1),
        scratch_shapes=[pltpu.SemaphoreType.DMA((len(sizes),))],
        compiler_params=compiler(VMEM),
        name="pieces",
    )(in_hbm(stash), *after)


def in_rows(row, size):
    tokens = row.shape[1]
    rows = []
    for _ in range(3):
        term = row.astype(BF16)
        row = row - term.astype(F32)
        rows += [term[:, i : i + size] for i in range(0, tokens, size)]
    fill = -len(rows) % 16
    return jnp.concatenate(rows + [jnp.zeros((fill, size), BF16)] * (fill > 0), axis=0)


def row_kernel(extra_ref, o_ref):
    tokens, size = o_ref.shape[1], extra_ref.shape[1]
    each = tokens // size
    extra = extra_ref[...].astype(F32)
    for i in range(each):
        o_ref[:, i * size : (i + 1) * size] = sum(extra[p * each + i : p * each + i + 1] for p in range(3))


def row_from(piece, tokens):
    extra = piece.shape[0] - tokens
    size = piece.shape[1]
    return pl.pallas_call(
        row_kernel,
        out_shape=jax.ShapeDtypeStruct((1, tokens), F32),
        grid=(1,),
        in_specs=[pl.BlockSpec((extra, size), lambda i: (tokens // extra, 0))],
        out_specs=pl.BlockSpec((1, tokens), lambda i: (0, 0)),
        compiler_params=compiler(VMEM),
        name="row",
    )(piece)


def piece_and_row_kernel(start, stash_ref, t_ref, *rest):
    out, sem = rest[-2:]
    tokens, size = stash_ref.shape[2], out.shape[1]
    copy = pltpu.make_async_copy(stash_ref.at[(0, 1) + lanes_of(start, size)], out.at[:tokens, :], sem.at[0])
    copy.start()
    out[tokens:, :] = in_rows(t_ref[2:3, :], size)
    copy.wait()


def piece_and_row(stash, totals, start, size, after):
    tokens = stash.shape[2]
    extra = -(-3 * tokens // size // 16) * 16
    return pl.pallas_call(
        functools.partial(piece_and_row_kernel, start),
        out_shape=jax.ShapeDtypeStruct((tokens + extra, size), BF16),
        in_specs=[IN_HBM, IN_VMEM] + [ANYWHERE] * len(after),
        out_specs=IN_VMEM,
        scratch_shapes=[pltpu.SemaphoreType.DMA((1,))],
        compiler_params=compiler(VMEM),
        name="piece_and_row",
    )(in_hbm(stash), totals, *after)


def send(x, pairs):
    return lax.ppermute(x, "section", pairs)


def local(width_all, layer_input, grad_input, stashed, eviction, query_gain, key_gain):
    n = lax.axis_size("section")
    partner = [(s, (s + n // 2) % n) for s in range(n)]
    prior = [(s, (s - 1) % n) for s in range(n)]
    current = layer_input[0]
    tokens, width = current.shape
    count = width // HDIM
    each = max(1, count // 6)
    pieces = count // each
    size = each * HDIM
    third = count // 3 * HDIM

    *away, mark = pieces_of(stashed, (0, size), (size, size))
    fetched = [send(x, partner) for x in away]
    totals = lax.psum(squares(current, stashed, third, (mark,)), "tensor")
    output = forward(width_all, current, totals, query_gain, key_gain, third // HDIM)

    def fetch(p, after):
        away, mark = pieces_of(stashed, (p * size,), (size,), (fetched[p - 2], after))
        fetched.append(send(away, partner))
        return mark

    fetched.append(send(piece_and_row(stashed, totals, 2 * size, size, (fetched[0],)), partner))
    held = row_from(fetched[2], tokens)
    marks = [fetch(p, in_hbm(output)) for p in range(3, min(5, pieces))]
    base = max(1, count // 4) * HDIM

    def share(inner, first, last, sofar, after):
        heads = range(first // HDIM, last // HDIM)
        used = sorted({h // each for h in heads})
        found = tuple((used.index(h // each), h % each * HDIM) for h in heads)
        return backward(
            width_all, eviction, stashed, grad_input, totals, held, query_gain, key_gain, inner,
            [fetched[p] for p in used], found, first, base, sofar, after,
        )

    pair, inner = share(jnp.zeros((1, tokens), F32), 0, base, (), (in_hbm(output), *marks))
    marks = []
    sofar, inners = (), [inner]
    ends = sorted({base, max(base, 3 * size), *(p * size for p in range(4, pieces + 1))})
    for first, last in zip(ends[:-1], ends[1:]):
        *sofar, inner = share(inner, first, last, tuple(sofar), tuple(marks))
        inners.append(inner)
        marks = [fetch(p, inner) for p in range(len(fetched), pieces)]
    pair = send(hold(pair, (*fetched[-2:], inners[-2])), prior)
    inner = lax.psum(inner, "tensor")
    left = width - base
    cut = (left // HDIM + 1) // 2 * HDIM
    ends = (*sofar, totals, held, inner)
    early, row = finish(width_all, eviction, *ends, 0, cut)
    early = send(early, prior)
    late, _ = finish(width_all, eviction, *ends, cut, left)
    result = place(pair, send(row, prior), early, send(late, prior))
    return (output[None], result[None])


def solution(mesh):
    placed = (
        P("section", None, "tensor"),
        P("section", None, "tensor"),
        P("section", None, None, "tensor"),
        P("section"),
        P("section", "tensor"),
        P("section", "tensor"),
    )

    def whole(layer_input, *others):
        return jax.shard_map(
            functools.partial(local, layer_input.shape[-1]),
            mesh=mesh,
            in_specs=placed,
            out_specs=(P("section", None, "tensor"), P("section", None, "tensor")),
            check_vma=False,
        )(layer_input, *others)

    return whole
```

```python
import functools
import math

import jax
import jax.numpy as jnp
from jax import lax
from jax.experimental import pallas as pl
from jax.experimental.pallas import tpu as pltpu
from jax.sharding import PartitionSpec as P

HDIM = 128
EPSILON = 1e-05
SCALE = 1.0 / math.sqrt(HDIM)
LOG2E = math.log2(math.e)
VMEM = 32 * 1024 * 1024
MOST = 60 * 1024 * 1024

F32 = jnp.float32
BF16 = jnp.bfloat16


def dot(a, b, contract):
    return lax.dot_general(a, b, ((contract[0], contract[1]), ((), ())), preferred_element_type=F32)


def nt(a, b):
    return dot(a, b, ((1,), (1,)))


def nn(a, b):
    return dot(a, b, ((1,), (0,)))


def block_of(tokens):
    return 256 if tokens % 256 == 0 else tokens


def masked(block, kept):
    return jnp.where(kept, block, -1e30)


def kept_keys(size):
    keys = lax.broadcasted_iota(jnp.int32, (size, size), 0)
    return keys <= lax.broadcasted_iota(jnp.int32, (size, size), 1)


def scores_of(keys, queries, j, size, kept):
    mine = queries[j * size : (j + 1) * size]
    diagonal = masked(nt(keys[j * size : (j + 1) * size], mine), kept)
    if j == 0:
        return [diagonal]
    return [nt(keys[: j * size], mine), diagonal]


def exponents(parts):
    top = functools.reduce(jnp.maximum, [jnp.max(p, axis=0, keepdims=True) for p in parts])
    exps = [jnp.exp2((p - top) * (SCALE * LOG2E)) for p in parts]
    total = sum(jnp.sum(e, axis=0, keepdims=True) for e in exps)
    return exps, total


def stacked(parts):
    return parts[0] if len(parts) == 1 else jnp.concatenate(parts, axis=0)


def normed_head(x, factor, gain_q, gain_k):
    wide = x.astype(F32)
    normed = wide * factor
    return wide, (normed * gain_q).astype(BF16), (normed * gain_k).astype(BF16), normed.astype(BF16)


def column_of(row):
    return jnp.broadcast_to(row, (HDIM, row.shape[1])).T[:, 0:1]


def inverse_rms(total, width_all):
    return lax.rsqrt(total / width_all + EPSILON)


def lanes_of(start, size):
    return (slice(None), slice(start, start + size))


def compiler(limit):
    return pltpu.CompilerParams(vmem_limit_bytes=limit)


IN_VMEM = pl.BlockSpec(memory_space=pltpu.VMEM)
ANYWHERE = pl.BlockSpec(memory_space=pl.ANY)
IN_HBM = pl.BlockSpec(memory_space=pltpu.HBM)


def in_hbm(x):
    return pltpu.with_memory_space_constraint(x, pltpu.HBM)


def forward_kernel(heads, width_all, x_ref, t_ref, gq_ref, gk_ref, *rest):
    o_ref = rest[-1]
    tokens = x_ref.shape[0]
    size = block_of(tokens)
    kept = kept_keys(size)
    factor = column_of(inverse_rms(t_ref[0:1, :], width_all))
    for h in range(heads):
        lanes = slice(h * HDIM, (h + 1) * HDIM)
        wide, q, k, v = normed_head(x_ref[:, lanes], factor, gq_ref[:, lanes], gk_ref[:, lanes])
        vt = v.T
        for j in range(tokens // size):
            exps, total = exponents(scores_of(k, q, j, size, kept))
            mixed = nn(vt[:, : (j + 1) * size], stacked(exps).astype(BF16)) * (1.0 / total)
            rows = slice(j * size, (j + 1) * size)
            o_ref[rows, lanes] = (wide[rows] + mixed.T).astype(BF16)


def forward(width_all, x, totals, gain_q, gain_k, heads, after=()):
    tokens, width = x.shape
    lanes = heads * HDIM
    block = pl.BlockSpec((tokens, lanes), lambda i: (0, i))
    gain = pl.BlockSpec((1, lanes), lambda i: (0, i))
    return pl.pallas_call(
        functools.partial(forward_kernel, heads, width_all),
        out_shape=jax.ShapeDtypeStruct(x.shape, BF16),
        grid=(width // lanes,),
        in_specs=[block, pl.BlockSpec(totals.shape, lambda i: (0, 0)), gain, gain] + [IN_HBM] * len(after),
        out_specs=block,
        compiler_params=compiler(VMEM),
        name="forward",
    )(in_hbm(x), totals, gain_q, gain_k, *map(in_hbm, after))


def backward_head(x, g, factor, gain_q, gain_k):
    tokens = x.shape[0]
    size = block_of(tokens)
    kept = kept_keys(size)
    wide, q, k, v = normed_head(x, factor, gain_q, gain_k)
    kt = k.T
    blocks = tokens // size
    d_q = []
    d_k = [None] * blocks
    d_v = [None] * blocks
    for j in range(blocks):
        rows = slice(j * size, (j + 1) * size)
        exps, total = exponents(scores_of(k, q, j, size, kept))
        inverse = 1.0 / total
        weights = [e * inverse for e in exps]
        grads = [nt(v[: j * size], g[rows])] if j else []
        grads.append(nt(v[rows], g[rows]))
        delta = sum(jnp.sum(w * d, axis=0, keepdims=True) for w, d in zip(weights, grads))
        scores = stacked([(w * ((d - delta) * SCALE)).astype(BF16) for w, d in zip(weights, grads)])
        rounded = stacked([w.astype(BF16) for w in weights])
        d_q.append(nn(kt[:, : (j + 1) * size], scores).T)
        part_k = nn(scores, q[rows])
        part_v = nn(rounded, g[rows])
        for i in range(j + 1):
            mine = slice(i * size, (i + 1) * size)
            d_k[i] = part_k[mine] if d_k[i] is None else d_k[i] + part_k[mine]
            d_v[i] = part_v[mine] if d_v[i] is None else d_v[i] + part_v[mine]
    d_normed = stacked(d_q) * gain_q + stacked(d_k) * gain_k + stacked(d_v)
    return wide, d_normed


def backward_kernel(
    first, base, found, width_all, evicted_ref, own_ref, g_ref, t_ref, held_ref, gq_ref, gk_ref, past_ref, *refs
):
    evicted = evicted_ref[0] == 1
    heads = len(found)
    ahead = first < base
    if ahead:
        outs, inner_ref, xs, gs, x_sem, g_sem = refs[-6:]
    else:
        a_out, x_out, inner_ref, xs, gs, outs, x_sem, g_sem, a_sem, out_sem = refs[-10:]
    copies = []
    for h, (p, lane) in enumerate(found):
        to = lanes_of(h * HDIM, HDIM)
        there = lanes_of(first + h * HDIM, HDIM)
        far = pltpu.make_async_copy(refs[p].at[: t_ref.shape[1], lane : lane + HDIM], xs.at[to], x_sem.at[h])
        near = pltpu.make_async_copy(own_ref.at[(0, 0) + there], xs.at[to], x_sem.at[h])
        g = pltpu.make_async_copy(g_ref.at[(0,) + there], gs.at[to], g_sem.at[h])
        pl.when(evicted)(far.start)
        pl.when(jnp.logical_not(evicted))(near.start)
        g.start()
        copies.append((far, near, g))
    factor = column_of(inverse_rms(total_of(evicted_ref, t_ref, held_ref), width_all))
    part = None
    sent = []
    for h in range(heads):
        far, near, copy = copies[h]
        pl.when(evicted)(far.wait)
        pl.when(jnp.logical_not(evicted))(near.wait)
        copy.wait()
        mine = lanes_of(h * HDIM, HDIM)
        there = lanes_of(first + h * HDIM, HDIM)
        g = gs[mine]
        wide, d_normed = backward_head(xs[mine], g, factor, gq_ref[there], gk_ref[there])
        term = g.astype(F32) + factor * d_normed
        if ahead:
            outs[mine] = term.astype(BF16)
            outs[lanes_of((heads + h) * HDIM, HDIM)] = xs[mine]
        else:
            outs[mine] = term
            to = lanes_of(first - base + h * HDIM, HDIM)
            sent.append(pltpu.make_async_copy(outs.at[mine], a_out.at[to], a_sem.at[h]))
            sent.append(pltpu.make_async_copy(xs.at[mine], x_out.at[to], out_sem.at[h]))
            for copy in sent[-2:]:
                copy.start()
        product = d_normed * wide
        part = product if part is None else part + product
    inner_ref[...] = jnp.sum(part.T, axis=0, keepdims=True) + past_ref[...]
    for copy in sent:
        copy.wait()


def total_of(evicted_ref, t_ref, held_ref):
    return jnp.where(evicted_ref[0] == 1, held_ref[...], t_ref[1:2, :])


def backward(
    width_all, evicted, stash, g, totals, held, gain_q, gain_k, past, far, found, first, base, sofar=(), after=()
):
    tokens, width = totals.shape[1], gain_q.shape[1]
    heads = len(found)
    small = (tokens, heads * HDIM)
    dma = pltpu.SemaphoreType.DMA((heads,))
    inner = jax.ShapeDtypeStruct((1, tokens), F32)
    if first < base:
        shapes = (jax.ShapeDtypeStruct((tokens, 2 * heads * HDIM), BF16), inner)
        scratch = [pltpu.VMEM(small, BF16)] * 2 + [dma] * 2
    else:
        shapes = (pltpu.HBM((tokens, width - base), F32), pltpu.HBM((tokens, width - base), BF16), inner)
        scratch = [pltpu.VMEM(small, BF16)] * 2 + [pltpu.VMEM(small, F32)] + [dma] * 4
    return pl.pallas_call(
        functools.partial(backward_kernel, first, base, found, width_all),
        out_shape=shapes,
        in_specs=[pl.BlockSpec(memory_space=pltpu.SMEM)] + [ANYWHERE] * 2 + [IN_VMEM] * 5
        + [ANYWHERE] * len(far) + [IN_HBM] * len(sofar) + [ANYWHERE] * len(after),
        out_specs=(IN_VMEM,) * 2 if first < base else (IN_HBM, IN_HBM, IN_VMEM),
        input_output_aliases={8 + len(far): 0, 9 + len(far): 1} if sofar else {},
        scratch_shapes=scratch,
        compiler_params=compiler(VMEM),
        name="backward",
    )(evicted, in_hbm(stash), in_hbm(g), totals, held, gain_q, gain_k, past, *far, *sofar, *after)


def row_of(total, inner, width_all):
    return inverse_rms(total, width_all) ** 3 * inner / width_all


def finish_kernel(
    first, width_all, evicted_ref, a_ref, x_ref, t_ref, held_ref, inner_ref, o_ref, row_ref, terms, xs, a_sem, x_sem
):
    heads = o_ref.shape[1] // HDIM
    copies = []
    for h in range(heads):
        mine = lanes_of(h * HDIM, HDIM)
        there = lanes_of(first + h * HDIM, HDIM)
        copies.append(
            (
                pltpu.make_async_copy(a_ref.at[there], terms.at[mine], a_sem.at[h]),
                pltpu.make_async_copy(x_ref.at[there], xs.at[mine], x_sem.at[h]),
            )
        )
        for copy in copies[-1]:
            copy.start()
    row = row_of(total_of(evicted_ref, t_ref, held_ref), inner_ref[...], width_all)
    row_ref[...] = row
    column = column_of(row)
    for h in range(heads):
        mine = lanes_of(h * HDIM, HDIM)
        for copy in copies[h]:
            copy.wait()
        o_ref[mine] = (terms[mine] - xs[mine].astype(F32) * column).astype(BF16)


def finish(width_all, evicted, a, x, totals, held, inner, first, last):
    shape = (a.shape[0], last - first)
    dma = pltpu.SemaphoreType.DMA(((last - first) // HDIM,))
    return pl.pallas_call(
        functools.partial(finish_kernel, first, width_all),
        out_shape=(jax.ShapeDtypeStruct(shape, BF16), jax.ShapeDtypeStruct((1, a.shape[0]), F32)),
        in_specs=[pl.BlockSpec(memory_space=pltpu.SMEM)] + [IN_HBM] * 2 + [IN_VMEM] * 3,
        out_specs=(IN_VMEM, IN_VMEM),
        scratch_shapes=[pltpu.VMEM(shape, F32), pltpu.VMEM(shape, BF16), dma, dma],
        compiler_params=compiler(VMEM),
        name="finish",
    )(evicted, in_hbm(a), in_hbm(x), totals, held, inner)


def place_kernel(crossed_ref, far_ref, near_ref, row_ref, *refs):
    rest_refs, (o_ref, outs, sems) = refs[:-3], refs[-3:]
    lanes = outs.shape[1]
    ahead = lanes // HDIM
    copies, at = [], lanes
    for i, ref in enumerate(rest_refs):
        copies.append(pltpu.make_async_copy(ref, o_ref.at[lanes_of(at, ref.shape[1])], sems.at[ahead + i]))
        copies[-1].start()
        at += ref.shape[1]
    row = column_of(row_ref[...])
    for h in range(ahead):
        mine = lanes_of(h * HDIM, HDIM)
        term, x = (
            jnp.where(crossed_ref[0] == 1, far_ref[at], near_ref[at])
            for at in (mine, lanes_of(lanes + h * HDIM, HDIM))
        )
        outs[mine] = (term.astype(F32) - x.astype(F32) * row).astype(BF16)
        copies.append(pltpu.make_async_copy(outs.at[mine], o_ref.at[mine], sems.at[h]))
        copies[-1].start()
    for copy in copies:
        copy.wait()


def place(crossed, pairs, row, *rest):
    tokens, lanes = pairs[0].shape[0], pairs[0].shape[1] // 2
    return pl.pallas_call(
        place_kernel,
        out_shape=jax.ShapeDtypeStruct((tokens, lanes + sum(r.shape[1] for r in rest)), BF16),
        in_specs=[pl.BlockSpec(memory_space=pltpu.SMEM)] + [IN_VMEM] * (3 + len(rest)),
        out_specs=ANYWHERE,
        scratch_shapes=[pltpu.VMEM((tokens, lanes), BF16), pltpu.SemaphoreType.DMA((lanes // HDIM + len(rest),))],
        compiler_params=compiler(VMEM),
        name="place",
    )(crossed, *pairs, row, *rest)


def hold_kernel(x_ref, *rest):
    pass


def hold(x, after):
    return pl.pallas_call(
        hold_kernel,
        out_shape=jax.ShapeDtypeStruct(x.shape, x.dtype),
        in_specs=[IN_VMEM] + [ANYWHERE] * len(after),
        out_specs=IN_VMEM,
        input_output_aliases={0: 0},
        compiler_params=compiler(VMEM),
        name="hold",
    )(x, *after)


def squares_kernel(current_ref, stash_ref, *rest):
    rows_ref, sums = rest[-2:]
    step = pl.program_id(0)

    def total(x):
        wide = x.astype(F32)
        square = wide * wide
        return sum(square[:, i : i + HDIM] for i in range(0, square.shape[1], HDIM))

    for i, x in enumerate((current_ref[...], stash_ref[0], stash_ref[1])):
        part = total(x)

        @pl.when(step == 0)
        def _():
            sums[i] = part

        @pl.when(step > 0)
        def _():
            sums[i] += part

    @pl.when(step == pl.num_programs(0) - 1)
    def _():
        for i in range(3):
            rows_ref[i : i + 1, :] = jnp.sum(sums[i].T, axis=0, keepdims=True)


def squares(current, stash, lanes, after=()):
    tokens, width = current.shape
    return pl.pallas_call(
        squares_kernel,
        out_shape=jax.ShapeDtypeStruct((3, tokens), F32),
        grid=(width // lanes,),
        in_specs=[
            pl.BlockSpec((tokens, lanes), lambda i: (0, i)),
            pl.BlockSpec((None, 2, tokens, lanes), lambda i: (0, 0, 0, i)),
        ] + [ANYWHERE] * len(after),
        out_specs=pl.BlockSpec((3, tokens), lambda i: (0, 0)),
        scratch_shapes=[pltpu.VMEM((3, tokens, HDIM), F32)],
        compiler_params=compiler(MOST),
        name="squares",
    )(in_hbm(current), in_hbm(stash), *after)


def piece_kernel(starts, sizes, stash_ref, *rest):
    outs, mark, sems = rest[-2 - len(sizes) : -2], rest[-2], rest[-1]
    mark[...] = jnp.zeros_like(mark)
    copies = [
        pltpu.make_async_copy(stash_ref.at[(0, 1) + lanes_of(start, size)], out, sems.at[i])
        for i, (start, size, out) in enumerate(zip(starts, sizes, outs))
    ]
    for copy in copies:
        copy.start()
    for copy in copies:
        copy.wait()


def pieces_of(stash, starts, sizes, after=()):
    tokens = stash.shape[2]
    return pl.pallas_call(
        functools.partial(piece_kernel, starts, sizes),
        out_shape=[jax.ShapeDtypeStruct((tokens, size), BF16) for size in sizes] + [jax.ShapeDtypeStruct((8, HDIM), F32)],
        in_specs=[IN_HBM] + [ANYWHERE] * len(after),
        out_specs=[IN_VMEM] * (len(sizes) + 1),
        scratch_shapes=[pltpu.SemaphoreType.DMA((len(sizes),))],
        compiler_params=compiler(VMEM),
        name="pieces",
    )(in_hbm(stash), *after)


def in_rows(row, size):
    tokens = row.shape[1]
    rows = []
    for _ in range(3):
        term = row.astype(BF16)
        row = row - term.astype(F32)
        rows += [term[:, i : i + size] for i in range(0, tokens, size)]
    fill = -len(rows) % 16
    return jnp.concatenate(rows + [jnp.zeros((fill, size), BF16)] * (fill > 0), axis=0)


def row_kernel(extra_ref, o_ref):
    tokens, size = o_ref.shape[1], extra_ref.shape[1]
    each = tokens // size
    extra = extra_ref[...].astype(F32)
    for i in range(each):
        o_ref[:, i * size : (i + 1) * size] = sum(extra[p * each + i : p * each + i + 1] for p in range(3))


def row_from(piece, tokens):
    extra = piece.shape[0] - tokens
    size = piece.shape[1]
    return pl.pallas_call(
        row_kernel,
        out_shape=jax.ShapeDtypeStruct((1, tokens), F32),
        grid=(1,),
        in_specs=[pl.BlockSpec((extra, size), lambda i: (tokens // extra, 0))],
        out_specs=pl.BlockSpec((1, tokens), lambda i: (0, 0)),
        compiler_params=compiler(VMEM),
        name="row",
    )(piece)


def piece_and_row_kernel(start, stash_ref, t_ref, *rest):
    out, sem = rest[-2:]
    tokens, size = stash_ref.shape[2], out.shape[1]
    copy = pltpu.make_async_copy(stash_ref.at[(0, 1) + lanes_of(start, size)], out.at[:tokens, :], sem.at[0])
    copy.start()
    out[tokens:, :] = in_rows(t_ref[2:3, :], size)
    copy.wait()


def piece_and_row(stash, totals, start, size, after):
    tokens = stash.shape[2]
    extra = -(-3 * tokens // size // 16) * 16
    return pl.pallas_call(
        functools.partial(piece_and_row_kernel, start),
        out_shape=jax.ShapeDtypeStruct((tokens + extra, size), BF16),
        in_specs=[IN_HBM, IN_VMEM] + [ANYWHERE] * len(after),
        out_specs=IN_VMEM,
        scratch_shapes=[pltpu.SemaphoreType.DMA((1,))],
        compiler_params=compiler(VMEM),
        name="piece_and_row",
    )(in_hbm(stash), totals, *after)


def send(x, pairs):
    return lax.ppermute(x, "section", pairs)


def local(width_all, layer_input, grad_input, stashed, eviction, query_gain, key_gain):
    n = lax.axis_size("section")
    partner = [(s, (s + n // 2) % n) for s in range(n)]
    prior = [(s, (s - 1) % n) for s in range(n)]
    crossing = [(0, n - 1), (n // 2, n // 2 - 1)]
    me = lax.axis_index("section")
    crossed = jnp.logical_or(me == n - 1, me == n // 2 - 1).astype(jnp.int32)[None]
    current = layer_input[0]
    tokens, width = current.shape
    count = width // HDIM
    each = max(1, count // 6)
    pieces = count // each
    size = each * HDIM
    third = count // 3 * HDIM

    *away, mark = pieces_of(stashed, (0, size), (size, size))
    fetched = [send(x, partner) for x in away]
    totals = lax.psum(squares(current, stashed, third, (mark,)), "tensor")
    output = forward(width_all, current, totals, query_gain, key_gain, third // HDIM)

    def fetch(p, after):
        away, mark = pieces_of(stashed, (p * size,), (size,), (fetched[p - 2], after))
        fetched.append(send(away, partner))
        return mark

    fetched.append(send(piece_and_row(stashed, totals, 2 * size, size, (fetched[0],)), partner))
    held = row_from(fetched[2], tokens)
    marks = [fetch(p, in_hbm(output)) for p in range(3, min(5, pieces))]
    base = max(1, count // 4) * HDIM

    def share(inner, first, last, sofar, after):
        heads = range(first // HDIM, last // HDIM)
        used = sorted({h // each for h in heads})
        found = tuple((used.index(h // each), h % each * HDIM) for h in heads)
        return backward(
            width_all, eviction, stashed, grad_input, totals, held, query_gain, key_gain, inner,
            [fetched[p] for p in used], found, first, base, sofar, after,
        )

    pair, inner = share(jnp.zeros((1, tokens), F32), 0, base, (), (in_hbm(output), *marks))
    marks = []
    sofar, inners = (), [inner]
    ends = sorted({base, max(base, 3 * size), *(p * size for p in range(4, pieces + 1))})
    for first, last in zip(ends[:-1], ends[1:]):
        *sofar, inner = share(inner, first, last, tuple(sofar), tuple(marks))
        inners.append(inner)
        marks = [fetch(p, inner) for p in range(len(fetched), pieces)]
    pair = hold(pair, (*fetched[-2:], inners[-2]))
    pairs = [send(pair, crossing), send(pair, [p for p in prior if p not in crossing])]
    inner = lax.psum(inner, "tensor")
    left = width - base
    cut = (left // HDIM + 1) // 2 * HDIM
    ends = (*sofar, totals, held, inner)
    early, row = finish(width_all, eviction, *ends, 0, cut)
    early = send(early, prior)
    late, _ = finish(width_all, eviction, *ends, cut, left)
    result = place(crossed, pairs, send(row, prior), early, send(late, prior))
    return (output[None], result[None])


def solution(mesh):
    placed = (
        P("section", None, "tensor"),
        P("section", None, "tensor"),
        P("section", None, None, "tensor"),
        P("section"),
        P("section", "tensor"),
        P("section", "tensor"),
    )

    def whole(layer_input, *others):
        return jax.shard_map(
            functools.partial(local, layer_input.shape[-1]),
            mesh=mesh,
            in_specs=placed,
            out_specs=(P("section", None, "tensor"), P("section", None, "tensor")),
            check_vma=False,
        )(layer_input, *others)

    return whole
```

```python
import functools
import math

import jax
import jax.numpy as jnp
from jax import lax
from jax.experimental import pallas as pl
from jax.experimental.pallas import tpu as pltpu
from jax.sharding import PartitionSpec as P

HDIM = 128
EPSILON = 1e-05
SCALE = 1.0 / math.sqrt(HDIM)
LOG2E = math.log2(math.e)
VMEM = 32 * 1024 * 1024
MOST = 60 * 1024 * 1024

F32 = jnp.float32
BF16 = jnp.bfloat16


def dot(a, b, contract):
    return lax.dot_general(a, b, ((contract[0], contract[1]), ((), ())), preferred_element_type=F32)


def nt(a, b):
    return dot(a, b, ((1,), (1,)))


def nn(a, b):
    return dot(a, b, ((1,), (0,)))


def block_of(tokens):
    return 256 if tokens % 256 == 0 else tokens


def masked(block, kept):
    return jnp.where(kept, block, -1e30)


def kept_keys(size):
    keys = lax.broadcasted_iota(jnp.int32, (size, size), 0)
    return keys <= lax.broadcasted_iota(jnp.int32, (size, size), 1)


def scores_of(keys, queries, j, size, kept):
    mine = queries[j * size : (j + 1) * size]
    diagonal = masked(nt(keys[j * size : (j + 1) * size], mine), kept)
    if j == 0:
        return [diagonal]
    return [nt(keys[: j * size], mine), diagonal]


def exponents(parts):
    top = functools.reduce(jnp.maximum, [jnp.max(p, axis=0, keepdims=True) for p in parts])
    exps = [jnp.exp2((p - top) * (SCALE * LOG2E)) for p in parts]
    total = sum(jnp.sum(e, axis=0, keepdims=True) for e in exps)
    return exps, total


def stacked(parts):
    return parts[0] if len(parts) == 1 else jnp.concatenate(parts, axis=0)


def normed_head(x, factor, gain_q, gain_k):
    wide = x.astype(F32)
    normed = wide * factor
    return wide, (normed * gain_q).astype(BF16), (normed * gain_k).astype(BF16), normed.astype(BF16)


def column_of(row):
    return jnp.broadcast_to(row, (HDIM, row.shape[1])).T[:, 0:1]


def inverse_rms(total, width_all):
    return lax.rsqrt(total / width_all + EPSILON)


def lanes_of(start, size):
    return (slice(None), slice(start, start + size))


def compiler(limit):
    return pltpu.CompilerParams(vmem_limit_bytes=limit)


IN_VMEM = pl.BlockSpec(memory_space=pltpu.VMEM)
ANYWHERE = pl.BlockSpec(memory_space=pl.ANY)
IN_HBM = pl.BlockSpec(memory_space=pltpu.HBM)


def in_hbm(x):
    return pltpu.with_memory_space_constraint(x, pltpu.HBM)


def forward_kernel(heads, width_all, x_ref, t_ref, gq_ref, gk_ref, *rest):
    o_ref = rest[-1]
    tokens = x_ref.shape[0]
    size = block_of(tokens)
    kept = kept_keys(size)
    factor = column_of(inverse_rms(t_ref[0:1, :], width_all))
    for h in range(heads):
        lanes = slice(h * HDIM, (h + 1) * HDIM)
        wide, q, k, v = normed_head(x_ref[:, lanes], factor, gq_ref[:, lanes], gk_ref[:, lanes])
        vt = v.T
        for j in range(tokens // size):
            exps, total = exponents(scores_of(k, q, j, size, kept))
            mixed = nn(vt[:, : (j + 1) * size], stacked(exps).astype(BF16)) * (1.0 / total)
            rows = slice(j * size, (j + 1) * size)
            o_ref[rows, lanes] = (wide[rows] + mixed.T).astype(BF16)


def forward(width_all, x, totals, gain_q, gain_k, heads, after=()):
    tokens, width = x.shape
    lanes = heads * HDIM
    block = pl.BlockSpec((tokens, lanes), lambda i: (0, i))
    gain = pl.BlockSpec((1, lanes), lambda i: (0, i))
    return pl.pallas_call(
        functools.partial(forward_kernel, heads, width_all),
        out_shape=jax.ShapeDtypeStruct(x.shape, BF16),
        grid=(width // lanes,),
        in_specs=[block, pl.BlockSpec(totals.shape, lambda i: (0, 0)), gain, gain] + [IN_HBM] * len(after),
        out_specs=block,
        compiler_params=compiler(VMEM),
        name="forward",
    )(in_hbm(x), totals, gain_q, gain_k, *map(in_hbm, after))


def backward_head(x, g, factor, gain_q, gain_k):
    tokens = x.shape[0]
    size = block_of(tokens)
    kept = kept_keys(size)
    wide, q, k, v = normed_head(x, factor, gain_q, gain_k)
    kt = k.T
    blocks = tokens // size
    d_q = []
    d_k = [None] * blocks
    d_v = [None] * blocks
    for j in range(blocks):
        rows = slice(j * size, (j + 1) * size)
        exps, total = exponents(scores_of(k, q, j, size, kept))
        inverse = 1.0 / total
        weights = [e * inverse for e in exps]
        grads = [nt(v[: j * size], g[rows])] if j else []
        grads.append(nt(v[rows], g[rows]))
        delta = sum(jnp.sum(w * d, axis=0, keepdims=True) for w, d in zip(weights, grads))
        scores = stacked([(w * ((d - delta) * SCALE)).astype(BF16) for w, d in zip(weights, grads)])
        rounded = stacked([w.astype(BF16) for w in weights])
        d_q.append(nn(kt[:, : (j + 1) * size], scores).T)
        part_k = nn(scores, q[rows])
        part_v = nn(rounded, g[rows])
        for i in range(j + 1):
            mine = slice(i * size, (i + 1) * size)
            d_k[i] = part_k[mine] if d_k[i] is None else d_k[i] + part_k[mine]
            d_v[i] = part_v[mine] if d_v[i] is None else d_v[i] + part_v[mine]
    d_normed = stacked(d_q) * gain_q + stacked(d_k) * gain_k + stacked(d_v)
    return wide, d_normed


def backward_kernel(
    first, base, found, width_all, evicted_ref, own_ref, g_ref, t_ref, held_ref, gq_ref, gk_ref, past_ref, *refs
):
    evicted = evicted_ref[0] == 1
    heads = len(found)
    ahead = first < base
    if ahead:
        outs, inner_ref, xs, gs, x_sem, g_sem = refs[-6:]
    else:
        a_out, x_out, inner_ref, xs, gs, outs, x_sem, g_sem, a_sem, out_sem = refs[-10:]
    copies = []
    for h, (p, lane) in enumerate(found):
        to = lanes_of(h * HDIM, HDIM)
        there = lanes_of(first + h * HDIM, HDIM)
        far = pltpu.make_async_copy(refs[p].at[: t_ref.shape[1], lane : lane + HDIM], xs.at[to], x_sem.at[h])
        near = pltpu.make_async_copy(own_ref.at[(0, 0) + there], xs.at[to], x_sem.at[h])
        g = pltpu.make_async_copy(g_ref.at[(0,) + there], gs.at[to], g_sem.at[h])
        pl.when(evicted)(far.start)
        pl.when(jnp.logical_not(evicted))(near.start)
        g.start()
        copies.append((far, near, g))
    factor = column_of(inverse_rms(total_of(evicted_ref, t_ref, held_ref), width_all))
    part = None
    sent = []
    for h in range(heads):
        far, near, copy = copies[h]
        pl.when(evicted)(far.wait)
        pl.when(jnp.logical_not(evicted))(near.wait)
        copy.wait()
        mine = lanes_of(h * HDIM, HDIM)
        there = lanes_of(first + h * HDIM, HDIM)
        g = gs[mine]
        wide, d_normed = backward_head(xs[mine], g, factor, gq_ref[there], gk_ref[there])
        term = g.astype(F32) + factor * d_normed
        if ahead:
            outs[mine] = term.astype(BF16)
            outs[lanes_of((heads + h) * HDIM, HDIM)] = xs[mine]
        else:
            outs[mine] = term
            to = lanes_of(first - base + h * HDIM, HDIM)
            sent.append(pltpu.make_async_copy(outs.at[mine], a_out.at[to], a_sem.at[h]))
            sent.append(pltpu.make_async_copy(xs.at[mine], x_out.at[to], out_sem.at[h]))
            for copy in sent[-2:]:
                copy.start()
        product = d_normed * wide
        part = product if part is None else part + product
    inner_ref[...] = jnp.sum(part.T, axis=0, keepdims=True) + past_ref[...]
    for copy in sent:
        copy.wait()


def total_of(evicted_ref, t_ref, held_ref):
    return jnp.where(evicted_ref[0] == 1, held_ref[...], t_ref[1:2, :])


def backward(
    width_all, evicted, stash, g, totals, held, gain_q, gain_k, past, far, found, first, base, sofar=(), after=()
):
    tokens, width = totals.shape[1], gain_q.shape[1]
    heads = len(found)
    small = (tokens, heads * HDIM)
    dma = pltpu.SemaphoreType.DMA((heads,))
    inner = jax.ShapeDtypeStruct((1, tokens), F32)
    if first < base:
        shapes = (jax.ShapeDtypeStruct((tokens, 2 * heads * HDIM), BF16), inner)
        scratch = [pltpu.VMEM(small, BF16)] * 2 + [dma] * 2
    else:
        shapes = (pltpu.HBM((tokens, width - base), F32), pltpu.HBM((tokens, width - base), BF16), inner)
        scratch = [pltpu.VMEM(small, BF16)] * 2 + [pltpu.VMEM(small, F32)] + [dma] * 4
    return pl.pallas_call(
        functools.partial(backward_kernel, first, base, found, width_all),
        out_shape=shapes,
        in_specs=[pl.BlockSpec(memory_space=pltpu.SMEM)] + [ANYWHERE] * 2 + [IN_VMEM] * 5
        + [ANYWHERE] * len(far) + [IN_HBM] * len(sofar) + [ANYWHERE] * len(after),
        out_specs=(IN_VMEM,) * 2 if first < base else (IN_HBM, IN_HBM, IN_VMEM),
        input_output_aliases={8 + len(far): 0, 9 + len(far): 1} if sofar else {},
        scratch_shapes=scratch,
        compiler_params=compiler(VMEM),
        name="backward",
    )(evicted, in_hbm(stash), in_hbm(g), totals, held, gain_q, gain_k, past, *far, *sofar, *after)


def row_of(total, inner, width_all):
    return inverse_rms(total, width_all) ** 3 * inner / width_all


def finish_kernel(
    first, width_all, evicted_ref, a_ref, x_ref, t_ref, held_ref, inner_ref, o_ref, row_ref, terms, xs, a_sem, x_sem
):
    heads = o_ref.shape[1] // HDIM
    copies = []
    for h in range(heads):
        mine = lanes_of(h * HDIM, HDIM)
        there = lanes_of(first + h * HDIM, HDIM)
        copies.append(
            (
                pltpu.make_async_copy(a_ref.at[there], terms.at[mine], a_sem.at[h]),
                pltpu.make_async_copy(x_ref.at[there], xs.at[mine], x_sem.at[h]),
            )
        )
        for copy in copies[-1]:
            copy.start()
    row = row_of(total_of(evicted_ref, t_ref, held_ref), inner_ref[...], width_all)
    row_ref[...] = row
    column = column_of(row)
    for h in range(heads):
        mine = lanes_of(h * HDIM, HDIM)
        for copy in copies[h]:
            copy.wait()
        o_ref[mine] = (terms[mine] - xs[mine].astype(F32) * column).astype(BF16)


def finish(width_all, evicted, a, x, totals, held, inner, first, last):
    shape = (a.shape[0], last - first)
    dma = pltpu.SemaphoreType.DMA(((last - first) // HDIM,))
    return pl.pallas_call(
        functools.partial(finish_kernel, first, width_all),
        out_shape=(jax.ShapeDtypeStruct(shape, BF16), jax.ShapeDtypeStruct((1, a.shape[0]), F32)),
        in_specs=[pl.BlockSpec(memory_space=pltpu.SMEM)] + [IN_HBM] * 2 + [IN_VMEM] * 3,
        out_specs=(IN_VMEM, IN_VMEM),
        scratch_shapes=[pltpu.VMEM(shape, F32), pltpu.VMEM(shape, BF16), dma, dma],
        compiler_params=compiler(VMEM),
        name="finish",
    )(evicted, in_hbm(a), in_hbm(x), totals, held, inner)


def place_kernel(pair_ref, row_ref, *refs):
    rest_refs, (o_ref, outs, sems) = refs[:-3], refs[-3:]
    lanes = outs.shape[1]
    ahead = lanes // HDIM
    copies, at = [], lanes
    for i, ref in enumerate(rest_refs):
        copies.append(pltpu.make_async_copy(ref, o_ref.at[lanes_of(at, ref.shape[1])], sems.at[ahead + i]))
        copies[-1].start()
        at += ref.shape[1]
    row = column_of(row_ref[...])
    for h in range(ahead):
        mine = lanes_of(h * HDIM, HDIM)
        x = pair_ref[lanes_of(lanes + h * HDIM, HDIM)]
        outs[mine] = (pair_ref[mine].astype(F32) - x.astype(F32) * row).astype(BF16)
        copies.append(pltpu.make_async_copy(outs.at[mine], o_ref.at[mine], sems.at[h]))
        copies[-1].start()
    for copy in copies:
        copy.wait()


def place(pair, row, *rest):
    tokens, lanes = pair.shape[0], pair.shape[1] // 2
    return pl.pallas_call(
        place_kernel,
        out_shape=jax.ShapeDtypeStruct((tokens, lanes + sum(r.shape[1] for r in rest)), BF16),
        in_specs=[IN_VMEM] * (2 + len(rest)),
        out_specs=ANYWHERE,
        scratch_shapes=[pltpu.VMEM((tokens, lanes), BF16), pltpu.SemaphoreType.DMA((lanes // HDIM + len(rest),))],
        compiler_params=compiler(VMEM),
        name="place",
    )(pair, row, *rest)


def hold_kernel(x_ref, *rest):
    pass


def hold(x, after):
    return pl.pallas_call(
        hold_kernel,
        out_shape=jax.ShapeDtypeStruct(x.shape, x.dtype),
        in_specs=[IN_VMEM] + [ANYWHERE] * len(after),
        out_specs=IN_VMEM,
        input_output_aliases={0: 0},
        compiler_params=compiler(VMEM),
        name="hold",
    )(x, *after)


def squares_kernel(current_ref, stash_ref, *rest):
    rows_ref, sums = rest[-2:]
    step = pl.program_id(0)

    def total(x):
        wide = x.astype(F32)
        square = wide * wide
        return sum(square[:, i : i + HDIM] for i in range(0, square.shape[1], HDIM))

    for i, x in enumerate((current_ref[...], stash_ref[0], stash_ref[1])):
        part = total(x)

        @pl.when(step == 0)
        def _():
            sums[i] = part

        @pl.when(step > 0)
        def _():
            sums[i] += part

    @pl.when(step == pl.num_programs(0) - 1)
    def _():
        for i in range(3):
            rows_ref[i : i + 1, :] = jnp.sum(sums[i].T, axis=0, keepdims=True)


def squares(current, stash, lanes, after=()):
    tokens, width = current.shape
    return pl.pallas_call(
        squares_kernel,
        out_shape=jax.ShapeDtypeStruct((3, tokens), F32),
        grid=(width // lanes,),
        in_specs=[
            pl.BlockSpec((tokens, lanes), lambda i: (0, i)),
            pl.BlockSpec((None, 2, tokens, lanes), lambda i: (0, 0, 0, i)),
        ] + [ANYWHERE] * len(after),
        out_specs=pl.BlockSpec((3, tokens), lambda i: (0, 0)),
        scratch_shapes=[pltpu.VMEM((3, tokens, HDIM), F32)],
        compiler_params=compiler(MOST),
        name="squares",
    )(in_hbm(current), in_hbm(stash), *after)


def piece_kernel(starts, sizes, stash_ref, *rest):
    outs, mark, sems = rest[-2 - len(sizes) : -2], rest[-2], rest[-1]
    mark[...] = jnp.zeros_like(mark)
    copies = [
        pltpu.make_async_copy(stash_ref.at[(0, 1) + lanes_of(start, size)], out, sems.at[i])
        for i, (start, size, out) in enumerate(zip(starts, sizes, outs))
    ]
    for copy in copies:
        copy.start()
    for copy in copies:
        copy.wait()


def pieces_of(stash, starts, sizes, after=()):
    tokens = stash.shape[2]
    return pl.pallas_call(
        functools.partial(piece_kernel, starts, sizes),
        out_shape=[jax.ShapeDtypeStruct((tokens, size), BF16) for size in sizes] + [jax.ShapeDtypeStruct((8, HDIM), F32)],
        in_specs=[IN_HBM] + [ANYWHERE] * len(after),
        out_specs=[IN_VMEM] * (len(sizes) + 1),
        scratch_shapes=[pltpu.SemaphoreType.DMA((len(sizes),))],
        compiler_params=compiler(VMEM),
        name="pieces",
    )(in_hbm(stash), *after)


def in_rows(row, size):
    tokens = row.shape[1]
    rows = []
    for _ in range(3):
        term = row.astype(BF16)
        row = row - term.astype(F32)
        rows += [term[:, i : i + size] for i in range(0, tokens, size)]
    fill = -len(rows) % 16
    return jnp.concatenate(rows + [jnp.zeros((fill, size), BF16)] * (fill > 0), axis=0)


def row_kernel(extra_ref, o_ref):
    tokens, size = o_ref.shape[1], extra_ref.shape[1]
    each = tokens // size
    extra = extra_ref[...].astype(F32)
    for i in range(each):
        o_ref[:, i * size : (i + 1) * size] = sum(extra[p * each + i : p * each + i + 1] for p in range(3))


def row_from(piece, tokens):
    extra = piece.shape[0] - tokens
    size = piece.shape[1]
    return pl.pallas_call(
        row_kernel,
        out_shape=jax.ShapeDtypeStruct((1, tokens), F32),
        grid=(1,),
        in_specs=[pl.BlockSpec((extra, size), lambda i: (tokens // extra, 0))],
        out_specs=pl.BlockSpec((1, tokens), lambda i: (0, 0)),
        compiler_params=compiler(VMEM),
        name="row",
    )(piece)


def piece_and_row_kernel(start, stash_ref, t_ref, *rest):
    out, sem = rest[-2:]
    tokens, size = stash_ref.shape[2], out.shape[1]
    copy = pltpu.make_async_copy(stash_ref.at[(0, 1) + lanes_of(start, size)], out.at[:tokens, :], sem.at[0])
    copy.start()
    out[tokens:, :] = in_rows(t_ref[2:3, :], size)
    copy.wait()


def piece_and_row(stash, totals, start, size, after):
    tokens = stash.shape[2]
    extra = -(-3 * tokens // size // 16) * 16
    return pl.pallas_call(
        functools.partial(piece_and_row_kernel, start),
        out_shape=jax.ShapeDtypeStruct((tokens + extra, size), BF16),
        in_specs=[IN_HBM, IN_VMEM] + [ANYWHERE] * len(after),
        out_specs=IN_VMEM,
        scratch_shapes=[pltpu.SemaphoreType.DMA((1,))],
        compiler_params=compiler(VMEM),
        name="piece_and_row",
    )(in_hbm(stash), totals, *after)


def send(x, pairs):
    return lax.ppermute(x, "section", pairs)


def local(width_all, layer_input, grad_input, stashed, eviction, query_gain, key_gain):
    n = lax.axis_size("section")
    partner = [(s, (s + n // 2) % n) for s in range(n)]
    prior = [(s, (s - 1) % n) for s in range(n)]
    current = layer_input[0]
    tokens, width = current.shape
    count = width // HDIM
    each = max(1, count // 6)
    pieces = count // each
    size = each * HDIM
    third = count // 3 * HDIM

    *away, mark = pieces_of(stashed, (0, size), (size, size))
    fetched = [send(x, partner) for x in away]
    totals = lax.psum(squares(current, stashed, third, (mark,)), "tensor")
    output = forward(width_all, current, totals, query_gain, key_gain, third // HDIM)

    def fetch(p, after):
        away, mark = pieces_of(stashed, (p * size,), (size,), (fetched[p - 2], after))
        fetched.append(send(away, partner))
        return mark

    fetched.append(send(piece_and_row(stashed, totals, 2 * size, size, (fetched[0],)), partner))
    held = row_from(fetched[2], tokens)
    marks = [fetch(p, in_hbm(output)) for p in range(3, min(5, pieces))]
    base = max(1, count // 4) * HDIM

    def share(inner, first, last, sofar, after):
        heads = range(first // HDIM, last // HDIM)
        used = sorted({h // each for h in heads})
        found = tuple((used.index(h // each), h % each * HDIM) for h in heads)
        return backward(
            width_all, eviction, stashed, grad_input, totals, held, query_gain, key_gain, inner,
            [fetched[p] for p in used], found, first, base, sofar, after,
        )

    pair, inner = share(jnp.zeros((1, tokens), F32), 0, base, (), (in_hbm(output), *marks))
    marks = []
    sofar, inners = (), [inner]
    ends = sorted({base, max(base, 3 * size), *(p * size for p in range(4, pieces + 1))})
    for first, last in zip(ends[:-1], ends[1:]):
        *sofar, inner = share(inner, first, last, tuple(sofar), tuple(marks))
        inners.append(inner)
        marks = [fetch(p, inner) for p in range(len(fetched), pieces)]
    pair = send(hold(pair, (inners[-2],)), prior)
    inner = lax.psum(inner, "tensor")
    left = width - base
    cut = (left // HDIM + 1) // 2 * HDIM
    ends = (*sofar, totals, held, inner)
    early, row = finish(width_all, eviction, *ends, 0, cut)
    early = send(early, prior)
    late, _ = finish(width_all, eviction, *ends, cut, left)
    result = place(pair, send(row, prior), early, send(late, prior))
    return (output[None], result[None])


def solution(mesh):
    placed = (
        P("section", None, "tensor"),
        P("section", None, "tensor"),
        P("section", None, None, "tensor"),
        P("section"),
        P("section", "tensor"),
        P("section", "tensor"),
    )

    def whole(layer_input, *others):
        return jax.shard_map(
            functools.partial(local, layer_input.shape[-1]),
            mesh=mesh,
            in_specs=placed,
            out_specs=(P("section", None, "tensor"), P("section", None, "tensor")),
            check_vma=False,
        )(layer_input, *others)

    return whole
```

```python
import functools
import math

import jax
import jax.numpy as jnp
from jax import lax
from jax.experimental import pallas as pl
from jax.experimental.pallas import tpu as pltpu
from jax.sharding import PartitionSpec as P

HDIM = 128
EPSILON = 1e-05
SCALE = 1.0 / math.sqrt(HDIM)
LOG2E = math.log2(math.e)
VMEM = 32 * 1024 * 1024
MOST = 60 * 1024 * 1024
PARTS = 4

F32 = jnp.float32
BF16 = jnp.bfloat16


def dot(a, b, contract):
    return lax.dot_general(a, b, ((contract[0], contract[1]), ((), ())), preferred_element_type=F32)


def nt(a, b):
    return dot(a, b, ((1,), (1,)))


def nn(a, b):
    return dot(a, b, ((1,), (0,)))


def block_of(tokens):
    return 256 if tokens % 256 == 0 else tokens


def masked(block, kept):
    return jnp.where(kept, block, -1e30)


def kept_keys(size):
    keys = lax.broadcasted_iota(jnp.int32, (size, size), 0)
    return keys <= lax.broadcasted_iota(jnp.int32, (size, size), 1)


def scores_of(keys, queries, j, size, kept):
    mine = queries[j * size : (j + 1) * size]
    diagonal = masked(nt(keys[j * size : (j + 1) * size], mine), kept)
    if j == 0:
        return [diagonal]
    return [nt(keys[: j * size], mine), diagonal]


def exponents(parts):
    top = functools.reduce(jnp.maximum, [jnp.max(p, axis=0, keepdims=True) for p in parts])
    exps = [jnp.exp2((p - top) * (SCALE * LOG2E)) for p in parts]
    total = sum(jnp.sum(e, axis=0, keepdims=True) for e in exps)
    return exps, total


def stacked(parts):
    return parts[0] if len(parts) == 1 else jnp.concatenate(parts, axis=0)


def normed_head(x, factor, gain_q, gain_k):
    wide = x.astype(F32)
    normed = wide * factor
    return wide, (normed * gain_q).astype(BF16), (normed * gain_k).astype(BF16), normed.astype(BF16)


def column_of(row):
    return jnp.broadcast_to(row, (HDIM, row.shape[1])).T[:, 0:1]


def inverse_rms(total, width_all):
    return lax.rsqrt(total / width_all + EPSILON)


def lanes_of(start, size):
    return (slice(None), slice(start, start + size))


def compiler(limit):
    return pltpu.CompilerParams(vmem_limit_bytes=limit)


IN_VMEM = pl.BlockSpec(memory_space=pltpu.VMEM)
ANYWHERE = pl.BlockSpec(memory_space=pl.ANY)
IN_HBM = pl.BlockSpec(memory_space=pltpu.HBM)


def in_hbm(x):
    return pltpu.with_memory_space_constraint(x, pltpu.HBM)


def forward_kernel(heads, width_all, x_ref, t_ref, gq_ref, gk_ref, *rest):
    o_ref = rest[-1]
    tokens = x_ref.shape[0]
    size = block_of(tokens)
    kept = kept_keys(size)
    factor = column_of(inverse_rms(t_ref[0:1, :], width_all))
    for h in range(heads):
        lanes = slice(h * HDIM, (h + 1) * HDIM)
        wide, q, k, v = normed_head(x_ref[:, lanes], factor, gq_ref[:, lanes], gk_ref[:, lanes])
        vt = v.T
        for j in range(tokens // size):
            exps, total = exponents(scores_of(k, q, j, size, kept))
            mixed = nn(vt[:, : (j + 1) * size], stacked(exps).astype(BF16)) * (1.0 / total)
            rows = slice(j * size, (j + 1) * size)
            o_ref[rows, lanes] = (wide[rows] + mixed.T).astype(BF16)


def forward(width_all, x, totals, gain_q, gain_k, heads, after=()):
    tokens, width = x.shape
    lanes = heads * HDIM
    block = pl.BlockSpec((tokens, lanes), lambda i: (0, i))
    gain = pl.BlockSpec((1, lanes), lambda i: (0, i))
    return pl.pallas_call(
        functools.partial(forward_kernel, heads, width_all),
        out_shape=jax.ShapeDtypeStruct(x.shape, BF16),
        grid=(width // lanes,),
        in_specs=[block, pl.BlockSpec(totals.shape, lambda i: (0, 0)), gain, gain] + [IN_HBM] * len(after),
        out_specs=block,
        compiler_params=compiler(VMEM),
        name="forward",
    )(in_hbm(x), totals, gain_q, gain_k, *map(in_hbm, after))


def backward_head(x, g, factor, gain_q, gain_k):
    tokens = x.shape[0]
    size = block_of(tokens)
    kept = kept_keys(size)
    wide, q, k, v = normed_head(x, factor, gain_q, gain_k)
    kt = k.T
    blocks = tokens // size
    d_q = []
    d_k = [None] * blocks
    d_v = [None] * blocks
    for j in range(blocks):
        rows = slice(j * size, (j + 1) * size)
        exps, total = exponents(scores_of(k, q, j, size, kept))
        inverse = 1.0 / total
        weights = [e * inverse for e in exps]
        grads = [nt(v[: j * size], g[rows])] if j else []
        grads.append(nt(v[rows], g[rows]))
        delta = sum(jnp.sum(w * d, axis=0, keepdims=True) for w, d in zip(weights, grads))
        scores = stacked([(w * ((d - delta) * SCALE)).astype(BF16) for w, d in zip(weights, grads)])
        rounded = stacked([w.astype(BF16) for w in weights])
        d_q.append(nn(kt[:, : (j + 1) * size], scores).T)
        part_k = nn(scores, q[rows])
        part_v = nn(rounded, g[rows])
        for i in range(j + 1):
            mine = slice(i * size, (i + 1) * size)
            d_k[i] = part_k[mine] if d_k[i] is None else d_k[i] + part_k[mine]
            d_v[i] = part_v[mine] if d_v[i] is None else d_v[i] + part_v[mine]
    d_normed = stacked(d_q) * gain_q + stacked(d_k) * gain_k + stacked(d_v)
    return wide, d_normed


def backward_kernel(
    first, base, found, width_all, evicted_ref, own_ref, g_ref, t_ref, held_ref, gq_ref, gk_ref, past_ref, *refs
):
    evicted = evicted_ref[0] == 1
    heads = len(found)
    ahead = first < base
    if ahead:
        outs, inner_ref, xs, gs, x_sem, g_sem = refs[-6:]
    else:
        a_out, x_out, inner_ref, xs, gs, outs, x_sem, g_sem, a_sem, out_sem = refs[-10:]
    copies = []
    for h, (p, lane) in enumerate(found):
        to = lanes_of(h * HDIM, HDIM)
        there = lanes_of(first + h * HDIM, HDIM)
        far = pltpu.make_async_copy(refs[p].at[: t_ref.shape[1], lane : lane + HDIM], xs.at[to], x_sem.at[h])
        near = pltpu.make_async_copy(own_ref.at[(0, 0) + there], xs.at[to], x_sem.at[h])
        g = pltpu.make_async_copy(g_ref.at[(0,) + there], gs.at[to], g_sem.at[h])
        pl.when(evicted)(far.start)
        pl.when(jnp.logical_not(evicted))(near.start)
        g.start()
        copies.append((far, near, g))
    factor = column_of(inverse_rms(total_of(evicted_ref, t_ref, held_ref), width_all))
    part = None
    sent = []
    for h in range(heads):
        far, near, copy = copies[h]
        pl.when(evicted)(far.wait)
        pl.when(jnp.logical_not(evicted))(near.wait)
        copy.wait()
        mine = lanes_of(h * HDIM, HDIM)
        there = lanes_of(first + h * HDIM, HDIM)
        g = gs[mine]
        wide, d_normed = backward_head(xs[mine], g, factor, gq_ref[there], gk_ref[there])
        term = g.astype(F32) + factor * d_normed
        if ahead:
            outs[mine] = term.astype(BF16)
            outs[lanes_of((heads + h) * HDIM, HDIM)] = xs[mine]
        else:
            outs[mine] = term
            to = lanes_of(first - base + h * HDIM, HDIM)
            sent.append(pltpu.make_async_copy(outs.at[mine], a_out.at[to], a_sem.at[h]))
            sent.append(pltpu.make_async_copy(xs.at[mine], x_out.at[to], out_sem.at[h]))
            for copy in sent[-2:]:
                copy.start()
        product = d_normed * wide
        part = product if part is None else part + product
    inner_ref[...] = jnp.sum(part.T, axis=0, keepdims=True) + past_ref[...]
    for copy in sent:
        copy.wait()


def total_of(evicted_ref, t_ref, held_ref):
    return jnp.where(evicted_ref[0] == 1, held_ref[...], t_ref[1:2, :])


def backward(
    width_all, evicted, stash, g, totals, held, gain_q, gain_k, past, far, found, first, base, sofar=(), after=()
):
    tokens, width = totals.shape[1], gain_q.shape[1]
    heads = len(found)
    small = (tokens, heads * HDIM)
    dma = pltpu.SemaphoreType.DMA((heads,))
    inner = jax.ShapeDtypeStruct((1, tokens), F32)
    if first < base:
        shapes = (jax.ShapeDtypeStruct((tokens, 2 * heads * HDIM), BF16), inner)
        scratch = [pltpu.VMEM(small, BF16)] * 2 + [dma] * 2
    else:
        shapes = (pltpu.HBM((tokens, width - base), F32), pltpu.HBM((tokens, width - base), BF16), inner)
        scratch = [pltpu.VMEM(small, BF16)] * 2 + [pltpu.VMEM(small, F32)] + [dma] * 4
    return pl.pallas_call(
        functools.partial(backward_kernel, first, base, found, width_all),
        out_shape=shapes,
        in_specs=[pl.BlockSpec(memory_space=pltpu.SMEM)] + [ANYWHERE] * 2 + [IN_VMEM] * 5
        + [ANYWHERE] * len(far) + [IN_HBM] * len(sofar) + [ANYWHERE] * len(after),
        out_specs=(IN_VMEM,) * 2 if first < base else (IN_HBM, IN_HBM, IN_VMEM),
        input_output_aliases={8 + len(far): 0, 9 + len(far): 1} if sofar else {},
        scratch_shapes=scratch,
        compiler_params=compiler(VMEM),
        name="backward",
    )(evicted, in_hbm(stash), in_hbm(g), totals, held, gain_q, gain_k, past, *far, *sofar, *after)


def row_of(total, inner, width_all):
    return inverse_rms(total, width_all) ** 3 * inner / width_all


def finish_kernel(
    first, width_all, evicted_ref, a_ref, x_ref, t_ref, held_ref, inner_ref, o_ref, terms, xs, a_sem, x_sem
):
    tokens = a_ref.shape[0]
    heads = o_ref.shape[1] // HDIM
    copies = []
    for h in range(heads):
        mine = lanes_of(h * HDIM, HDIM)
        there = lanes_of(first + h * HDIM, HDIM)
        copies.append(
            (
                pltpu.make_async_copy(a_ref.at[there], terms.at[mine], a_sem.at[h]),
                pltpu.make_async_copy(x_ref.at[there], xs.at[mine], x_sem.at[h]),
            )
        )
        for copy in copies[-1]:
            copy.start()
    row = row_of(total_of(evicted_ref, t_ref, held_ref), inner_ref[...], width_all)
    if o_ref.shape[0] > tokens:
        o_ref[tokens:, :] = in_rows(row, o_ref.shape[1])
    column = column_of(row)
    for h in range(heads):
        mine = lanes_of(h * HDIM, HDIM)
        for copy in copies[h]:
            copy.wait()
        o_ref[:tokens, mine[1]] = (terms[mine] - xs[mine].astype(F32) * column).astype(BF16)


def finish(width_all, evicted, a, x, totals, held, inner, first, last, carry):
    tokens = a.shape[0]
    shape = (tokens, last - first)
    dma = pltpu.SemaphoreType.DMA(((last - first) // HDIM,))
    return pl.pallas_call(
        functools.partial(finish_kernel, first, width_all),
        out_shape=jax.ShapeDtypeStruct((tokens + carry * below(tokens, last - first), last - first), BF16),
        in_specs=[pl.BlockSpec(memory_space=pltpu.SMEM)] + [IN_HBM] * 2 + [IN_VMEM] * 3,
        out_specs=IN_VMEM,
        scratch_shapes=[pltpu.VMEM(shape, F32), pltpu.VMEM(shape, BF16), dma, dma],
        compiler_params=compiler(VMEM),
        name="finish",
    )(evicted, in_hbm(a), in_hbm(x), totals, held, inner)


def place_kernel(pair_ref, *refs):
    rest_refs, (o_ref, outs, row_ref, sems) = refs[:-4], refs[-4:]
    tokens, lanes = outs.shape
    ahead = lanes // HDIM
    copies, at = [], lanes
    for i, ref in enumerate(rest_refs):
        to = o_ref.at[lanes_of(at, ref.shape[1])]
        copies.append(pltpu.make_async_copy(ref.at[:tokens, :], to, sems.at[ahead + i]))
        copies[-1].start()
        at += ref.shape[1]
    row_out_of(rest_refs[-1][tokens:, :], row_ref)
    row = column_of(row_ref[...])
    for h in range(ahead):
        mine = lanes_of(h * HDIM, HDIM)
        x = pair_ref[lanes_of(lanes + h * HDIM, HDIM)]
        outs[mine] = (pair_ref[mine].astype(F32) - x.astype(F32) * row).astype(BF16)
        copies.append(pltpu.make_async_copy(outs.at[mine], o_ref.at[mine], sems.at[h]))
        copies[-1].start()
    for copy in copies:
        copy.wait()


def place(pair, *rest):
    tokens, lanes = pair.shape[0], pair.shape[1] // 2
    return pl.pallas_call(
        place_kernel,
        out_shape=jax.ShapeDtypeStruct((tokens, lanes + sum(r.shape[1] for r in rest)), BF16),
        in_specs=[IN_VMEM] * (1 + len(rest)),
        out_specs=ANYWHERE,
        scratch_shapes=[
            pltpu.VMEM((tokens, lanes), BF16),
            pltpu.VMEM((1, tokens), F32),
            pltpu.SemaphoreType.DMA((lanes // HDIM + len(rest),)),
        ],
        compiler_params=compiler(VMEM),
        name="place",
    )(pair, *rest)


def hold_kernel(x_ref, *rest):
    pass


def hold(x, after):
    return pl.pallas_call(
        hold_kernel,
        out_shape=jax.ShapeDtypeStruct(x.shape, x.dtype),
        in_specs=[IN_VMEM] + [ANYWHERE] * len(after),
        out_specs=IN_VMEM,
        input_output_aliases={0: 0},
        compiler_params=compiler(VMEM),
        name="hold",
    )(x, *after)


def squares_kernel(current_ref, stash_ref, *rest):
    rows_ref, sums = rest[-2:]
    step = pl.program_id(0)

    def total(x):
        wide = x.astype(F32)
        square = wide * wide
        return sum(square[:, i : i + HDIM] for i in range(0, square.shape[1], HDIM))

    for i, x in enumerate((current_ref[...], stash_ref[0], stash_ref[1])):
        part = total(x)

        @pl.when(step == 0)
        def _():
            sums[i] = part

        @pl.when(step > 0)
        def _():
            sums[i] += part

    @pl.when(step == pl.num_programs(0) - 1)
    def _():
        for i in range(3):
            rows_ref[i : i + 1, :] = jnp.sum(sums[i].T, axis=0, keepdims=True)


def squares(current, stash, lanes, after=()):
    tokens, width = current.shape
    return pl.pallas_call(
        squares_kernel,
        out_shape=jax.ShapeDtypeStruct((3, tokens), F32),
        grid=(width // lanes,),
        in_specs=[
            pl.BlockSpec((tokens, lanes), lambda i: (0, i)),
            pl.BlockSpec((None, 2, tokens, lanes), lambda i: (0, 0, 0, i)),
        ] + [ANYWHERE] * len(after),
        out_specs=pl.BlockSpec((3, tokens), lambda i: (0, 0)),
        scratch_shapes=[pltpu.VMEM((3, tokens, HDIM), F32)],
        compiler_params=compiler(MOST),
        name="squares",
    )(in_hbm(current), in_hbm(stash), *after)


def piece_kernel(starts, sizes, stash_ref, *rest):
    outs, mark, sems = rest[-2 - len(sizes) : -2], rest[-2], rest[-1]
    mark[...] = jnp.zeros_like(mark)
    copies = [
        pltpu.make_async_copy(stash_ref.at[(0, 1) + lanes_of(start, size)], out, sems.at[i])
        for i, (start, size, out) in enumerate(zip(starts, sizes, outs))
    ]
    for copy in copies:
        copy.start()
    for copy in copies:
        copy.wait()


def pieces_of(stash, starts, sizes, after=()):
    tokens = stash.shape[2]
    return pl.pallas_call(
        functools.partial(piece_kernel, starts, sizes),
        out_shape=[jax.ShapeDtypeStruct((tokens, size), BF16) for size in sizes] + [jax.ShapeDtypeStruct((8, HDIM), F32)],
        in_specs=[IN_HBM] + [ANYWHERE] * len(after),
        out_specs=[IN_VMEM] * (len(sizes) + 1),
        scratch_shapes=[pltpu.SemaphoreType.DMA((len(sizes),))],
        compiler_params=compiler(VMEM),
        name="pieces",
    )(in_hbm(stash), *after)


def in_rows(row, size):
    tokens = row.shape[1]
    rows = []
    for _ in range(3):
        term = row.astype(BF16)
        row = row - term.astype(F32)
        rows += [term[:, i : i + size] for i in range(0, tokens, size)]
    fill = -len(rows) % 16
    return jnp.concatenate(rows + [jnp.zeros((fill, size), BF16)] * (fill > 0), axis=0)


def below(tokens, size):
    return -(-3 * tokens // size // 16) * 16


def row_out_of(extra, row_ref):
    tokens, size = row_ref.shape[1], extra.shape[1]
    each = tokens // size
    extra = extra.astype(F32)
    for i in range(each):
        row_ref[:, i * size : (i + 1) * size] = sum(extra[p * each + i : p * each + i + 1] for p in range(3))


def row_kernel(extra_ref, o_ref):
    row_out_of(extra_ref[...], o_ref)


def row_from(piece, tokens):
    extra = piece.shape[0] - tokens
    size = piece.shape[1]
    return pl.pallas_call(
        row_kernel,
        out_shape=jax.ShapeDtypeStruct((1, tokens), F32),
        grid=(1,),
        in_specs=[pl.BlockSpec((extra, size), lambda i: (tokens // extra, 0))],
        out_specs=pl.BlockSpec((1, tokens), lambda i: (0, 0)),
        compiler_params=compiler(VMEM),
        name="row",
    )(piece)


def piece_and_row_kernel(start, stash_ref, t_ref, *rest):
    out, sem = rest[-2:]
    tokens, size = stash_ref.shape[2], out.shape[1]
    copy = pltpu.make_async_copy(stash_ref.at[(0, 1) + lanes_of(start, size)], out.at[:tokens, :], sem.at[0])
    copy.start()
    out[tokens:, :] = in_rows(t_ref[2:3, :], size)
    copy.wait()


def piece_and_row(stash, totals, start, size, after):
    tokens = stash.shape[2]
    extra = below(tokens, size)
    return pl.pallas_call(
        functools.partial(piece_and_row_kernel, start),
        out_shape=jax.ShapeDtypeStruct((tokens + extra, size), BF16),
        in_specs=[IN_HBM, IN_VMEM] + [ANYWHERE] * len(after),
        out_specs=IN_VMEM,
        scratch_shapes=[pltpu.SemaphoreType.DMA((1,))],
        compiler_params=compiler(VMEM),
        name="piece_and_row",
    )(in_hbm(stash), totals, *after)


def send(x, pairs):
    return lax.ppermute(x, "section", pairs)


def local(width_all, layer_input, grad_input, stashed, eviction, query_gain, key_gain):
    n = lax.axis_size("section")
    partner = [(s, (s + n // 2) % n) for s in range(n)]
    prior = [(s, (s - 1) % n) for s in range(n)]
    current = layer_input[0]
    tokens, width = current.shape
    count = width // HDIM
    each = max(1, count // 6)
    pieces = count // each
    size = each * HDIM
    third = count // 3 * HDIM

    *away, mark = pieces_of(stashed, (0, size), (size, size))
    fetched = [send(x, partner) for x in away]
    totals = lax.psum(squares(current, stashed, third, (mark,)), "tensor")
    output = forward(width_all, current, totals, query_gain, key_gain, third // HDIM)

    def fetch(p, after):
        away, mark = pieces_of(stashed, (p * size,), (size,), (fetched[p - 2], after))
        fetched.append(send(away, partner))
        return mark

    fetched.append(send(piece_and_row(stashed, totals, 2 * size, size, (fetched[0],)), partner))
    held = row_from(fetched[2], tokens)
    marks = [fetch(p, in_hbm(output)) for p in range(3, min(5, pieces))]
    base = each * HDIM

    def share(inner, first, last, sofar, after):
        heads = range(first // HDIM, last // HDIM)
        used = sorted({h // each for h in heads})
        found = tuple((used.index(h // each), h % each * HDIM) for h in heads)
        return backward(
            width_all, eviction, stashed, grad_input, totals, held, query_gain, key_gain, inner,
            [fetched[p] for p in used], found, first, base, sofar, after,
        )

    pair, inner = share(jnp.zeros((1, tokens), F32), 0, base, (), (in_hbm(output), *marks))
    marks = []
    sofar, inners = (), [inner]
    ends = sorted({base, max(base, 3 * size), *(p * size for p in range(4, pieces + 1))})
    for first, last in zip(ends[:-1], ends[1:]):
        *sofar, inner = share(inner, first, last, tuple(sofar), tuple(marks))
        inners.append(inner)
        marks = [fetch(p, inner) for p in range(len(fetched), pieces)]
    pair = send(hold(pair, (inners[-2],)), prior)
    inner = lax.psum(inner, "tensor")
    left = (width - base) // HDIM
    ends = (*sofar, totals, held, inner)
    cuts = [-(-left * i // PARTS) * HDIM for i in range(PARTS + 1)]
    cuts = sorted(set(cuts))
    rests = [
        send(finish(width_all, eviction, *ends, first, last, last == cuts[-1]), prior)
        for first, last in zip(cuts[:-1], cuts[1:])
    ]
    result = place(pair, *rests)
    return (output[None], result[None])


def solution(mesh):
    placed = (
        P("section", None, "tensor"),
        P("section", None, "tensor"),
        P("section", None, None, "tensor"),
        P("section"),
        P("section", "tensor"),
        P("section", "tensor"),
    )

    def whole(layer_input, *others):
        return jax.shard_map(
            functools.partial(local, layer_input.shape[-1]),
            mesh=mesh,
            in_specs=placed,
            out_specs=(P("section", None, "tensor"), P("section", None, "tensor")),
            check_vma=False,
        )(layer_input, *others)

    return whole
```

```python
import functools
import math

import jax
import jax.numpy as jnp
from jax import lax
from jax.experimental import pallas as pl
from jax.experimental.pallas import tpu as pltpu
from jax.sharding import PartitionSpec as P

HDIM = 128
EPSILON = 1e-05
SCALE = 1.0 / math.sqrt(HDIM)
LOG2E = math.log2(math.e)
VMEM = 32 * 1024 * 1024
MOST = 60 * 1024 * 1024

F32 = jnp.float32
BF16 = jnp.bfloat16


def dot(a, b, contract):
    return lax.dot_general(a, b, ((contract[0], contract[1]), ((), ())), preferred_element_type=F32)


def nt(a, b):
    return dot(a, b, ((1,), (1,)))


def nn(a, b):
    return dot(a, b, ((1,), (0,)))


def block_of(tokens):
    return 256 if tokens % 256 == 0 else tokens


def masked(block, kept):
    return jnp.where(kept, block, -1e30)


def kept_keys(size):
    keys = lax.broadcasted_iota(jnp.int32, (size, size), 0)
    return keys <= lax.broadcasted_iota(jnp.int32, (size, size), 1)


def scores_of(keys, queries, j, size, kept):
    mine = queries[j * size : (j + 1) * size]
    diagonal = masked(nt(keys[j * size : (j + 1) * size], mine), kept)
    if j == 0:
        return [diagonal]
    return [nt(keys[: j * size], mine), diagonal]


def exponents(parts):
    top = functools.reduce(jnp.maximum, [jnp.max(p, axis=0, keepdims=True) for p in parts])
    exps = [jnp.exp2((p - top) * (SCALE * LOG2E)) for p in parts]
    total = sum(jnp.sum(e, axis=0, keepdims=True) for e in exps)
    return exps, total


def stacked(parts):
    return parts[0] if len(parts) == 1 else jnp.concatenate(parts, axis=0)


def normed_head(x, factor, gain_q, gain_k):
    wide = x.astype(F32)
    normed = wide * factor
    return wide, (normed * gain_q).astype(BF16), (normed * gain_k).astype(BF16), normed.astype(BF16)


def column_of(row):
    return jnp.broadcast_to(row, (HDIM, row.shape[1])).T[:, 0:1]


def inverse_rms(total, width_all):
    return lax.rsqrt(total / width_all + EPSILON)


def lanes_of(start, size):
    return (slice(None), slice(start, start + size))


def compiler(limit):
    return pltpu.CompilerParams(vmem_limit_bytes=limit)


IN_VMEM = pl.BlockSpec(memory_space=pltpu.VMEM)
ANYWHERE = pl.BlockSpec(memory_space=pl.ANY)
IN_HBM = pl.BlockSpec(memory_space=pltpu.HBM)


def in_hbm(x):
    return pltpu.with_memory_space_constraint(x, pltpu.HBM)


def forward_kernel(heads, width_all, x_ref, t_ref, gq_ref, gk_ref, *rest):
    o_ref = rest[-1]
    tokens = x_ref.shape[0]
    size = block_of(tokens)
    kept = kept_keys(size)
    factor = column_of(inverse_rms(t_ref[0:1, :], width_all))
    for h in range(heads):
        lanes = slice(h * HDIM, (h + 1) * HDIM)
        wide, q, k, v = normed_head(x_ref[:, lanes], factor, gq_ref[:, lanes], gk_ref[:, lanes])
        vt = v.T
        for j in range(tokens // size):
            exps, total = exponents(scores_of(k, q, j, size, kept))
            mixed = nn(vt[:, : (j + 1) * size], stacked(exps).astype(BF16)) * (1.0 / total)
            rows = slice(j * size, (j + 1) * size)
            o_ref[rows, lanes] = (wide[rows] + mixed.T).astype(BF16)


def forward(width_all, x, totals, gain_q, gain_k, heads, after=()):
    tokens, width = x.shape
    lanes = heads * HDIM
    block = pl.BlockSpec((tokens, lanes), lambda i: (0, i))
    gain = pl.BlockSpec((1, lanes), lambda i: (0, i))
    return pl.pallas_call(
        functools.partial(forward_kernel, heads, width_all),
        out_shape=jax.ShapeDtypeStruct(x.shape, BF16),
        grid=(width // lanes,),
        in_specs=[block, pl.BlockSpec(totals.shape, lambda i: (0, 0)), gain, gain] + [IN_HBM] * len(after),
        out_specs=block,
        compiler_params=compiler(VMEM),
        name="forward",
    )(in_hbm(x), totals, gain_q, gain_k, *map(in_hbm, after))


def backward_head(x, g, factor, gain_q, gain_k):
    tokens = x.shape[0]
    size = block_of(tokens)
    kept = kept_keys(size)
    wide, q, k, v = normed_head(x, factor, gain_q, gain_k)
    kt = k.T
    blocks = tokens // size
    d_q = []
    d_k = [None] * blocks
    d_v = [None] * blocks
    for j in range(blocks):
        rows = slice(j * size, (j + 1) * size)
        exps, total = exponents(scores_of(k, q, j, size, kept))
        inverse = 1.0 / total
        weights = [e * inverse for e in exps]
        grads = [nt(v[: j * size], g[rows])] if j else []
        grads.append(nt(v[rows], g[rows]))
        delta = sum(jnp.sum(w * d, axis=0, keepdims=True) for w, d in zip(weights, grads))
        scores = stacked([(w * ((d - delta) * SCALE)).astype(BF16) for w, d in zip(weights, grads)])
        rounded = stacked([w.astype(BF16) for w in weights])
        d_q.append(nn(kt[:, : (j + 1) * size], scores).T)
        part_k = nn(scores, q[rows])
        part_v = nn(rounded, g[rows])
        for i in range(j + 1):
            mine = slice(i * size, (i + 1) * size)
            d_k[i] = part_k[mine] if d_k[i] is None else d_k[i] + part_k[mine]
            d_v[i] = part_v[mine] if d_v[i] is None else d_v[i] + part_v[mine]
    d_normed = stacked(d_q) * gain_q + stacked(d_k) * gain_k + stacked(d_v)
    return wide, d_normed


def backward_kernel(
    first, base, found, width_all, evicted_ref, own_ref, g_ref, t_ref, held_ref, gq_ref, gk_ref, past_ref, *refs
):
    evicted = evicted_ref[0] == 1
    heads = len(found)
    ahead = first < base
    if ahead:
        outs, inner_ref, xs, gs, x_sem, g_sem = refs[-6:]
    else:
        a_out, x_out, inner_ref, xs, gs, outs, x_sem, g_sem, a_sem, out_sem = refs[-10:]
    copies = []
    for h, (p, lane) in enumerate(found):
        to = lanes_of(h * HDIM, HDIM)
        there = lanes_of(first + h * HDIM, HDIM)
        far = pltpu.make_async_copy(refs[p].at[: t_ref.shape[1], lane : lane + HDIM], xs.at[to], x_sem.at[h])
        near = pltpu.make_async_copy(own_ref.at[(0, 0) + there], xs.at[to], x_sem.at[h])
        g = pltpu.make_async_copy(g_ref.at[(0,) + there], gs.at[to], g_sem.at[h])
        pl.when(evicted)(far.start)
        pl.when(jnp.logical_not(evicted))(near.start)
        g.start()
        copies.append((far, near, g))
    factor = column_of(inverse_rms(total_of(evicted_ref, t_ref, held_ref), width_all))
    part = None
    sent = []
    for h in range(heads):
        far, near, copy = copies[h]
        pl.when(evicted)(far.wait)
        pl.when(jnp.logical_not(evicted))(near.wait)
        copy.wait()
        mine = lanes_of(h * HDIM, HDIM)
        there = lanes_of(first + h * HDIM, HDIM)
        g = gs[mine]
        wide, d_normed = backward_head(xs[mine], g, factor, gq_ref[there], gk_ref[there])
        term = g.astype(F32) + factor * d_normed
        if ahead:
            outs[mine] = term.astype(BF16)
            outs[lanes_of((heads + h) * HDIM, HDIM)] = xs[mine]
        else:
            outs[mine] = term
            to = lanes_of(first - base + h * HDIM, HDIM)
            sent.append(pltpu.make_async_copy(outs.at[mine], a_out.at[to], a_sem.at[h]))
            sent.append(pltpu.make_async_copy(xs.at[mine], x_out.at[to], out_sem.at[h]))
            for copy in sent[-2:]:
                copy.start()
        product = d_normed * wide
        part = product if part is None else part + product
    inner_ref[...] = jnp.sum(part.T, axis=0, keepdims=True) + past_ref[...]
    for copy in sent:
        copy.wait()


def total_of(evicted_ref, t_ref, held_ref):
    return jnp.where(evicted_ref[0] == 1, held_ref[...], t_ref[1:2, :])


def backward(
    width_all, evicted, stash, g, totals, held, gain_q, gain_k, past, far, found, first, base, sofar=(), after=()
):
    tokens, width = totals.shape[1], gain_q.shape[1]
    heads = len(found)
    small = (tokens, heads * HDIM)
    dma = pltpu.SemaphoreType.DMA((heads,))
    inner = jax.ShapeDtypeStruct((1, tokens), F32)
    if first < base:
        shapes = (jax.ShapeDtypeStruct((tokens, 2 * heads * HDIM), BF16), inner)
        scratch = [pltpu.VMEM(small, BF16)] * 2 + [dma] * 2
    else:
        shapes = (pltpu.HBM((tokens, width - base), F32), pltpu.HBM((tokens, width - base), BF16), inner)
        scratch = [pltpu.VMEM(small, BF16)] * 2 + [pltpu.VMEM(small, F32)] + [dma] * 4
    return pl.pallas_call(
        functools.partial(backward_kernel, first, base, found, width_all),
        out_shape=shapes,
        in_specs=[pl.BlockSpec(memory_space=pltpu.SMEM)] + [ANYWHERE] * 2 + [IN_VMEM] * 5
        + [ANYWHERE] * len(far) + [IN_HBM] * len(sofar) + [ANYWHERE] * len(after),
        out_specs=(IN_VMEM,) * 2 if first < base else (IN_HBM, IN_HBM, IN_VMEM),
        input_output_aliases={8 + len(far): 0, 9 + len(far): 1} if sofar else {},
        scratch_shapes=scratch,
        compiler_params=compiler(VMEM),
        name="backward",
    )(evicted, in_hbm(stash), in_hbm(g), totals, held, gain_q, gain_k, past, *far, *sofar, *after)


def row_of(total, inner, width_all):
    return inverse_rms(total, width_all) ** 3 * inner / width_all


def finish_kernel(
    first, width_all, evicted_ref, a_ref, x_ref, t_ref, held_ref, inner_ref, o_ref, row_ref, terms, xs, a_sem, x_sem
):
    heads = o_ref.shape[1] // HDIM
    copies = []
    for h in range(heads):
        mine = lanes_of(h * HDIM, HDIM)
        there = lanes_of(first + h * HDIM, HDIM)
        copies.append(
            (
                pltpu.make_async_copy(a_ref.at[there], terms.at[mine], a_sem.at[h]),
                pltpu.make_async_copy(x_ref.at[there], xs.at[mine], x_sem.at[h]),
            )
        )
        for copy in copies[-1]:
            copy.start()
    row = row_of(total_of(evicted_ref, t_ref, held_ref), inner_ref[...], width_all)
    row_ref[...] = row
    column = column_of(row)
    for h in range(heads):
        mine = lanes_of(h * HDIM, HDIM)
        for copy in copies[h]:
            copy.wait()
        o_ref[mine] = (terms[mine] - xs[mine].astype(F32) * column).astype(BF16)


def finish(width_all, evicted, a, x, totals, held, inner, first, last):
    shape = (a.shape[0], last - first)
    dma = pltpu.SemaphoreType.DMA(((last - first) // HDIM,))
    return pl.pallas_call(
        functools.partial(finish_kernel, first, width_all),
        out_shape=(jax.ShapeDtypeStruct(shape, BF16), jax.ShapeDtypeStruct((1, a.shape[0]), F32)),
        in_specs=[pl.BlockSpec(memory_space=pltpu.SMEM)] + [IN_HBM] * 2 + [IN_VMEM] * 3,
        out_specs=(IN_VMEM, IN_VMEM),
        scratch_shapes=[pltpu.VMEM(shape, F32), pltpu.VMEM(shape, BF16), dma, dma],
        compiler_params=compiler(VMEM),
        name="finish",
    )(evicted, in_hbm(a), in_hbm(x), totals, held, inner)


def place_kernel(pair_ref, row_ref, *refs):
    rest_refs, (o_ref, outs, sems) = refs[:-3], refs[-3:]
    lanes = outs.shape[1]
    ahead = lanes // HDIM
    copies, at = [], lanes
    for i, ref in enumerate(rest_refs):
        copies.append(pltpu.make_async_copy(ref, o_ref.at[lanes_of(at, ref.shape[1])], sems.at[ahead + i]))
        copies[-1].start()
        at += ref.shape[1]
    row = column_of(row_ref[...])
    for h in range(ahead):
        mine = lanes_of(h * HDIM, HDIM)
        x = pair_ref[lanes_of(lanes + h * HDIM, HDIM)]
        outs[mine] = (pair_ref[mine].astype(F32) - x.astype(F32) * row).astype(BF16)
        copies.append(pltpu.make_async_copy(outs.at[mine], o_ref.at[mine], sems.at[h]))
        copies[-1].start()
    for copy in copies:
        copy.wait()


def place(pair, row, *rest):
    tokens, lanes = pair.shape[0], pair.shape[1] // 2
    return pl.pallas_call(
        place_kernel,
        out_shape=jax.ShapeDtypeStruct((tokens, lanes + sum(r.shape[1] for r in rest)), BF16),
        in_specs=[IN_VMEM] * (2 + len(rest)),
        out_specs=ANYWHERE,
        scratch_shapes=[pltpu.VMEM((tokens, lanes), BF16), pltpu.SemaphoreType.DMA((lanes // HDIM + len(rest),))],
        compiler_params=compiler(VMEM),
        name="place",
    )(pair, row, *rest)


def hold_kernel(x_ref, *rest):
    pass


def hold(x, after):
    return pl.pallas_call(
        hold_kernel,
        out_shape=jax.ShapeDtypeStruct(x.shape, x.dtype),
        in_specs=[IN_VMEM] + [ANYWHERE] * len(after),
        out_specs=IN_VMEM,
        input_output_aliases={0: 0},
        compiler_params=compiler(VMEM),
        name="hold",
    )(x, *after)


def squares_kernel(current_ref, stash_ref, *rest):
    rows_ref, sums = rest[-2:]
    step = pl.program_id(0)

    def total(x):
        wide = x.astype(F32)
        square = wide * wide
        return sum(square[:, i : i + HDIM] for i in range(0, square.shape[1], HDIM))

    for i, x in enumerate((current_ref[...], stash_ref[0], stash_ref[1])):
        part = total(x)

        @pl.when(step == 0)
        def _():
            sums[i] = part

        @pl.when(step > 0)
        def _():
            sums[i] += part

    @pl.when(step == pl.num_programs(0) - 1)
    def _():
        for i in range(3):
            rows_ref[i : i + 1, :] = jnp.sum(sums[i].T, axis=0, keepdims=True)


def squares(current, stash, lanes, after=()):
    tokens, width = current.shape
    return pl.pallas_call(
        squares_kernel,
        out_shape=jax.ShapeDtypeStruct((3, tokens), F32),
        grid=(width // lanes,),
        in_specs=[
            pl.BlockSpec((tokens, lanes), lambda i: (0, i)),
            pl.BlockSpec((None, 2, tokens, lanes), lambda i: (0, 0, 0, i)),
        ] + [ANYWHERE] * len(after),
        out_specs=pl.BlockSpec((3, tokens), lambda i: (0, 0)),
        scratch_shapes=[pltpu.VMEM((3, tokens, HDIM), F32)],
        compiler_params=compiler(MOST),
        name="squares",
    )(in_hbm(current), in_hbm(stash), *after)


def piece_kernel(starts, sizes, stash_ref, *rest):
    outs, mark, sems = rest[-2 - len(sizes) : -2], rest[-2], rest[-1]
    mark[...] = jnp.zeros_like(mark)
    copies = [
        pltpu.make_async_copy(stash_ref.at[(0, 1) + lanes_of(start, size)], out, sems.at[i])
        for i, (start, size, out) in enumerate(zip(starts, sizes, outs))
    ]
    for copy in copies:
        copy.start()
    for copy in copies:
        copy.wait()


def pieces_of(stash, starts, sizes, after=()):
    tokens = stash.shape[2]
    return pl.pallas_call(
        functools.partial(piece_kernel, starts, sizes),
        out_shape=[jax.ShapeDtypeStruct((tokens, size), BF16) for size in sizes] + [jax.ShapeDtypeStruct((8, HDIM), F32)],
        in_specs=[IN_HBM] + [ANYWHERE] * len(after),
        out_specs=[IN_VMEM] * (len(sizes) + 1),
        scratch_shapes=[pltpu.SemaphoreType.DMA((len(sizes),))],
        compiler_params=compiler(VMEM),
        name="pieces",
    )(in_hbm(stash), *after)


def in_rows(row, size):
    tokens = row.shape[1]
    rows = []
    for _ in range(3):
        term = row.astype(BF16)
        row = row - term.astype(F32)
        rows += [term[:, i : i + size] for i in range(0, tokens, size)]
    fill = -len(rows) % 16
    return jnp.concatenate(rows + [jnp.zeros((fill, size), BF16)] * (fill > 0), axis=0)


def row_kernel(extra_ref, o_ref):
    tokens, size = o_ref.shape[1], extra_ref.shape[1]
    each = tokens // size
    extra = extra_ref[...].astype(F32)
    for i in range(each):
        o_ref[:, i * size : (i + 1) * size] = sum(extra[p * each + i : p * each + i + 1] for p in range(3))


def row_from(piece, tokens):
    extra = piece.shape[0] - tokens
    size = piece.shape[1]
    return pl.pallas_call(
        row_kernel,
        out_shape=jax.ShapeDtypeStruct((1, tokens), F32),
        grid=(1,),
        in_specs=[pl.BlockSpec((extra, size), lambda i: (tokens // extra, 0))],
        out_specs=pl.BlockSpec((1, tokens), lambda i: (0, 0)),
        compiler_params=compiler(VMEM),
        name="row",
    )(piece)


def piece_and_row_kernel(start, stash_ref, t_ref, *rest):
    out, sem = rest[-2:]
    tokens, size = stash_ref.shape[2], out.shape[1]
    copy = pltpu.make_async_copy(stash_ref.at[(0, 1) + lanes_of(start, size)], out.at[:tokens, :], sem.at[0])
    copy.start()
    out[tokens:, :] = in_rows(t_ref[2:3, :], size)
    copy.wait()


def piece_and_row(stash, totals, start, size, after):
    tokens = stash.shape[2]
    extra = -(-3 * tokens // size // 16) * 16
    return pl.pallas_call(
        functools.partial(piece_and_row_kernel, start),
        out_shape=jax.ShapeDtypeStruct((tokens + extra, size), BF16),
        in_specs=[IN_HBM, IN_VMEM] + [ANYWHERE] * len(after),
        out_specs=IN_VMEM,
        scratch_shapes=[pltpu.SemaphoreType.DMA((1,))],
        compiler_params=compiler(VMEM),
        name="piece_and_row",
    )(in_hbm(stash), totals, *after)


def send(x, pairs):
    return lax.ppermute(x, "section", pairs)


def local(width_all, layer_input, grad_input, stashed, eviction, query_gain, key_gain):
    n = lax.axis_size("section")
    partner = [(s, (s + n // 2) % n) for s in range(n)]
    prior = [(s, (s - 1) % n) for s in range(n)]
    current = layer_input[0]
    tokens, width = current.shape
    count = width // HDIM
    each = max(1, count // 6)
    pieces = count // each
    size = each * HDIM
    third = count // 3 * HDIM

    *away, mark = pieces_of(stashed, (0, size), (size, size))
    fetched = [send(x, partner) for x in away]
    totals = lax.psum(squares(current, stashed, third, (mark,)), "tensor")
    output = forward(width_all, current, totals, query_gain, key_gain, third // HDIM)

    def fetch(p, after):
        away, mark = pieces_of(stashed, (p * size,), (size,), (fetched[p - 2], after))
        fetched.append(send(away, partner))
        return mark

    fetched.append(send(piece_and_row(stashed, totals, 2 * size, size, (fetched[0],)), partner))
    held = row_from(fetched[2], tokens)
    marks = [fetch(p, in_hbm(output)) for p in range(3, min(5, pieces))]
    base = max(1, count // 4) * HDIM

    def share(inner, first, last, sofar, after):
        heads = range(first // HDIM, last // HDIM)
        used = sorted({h // each for h in heads})
        found = tuple((used.index(h // each), h % each * HDIM) for h in heads)
        return backward(
            width_all, eviction, stashed, grad_input, totals, held, query_gain, key_gain, inner,
            [fetched[p] for p in used], found, first, base, sofar, after,
        )

    pair, inner = share(jnp.zeros((1, tokens), F32), 0, base, (), (in_hbm(output), *marks))
    marks = []
    sofar, inners = (), [inner]
    ends = sorted({base, max(base, 3 * size), min(4, pieces) * size, width})
    for first, last in zip(ends[:-1], ends[1:]):
        *sofar, inner = share(inner, first, last, tuple(sofar), tuple(marks))
        inners.append(inner)
        marks = [fetch(p, inner) for p in range(len(fetched), pieces)]
    pair = send(hold(pair, (inners[-2],)), prior)
    inner = lax.psum(inner, "tensor")
    left = width - base
    cut = (left // HDIM + 1) // 2 * HDIM
    ends = (*sofar, totals, held, inner)
    early, row = finish(width_all, eviction, *ends, 0, cut)
    early = send(early, prior)
    late, _ = finish(width_all, eviction, *ends, cut, left)
    result = place(pair, send(row, prior), early, send(late, prior))
    return (output[None], result[None])


def solution(mesh):
    placed = (
        P("section", None, "tensor"),
        P("section", None, "tensor"),
        P("section", None, None, "tensor"),
        P("section"),
        P("section", "tensor"),
        P("section", "tensor"),
    )

    def whole(layer_input, *others):
        return jax.shard_map(
            functools.partial(local, layer_input.shape[-1]),
            mesh=mesh,
            in_specs=placed,
            out_specs=(P("section", None, "tensor"), P("section", None, "tensor")),
            check_vma=False,
        )(layer_input, *others)

    return whole
```

```python
import functools
import math

import jax
import jax.numpy as jnp
from jax import lax
from jax.experimental import pallas as pl
from jax.experimental.pallas import tpu as pltpu
from jax.sharding import PartitionSpec as P

HDIM = 128
EPSILON = 1e-05
SCALE = 1.0 / math.sqrt(HDIM)
LOG2E = math.log2(math.e)
VMEM = 32 * 1024 * 1024
MOST = 60 * 1024 * 1024

F32 = jnp.float32
BF16 = jnp.bfloat16


def dot(a, b, contract):
    return lax.dot_general(a, b, ((contract[0], contract[1]), ((), ())), preferred_element_type=F32)


def nt(a, b):
    return dot(a, b, ((1,), (1,)))


def nn(a, b):
    return dot(a, b, ((1,), (0,)))


def block_of(tokens):
    return 256 if tokens % 256 == 0 else tokens


def masked(block, kept):
    return jnp.where(kept, block, -1e30)


def kept_keys(size):
    keys = lax.broadcasted_iota(jnp.int32, (size, size), 0)
    return keys <= lax.broadcasted_iota(jnp.int32, (size, size), 1)


def scores_of(keys, queries, j, size, kept):
    mine = queries[j * size : (j + 1) * size]
    diagonal = masked(nt(keys[j * size : (j + 1) * size], mine), kept)
    if j == 0:
        return [diagonal]
    return [nt(keys[: j * size], mine), diagonal]


def exponents(parts):
    top = functools.reduce(jnp.maximum, [jnp.max(p, axis=0, keepdims=True) for p in parts])
    exps = [jnp.exp2((p - top) * (SCALE * LOG2E)) for p in parts]
    total = sum(jnp.sum(e, axis=0, keepdims=True) for e in exps)
    return exps, total


def stacked(parts):
    return parts[0] if len(parts) == 1 else jnp.concatenate(parts, axis=0)


def normed_head(x, factor, gain_q, gain_k):
    wide = x.astype(F32)
    normed = wide * factor
    return wide, (normed * gain_q).astype(BF16), (normed * gain_k).astype(BF16), normed.astype(BF16)


def column_of(row):
    return jnp.broadcast_to(row, (HDIM, row.shape[1])).T[:, 0:1]


def inverse_rms(total, width_all):
    return lax.rsqrt(total / width_all + EPSILON)


def lanes_of(start, size):
    return (slice(None), slice(start, start + size))


def compiler(limit):
    return pltpu.CompilerParams(vmem_limit_bytes=limit)


IN_VMEM = pl.BlockSpec(memory_space=pltpu.VMEM)
ANYWHERE = pl.BlockSpec(memory_space=pl.ANY)
IN_HBM = pl.BlockSpec(memory_space=pltpu.HBM)


def in_hbm(x):
    return pltpu.with_memory_space_constraint(x, pltpu.HBM)


def forward_kernel(heads, width_all, x_ref, t_ref, gq_ref, gk_ref, *rest):
    o_ref = rest[-1]
    tokens = x_ref.shape[0]
    size = block_of(tokens)
    kept = kept_keys(size)
    factor = column_of(inverse_rms(t_ref[0:1, :], width_all))
    for h in range(heads):
        lanes = slice(h * HDIM, (h + 1) * HDIM)
        wide, q, k, v = normed_head(x_ref[:, lanes], factor, gq_ref[:, lanes], gk_ref[:, lanes])
        vt = v.T
        for j in range(tokens // size):
            exps, total = exponents(scores_of(k, q, j, size, kept))
            mixed = nn(vt[:, : (j + 1) * size], stacked(exps).astype(BF16)) * (1.0 / total)
            rows = slice(j * size, (j + 1) * size)
            o_ref[rows, lanes] = (wide[rows] + mixed.T).astype(BF16)


def forward(width_all, x, totals, gain_q, gain_k, heads, after=()):
    tokens, width = x.shape
    lanes = heads * HDIM
    block = pl.BlockSpec((tokens, lanes), lambda i: (0, i))
    gain = pl.BlockSpec((1, lanes), lambda i: (0, i))
    return pl.pallas_call(
        functools.partial(forward_kernel, heads, width_all),
        out_shape=jax.ShapeDtypeStruct(x.shape, BF16),
        grid=(width // lanes,),
        in_specs=[block, pl.BlockSpec(totals.shape, lambda i: (0, 0)), gain, gain] + [IN_HBM] * len(after),
        out_specs=block,
        compiler_params=compiler(VMEM),
        name="forward",
    )(in_hbm(x), totals, gain_q, gain_k, *map(in_hbm, after))


def backward_head(x, g, factor, gain_q, gain_k):
    tokens = x.shape[0]
    size = block_of(tokens)
    kept = kept_keys(size)
    wide, q, k, v = normed_head(x, factor, gain_q, gain_k)
    kt = k.T
    blocks = tokens // size
    d_q = []
    d_k = [None] * blocks
    d_v = [None] * blocks
    for j in range(blocks):
        rows = slice(j * size, (j + 1) * size)
        exps, total = exponents(scores_of(k, q, j, size, kept))
        inverse = 1.0 / total
        weights = [e * inverse for e in exps]
        grads = [nt(v[: j * size], g[rows])] if j else []
        grads.append(nt(v[rows], g[rows]))
        delta = sum(jnp.sum(w * d, axis=0, keepdims=True) for w, d in zip(weights, grads))
        scores = stacked([(w * (d - delta)).astype(BF16) for w, d in zip(weights, grads)])
        rounded = stacked([w.astype(BF16) for w in weights])
        d_q.append(nn(kt[:, : (j + 1) * size], scores).T)
        part_k = nn(scores, q[rows])
        part_v = nn(rounded, g[rows])
        for i in range(j + 1):
            mine = slice(i * size, (i + 1) * size)
            d_k[i] = part_k[mine] if d_k[i] is None else d_k[i] + part_k[mine]
            d_v[i] = part_v[mine] if d_v[i] is None else d_v[i] + part_v[mine]
    d_normed = stacked(d_q) * (gain_q * SCALE) + stacked(d_k) * (gain_k * SCALE) + stacked(d_v)
    return wide, d_normed


def backward_kernel(
    first, base, found, width_all, evicted_ref, own_ref, g_ref, t_ref, held_ref, gq_ref, gk_ref, past_ref, *refs
):
    evicted = evicted_ref[0] == 1
    heads = len(found)
    ahead = first < base
    if ahead:
        outs, inner_ref, xs, gs, x_sem, g_sem = refs[-6:]
    else:
        a_out, x_out, inner_ref, xs, gs, outs, x_sem, g_sem, a_sem, out_sem = refs[-10:]
    copies = []
    for h, (p, lane) in enumerate(found):
        to = lanes_of(h * HDIM, HDIM)
        there = lanes_of(first + h * HDIM, HDIM)
        far = pltpu.make_async_copy(refs[p].at[: t_ref.shape[1], lane : lane + HDIM], xs.at[to], x_sem.at[h])
        near = pltpu.make_async_copy(own_ref.at[(0, 0) + there], xs.at[to], x_sem.at[h])
        g = pltpu.make_async_copy(g_ref.at[(0,) + there], gs.at[to], g_sem.at[h])
        pl.when(evicted)(far.start)
        pl.when(jnp.logical_not(evicted))(near.start)
        g.start()
        copies.append((far, near, g))
    factor = column_of(inverse_rms(total_of(evicted_ref, t_ref, held_ref), width_all))
    part = None
    sent = []
    for h in range(heads):
        far, near, copy = copies[h]
        pl.when(evicted)(far.wait)
        pl.when(jnp.logical_not(evicted))(near.wait)
        copy.wait()
        mine = lanes_of(h * HDIM, HDIM)
        there = lanes_of(first + h * HDIM, HDIM)
        g = gs[mine]
        wide, d_normed = backward_head(xs[mine], g, factor, gq_ref[there], gk_ref[there])
        term = g.astype(F32) + factor * d_normed
        if ahead:
            outs[mine] = term.astype(BF16)
            outs[lanes_of((heads + h) * HDIM, HDIM)] = xs[mine]
        else:
            outs[mine] = term
            to = lanes_of(first - base + h * HDIM, HDIM)
            sent.append(pltpu.make_async_copy(outs.at[mine], a_out.at[to], a_sem.at[h]))
            sent.append(pltpu.make_async_copy(xs.at[mine], x_out.at[to], out_sem.at[h]))
            for copy in sent[-2:]:
                copy.start()
        product = d_normed * wide
        part = product if part is None else part + product
    inner_ref[...] = jnp.sum(part.T, axis=0, keepdims=True) + past_ref[...]
    for copy in sent:
        copy.wait()


def total_of(evicted_ref, t_ref, held_ref):
    return jnp.where(evicted_ref[0] == 1, held_ref[...], t_ref[1:2, :])


def backward(
    width_all, evicted, stash, g, totals, held, gain_q, gain_k, past, far, found, first, base, sofar=(), after=()
):
    tokens, width = totals.shape[1], gain_q.shape[1]
    heads = len(found)
    small = (tokens, heads * HDIM)
    dma = pltpu.SemaphoreType.DMA((heads,))
    inner = jax.ShapeDtypeStruct((1, tokens), F32)
    if first < base:
        shapes = (jax.ShapeDtypeStruct((tokens, 2 * heads * HDIM), BF16), inner)
        scratch = [pltpu.VMEM(small, BF16)] * 2 + [dma] * 2
    else:
        shapes = (pltpu.HBM((tokens, width - base), F32), pltpu.HBM((tokens, width - base), BF16), inner)
        scratch = [pltpu.VMEM(small, BF16)] * 2 + [pltpu.VMEM(small, F32)] + [dma] * 4
    return pl.pallas_call(
        functools.partial(backward_kernel, first, base, found, width_all),
        out_shape=shapes,
        in_specs=[pl.BlockSpec(memory_space=pltpu.SMEM)] + [ANYWHERE] * 2 + [IN_VMEM] * 5
        + [ANYWHERE] * len(far) + [IN_HBM] * len(sofar) + [ANYWHERE] * len(after),
        out_specs=(IN_VMEM,) * 2 if first < base else (IN_HBM, IN_HBM, IN_VMEM),
        input_output_aliases={8 + len(far): 0, 9 + len(far): 1} if sofar else {},
        scratch_shapes=scratch,
        compiler_params=compiler(VMEM),
        name="backward",
    )(evicted, in_hbm(stash), in_hbm(g), totals, held, gain_q, gain_k, past, *far, *sofar, *after)


def row_of(total, inner, width_all):
    return inverse_rms(total, width_all) ** 3 * inner / width_all


def finish_kernel(
    first, width_all, evicted_ref, a_ref, x_ref, t_ref, held_ref, inner_ref, o_ref, row_ref, terms, xs, a_sem, x_sem
):
    heads = o_ref.shape[1] // HDIM
    copies = []
    for h in range(heads):
        mine = lanes_of(h * HDIM, HDIM)
        there = lanes_of(first + h * HDIM, HDIM)
        copies.append(
            (
                pltpu.make_async_copy(a_ref.at[there], terms.at[mine], a_sem.at[h]),
                pltpu.make_async_copy(x_ref.at[there], xs.at[mine], x_sem.at[h]),
            )
        )
        for copy in copies[-1]:
            copy.start()
    row = row_of(total_of(evicted_ref, t_ref, held_ref), inner_ref[...], width_all)
    row_ref[...] = row
    column = column_of(row)
    for h in range(heads):
        mine = lanes_of(h * HDIM, HDIM)
        for copy in copies[h]:
            copy.wait()
        o_ref[mine] = (terms[mine] - xs[mine].astype(F32) * column).astype(BF16)


def finish(width_all, evicted, a, x, totals, held, inner, first, last):
    shape = (a.shape[0], last - first)
    dma = pltpu.SemaphoreType.DMA(((last - first) // HDIM,))
    return pl.pallas_call(
        functools.partial(finish_kernel, first, width_all),
        out_shape=(jax.ShapeDtypeStruct(shape, BF16), jax.ShapeDtypeStruct((1, a.shape[0]), F32)),
        in_specs=[pl.BlockSpec(memory_space=pltpu.SMEM)] + [IN_HBM] * 2 + [IN_VMEM] * 3,
        out_specs=(IN_VMEM, IN_VMEM),
        scratch_shapes=[pltpu.VMEM(shape, F32), pltpu.VMEM(shape, BF16), dma, dma],
        compiler_params=compiler(VMEM),
        name="finish",
    )(evicted, in_hbm(a), in_hbm(x), totals, held, inner)


def place_kernel(pair_ref, row_ref, *refs):
    rest_refs, (o_ref, outs, sems) = refs[:-3], refs[-3:]
    lanes = outs.shape[1]
    ahead = lanes // HDIM
    copies, at = [], lanes
    for i, ref in enumerate(rest_refs):
        copies.append(pltpu.make_async_copy(ref, o_ref.at[lanes_of(at, ref.shape[1])], sems.at[ahead + i]))
        copies[-1].start()
        at += ref.shape[1]
    row = column_of(row_ref[...])
    for h in range(ahead):
        mine = lanes_of(h * HDIM, HDIM)
        x = pair_ref[lanes_of(lanes + h * HDIM, HDIM)]
        outs[mine] = (pair_ref[mine].astype(F32) - x.astype(F32) * row).astype(BF16)
        copies.append(pltpu.make_async_copy(outs.at[mine], o_ref.at[mine], sems.at[h]))
        copies[-1].start()
    for copy in copies:
        copy.wait()


def place(pair, row, *rest):
    tokens, lanes = pair.shape[0], pair.shape[1] // 2
    return pl.pallas_call(
        place_kernel,
        out_shape=jax.ShapeDtypeStruct((tokens, lanes + sum(r.shape[1] for r in rest)), BF16),
        in_specs=[IN_VMEM] * (2 + len(rest)),
        out_specs=ANYWHERE,
        scratch_shapes=[pltpu.VMEM((tokens, lanes), BF16), pltpu.SemaphoreType.DMA((lanes // HDIM + len(rest),))],
        compiler_params=compiler(VMEM),
        name="place",
    )(pair, row, *rest)


def hold_kernel(x_ref, *rest):
    pass


def hold(x, after):
    return pl.pallas_call(
        hold_kernel,
        out_shape=jax.ShapeDtypeStruct(x.shape, x.dtype),
        in_specs=[IN_VMEM] + [ANYWHERE] * len(after),
        out_specs=IN_VMEM,
        input_output_aliases={0: 0},
        compiler_params=compiler(VMEM),
        name="hold",
    )(x, *after)


def squares_kernel(current_ref, stash_ref, *rest):
    rows_ref, sums = rest[-2:]
    step = pl.program_id(0)

    def total(x):
        wide = x.astype(F32)
        square = wide * wide
        return sum(square[:, i : i + HDIM] for i in range(0, square.shape[1], HDIM))

    for i, x in enumerate((current_ref[...], stash_ref[0], stash_ref[1])):
        part = total(x)

        @pl.when(step == 0)
        def _():
            sums[i] = part

        @pl.when(step > 0)
        def _():
            sums[i] += part

    @pl.when(step == pl.num_programs(0) - 1)
    def _():
        for i in range(3):
            rows_ref[i : i + 1, :] = jnp.sum(sums[i].T, axis=0, keepdims=True)


def squares(current, stash, lanes, after=()):
    tokens, width = current.shape
    return pl.pallas_call(
        squares_kernel,
        out_shape=jax.ShapeDtypeStruct((3, tokens), F32),
        grid=(width // lanes,),
        in_specs=[
            pl.BlockSpec((tokens, lanes), lambda i: (0, i)),
            pl.BlockSpec((None, 2, tokens, lanes), lambda i: (0, 0, 0, i)),
        ] + [ANYWHERE] * len(after),
        out_specs=pl.BlockSpec((3, tokens), lambda i: (0, 0)),
        scratch_shapes=[pltpu.VMEM((3, tokens, HDIM), F32)],
        compiler_params=compiler(MOST),
        name="squares",
    )(in_hbm(current), in_hbm(stash), *after)


def piece_kernel(starts, sizes, stash_ref, *rest):
    outs, mark, sems = rest[-2 - len(sizes) : -2], rest[-2], rest[-1]
    mark[...] = jnp.zeros_like(mark)
    copies = [
        pltpu.make_async_copy(stash_ref.at[(0, 1) + lanes_of(start, size)], out, sems.at[i])
        for i, (start, size, out) in enumerate(zip(starts, sizes, outs))
    ]
    for copy in copies:
        copy.start()
    for copy in copies:
        copy.wait()


def pieces_of(stash, starts, sizes, after=()):
    tokens = stash.shape[2]
    return pl.pallas_call(
        functools.partial(piece_kernel, starts, sizes),
        out_shape=[jax.ShapeDtypeStruct((tokens, size), BF16) for size in sizes] + [jax.ShapeDtypeStruct((8, HDIM), F32)],
        in_specs=[IN_HBM] + [ANYWHERE] * len(after),
        out_specs=[IN_VMEM] * (len(sizes) + 1),
        scratch_shapes=[pltpu.SemaphoreType.DMA((len(sizes),))],
        compiler_params=compiler(VMEM),
        name="pieces",
    )(in_hbm(stash), *after)


def in_rows(row, size):
    tokens = row.shape[1]
    rows = []
    for _ in range(3):
        term = row.astype(BF16)
        row = row - term.astype(F32)
        rows += [term[:, i : i + size] for i in range(0, tokens, size)]
    fill = -len(rows) % 16
    return jnp.concatenate(rows + [jnp.zeros((fill, size), BF16)] * (fill > 0), axis=0)


def row_kernel(extra_ref, o_ref):
    tokens, size = o_ref.shape[1], extra_ref.shape[1]
    each = tokens // size
    extra = extra_ref[...].astype(F32)
    for i in range(each):
        o_ref[:, i * size : (i + 1) * size] = sum(extra[p * each + i : p * each + i + 1] for p in range(3))


def row_from(piece, tokens):
    extra = piece.shape[0] - tokens
    size = piece.shape[1]
    return pl.pallas_call(
        row_kernel,
        out_shape=jax.ShapeDtypeStruct((1, tokens), F32),
        grid=(1,),
        in_specs=[pl.BlockSpec((extra, size), lambda i: (tokens // extra, 0))],
        out_specs=pl.BlockSpec((1, tokens), lambda i: (0, 0)),
        compiler_params=compiler(VMEM),
        name="row",
    )(piece)


def piece_and_row_kernel(start, stash_ref, t_ref, *rest):
    out, sem = rest[-2:]
    tokens, size = stash_ref.shape[2], out.shape[1]
    copy = pltpu.make_async_copy(stash_ref.at[(0, 1) + lanes_of(start, size)], out.at[:tokens, :], sem.at[0])
    copy.start()
    out[tokens:, :] = in_rows(t_ref[2:3, :], size)
    copy.wait()


def piece_and_row(stash, totals, start, size, after):
    tokens = stash.shape[2]
    extra = -(-3 * tokens // size // 16) * 16
    return pl.pallas_call(
        functools.partial(piece_and_row_kernel, start),
        out_shape=jax.ShapeDtypeStruct((tokens + extra, size), BF16),
        in_specs=[IN_HBM, IN_VMEM] + [ANYWHERE] * len(after),
        out_specs=IN_VMEM,
        scratch_shapes=[pltpu.SemaphoreType.DMA((1,))],
        compiler_params=compiler(VMEM),
        name="piece_and_row",
    )(in_hbm(stash), totals, *after)


def send(x, pairs):
    return lax.ppermute(x, "section", pairs)


def local(width_all, layer_input, grad_input, stashed, eviction, query_gain, key_gain):
    n = lax.axis_size("section")
    partner = [(s, (s + n // 2) % n) for s in range(n)]
    prior = [(s, (s - 1) % n) for s in range(n)]
    current = layer_input[0]
    tokens, width = current.shape
    count = width // HDIM
    each = max(1, count // 6)
    pieces = count // each
    size = each * HDIM
    third = count // 3 * HDIM

    *away, mark = pieces_of(stashed, (0, size), (size, size))
    fetched = [send(x, partner) for x in away]
    totals = lax.psum(squares(current, stashed, third, (mark,)), "tensor")
    output = forward(width_all, current, totals, query_gain, key_gain, third // HDIM)

    def fetch(p, after):
        away, mark = pieces_of(stashed, (p * size,), (size,), (fetched[p - 2], after))
        fetched.append(send(away, partner))
        return mark

    fetched.append(send(piece_and_row(stashed, totals, 2 * size, size, (fetched[0],)), partner))
    held = row_from(fetched[2], tokens)
    marks = [fetch(p, in_hbm(output)) for p in range(3, min(5, pieces))]
    base = max(1, count // 4) * HDIM

    def share(inner, first, last, sofar, after):
        heads = range(first // HDIM, last // HDIM)
        used = sorted({h // each for h in heads})
        found = tuple((used.index(h // each), h % each * HDIM) for h in heads)
        return backward(
            width_all, eviction, stashed, grad_input, totals, held, query_gain, key_gain, inner,
            [fetched[p] for p in used], found, first, base, sofar, after,
        )

    pair, inner = share(jnp.zeros((1, tokens), F32), 0, base, (), (in_hbm(output), *marks))
    marks = []
    sofar, inners = (), [inner]
    ends = sorted({base, max(base, 3 * size), *(p * size for p in range(4, pieces + 1))})
    for first, last in zip(ends[:-1], ends[1:]):
        *sofar, inner = share(inner, first, last, tuple(sofar), tuple(marks))
        inners.append(inner)
        marks = [fetch(p, inner) for p in range(len(fetched), pieces)]
    pair = send(hold(pair, (inners[-2],)), prior)
    inner = lax.psum(inner, "tensor")
    left = width - base
    cut = (left // HDIM + 1) // 2 * HDIM
    ends = (*sofar, totals, held, inner)
    early, row = finish(width_all, eviction, *ends, 0, cut)
    early = send(early, prior)
    late, _ = finish(width_all, eviction, *ends, cut, left)
    result = place(pair, send(row, prior), early, send(late, prior))
    return (output[None], result[None])


def solution(mesh):
    placed = (
        P("section", None, "tensor"),
        P("section", None, "tensor"),
        P("section", None, None, "tensor"),
        P("section"),
        P("section", "tensor"),
        P("section", "tensor"),
    )

    def whole(layer_input, *others):
        return jax.shard_map(
            functools.partial(local, layer_input.shape[-1]),
            mesh=mesh,
            in_specs=placed,
            out_specs=(P("section", None, "tensor"), P("section", None, "tensor")),
            check_vma=False,
        )(layer_input, *others)

    return whole
```

```python
import functools
import math

import jax
import jax.numpy as jnp
from jax import lax
from jax.experimental import pallas as pl
from jax.experimental.pallas import tpu as pltpu
from jax.sharding import PartitionSpec as P

HDIM = 128
EPSILON = 1e-05
SCALE = 1.0 / math.sqrt(HDIM)
LOG2E = math.log2(math.e)
VMEM = 32 * 1024 * 1024
MOST = 60 * 1024 * 1024

F32 = jnp.float32
BF16 = jnp.bfloat16


def dot(a, b, contract):
    return lax.dot_general(a, b, ((contract[0], contract[1]), ((), ())), preferred_element_type=F32)


def nt(a, b):
    return dot(a, b, ((1,), (1,)))


def nn(a, b):
    return dot(a, b, ((1,), (0,)))


def block_of(tokens):
    return 256 if tokens % 256 == 0 else tokens


def masked(block, kept):
    return jnp.where(kept, block, -1e30)


def kept_keys(size):
    keys = lax.broadcasted_iota(jnp.int32, (size, size), 0)
    return keys <= lax.broadcasted_iota(jnp.int32, (size, size), 1)


def scores_of(keys, queries, j, size, kept):
    mine = queries[j * size : (j + 1) * size]
    diagonal = masked(nt(keys[j * size : (j + 1) * size], mine), kept)
    if j == 0:
        return [diagonal]
    return [nt(keys[: j * size], mine), diagonal]


def exponents(parts):
    top = functools.reduce(jnp.maximum, [jnp.max(p, axis=0, keepdims=True) for p in parts])
    exps = [jnp.exp2((p - top) * (SCALE * LOG2E)) for p in parts]
    total = sum(jnp.sum(e, axis=0, keepdims=True) for e in exps)
    return exps, total


def stacked(parts):
    return parts[0] if len(parts) == 1 else jnp.concatenate(parts, axis=0)


def normed_head(x, factor, gain_q, gain_k):
    wide = x.astype(F32)
    normed = wide * factor
    return wide, (normed * gain_q).astype(BF16), (normed * gain_k).astype(BF16), normed.astype(BF16)


def column_of(row):
    return jnp.broadcast_to(row, (HDIM, row.shape[1])).T[:, 0:1]


def inverse_rms(total, width_all):
    return lax.rsqrt(total / width_all + EPSILON)


def lanes_of(start, size):
    return (slice(None), slice(start, start + size))


def compiler(limit):
    return pltpu.CompilerParams(vmem_limit_bytes=limit)


IN_VMEM = pl.BlockSpec(memory_space=pltpu.VMEM)
ANYWHERE = pl.BlockSpec(memory_space=pl.ANY)
IN_HBM = pl.BlockSpec(memory_space=pltpu.HBM)


def in_hbm(x):
    return pltpu.with_memory_space_constraint(x, pltpu.HBM)


def forward_kernel(heads, width_all, x_ref, t_ref, gq_ref, gk_ref, *rest):
    o_ref = rest[-1]
    tokens = x_ref.shape[0]
    size = block_of(tokens)
    kept = kept_keys(size)
    factor = column_of(inverse_rms(t_ref[0:1, :], width_all))
    for h in range(heads):
        lanes = slice(h * HDIM, (h + 1) * HDIM)
        wide, q, k, v = normed_head(x_ref[:, lanes], factor, gq_ref[:, lanes], gk_ref[:, lanes])
        vt = v.T
        for j in range(tokens // size):
            exps, total = exponents(scores_of(k, q, j, size, kept))
            mixed = nn(vt[:, : (j + 1) * size], stacked(exps).astype(BF16)) * (1.0 / total)
            rows = slice(j * size, (j + 1) * size)
            o_ref[rows, lanes] = (wide[rows] + mixed.T).astype(BF16)


def forward(width_all, x, totals, gain_q, gain_k, heads, after=()):
    tokens, width = x.shape
    lanes = heads * HDIM
    block = pl.BlockSpec((tokens, lanes), lambda i: (0, i))
    gain = pl.BlockSpec((1, lanes), lambda i: (0, i))
    return pl.pallas_call(
        functools.partial(forward_kernel, heads, width_all),
        out_shape=jax.ShapeDtypeStruct(x.shape, BF16),
        grid=(width // lanes,),
        in_specs=[block, pl.BlockSpec(totals.shape, lambda i: (0, 0)), gain, gain] + [IN_HBM] * len(after),
        out_specs=block,
        compiler_params=compiler(VMEM),
        name="forward",
    )(in_hbm(x), totals, gain_q, gain_k, *map(in_hbm, after))


def backward_head(x, g, factor, gain_q, gain_k):
    tokens = x.shape[0]
    size = block_of(tokens)
    kept = kept_keys(size)
    wide, q, k, v = normed_head(x, factor, gain_q, gain_k)
    kt = k.T
    blocks = tokens // size
    d_q = []
    d_k = [None] * blocks
    d_v = [None] * blocks
    for j in range(blocks):
        rows = slice(j * size, (j + 1) * size)
        exps, total = exponents(scores_of(k, q, j, size, kept))
        inverse = 1.0 / total
        weights = [e * inverse for e in exps]
        grads = [nt(v[: j * size], g[rows])] if j else []
        grads.append(nt(v[rows], g[rows]))
        delta = sum(jnp.sum(w * d, axis=0, keepdims=True) for w, d in zip(weights, grads))
        scores = stacked([(w * (d - delta)).astype(BF16) for w, d in zip(weights, grads)])
        rounded = stacked([w.astype(BF16) for w in weights])
        d_q.append(nn(kt[:, : (j + 1) * size], scores).T)
        part_k = nn(scores, q[rows])
        part_v = nn(rounded, g[rows])
        for i in range(j + 1):
            mine = slice(i * size, (i + 1) * size)
            d_k[i] = part_k[mine] if d_k[i] is None else d_k[i] + part_k[mine]
            d_v[i] = part_v[mine] if d_v[i] is None else d_v[i] + part_v[mine]
    d_normed = stacked(d_q) * (gain_q * SCALE) + stacked(d_k) * (gain_k * SCALE) + stacked(d_v)
    return wide, d_normed


def backward_kernel(
    first, base, found, width_all, evicted_ref, own_ref, g_ref, t_ref, held_ref, gq_ref, gk_ref, past_ref, *refs
):
    evicted = evicted_ref[0] == 1
    heads = len(found)
    ahead = first < base
    if ahead:
        outs, inner_ref, xs, gs, x_sem, g_sem = refs[-6:]
    else:
        a_out, x_out, inner_ref, xs, gs, outs, x_sem, g_sem, a_sem, out_sem = refs[-10:]
    copies = []
    for h, (p, lane) in enumerate(found):
        to = lanes_of(h * HDIM, HDIM)
        there = lanes_of(first + h * HDIM, HDIM)
        far = pltpu.make_async_copy(refs[p].at[: t_ref.shape[1], lane : lane + HDIM], xs.at[to], x_sem.at[h])
        near = pltpu.make_async_copy(own_ref.at[(0, 0) + there], xs.at[to], x_sem.at[h])
        g = pltpu.make_async_copy(g_ref.at[(0,) + there], gs.at[to], g_sem.at[h])
        pl.when(evicted)(far.start)
        pl.when(jnp.logical_not(evicted))(near.start)
        g.start()
        copies.append((far, near, g))
    factor = column_of(inverse_rms(total_of(evicted_ref, t_ref, held_ref), width_all))
    part = None
    sent = []
    for h in range(heads):
        far, near, copy = copies[h]
        pl.when(evicted)(far.wait)
        pl.when(jnp.logical_not(evicted))(near.wait)
        copy.wait()
        mine = lanes_of(h * HDIM, HDIM)
        there = lanes_of(first + h * HDIM, HDIM)
        g = gs[mine]
        wide, d_normed = backward_head(xs[mine], g, factor, gq_ref[there], gk_ref[there])
        term = g.astype(F32) + factor * d_normed
        if ahead:
            outs[mine] = term.astype(BF16)
            outs[lanes_of((heads + h) * HDIM, HDIM)] = xs[mine]
        else:
            outs[mine] = term
            to = lanes_of(first - base + h * HDIM, HDIM)
            sent.append(pltpu.make_async_copy(outs.at[mine], a_out.at[to], a_sem.at[h]))
            sent.append(pltpu.make_async_copy(xs.at[mine], x_out.at[to], out_sem.at[h]))
            for copy in sent[-2:]:
                copy.start()
        product = d_normed * wide
        part = product if part is None else part + product
    inner_ref[...] = jnp.sum(part.T, axis=0, keepdims=True) + past_ref[...]
    for copy in sent:
        copy.wait()


def total_of(evicted_ref, t_ref, held_ref):
    return jnp.where(evicted_ref[0] == 1, held_ref[...], t_ref[1:2, :])


def backward(
    width_all, evicted, stash, g, totals, held, gain_q, gain_k, past, far, found, first, base, sofar=(), after=()
):
    tokens, width = totals.shape[1], gain_q.shape[1]
    heads = len(found)
    small = (tokens, heads * HDIM)
    dma = pltpu.SemaphoreType.DMA((heads,))
    inner = jax.ShapeDtypeStruct((1, tokens), F32)
    if first < base:
        shapes = (jax.ShapeDtypeStruct((tokens, 2 * heads * HDIM), BF16), inner)
        scratch = [pltpu.VMEM(small, BF16)] * 2 + [dma] * 2
    else:
        shapes = (pltpu.HBM((tokens, width - base), F32), pltpu.HBM((tokens, width - base), BF16), inner)
        scratch = [pltpu.VMEM(small, BF16)] * 2 + [pltpu.VMEM(small, F32)] + [dma] * 4
    return pl.pallas_call(
        functools.partial(backward_kernel, first, base, found, width_all),
        out_shape=shapes,
        in_specs=[pl.BlockSpec(memory_space=pltpu.SMEM)] + [ANYWHERE] * 2 + [IN_VMEM] * 5
        + [ANYWHERE] * len(far) + [IN_HBM] * len(sofar) + [ANYWHERE] * len(after),
        out_specs=(IN_VMEM,) * 2 if first < base else (IN_HBM, IN_HBM, IN_VMEM),
        input_output_aliases={8 + len(far): 0, 9 + len(far): 1} if sofar else {},
        scratch_shapes=scratch,
        compiler_params=compiler(VMEM),
        name="backward",
    )(evicted, in_hbm(stash), in_hbm(g), totals, held, gain_q, gain_k, past, *far, *sofar, *after)


def row_of(total, inner, width_all):
    return inverse_rms(total, width_all) ** 3 * inner / width_all


def finish_kernel(
    first, width_all, evicted_ref, a_ref, x_ref, t_ref, held_ref, inner_ref, o_ref, row_ref, terms, xs, a_sem, x_sem
):
    heads = o_ref.shape[1] // HDIM
    copies = []
    for h in range(heads):
        mine = lanes_of(h * HDIM, HDIM)
        there = lanes_of(first + h * HDIM, HDIM)
        copies.append(
            (
                pltpu.make_async_copy(a_ref.at[there], terms.at[mine], a_sem.at[h]),
                pltpu.make_async_copy(x_ref.at[there], xs.at[mine], x_sem.at[h]),
            )
        )
        for copy in copies[-1]:
            copy.start()
    row = row_of(total_of(evicted_ref, t_ref, held_ref), inner_ref[...], width_all)
    row_ref[...] = row
    column = column_of(row)
    for h in range(heads):
        mine = lanes_of(h * HDIM, HDIM)
        for copy in copies[h]:
            copy.wait()
        o_ref[mine] = (terms[mine] - xs[mine].astype(F32) * column).astype(BF16)


def finish(width_all, evicted, a, x, totals, held, inner, first, last):
    shape = (a.shape[0], last - first)
    dma = pltpu.SemaphoreType.DMA(((last - first) // HDIM,))
    return pl.pallas_call(
        functools.partial(finish_kernel, first, width_all),
        out_shape=(jax.ShapeDtypeStruct(shape, BF16), jax.ShapeDtypeStruct((1, a.shape[0]), F32)),
        in_specs=[pl.BlockSpec(memory_space=pltpu.SMEM)] + [IN_HBM] * 2 + [IN_VMEM] * 3,
        out_specs=(IN_VMEM, IN_VMEM),
        scratch_shapes=[pltpu.VMEM(shape, F32), pltpu.VMEM(shape, BF16), dma, dma],
        compiler_params=compiler(VMEM),
        name="finish",
    )(evicted, in_hbm(a), in_hbm(x), totals, held, inner)


def place_kernel(pair_ref, row_ref, *refs):
    rest_refs, (o_ref, outs, sems) = refs[:-3], refs[-3:]
    lanes = outs.shape[1]
    ahead = lanes // HDIM
    copies, at = [], lanes
    for i, ref in enumerate(rest_refs):
        copies.append(pltpu.make_async_copy(ref, o_ref.at[lanes_of(at, ref.shape[1])], sems.at[ahead + i]))
        copies[-1].start()
        at += ref.shape[1]
    row = column_of(row_ref[...])
    for h in range(ahead):
        mine = lanes_of(h * HDIM, HDIM)
        x = pair_ref[lanes_of(lanes + h * HDIM, HDIM)]
        outs[mine] = (pair_ref[mine].astype(F32) - x.astype(F32) * row).astype(BF16)
        copies.append(pltpu.make_async_copy(outs.at[mine], o_ref.at[mine], sems.at[h]))
        copies[-1].start()
    for copy in copies:
        copy.wait()


def place(pair, row, *rest):
    tokens, lanes = pair.shape[0], pair.shape[1] // 2
    return pl.pallas_call(
        place_kernel,
        out_shape=jax.ShapeDtypeStruct((tokens, lanes + sum(r.shape[1] for r in rest)), BF16),
        in_specs=[IN_VMEM] * (2 + len(rest)),
        out_specs=ANYWHERE,
        scratch_shapes=[pltpu.VMEM((tokens, lanes), BF16), pltpu.SemaphoreType.DMA((lanes // HDIM + len(rest),))],
        compiler_params=compiler(VMEM),
        name="place",
    )(pair, row, *rest)


def hold_kernel(x_ref, *rest):
    pass


def hold(x, after):
    return pl.pallas_call(
        hold_kernel,
        out_shape=jax.ShapeDtypeStruct(x.shape, x.dtype),
        in_specs=[IN_VMEM] + [ANYWHERE] * len(after),
        out_specs=IN_VMEM,
        input_output_aliases={0: 0},
        compiler_params=compiler(VMEM),
        name="hold",
    )(x, *after)


def squares_kernel(current_ref, stash_ref, *rest):
    rows_ref, sums = rest[-2:]
    step = pl.program_id(0)

    def total(x):
        wide = x.astype(F32)
        square = wide * wide
        return sum(square[:, i : i + HDIM] for i in range(0, square.shape[1], HDIM))

    for i, x in enumerate((current_ref[...], stash_ref[0], stash_ref[1])):
        part = total(x)

        @pl.when(step == 0)
        def _():
            sums[i] = part

        @pl.when(step > 0)
        def _():
            sums[i] += part

    @pl.when(step == pl.num_programs(0) - 1)
    def _():
        for i in range(3):
            rows_ref[i : i + 1, :] = jnp.sum(sums[i].T, axis=0, keepdims=True)


def squares(current, stash, lanes, after=()):
    tokens, width = current.shape
    return pl.pallas_call(
        squares_kernel,
        out_shape=jax.ShapeDtypeStruct((3, tokens), F32),
        grid=(width // lanes,),
        in_specs=[
            pl.BlockSpec((tokens, lanes), lambda i: (0, i)),
            pl.BlockSpec((None, 2, tokens, lanes), lambda i: (0, 0, 0, i)),
        ] + [ANYWHERE] * len(after),
        out_specs=pl.BlockSpec((3, tokens), lambda i: (0, 0)),
        scratch_shapes=[pltpu.VMEM((3, tokens, HDIM), F32)],
        compiler_params=compiler(MOST),
        name="squares",
    )(in_hbm(current), in_hbm(stash), *after)


def piece_kernel(starts, sizes, stash_ref, *rest):
    outs, mark, sems = rest[-2 - len(sizes) : -2], rest[-2], rest[-1]
    mark[...] = jnp.zeros_like(mark)
    copies = [
        pltpu.make_async_copy(stash_ref.at[(0, 1) + lanes_of(start, size)], out, sems.at[i])
        for i, (start, size, out) in enumerate(zip(starts, sizes, outs))
    ]
    for copy in copies:
        copy.start()
    for copy in copies:
        copy.wait()


def pieces_of(stash, starts, sizes, after=()):
    tokens = stash.shape[2]
    return pl.pallas_call(
        functools.partial(piece_kernel, starts, sizes),
        out_shape=[jax.ShapeDtypeStruct((tokens, size), BF16) for size in sizes] + [jax.ShapeDtypeStruct((8, HDIM), F32)],
        in_specs=[IN_HBM] + [ANYWHERE] * len(after),
        out_specs=[IN_VMEM] * (len(sizes) + 1),
        scratch_shapes=[pltpu.SemaphoreType.DMA((len(sizes),))],
        compiler_params=compiler(VMEM),
        name="pieces",
    )(in_hbm(stash), *after)


def in_rows(row, size):
    tokens = row.shape[1]
    rows = []
    for _ in range(3):
        term = row.astype(BF16)
        row = row - term.astype(F32)
        rows += [term[:, i : i + size] for i in range(0, tokens, size)]
    fill = -len(rows) % 16
    return jnp.concatenate(rows + [jnp.zeros((fill, size), BF16)] * (fill > 0), axis=0)


def row_kernel(extra_ref, o_ref):
    tokens, size = o_ref.shape[1], extra_ref.shape[1]
    each = tokens // size
    extra = extra_ref[...].astype(F32)
    for i in range(each):
        o_ref[:, i * size : (i + 1) * size] = sum(extra[p * each + i : p * each + i + 1] for p in range(3))


def row_from(piece, tokens):
    extra = piece.shape[0] - tokens
    size = piece.shape[1]
    return pl.pallas_call(
        row_kernel,
        out_shape=jax.ShapeDtypeStruct((1, tokens), F32),
        grid=(1,),
        in_specs=[pl.BlockSpec((extra, size), lambda i: (tokens // extra, 0))],
        out_specs=pl.BlockSpec((1, tokens), lambda i: (0, 0)),
        compiler_params=compiler(VMEM),
        name="row",
    )(piece)


def piece_and_row_kernel(start, stash_ref, t_ref, *rest):
    out, sem = rest[-2:]
    tokens, size = stash_ref.shape[2], out.shape[1]
    copy = pltpu.make_async_copy(stash_ref.at[(0, 1) + lanes_of(start, size)], out.at[:tokens, :], sem.at[0])
    copy.start()
    out[tokens:, :] = in_rows(t_ref[2:3, :], size)
    copy.wait()


def piece_and_row(stash, totals, start, size, after):
    tokens = stash.shape[2]
    extra = -(-3 * tokens // size // 16) * 16
    return pl.pallas_call(
        functools.partial(piece_and_row_kernel, start),
        out_shape=jax.ShapeDtypeStruct((tokens + extra, size), BF16),
        in_specs=[IN_HBM, IN_VMEM] + [ANYWHERE] * len(after),
        out_specs=IN_VMEM,
        scratch_shapes=[pltpu.SemaphoreType.DMA((1,))],
        compiler_params=compiler(VMEM),
        name="piece_and_row",
    )(in_hbm(stash), totals, *after)


def send(x, pairs):
    return lax.ppermute(x, "section", pairs)


def local(width_all, layer_input, grad_input, stashed, eviction, query_gain, key_gain):
    n = lax.axis_size("section")
    partner = [(s, (s + n // 2) % n) for s in range(n)]
    prior = [(s, (s - 1) % n) for s in range(n)]
    current = layer_input[0]
    tokens, width = current.shape
    count = width // HDIM
    each = max(1, count // 6)
    pieces = count // each
    size = each * HDIM
    third = count // 3 * HDIM

    *away, mark = pieces_of(stashed, (0, size), (size, size))
    fetched = [send(x, partner) for x in away]
    totals = lax.psum(squares(current, stashed, third, (mark,)), "tensor")
    output = forward(width_all, current, totals, query_gain, key_gain, third // HDIM)

    def fetch(p, after):
        away, mark = pieces_of(stashed, (p * size,), (size,), (fetched[p - 2], after))
        fetched.append(send(away, partner))
        return mark

    fetched.append(send(piece_and_row(stashed, totals, 2 * size, size, (fetched[0],)), partner))
    held = row_from(fetched[2], tokens)
    marks = [fetch(p, in_hbm(output)) for p in range(3, min(5, pieces))]
    base = max(1, count // 4) * HDIM

    def share(inner, first, last, sofar, after):
        heads = range(first // HDIM, last // HDIM)
        used = sorted({h // each for h in heads})
        found = tuple((used.index(h // each), h % each * HDIM) for h in heads)
        return backward(
            width_all, eviction, stashed, grad_input, totals, held, query_gain, key_gain, inner,
            [fetched[p] for p in used], found, first, base, sofar, after,
        )

    pair, inner = share(jnp.zeros((1, tokens), F32), 0, base, (), (in_hbm(output), *marks))
    marks = []
    sofar, inners = (), [inner]
    ends = sorted({base, max(base, 3 * size), *(p * size for p in range(4, pieces + 1))})
    for first, last in zip(ends[:-1], ends[1:]):
        *sofar, inner = share(inner, first, last, tuple(sofar), tuple(marks))
        inners.append(inner)
        marks = [fetch(p, inner) for p in range(len(fetched), pieces)]
    pair = send(hold(pair, (inners[-2],)), prior)
    inner = lax.psum(inner, "tensor")
    left = width - base
    cut = max(1, left // HDIM // 2) * HDIM
    ends = (*sofar, totals, held, inner)
    early, row = finish(width_all, eviction, *ends, 0, cut)
    early = send(early, prior)
    late, _ = finish(width_all, eviction, *ends, cut, left)
    result = place(pair, send(row, prior), early, send(late, prior))
    return (output[None], result[None])


def solution(mesh):
    placed = (
        P("section", None, "tensor"),
        P("section", None, "tensor"),
        P("section", None, None, "tensor"),
        P("section"),
        P("section", "tensor"),
        P("section", "tensor"),
    )

    def whole(layer_input, *others):
        return jax.shard_map(
            functools.partial(local, layer_input.shape[-1]),
            mesh=mesh,
            in_specs=placed,
            out_specs=(P("section", None, "tensor"), P("section", None, "tensor")),
            check_vma=False,
        )(layer_input, *others)

    return whole
```
